32 devices in a mesh: dp: 16 (over z, x, core), mp: 2 (over y).
Axes of the slice: x: 2, y: 2, z: 4, core: 2. Of those that a mesh axis runs over, the one named last changes fastest.
Arguments:
- tokens: bfloat16 [16, 8, 197, 768], P('dp'), may hold values from -6 to 6
- captions: bfloat16 [16, 512], P('dp'), may hold values from -0.29882812 to 0.29882812
- clip_groups: int32 [16], P('dp'), may hold values from 0 to 3, as said below
- caption_groups: int32 [16], P('dp'), may hold values from 0 to 3, as said below
- msg_weight: bfloat16 [768, 768], replicated, may hold values from -0.21875 to 0.21875
- msg_gain: float32 [768], replicated, may hold values from 0.5 to 1.5
- msg_in: bfloat16 [3, 768, 768], P(None, None, 'mp'), may hold values from -0.21875 to 0.21875
- msg_out: bfloat16 [768, 768], P('mp'), may hold values from -0.625 to 0.625
- frame_gain: float32 [768], replicated, may hold values from 0.5 to 1.5
- frame_in: bfloat16 [3, 768, 768], P(None, None, 'mp'), may hold values from -0.21875 to 0.21875
- frame_out: bfloat16 [768, 768], P('mp'), may hold values from -0.875 to 0.875
- mlp_gain: float32 [768], replicated, may hold values from 0.5 to 1.5
- up_weight: bfloat16 [768, 3072], P(None, 'mp'), may hold values from -0.21875 to 0.21875
- down_weight: bfloat16 [3072, 768], P('mp'), may hold values from -0.15625 to 0.15625
- proj_weight: bfloat16 [768, 512], replicated, may hold values from -0.21875 to 0.21875
- out_cot: bfloat16 [16, 8, 197, 768], P('dp'), may hold values from -6 to 6
Outputs:
- layer_out: bfloat16 [16, 8, 197, 768], P('dp')
- loss: float32 [], replicated
- token_grad: bfloat16 [16, 8, 197, 768], P('dp')
- caption_grad: float32 [16, 512], P('dp')
- msg_weight_grad: float32 [768, 768], P('dp')
- msg_gain_grad: float32 [768], P('dp')
- msg_in_grad: float32 [3, 768, 768], P(None, 'dp', 'mp')
- msg_out_grad: float32 [768, 768], P('mp', 'dp')
- frame_gain_grad: float32 [768], P('dp')
- frame_in_grad: float32 [3, 768, 768], P(None, 'dp', 'mp')
- frame_out_grad: float32 [768, 768], P('mp', 'dp')
- mlp_gain_grad: float32 [768], P('dp')
- up_grad: float32 [768, 3072], P('dp', 'mp')
- down_grad: float32 [3072, 768], P('mp', 'dp')
- proj_grad: float32 [768, 512], P('dp')
The draws below stay inside these ranges and needn't reach their ends.
Inputs may be any that keep to these rules, and one draw needn't show every extreme that they name: `clip_groups`: each video id is held by exactly 4 clips. `caption_groups`: each video id is held by exactly 4 captions.
All inputs are finite; a program needn't handle non-finite values.
Results may differ from the reference program's by a relative error of at most 0.025.
Values may be sent and summed in bfloat16 or wider, within the bound.
No kernel may reach another device: no remote copies, remote signals or barrier semaphores. Data moves between devices by JAX's collectives and lax.ppermute only.
A program may use at most 192 MiB of HBM per device.

```python
import jax
import jax.numpy as jnp
from jax import lax

D = 768
HEADS = 12
FF = 3072
EMBED = 512
FRAMES = 8
PATCHES = 197
CLIPS = 16


def draw_clip_groups(key, part):
    key = jax.random.fold_in(key, 11)
    return (jax.random.permutation(key, CLIPS) // 4).astype(jnp.int32)


def draw_caption_groups(key, part):
    key = jax.random.fold_in(key, 23)
    return (jax.random.permutation(key, CLIPS) // 4).astype(jnp.int32)


def level_of(rng, extent, cuts, smallest, largest):
    def one(dim, shards_of):
        draws = jax.random.uniform(jax.random.fold_in(jax.random.fold_in(rng, 6), dim), (shards_of,), jnp.float32, smallest / len(cuts), largest / len(cuts))
        return jnp.repeat(jnp.exp(draws), extent[dim] // shards_of).reshape((-1,) + (1,) * (len(extent) - dim - 1))

    loudness = one(*cuts[0])
    for cut in cuts[1:]:
        loudness = loudness * one(*cut)
    return loudness


def noise(own_key, dims, scale, most, pieces=(), dtype=jnp.bfloat16):
    entries = jax.random.normal(own_key, dims, jnp.float32) * scale
    if len(pieces) > 0:
        entries = level_of(own_key, dims, pieces, -0.22, 0.18) * entries
    return jnp.clip(entries, min=-most, max=most).astype(dtype)


def setup_inputs(seed: int = 0) -> dict:
    seeds = jax.random.split(jax.random.key(seed), 17)
    tokens = noise(seeds[0], (CLIPS, FRAMES, PATCHES, D), 1.0, 6.0, ((0, 16),))
    captions = noise(seeds[1], (CLIPS, EMBED), 0.05, 0.29882812, ((0, 16),))
    clip_groups = draw_clip_groups(jax.random.fold_in(seeds[16], 71), 0)
    caption_groups = draw_caption_groups(jax.random.fold_in(seeds[16], 71), 0)
    msg_weight = noise(seeds[4], (D, D), D ** -0.5, 0.21875)
    msg_gain = jnp.clip(1.0 + 0.1 * jax.random.normal(seeds[5], (D,), jnp.float32), 0.5, 1.5)
    msg_in = noise(seeds[6], (3, D, D), D ** -0.5, 0.21875, ((2, 2),))
    msg_out = noise(seeds[7], (D, D), (D // 8) ** -0.5, 0.625, ((0, 2),))
    frame_gain = jnp.clip(1.0 + 0.1 * jax.random.normal(seeds[8], (D,), jnp.float32), 0.5, 1.5)
    frame_in = noise(seeds[9], (3, D, D), D ** -0.5, 0.21875, ((2, 2),))
    frame_out = noise(seeds[10], (D, D), (D // 16) ** -0.5, 0.875, ((0, 2),))
    mlp_gain = jnp.clip(1.0 + 0.1 * jax.random.normal(seeds[11], (D,), jnp.float32), 0.5, 1.5)
    up_weight = noise(seeds[12], (D, FF), D ** -0.5, 0.21875, ((1, 2),))
    down_weight = noise(seeds[13], (FF, D), (FF // 2) ** -0.5, 0.15625, ((0, 2),))
    proj_weight = noise(seeds[14], (D, EMBED), D ** -0.5, 0.21875)
    out_cot = noise(seeds[15], (CLIPS, FRAMES, PATCHES, D), 1.0, 6.0, ((0, 16),))
    return dict(tokens=tokens, captions=captions, clip_groups=clip_groups, caption_groups=caption_groups, msg_weight=msg_weight, msg_gain=msg_gain, msg_in=msg_in, msg_out=msg_out, frame_gain=frame_gain, frame_in=frame_in, frame_out=frame_out, mlp_gain=mlp_gain, up_weight=up_weight, down_weight=down_weight, proj_weight=proj_weight, out_cot=out_cot)


@jax.custom_vjp
def low(v):
    return lax.optimization_barrier(v.astype(jnp.bfloat16)).astype(jnp.float32)

@jax.custom_vjp
def low_back(v):
    return v

def low_keep(v):
    return (low(v), None)

def low_pass(kept, grad):
    return (grad,)

def back_keep(v):
    return (v, None)

def back_low(kept, grad):
    return (low(grad),)
low.defvjp(low_keep, low_pass)
low_back.defvjp(back_keep, back_low)
softmax_sharpness_factor = 50.0
exact_matmul_mode = lax.Precision.HIGHEST
lowest = -1e+30

def layer_norm(value, gain):
    centered = value - lax.optimization_barrier(jnp.mean(value, axis=-1, keepdims=True))
    variance = lax.optimization_barrier(jnp.mean(centered * centered, axis=-1, keepdims=True))
    return centered * lax.rsqrt(variance + 1e-05) * gain

def linear(value, weight):
    return jnp.einsum('...d,de->...e', value, weight, precision=exact_matmul_mode)

def attend(normed, w_in, w_out):
    batch, length, width = normed.shape
    head_size = width // HEADS

    def split(which):
        return low(low_back(linear(normed, w_in[which]))).reshape(batch, length, HEADS, head_size)
    query = split(0)
    keys = split(1)
    values = split(2)
    scores = low_back(jnp.einsum('bqhe,bkhe->bhqk', query, keys, precision=exact_matmul_mode) * head_size ** (-0.5))
    weights = jax.nn.softmax(scores, axis=-1)
    context = jnp.einsum('bhqk,bkhe->bqhe', low(weights), values, precision=exact_matmul_mode)
    context = low(low_back(context.reshape(batch, length, width)))
    return low_back(linear(context, w_out))

def one_clip(params, clip):
    msg_weight, msg_gain, msg_in, msg_out, frame_gain, frame_in, frame_out, mlp_gain, up_weight, down_weight = params
    patches = clip.shape[1]
    message = low_back(linear(clip[:, 0, :], msg_weight))
    message = message + attend(low(layer_norm(message, msg_gain))[None], msg_in, msg_out)[0]
    stream = jnp.concatenate([clip, message[:, None, :]], axis=1)
    stream = stream + attend(low(layer_norm(stream, frame_gain)), frame_in, frame_out)
    hidden = low_back(linear(low(layer_norm(stream, mlp_gain)), up_weight))
    activ = low(hidden * jax.nn.sigmoid(1.702 * hidden))
    stream = stream + low_back(linear(activ, down_weight))
    return (stream[:, :patches, :], lax.optimization_barrier(jnp.mean(stream[:, 0, :], axis=0)))

def contrast(pooled, captions, proj_weight, clip_groups, caption_groups):
    embed = low_back(linear(low(pooled), proj_weight))
    normalized_clip_vectors = low(embed * lax.rsqrt(lax.optimization_barrier(jnp.sum(embed * embed, axis=-1, keepdims=True)) + 1e-06))
    normalized_text_vectors = low(captions * lax.rsqrt(lax.optimization_barrier(jnp.sum(captions * captions, axis=-1, keepdims=True)) + 1e-06))
    cosine_match_matrix = low_back(softmax_sharpness_factor * jnp.einsum('bq,kq->bk', normalized_clip_vectors, normalized_text_vectors, precision=exact_matmul_mode))
    positive = clip_groups[:, None] == caption_groups[None, :]
    masked = jnp.where(positive, cosine_match_matrix, lowest)
    rows = jax.nn.logsumexp(cosine_match_matrix, axis=1) - jax.nn.logsumexp(masked, axis=1)
    columns = jax.nn.logsumexp(cosine_match_matrix, axis=0) - jax.nn.logsumexp(masked, axis=0)
    return 0.5 * (jnp.sum(rows) + jnp.sum(columns))

def reference(tokens, captions, clip_groups, caption_groups, msg_weight, msg_gain, msg_in, msg_out, frame_gain, frame_in, frame_out, mlp_gain, up_weight, down_weight, proj_weight, out_cot):

    def forward(tokens_f, captions_f, msg_weight_f, msg_gain_f, msg_in_f, msg_out_f, frame_gain_f, frame_in_f, frame_out_f, mlp_gain_f, up_f, down_f, proj_f):
        params = (msg_weight_f, msg_gain_f, msg_in_f, msg_out_f, frame_gain_f, frame_in_f, frame_out_f, mlp_gain_f, up_f, down_f)

        def run_clip(clip):
            return one_clip(params, clip)
        outputs, pooled = lax.map(jax.checkpoint(run_clip), tokens_f)
        loss = contrast(pooled, captions_f, proj_f, clip_groups, caption_groups)
        return (outputs, loss)
    floats = (tokens.astype(jnp.float32), captions.astype(jnp.float32), msg_weight.astype(jnp.float32), msg_gain.astype(jnp.float32), msg_in.astype(jnp.float32), msg_out.astype(jnp.float32), frame_gain.astype(jnp.float32), frame_in.astype(jnp.float32), frame_out.astype(jnp.float32), mlp_gain.astype(jnp.float32), up_weight.astype(jnp.float32), down_weight.astype(jnp.float32), proj_weight.astype(jnp.float32))
    (outputs, loss), pullback = jax.vjp(forward, *floats)
    grads = pullback((out_cot.astype(jnp.float32), jnp.ones((), jnp.float32)))
    return (outputs.astype(jnp.bfloat16), loss, grads[0].astype(jnp.bfloat16), grads[1], grads[2], grads[3], grads[4], grads[5], grads[6], grads[7], grads[8], grads[9], grads[10], grads[11], grads[12])
```

```python
import jax
import jax.numpy as jnp
from jax import lax
from jax.sharding import PartitionSpec as P

HEADS = 12
SHARPNESS = 50.0
LOWEST = -1e30
BF = jnp.bfloat16
F32 = jnp.float32


def swap(value):
    return lax.ppermute(value, "mp", [(0, 1), (1, 0)])


def flip(value, bit):
    size = lax.axis_size("dp")
    return lax.ppermute(value, "dp", [(i, i ^ bit) for i in range(size)])


def bits_of(size):
    bits = []
    bit = 1
    while bit < size:
        bits.append(bit)
        bit *= 2
    return bits


def row_order(size):
    bits = bits_of(size)
    order = []
    for p in range(size):
        mask = 0
        for k, bit in enumerate(bits):
            if (p >> (len(bits) - 1 - k)) & 1:
                mask |= bit
        order.append(mask)
    return order


def own_first(rows_first):
    size = lax.axis_size("dp")
    me = lax.axis_index("dp")
    blocks = rows_first.reshape((size, rows_first.shape[0] // size) + rows_first.shape[1:])
    order = jnp.bitwise_xor(jnp.asarray(row_order(size), jnp.int32), me)
    return jnp.take(blocks, order, axis=0).reshape(rows_first.shape)


def halve(value, bit, dtype=BF):
    rows = value.shape[-2] // 2
    keep, send = value[..., :rows, :], value[..., rows:, :]
    got = flip(send, bit)
    return (keep.astype(F32) + got.astype(F32)).astype(dtype)


def reduce_rows(value):
    bits = bits_of(lax.axis_size("dp"))
    value = halve(value, bits[0])
    value = (value[0].astype(F32) + swap(value[1]).astype(F32)).astype(BF)
    for bit in bits[1:-1]:
        value = halve(value, bit)
    return halve(value, bits[-1], F32)


def norm_forward(value, gain):
    centered = value - jnp.mean(value, axis=-1, keepdims=True)
    rstd = lax.rsqrt(jnp.mean(centered * centered, axis=-1, keepdims=True) + 1e-05)
    normal = centered * rstd
    return ((normal * gain).astype(BF), normal, rstd)


def norm_backward(grad, gain, normal, rstd):
    scaled = grad * gain
    inner = (
        scaled
        - jnp.mean(scaled, axis=-1, keepdims=True)
        - normal * jnp.mean(scaled * normal, axis=-1, keepdims=True)
    )
    gain_grad = jnp.sum((grad * normal).reshape(-1, grad.shape[-1]), axis=0)
    return (rstd * inner, gain_grad)


def dot(a, b):
    return jnp.dot(a, b, preferred_element_type=F32)


def attn_forward(normed, w_in, w_out, valid):
    batch, length, width = normed.shape
    head_size = width // HEADS
    local = w_in.shape[2]
    packed = jnp.einsum("bsd,kde->kbse", normed, w_in, preferred_element_type=F32).astype(BF)
    shape = (batch, length, local // head_size, head_size)
    query, keys, values = (packed[k].reshape(shape) for k in range(3))
    scores = jnp.einsum("bqhe,bkhe->bhqk", query, keys, preferred_element_type=F32) * head_size ** (-0.5)
    if valid < length:
        scores = jnp.where(jnp.arange(length) < valid, scores, LOWEST)
    top = jnp.max(scores, axis=-1, keepdims=True)
    logsum = top + jnp.log(jnp.sum(jnp.exp(scores - top), axis=-1, keepdims=True))
    weights = jnp.exp(scores - logsum).astype(BF)
    context = jnp.einsum("bhqk,bkhe->bqhe", weights, values, preferred_element_type=F32)
    context = context.reshape(batch, length, local).astype(BF)
    branch = jnp.einsum("bse,ed->bsd", context, w_out, preferred_element_type=F32)
    return (branch, (query, keys, values, logsum, context))


def attn_backward(w_in, w_out, kept, grad_low, valid):
    query, keys, values, logsum, context = kept
    batch, length, heads, head_size = query.shape
    scale = head_size ** (-0.5)
    context_grad = jnp.einsum("bsd,ed->bse", grad_low, w_out, preferred_element_type=F32)
    context_grad = context_grad.astype(BF).reshape(batch, length, heads, head_size)
    scores = jnp.einsum("bqhe,bkhe->bhqk", query, keys, preferred_element_type=F32) * scale
    if valid < length:
        scores = jnp.where(jnp.arange(length) < valid, scores, LOWEST)
    weights = jnp.exp(scores - logsum)
    weight_grad = jnp.einsum("bqhe,bkhe->bhqk", context_grad, values, preferred_element_type=F32)
    value_grad = jnp.einsum("bhqk,bqhe->bkhe", weights.astype(BF), context_grad, preferred_element_type=F32)
    score_grad = (weights * (weight_grad - jnp.sum(weights * weight_grad, axis=-1, keepdims=True))).astype(BF)
    query_grad = jnp.einsum("bhqk,bkhe->bqhe", score_grad, keys, preferred_element_type=F32) * scale
    key_grad = jnp.einsum("bhqk,bqhe->bkhe", score_grad, query, preferred_element_type=F32) * scale
    stacked = (
        jnp.stack([query_grad, key_grad, value_grad]).reshape(3, batch, length, heads * head_size).astype(BF)
    )
    normed_grad = jnp.einsum("kbse,kde->bsd", stacked, w_in, preferred_element_type=F32)
    return (normed_grad, stacked)


def contrast(pooled_all, captions_all, clip_groups, caption_groups, proj_weight):
    embed = dot(pooled_all, proj_weight)
    embed_rinv = lax.rsqrt(jnp.sum(embed * embed, axis=-1, keepdims=True) + 1e-06)
    embed_low = (embed * embed_rinv).astype(BF)
    caption_f = captions_all.astype(F32)
    caption_rinv = lax.rsqrt(jnp.sum(caption_f * caption_f, axis=-1, keepdims=True) + 1e-06)
    caption_low = (caption_f * caption_rinv).astype(BF)
    scores = SHARPNESS * dot(embed_low, caption_low.T)
    positive = clip_groups[:, None] == caption_groups[None, :]
    masked = jnp.where(positive, scores, LOWEST)

    def side(axis):
        top = jnp.max(scores, axis=axis, keepdims=True)
        each = jnp.exp(scores - top)
        total = jnp.sum(each, axis=axis, keepdims=True)
        pos_top = jnp.max(masked, axis=axis, keepdims=True)
        pos_each = jnp.where(positive, jnp.exp(masked - pos_top), 0.0)
        pos_total = jnp.sum(pos_each, axis=axis, keepdims=True)
        part = jnp.sum(top + jnp.log(total) - pos_top - jnp.log(pos_total))
        return (part, each / total - pos_each / pos_total)

    row_loss, row_grad = side(1)
    column_loss, column_grad = side(0)
    loss = 0.5 * (row_loss + column_loss)
    dscore = (0.5 * (row_grad + column_grad)).astype(BF)
    embed_grad = SHARPNESS * dot(dscore, caption_low)
    caps_grad = SHARPNESS * dot(dscore.T, embed_low)
    caption_grad = caption_rinv * caps_grad - caption_f * caption_rinv**3 * jnp.sum(
        caption_f * caps_grad, axis=-1, keepdims=True
    )
    embed_diff = embed_rinv * embed_grad - embed * embed_rinv**3 * jnp.sum(
        embed * embed_grad, axis=-1, keepdims=True
    )
    return (loss, caption_grad, embed_diff.astype(BF))


def on_device(
    tokens,
    captions,
    clip_groups,
    caption_groups,
    msg_weight,
    msg_gain,
    msg_in,
    msg_out,
    frame_gain,
    frame_in,
    frame_out,
    mlp_gain,
    up_weight,
    down_weight,
    proj_weight,
    out_cot,
):
    clips, frames, patches, width = tokens.shape
    valid = patches + 1
    seq = -(-valid // 16) * 16
    half = frames // lax.axis_size("mp")
    me_dp, me_mp = (lax.axis_index("dp"), lax.axis_index("mp"))
    share = width // lax.axis_size("dp")

    def gather(value):
        return lax.all_gather(value, "dp", axis=0, tiled=True)

    def mine(value, axis=1):
        return lax.dynamic_slice_in_dim(value, me_dp * share, share, axis)

    def own(value):
        return lax.dynamic_slice_in_dim(value, me_mp * half, half, 1)

    def both(value):
        other = swap(value)
        first = jnp.where(me_mp == 0, value, other)
        second = jnp.where(me_mp == 0, other, value)
        return jnp.concatenate([first, second], axis=1)

    w_in = jnp.concatenate([frame_in, swap(frame_in)], axis=2)
    w_out = jnp.concatenate([frame_out, swap(frame_out)], axis=0)
    w_up = jnp.concatenate([up_weight, swap(up_weight)], axis=1)
    w_down = jnp.concatenate([down_weight, swap(down_weight)], axis=0)

    cls_tokens = tokens[:, :, 0, :]
    message = jnp.einsum("cfd,de->cfe", cls_tokens, msg_weight, preferred_element_type=F32)
    msg_low, msg_hat, msg_rstd = norm_forward(message, msg_gain)
    msg_part, msg_kept = attn_forward(msg_low, msg_in, msg_out, frames)
    message_next = message + (msg_part + swap(msg_part))

    pad = jnp.zeros((clips, half, seq - valid, width), F32)
    stream = jnp.concatenate([own(tokens).astype(F32), own(message_next)[:, :, None, :], pad], axis=2)
    stream = stream.reshape(clips * half, seq, width)
    frame_low, frame_hat, frame_rstd = norm_forward(stream, frame_gain)
    branch, frame_kept = attn_forward(frame_low, w_in, w_out, valid)
    middle = stream + branch
    mlp_low, mlp_hat, mlp_rstd = norm_forward(middle, mlp_gain)
    rows = clips * half * seq
    mlp_low = mlp_low.reshape(rows, width)
    hidden = dot(mlp_low, w_up)
    sigmo = jax.nn.sigmoid(1.702 * hidden)
    activ = (hidden * sigmo).astype(BF)
    slope = sigmo + 1.702 * hidden * sigmo * (1.0 - sigmo)
    result = (middle + dot(activ, w_down).reshape(middle.shape)).reshape(clips, half, seq, width)
    layer_out = both(result[:, :, :patches, :].astype(BF))

    pooled = jnp.sum(result[:, :, 0, :], axis=1)
    pooled_low = ((pooled + swap(pooled)) / frames).astype(BF)
    pooled_all = gather(pooled_low)
    ids = jnp.stack([clip_groups, caption_groups], axis=1)
    ids_all = gather(ids)
    loss, caption_grad_all, embed_dlow = contrast(
        pooled_all, gather(captions), ids_all[:, 0], ids_all[:, 1], proj_weight
    )
    caption_grad = lax.dynamic_slice_in_dim(caption_grad_all, me_dp * clips, clips, 0)
    proj_share = dot(mine(pooled_all).T, embed_dlow)
    embed_own = lax.dynamic_slice_in_dim(embed_dlow, me_dp * clips, clips, 0)
    pooled_grad = dot(embed_own, proj_weight.T)

    grad_stream = jnp.concatenate(
        [own(out_cot).astype(F32), jnp.zeros((clips, half, seq - patches, width), F32)], axis=2
    )
    grad_stream = grad_stream.at[:, :, 0, :].add(pooled_grad[:, None, :] / frames)
    grad_low = grad_stream.astype(BF).reshape(rows, width)
    grad_stream = grad_stream.reshape(clips * half, seq, width)
    f_half = w_up.shape[1] // 2

    def columns(value):
        return jnp.stack([value[:, : value.shape[1] // 2], value[:, value.shape[1] // 2 :]])

    down_t = jnp.einsum("dr,mrf->mdf", own_first(grad_low.T), columns(activ), preferred_element_type=F32)
    down_share = reduce_rows(down_t.astype(BF)).T
    hidden_low = (dot(grad_low, w_down.T) * slope).astype(BF)
    up_grad = jnp.einsum("dr,mrf->mdf", own_first(mlp_low.T), columns(hidden_low), preferred_element_type=F32)
    up_share = reduce_rows(up_grad.astype(BF))
    mlp_normed_grad = dot(hidden_low, w_up.T).reshape(middle.shape)
    middle_part, mlp_gain_grad = norm_backward(mlp_normed_grad, mlp_gain, mlp_hat, mlp_rstd)
    middle_grad = grad_stream + middle_part
    middle_low = middle_grad.astype(BF)
    frame_normed_grad, stacked = attn_backward(w_in, w_out, frame_kept, middle_low, valid)
    stream_part, frame_gain_grad = norm_backward(frame_normed_grad, frame_gain, frame_hat, frame_rstd)
    stream_grad = (middle_grad + stream_part).reshape(clips, half, seq, width)
    h_half = w_in.shape[2] // 2
    stacked = stacked.reshape(3, rows, 2, h_half).transpose(2, 1, 0, 3).reshape(2, rows, 3 * h_half)
    in_grad = jnp.einsum(
        "dr,mrf->mdf", own_first(frame_low.reshape(rows, width).T), stacked, preferred_element_type=F32
    )
    in_share = reduce_rows(in_grad.astype(BF)).reshape(share, 3, h_half).transpose(1, 0, 2)
    out_t = jnp.einsum(
        "dr,mrf->mdf",
        own_first(middle_low.reshape(rows, width).T),
        columns(frame_kept[4].reshape(rows, width)),
        preferred_element_type=F32,
    )
    out_share = reduce_rows(out_t.astype(BF)).T

    next_grad = both(stream_grad[:, :, patches, :])
    next_low = next_grad.astype(BF)
    msg_normed_part, msg_stacked = attn_backward(msg_in, msg_out, msg_kept, next_low, frames)
    msg_normed_grad = msg_normed_part + swap(msg_normed_part)
    message_part, msg_gain_grad = norm_backward(msg_normed_grad, msg_gain, msg_hat, msg_rstd)
    message_low = (next_grad + message_part).astype(BF)
    cls_grad = jnp.einsum("cfe,de->cfd", message_low, msg_weight, preferred_element_type=F32)
    token_own = stream_grad[:, :, :patches, :].at[:, :, 0, :].add(own(cls_grad)).astype(BF)
    token_grad = both(token_own)

    def flat(value):
        return value.reshape(clips * frames, value.shape[-1])

    factors = jnp.concatenate(
        [
            flat(cls_tokens),
            flat(message_low),
            flat(msg_low),
            flat(msg_stacked.transpose(1, 2, 0, 3).reshape(clips, frames, -1)),
            flat(msg_kept[4]),
            flat(next_low),
        ],
        axis=1,
    )
    factors = gather(factors)
    at = 0
    parts = []
    for wide in (width, width, width, 3 * h_half, h_half, width):
        parts.append(factors[:, at : at + wide])
        at += wide
    msg_weight_share = dot(mine(parts[0]).T, parts[1])
    msg_in_share = dot(mine(parts[2]).T, parts[3]).reshape(share, 3, h_half).transpose(1, 0, 2)
    msg_out_share = dot(parts[4].T, mine(parts[5]))
    gains = jnp.stack([mlp_gain_grad, frame_gain_grad])
    gains = gains + swap(gains)
    gains = jnp.concatenate([gains, msg_gain_grad[None]], axis=0)
    gains = jnp.sum(gather(gains[None]), axis=0)
    gains = mine(gains)
    return (
        layer_out,
        loss,
        token_grad,
        caption_grad,
        msg_weight_share,
        gains[2],
        msg_in_share,
        msg_out_share,
        gains[1],
        in_share,
        out_share,
        gains[0],
        up_share,
        down_share,
        proj_share,
    )


def solution(mesh):
    in_specs = (
        P("dp", None, None, None),
        P("dp", None),
        P("dp"),
        P("dp"),
        P(),
        P(),
        P(None, None, "mp"),
        P("mp", None),
        P(),
        P(None, None, "mp"),
        P("mp", None),
        P(),
        P(None, "mp"),
        P("mp", None),
        P(),
        P("dp", None, None, None),
    )
    out_specs = (
        P("dp", None, None, None),
        P(),
        P("dp", None, None, None),
        P("dp", None),
        P("dp", None),
        P("dp"),
        P(None, "dp", "mp"),
        P("mp", "dp"),
        P("dp"),
        P(None, "dp", "mp"),
        P("mp", "dp"),
        P("dp"),
        P("dp", "mp"),
        P("mp", "dp"),
        P("dp", None),
    )
    return jax.shard_map(
        on_device, mesh=mesh, in_specs=in_specs, out_specs=out_specs, check_vma=False
    )
```

```python
import functools

import jax
import jax.numpy as jnp
from jax import lax
from jax.experimental import pallas as pl
from jax.experimental.pallas import tpu as pltpu
from jax.sharding import PartitionSpec as P

HEADS = 12
SHARPNESS = 50.0
LOWEST = -1e30
BF = jnp.bfloat16
F32 = jnp.float32
VMEM_BYTES = 52 * 1024 * 1024
KERNEL_US = {
    "frame_first": 7,
    "cotangent": 4,
    "frame_second": 6,
    "mlp_first": 16,
    "mlp_second": 5,
    "mlp_third": 5,
    "hidden_backward_a": 5,
    "hidden_backward_b": 5,
    "class_backward": 5,
    "mlp_weight_first": 8,
    "mlp_weight_second": 7,
    "frame_backward_a": 14,
    "frame_backward_b": 14,
    "frame_weights": 11,
}


def swap(value):
    return lax.ppermute(value, "mp", [(0, 1), (1, 0)])


def flip(value, bit):
    size = lax.axis_size("dp")
    return lax.ppermute(value, "dp", [(i, i ^ bit) for i in range(size)])


def after(value, *deps):
    return lax.optimization_barrier((value,) + deps)[0]


def bits_of(size):
    return [1 << k for k in range(size.bit_length() - 1)]


def row_order(bits):
    order = [0]
    for bit in reversed(bits):
        order = order + [mask | bit for mask in order]
    return order


def mlp_ways(bits):
    return (bits[:1] + ["mp"] + bits[1:], bits[1:] + bits[:1] + ["mp"])


def frame_ways(bits):
    return (bits[:1] + ["mp"] + bits[1:], ["mp"] + bits)


def gather_bits():
    bits = bits_of(lax.axis_size("dp"))
    return bits[1:] + bits[:1]


def gather(value):
    for bit in gather_bits():
        value = jnp.concatenate([value, flip(value, bit)], axis=0)
    return value


def dot(a, b):
    return jnp.dot(a, b, preferred_element_type=F32)


def dot_nt(a, b):
    return lax.dot_general(a, b, (((1,), (1,)), ((), ())), preferred_element_type=F32)


def dot_tn(a, b):
    return lax.dot_general(a, b, (((0,), (0,)), ((), ())), preferred_element_type=F32)


def standardized(value):
    centered = value - jnp.mean(value, axis=-1, keepdims=True)
    rstd = lax.rsqrt(jnp.mean(centered * centered, axis=-1, keepdims=True) + 1e-05)
    return (centered * rstd, rstd)


def norm_backward(grad, gain, normal, rstd):
    scaled = grad * gain
    inner = (
        scaled
        - jnp.mean(scaled, axis=-1, keepdims=True)
        - normal * jnp.mean(scaled * normal, axis=-1, keepdims=True)
    )
    return (rstd * inner, jnp.sum(grad * normal, axis=0, keepdims=True))


def lane_half(rows, pair, which):
    lane = lax.broadcasted_iota(jnp.int32, (rows, pair), 1)
    return (lane < pair // 2) if which == 0 else (lane >= pair // 2)


def only(value, which):
    return jnp.where(lane_half(*value.shape, which), value, jnp.zeros_like(value))


def attend_pair(query, keys, values, valid):
    rows, pair = query.shape
    out = None
    for which in range(2):
        scores = dot_nt(only(query, which), keys)
        if valid < rows:
            key = lax.broadcasted_iota(jnp.int32, scores.shape, 1)
            scores = jnp.where(key < valid, scores, LOWEST)
        top = jnp.max(scores, axis=1, keepdims=True)
        each = jnp.exp(scores - top)
        total = jnp.sum(each, axis=1, keepdims=True)
        part = dot(each.astype(BF), only(values, which)) * (1.0 / total)
        out = part if out is None else out + part
    return out


def attend_pair_backward(query, keys, values, grad, valid, scale):
    rows, _ = query.shape
    sums = [None, None, None]
    for which in range(2):
        query_own, key_own, grad_own = (only(query, which), only(keys, which), only(grad, which))
        scores = dot_nt(keys, query_own)
        if valid < rows:
            key = lax.broadcasted_iota(jnp.int32, scores.shape, 0)
            scores = jnp.where(key < valid, scores, LOWEST)
        top = jnp.max(scores, axis=0, keepdims=True)
        each = jnp.exp(scores - top)
        weights = each * (1.0 / jnp.sum(each, axis=0, keepdims=True))
        weight_grad = dot_nt(values, grad_own)
        value_grad = dot(weights.astype(BF), grad_own)
        inner = jnp.sum(weights * weight_grad, axis=0, keepdims=True)
        score_grad = (weights * (weight_grad - inner)).astype(BF)
        key_grad = dot(score_grad, query_own)
        query_grad = dot_tn(score_grad, key_own) * scale
        parts = (query_grad, key_grad, value_grad)
        sums = [part if one is None else one + part for one, part in zip(sums, parts)]
    return [one.astype(BF) for one in sums]


def project(normed, in_ref, scale):
    wide = in_ref.shape[2]
    query = dot(normed, in_ref[0]).astype(BF) * jnp.asarray(scale, BF)
    keys = dot(normed, in_ref[1]).astype(BF)
    values = dot(normed, in_ref[2]).astype(BF)
    return (query, keys, values, wide)


def split_rows(ways, count, which, keep_ref, send_ref, lead, value, place_ref):
    rows = keep_ref.shape[1]
    pairs = 8 if count is None else 1 << count
    block = rows // pairs
    me = place_ref[1]
    first = (me & 1) == 0
    for j in range(pairs):
        even = value[2 * block * j : 2 * block * j + block]
        odd = value[2 * block * j + block : 2 * block * (j + 1)]
        if count is None:
            keep_ref[lead, block * j : block * (j + 1), :] = even.astype(BF)
            send_ref[lead, block * j : block * (j + 1), :] = odd.astype(BF)
            continue
        mask = (me >> 1) ^ j
        order = [k for k in ways(list(range(count)))[which] if k != "mp"]
        spot = sum(((mask >> k) & 1) << (count - 1 - i) for i, k in enumerate(order))
        at = pl.ds(pl.multiple_of(spot * block, 16), block)
        keep_ref[lead, at, :] = jnp.where(first, even, odd).astype(BF)
        send_ref[lead, at, :] = jnp.where(first, odd, even).astype(BF)


def frame_rows(wide_ref, frame, patches):
    at = pl.ds(frame, patches, stride=8)
    return jnp.concatenate([wide_ref[j, at, :] for j in range(wide_ref.shape[0])], axis=1)


def widen(wide_ref, from_ref):
    for j in range(wide_ref.shape[0]):
        value = from_ref[:, :, 128 * j : 128 * (j + 1)].astype(F32)
        wide_ref[j] = value.reshape(wide_ref.shape[1:])


def put_class_rows(to_ref, rows_ref, half):
    seq = to_ref.shape[0] // half
    for f in range(half):
        old = to_ref[f * seq : f * seq + 16, :].astype(F32)
        row = lax.broadcasted_iota(jnp.int32, old.shape, 0)
        new = jnp.where(row == 0, rows_ref[f : f + 1, :].astype(F32), old)
        to_ref[f * seq : f * seq + 16, :] = new.astype(to_ref.dtype)


def class_rows(from_ref, half, dtype, count):
    seq = from_ref.shape[0] // half
    rows = [from_ref[f * seq : f * seq + 16, :].astype(F32)[0:1] for f in range(half)]
    rows.append(jnp.zeros((count - half, from_ref.shape[1]), F32))
    return jnp.concatenate(rows, axis=0).astype(dtype)


def message_forward_kernel(
    heads, place_ref, tok_ref, captions_ref, w_ref, gain_ref, in_ref, out_ref, message_ref, early_ref, qkv_ref, part_ref
):
    cls = tok_ref[0, 0]
    frames, width = cls.shape
    message = dot(cls, w_ref[...])
    message_ref[...] = message
    normal, _ = standardized(message)
    low = (normal * gain_ref[...]).astype(BF)
    size = width // heads
    query, keys, values, wide = project(low, in_ref, size**-0.5)
    contexts = []
    for j in range(wide // (2 * size)):
        at = slice(2 * size * j, 2 * size * (j + 1))
        contexts.append(attend_pair(query[:, at], keys[:, at], values[:, at], frames))
    context = jnp.concatenate(contexts, axis=1).astype(BF)
    part_ref[...] = dot(context, out_ref[...])
    qkv_ref[:, :wide] = query
    qkv_ref[:, wide : 2 * wide] = keys
    qkv_ref[:, 2 * wide :] = values

    def padded(value):
        value = value.astype(F32)
        return jnp.concatenate([value, jnp.zeros((16 - value.shape[0], value.shape[1]), F32)], axis=0)

    early_ref[:, width : 2 * width] = padded(low).astype(BF)
    early_ref[:, 2 * width :] = padded(context).astype(BF)
    embed = captions_ref.shape[1]
    lane = lax.broadcasted_iota(jnp.int32, (1, width - embed), 1)
    ids = jnp.where(lane == 0, place_ref[2], jnp.where(lane == 1, place_ref[3], 0)).astype(F32)
    text = jnp.concatenate([captions_ref[...].astype(F32), ids], axis=1)
    row = lax.broadcasted_iota(jnp.int32, (8, width), 0)
    text = jnp.where(row == 0, text, 0.0)
    early_ref[:, :width] = jnp.concatenate([cls.astype(F32), text], axis=0).astype(BF)


def frame_attention(heads, valid, low, in_ref, qkv_ref, context_ref):
    size = low.shape[1] // heads
    wide = in_ref.shape[2]
    for k in range(3):
        value = dot(low, in_ref[k]).astype(BF)
        if k == 0:
            value = value * jnp.asarray(size**-0.5, BF)
        qkv_ref[0, :, wide * k : wide * (k + 1)] = value
    for j in range(wide // (2 * size)):
        query, keys, values = (
            qkv_ref[0, :, wide * k + 2 * size * j : wide * k + 2 * size * (j + 1)] for k in range(3)
        )
        context_ref[0, :, 2 * size * j : 2 * size * (j + 1)] = attend_pair(query, keys, values, valid).astype(BF)


def frame_first_kernel(
    heads, half, place_ref, tok_ref, message_ref, part_ref, other_ref, gain_ref, in_ref,
    stream_ref, low_ref, qkv_ref, context_ref, wide_ref,
):
    patches, frames, width = tok_ref.shape
    seq = stream_ref.shape[1]
    frame = place_ref[0] * half + pl.program_id(0)

    @pl.when(pl.program_id(0) == 0)
    def _():
        widen(wide_ref, tok_ref)

    at = pl.ds(frame, 1)
    message = message_ref[at, :] + (part_ref[at, :] + other_ref[at, :])
    edge = patches // 8 * 8
    stream_ref[0, edge:seq, :] = jnp.zeros((seq - edge, width), F32)
    stream_ref[0, 0:patches, :] = frame_rows(wide_ref, frame, patches)
    stream_ref[0, patches : patches + 1, :] = message
    normal, _ = standardized(stream_ref[0])
    low = (normal * gain_ref[...]).astype(BF)
    low_ref[0] = low
    frame_attention(heads, patches + 1, low, in_ref, qkv_ref, context_ref)


def joined(place_ref, to_ref, mine_ref, theirs_ref, axis):
    rows = mine_ref.shape[axis]
    core = place_ref[1] & 1
    lead = (slice(None),) * axis
    to_ref[lead + (pl.ds(pl.multiple_of(core * rows, 16), rows),)] = mine_ref[...]
    to_ref[lead + (pl.ds(pl.multiple_of((1 - core) * rows, 16), rows),)] = theirs_ref[...]


def frame_second_kernel(heads, valid, place_ref, low_ref, mine_ref, theirs_ref, qkv_ref, context_ref, in_ref):
    @pl.when(pl.program_id(0) == 0)
    def _():
        joined(place_ref, in_ref, mine_ref, theirs_ref, 1)

    frame_attention(heads, valid, low_ref[0], in_ref, qkv_ref, context_ref)


def cotangent_kernel(half, place_ref, cot_ref, down_ref, grad_ref, dact_ref, wide_ref):
    patches, frames, width = cot_ref.shape
    seq = grad_ref.shape[0] // half

    @pl.when(pl.program_id(0) == 0)
    def _():
        widen(wide_ref, cot_ref)
        edge = patches // 16 * 16
        for f in range(half):
            value = frame_rows(wide_ref, place_ref[0] * half + f, patches)
            tail = jnp.concatenate([value[edge:], jnp.zeros((seq - patches, width), F32)], axis=0)
            grad_ref[f * seq : f * seq + edge, :] = value[:edge].astype(BF)
            grad_ref[f * seq + edge : (f + 1) * seq, :] = tail.astype(BF)

    dact_ref[...] = dot_nt(grad_ref[...], down_ref[...]).astype(BF)


def gate(hidden):
    sigmo = 1.0 / (1.0 + jnp.exp(-1.702 * hidden))
    gated = hidden * sigmo
    return (gated, sigmo + 1.702 * gated * (1.0 - sigmo))


def up_block(ref):
    return ref[...].reshape(ref.shape[0] * ref.shape[1], ref.shape[2])


def mlp_first_kernel(
    half, place_ref, stream_ref, own_ref, other_ref, out_own_ref, mine_ref, theirs_ref, gain_ref, up_ref, down_ref, dact_ref,
    middle_ref, low_ref, activ_ref, dhid_ref, slope_ref, total_ref, back_ref, cls_low_ref, cls_total_ref, out_other_ref,
):
    step = pl.program_id(0)

    @pl.when(step == 0)
    def _():
        joined(place_ref, out_other_ref, mine_ref, theirs_ref, 0)
        branch = dot(own_ref[...], out_own_ref[...]) + dot(other_ref[...], out_other_ref[...])
        middle = stream_ref[...] + branch
        middle_ref[...] = middle
        normal, _ = standardized(middle)
        low_ref[...] = (normal * gain_ref[...]).astype(BF)
        total_ref[...] = middle
        back_ref[...] = jnp.zeros_like(back_ref)
        cls_low_ref[...] = class_rows(low_ref, half, BF, 16)

    seq = low_ref.shape[0] // half
    activ, slope = gate(dot(low_ref[...], up_ref[...]))
    activ_ref[...] = activ.astype(BF)
    dhid_ref[...] = (dact_ref[...].astype(F32) * slope).astype(BF)
    rows = [slope[f * seq : f * seq + 1] for f in range(half)]
    slope_ref[...] = jnp.concatenate(rows + [jnp.zeros((16 - half, slope.shape[1]), F32)], axis=0)
    total_ref[...] += dot(activ_ref[...], down_ref[...])
    back_ref[...] += dot_nt(dhid_ref[...], up_ref[...])

    @pl.when(step == pl.num_programs(0) - 1)
    def _():
        cls_total_ref[...] = class_rows(total_ref, half, F32, 16)


def class_forward_kernel(half, low_ref, start_ref, up_ref, down_ref, pooled_ref, total_ref):
    step = pl.program_id(0)

    @pl.when(step == 0)
    def _():
        total_ref[...] = start_ref[...]

    activ, _ = gate(dot(low_ref[...], up_block(up_ref)))
    total_ref[...] += dot(activ.astype(BF), up_block(down_ref))

    @pl.when(step == pl.num_programs(0) - 1)
    def _():
        pooled_ref[...] = jnp.sum(total_ref[0:half, :], axis=0, keepdims=True)


def mlp_second_kernel(half, start_ref, low_ref, up_ref, down_ref, activ_ref, slope_ref, total_ref):
    @pl.when(pl.program_id(0) == 0)
    def _():
        total_ref[...] = start_ref[...]

    activ, slope = gate(dot(low_ref[...], up_block(up_ref)))
    activ_ref[...] = activ.astype(BF)
    slope_ref[...] = slope.astype(BF)
    total_ref[...] += dot(activ_ref[...], up_block(down_ref))


def mlp_third_kernel(half, start_ref, low_ref, up_ref, down_ref, _, __, activ_ref, slope_ref, result_ref, total_ref):
    mlp_second_kernel(half, start_ref, low_ref, up_ref, down_ref, activ_ref, slope_ref, total_ref)

    @pl.when(pl.program_id(0) == pl.num_programs(0) - 1)
    def _():
        result_ref[...] = total_ref[...].astype(BF)


def hidden_backward_kernel(start_ref, grad_ref, slope_ref, up_ref, down_ref, *refs):
    dhid_ref, back_ref = refs[-2:]

    @pl.when(pl.program_id(0) == 0)
    def _():
        back_ref[...] = start_ref[...]

    dact = dot_nt(grad_ref[...], up_block(down_ref))
    dhid_ref[...] = (dact * slope_ref[...].astype(F32)).astype(BF)
    back_ref[...] += dot_nt(dhid_ref[...], up_block(up_ref))


def loss_kernel(
    order, frames, place_ref, pooled_ref, text_ref, proj_ref,
    loss_ref, caption_grad_ref, embed_grad_ref, pooled_all_ref, pooled_grad_ref,
):
    clips, width = pooled_ref.shape
    wide = proj_ref.shape[1]
    me = place_ref[1]
    block = lax.broadcasted_iota(jnp.int32, (clips, clips), 1)
    mask = jnp.zeros_like(block)
    for k, bit in enumerate(order):
        mask = mask + ((block >> k) & 1) * bit
    row = lax.broadcasted_iota(jnp.int32, (clips, clips), 0)
    pick = (row == jnp.bitwise_xor(mask, me)).astype(F32).astype(BF)
    pooled = dot(pick, pooled_ref[...]).astype(BF)
    text = dot(pick, text_ref[...]).astype(BF)
    pooled_all_ref[...] = pooled
    embed = dot(pooled, proj_ref[...])
    embed_rinv = lax.rsqrt(jnp.sum(embed * embed, axis=-1, keepdims=True) + 1e-06)
    embed_low = (embed * embed_rinv).astype(BF)
    caption_f = text[:, :wide].astype(F32)
    caption_rinv = lax.rsqrt(jnp.sum(caption_f * caption_f, axis=-1, keepdims=True) + 1e-06)
    caption_low = (caption_f * caption_rinv).astype(BF)
    scores = SHARPNESS * dot_nt(embed_low, caption_low)
    lane = lax.broadcasted_iota(jnp.int32, (8, text.shape[1] - wide), 1)
    pick_id = (lane == 1).astype(F32).astype(BF)
    caption_ids = dot_nt(pick_id, text[:, wide:])[0:1, :]
    clip_ids = text[:, wide:].astype(F32)[:, 0:1]
    positive = clip_ids == caption_ids
    masked = jnp.where(positive, scores, LOWEST)

    def side(axis):
        top = jnp.max(scores, axis=axis, keepdims=True)
        each = jnp.exp(scores - top)
        total = jnp.sum(each, axis=axis, keepdims=True)
        pos_top = jnp.max(masked, axis=axis, keepdims=True)
        pos_each = jnp.where(positive, jnp.exp(masked - pos_top), 0.0)
        pos_total = jnp.sum(pos_each, axis=axis, keepdims=True)
        part = jnp.sum(top + jnp.log(total) - pos_top - jnp.log(pos_total), axis=1 - axis, keepdims=True)
        return (part, each / total - pos_each / pos_total)

    row_loss, row_grad = side(1)
    column_loss, column_grad = side(0)
    loss_ref[...] = 0.5 * (row_loss + column_loss)
    dscore = 0.5 * (row_grad + column_grad)
    embed_grad = SHARPNESS * dot(dscore.astype(BF), caption_low)
    caps_grad = SHARPNESS * dot_tn(dscore.astype(BF), embed_low)
    caption_grad = caption_rinv * caps_grad - caption_f * (
        caption_rinv * caption_rinv * caption_rinv * jnp.sum(caption_f * caps_grad, axis=-1, keepdims=True)
    )
    embed_diff = embed_rinv * embed_grad - embed * (
        embed_rinv * embed_rinv * embed_rinv * jnp.sum(embed * embed_grad, axis=-1, keepdims=True)
    )
    embed_diff = embed_diff.astype(BF)
    embed_grad_ref[...] = embed_diff
    grads = dot_nt(embed_diff, proj_ref[...])

    def own_row(value):
        own = lax.broadcasted_iota(jnp.int32, value.shape, 0) == me
        return jnp.sum(jnp.where(own, value, 0.0), axis=0, keepdims=True)

    caption_grad_ref[...] = own_row(caption_grad)
    pooled_grad_ref[...] = own_row(grads) / frames


def class_backward_kernel(
    half, place_ref, cot_ref, pooled_ref, slope_own_ref, slope_other_ref, up_own_ref, down_own_ref, up_ref, down_ref,
    grad_ref, dhid_own_ref, dhid_other_ref, back_ref,
):
    @pl.when(pl.program_id(0) == 0)
    def _():
        cot = cot_ref[0, 0].astype(F32)
        cot = jnp.where(place_ref[0] == 0, cot[:half], cot[half:]) + pooled_ref[...]
        grad_ref[...] = jnp.concatenate([cot, jnp.zeros((16 - half, cot.shape[1]), F32)], axis=0).astype(BF)
        back_ref[...] = jnp.zeros_like(back_ref)

    grad = grad_ref[...]
    dhid_own_ref[...] = (dot_nt(grad, down_own_ref[...]) * slope_own_ref[...]).astype(BF)
    dhid_other_ref[...] = (dot_nt(grad, up_block(down_ref)) * slope_other_ref[...]).astype(BF)
    back_ref[...] += dot_nt(dhid_own_ref[...], up_own_ref[...]) + dot_nt(dhid_other_ref[...], up_block(up_ref))


def mlp_weight_first_kernel(
    half, count, place_ref, grad_ref, grad_cls_ref, low_ref, activ_ref, dhid_ref, dhid_cls_ref,
    keep_ref, send_ref, grad_t_ref, low_t_ref, fixed_ref, rows_ref,
):
    @pl.when(pl.program_id(0) == 0)
    def _():
        rows_ref[...] = grad_ref[...]
        put_class_rows(rows_ref, grad_cls_ref, half)
        grad_t_ref[...] = rows_ref[...].T
        low_t_ref[...] = low_ref[...].T

    mlp_weight_second_kernel(
        half, count, place_ref, grad_t_ref, low_t_ref, activ_ref, dhid_ref, dhid_cls_ref, keep_ref, send_ref, fixed_ref
    )


def mlp_weight_second_kernel(
    half, count, place_ref, grad_t_ref, low_t_ref, activ_ref, dhid_ref, dhid_cls_ref, keep_ref, send_ref, fixed_ref
):
    fixed_ref[...] = dhid_ref[...]
    put_class_rows(fixed_ref, dhid_cls_ref, half)
    split_rows(mlp_ways, count, 0, keep_ref, send_ref, 0, dot(low_t_ref[...], fixed_ref[...]), place_ref)
    split_rows(mlp_ways, count, 1, keep_ref, send_ref, 1, dot(grad_t_ref[...], activ_ref[...]), place_ref)


def mlp_norm_kernel(half, back_ref, back_cls_ref, grad_ref, grad_cls_ref, middle_ref, gain_ref, out_ref, gain_grad_ref):
    f = pl.program_id(0)
    row = lax.broadcasted_iota(jnp.int32, back_ref.shape, 0)
    at = pl.ds(f, 1)
    back = jnp.where(row == 0, back_cls_ref[at, :], back_ref[...])
    cls = jnp.zeros((1, back.shape[1]), F32)
    for k in range(half):
        cls = jnp.where(f == k, grad_cls_ref[...].astype(F32)[k : k + 1], cls)
    grad = jnp.where(row == 0, cls, grad_ref[...].astype(F32))
    normal, rstd = standardized(middle_ref[...])
    part, gain_grad = norm_backward(back, gain_ref[...], normal, rstd)
    out_ref[...] = grad + part

    @pl.when(f == 0)
    def _():
        gain_grad_ref[...] = jnp.zeros_like(gain_grad_ref)

    gain_grad_ref[...] += gain_grad


def frame_backward_kernel(
    heads, valid, half, first, grad_ref, own_ref, other_ref, stream_ref, gain_ref, out_own_ref, out_other_ref, in_own_ref,
    in_other_ref, mlp_gain_ref, *refs,
):
    low_ref, down_ref, dother_ref, token_ref, edge_ref = refs[-5:]
    step = pl.program_id(0)
    f = first + step
    width = grad_ref.shape[2]
    size = width // heads
    scale = size**-0.5
    grad = grad_ref[0]
    low = grad.astype(BF)
    low_ref[0] = low
    normed_grad = None
    for qkv_ref, out_ref, in_ref, to_ref in (
        (own_ref, out_own_ref, in_own_ref, down_ref),
        (other_ref, out_other_ref, in_other_ref, dother_ref),
    ):
        wide = in_ref.shape[2]
        context_grad = dot_nt(low, out_ref[...]).astype(BF)
        for j in range(wide // (2 * size)):
            query, keys, values = (
                qkv_ref[0, :, wide * k + 2 * size * j : wide * k + 2 * size * (j + 1)] for k in range(3)
            )
            grads = attend_pair_backward(
                query, keys, values, context_grad[:, 2 * size * j : 2 * size * (j + 1)], valid, scale
            )
            for k in range(3):
                to_ref[0, :, wide * k + 2 * size * j : wide * k + 2 * size * (j + 1)] = grads[k]
        for k in range(3):
            part = dot_nt(to_ref[0, :, wide * k : wide * (k + 1)], in_ref[k])
            normed_grad = part if normed_grad is None else normed_grad + part
    normal, rstd = standardized(stream_ref[0])
    part, gain_grad = norm_backward(normed_grad, gain_ref[...], normal, rstd)
    total = grad + part
    token_ref[0] = total.astype(BF)

    @pl.when(step == 0)
    def _():
        if first == 0:
            edge_ref[...] = jnp.zeros_like(edge_ref)
            edge_ref[2 * half + 1 : 2 * half + 2, :] = mlp_gain_ref[...]
        else:
            edge_ref[...] = refs[3][...]

    edge_ref[pl.ds(f, 1), :] = total[0:1]
    edge_ref[pl.ds(half + f, 1), :] = total[valid - 1 : valid]
    edge_ref[2 * half : 2 * half + 1, :] += gain_grad


def frame_weight_kernel(
    count, place_ref, low_ref, grad_ref, down_ref, dother_ref, own_ref, other_ref,
    keep_own_ref, send_own_ref, keep_other_ref, send_other_ref, low_t_ref, grad_t_ref,
):
    step = pl.program_id(0)

    @pl.when(step == 0)
    def _():
        low_t_ref[...] = low_ref[...].T
        grad_t_ref[...] = grad_ref[...].T

    for first, dqkv_ref, context_ref, keep_ref, send_ref in (
        (0, dother_ref, other_ref, keep_other_ref, send_other_ref),
        (4, down_ref, own_ref, keep_own_ref, send_own_ref),
    ):

        @pl.when((step >= first) & (step < first + 3))
        def _(dqkv_ref=dqkv_ref, keep_ref=keep_ref, send_ref=send_ref):
            split_rows(frame_ways, count, 0, keep_ref, send_ref, 0, dot(low_t_ref[...], dqkv_ref[...]), place_ref)

        @pl.when(step == first + 3)
        def _(context_ref=context_ref, keep_ref=keep_ref, send_ref=send_ref):
            split_rows(frame_ways, count, 0, keep_ref, send_ref, 0, dot(grad_t_ref[...], context_ref[...]), place_ref)


def both_halves(place, own, other):
    return jnp.concatenate(
        [jnp.where(place == 0, own, other), jnp.where(place == 0, other, own)], axis=0
    )


def message_backward_kernel(
    heads, place_ref, own_ref, other_ref, qkv_ref, out_ref, in_ref, next_ref, low_ref, dqkv_ref, part_ref
):
    frames, width = next_ref.shape
    half = frames // 2
    at = slice(half, 2 * half)
    grad = both_halves(place_ref[0], own_ref[at, :], other_ref[at, :])
    next_ref[...] = grad
    low = grad.astype(BF)
    low_ref[...] = low
    size = width // heads
    scale = size**-0.5
    wide = in_ref.shape[2]
    context_grad = dot_nt(low, out_ref[...]).astype(BF)
    for j in range(wide // (2 * size)):
        query, keys, values = (
            qkv_ref[:, wide * k + 2 * size * j : wide * k + 2 * size * (j + 1)] for k in range(3)
        )
        grads = attend_pair_backward(
            query, keys, values, context_grad[:, 2 * size * j : 2 * size * (j + 1)], frames, scale
        )
        for k in range(3):
            dqkv_ref[:, wide * k + 2 * size * j : wide * k + 2 * size * (j + 1)] = grads[k]
    total = None
    for k in range(3):
        part = dot_nt(dqkv_ref[:, wide * k : wide * (k + 1)], in_ref[k])
        total = part if total is None else total + part
    part_ref[...] = total


def message_last_kernel(
    place_ref, own_ref, other_ref, next_ref, low_ref, dqkv_ref, part_ref, part_other_ref, message_ref, gain_ref, w_ref,
    late_ref, cls_ref,
):
    frames, width = next_ref.shape
    half = frames // 2
    normal, rstd = standardized(message_ref[...])
    part, gain_grad = norm_backward(part_ref[...] + part_other_ref[...], gain_ref[...], normal, rstd)
    message_low = (next_ref[...] + part).astype(BF)
    cls = both_halves(place_ref[0], own_ref[0:half, :], other_ref[0:half, :])
    cls_ref[...] = (cls + dot_nt(message_low, w_ref[...])).astype(BF)
    wide = dqkv_ref.shape[1]
    late_ref[0:frames, 0:width] = low_ref[...]
    late_ref[0:frames, width : 2 * width] = message_low
    late_ref[0:frames, 2 * width : 2 * width + wide] = dqkv_ref[...]
    both = own_ref[2 * half : 2 * half + 2, :] + other_ref[2 * half : 2 * half + 2, :]
    gains = jnp.concatenate([both[1:2], both[0:1], gain_grad], axis=1)
    room = late_ref.shape[1] - 2 * width - wide
    gains = jnp.concatenate([gains, jnp.zeros((1, frames * room - 3 * width), F32)], axis=1)
    gains = jnp.concatenate([gains[:, room * r : room * (r + 1)] for r in range(frames)], axis=0)
    late_ref[:, 2 * width + wide :] = gains.astype(BF)


def assemble_kernel(pieces, place_ref, *refs):
    out_ref, wide_ref = refs[-2:]
    tile, frames, width = out_ref.shape
    half = frames // 2
    for side in range(2):
        mp = place_ref[0] if side == 0 else 1 - place_ref[0]
        for k in range(half):
            per = half // pieces
            value = refs[side * pieces + k // per][k % per].astype(F32)
            for j in range(width // 128):
                wide_ref[j, pl.ds(mp * half + k, tile, stride=8), :] = value[:, 128 * j : 128 * (j + 1)]
    for j in range(width // 128):
        out_ref[:, :, 128 * j : 128 * (j + 1)] = wide_ref[j].reshape(tile, frames, 128).astype(BF)
    if len(refs) > 2 * pieces + 2:

        @pl.when(pl.program_id(0) == 0)
        def _():
            out_ref[0] = refs[2 * pieces][...]


def factor_kernel(
    frames, place_ref, early_ref, late_ref, pooled_ref, embed_ref,
    weight_ref, in_ref, out_ref, proj_ref, gains_ref,
):
    size = early_ref.shape[0]
    share, width = weight_ref.shape
    wide = out_ref.shape[1]
    column = lax.broadcasted_iota(jnp.int32, (share, width), 1)
    row = lax.broadcasted_iota(jnp.int32, (share, width), 0)
    pick = (column == place_ref[1] * share + row).astype(F32).astype(BF)

    def early(first, wide):
        value = early_ref[:, :, first : first + wide].astype(F32)[:, :frames]
        return value.reshape(size * frames, wide).astype(BF)

    def late(first, wide):
        return late_ref[:, :, first : first + wide].astype(F32).reshape(size * frames, wide).astype(BF)

    def own(value):
        return dot_nt(pick, value).astype(BF)

    weight_ref[...] = dot(own(early(0, width)), late(width, width))
    product = dot(own(early(width, width)), late(2 * width, 3 * wide))
    for k in range(3):
        in_ref[k] = product[:, wide * k : wide * (k + 1)]
    out_ref[...] = dot(own(late(0, width)), early(2 * width, wide))
    proj_ref[...] = dot(own(pooled_ref[...]), embed_ref[...])
    room = late_ref.shape[2] - 2 * width - 3 * wide
    gains = jnp.sum(late_ref[:, :, 2 * width + 3 * wide :].astype(F32), axis=0)
    gains = jnp.concatenate([gains[r : r + 1, :] for r in range(frames)], axis=1)
    for k in range(3):
        gains_ref[k : k + 1, :] = gains[:, width * k : width * (k + 1)]


def whole(shape):
    return pl.BlockSpec(tuple(shape), lambda *_: (0,) * len(shape))


def run(kernel, name, args, outs, grid=(1,), prefetch=0, specs=None, out_specs=None, scratch=(), aliases=None, deps=(), cost=2):
    specs = specs or {}
    out_specs = out_specs or {}
    tensors = args[prefetch:]
    taken = len(args)

    def body(*refs):
        kernel(*refs[:taken], *refs[taken + len(deps) :])

    return pl.pallas_call(
        body,
        out_shape=list(outs),
        grid_spec=pltpu.PrefetchScalarGridSpec(
            num_scalar_prefetch=prefetch,
            grid=grid,
            in_specs=[specs.get(k, whole(t.shape)) for k, t in enumerate(tensors)]
            + [pl.BlockSpec(memory_space=pl.ANY)] * len(deps),
            out_specs=[out_specs.get(k, whole(o.shape)) for k, o in enumerate(outs)],
            scratch_shapes=list(scratch),
        ),
        compiler_params=pltpu.CompilerParams(
            dimension_semantics=("arbitrary",) * len(grid), vmem_limit_bytes=VMEM_BYTES
        ),
        cost_estimate=pl.CostEstimate(flops=round(KERNEL_US.get(name, cost) * 2.3e9), bytes_accessed=0, transcendentals=0),
        input_output_aliases={prefetch + k: out for k, out in (aliases or {}).items()},
        name=name,
    )(*args, *deps)


def shape_of(shape, dtype):
    return jax.ShapeDtypeStruct(tuple(shape), dtype)


def plus(a, b, dtype=BF):
    return (a.astype(F32) + b.astype(F32)).astype(dtype)


def reorder(ways, keep, send):
    size = lax.axis_size("dp")
    bits = bits_of(size)
    lead, rows, wide = keep.shape
    block = 2 * rows // 16
    value = jnp.stack([keep.reshape(lead, 8, block, wide), send.reshape(lead, 8, block, wide)], axis=2)
    value = value.reshape(lead, size, 2 * rows // size, wide)
    turned = []
    for one, order in zip(value, ways(bits[1:])):
        order = [bit for bit in order if bit != "mp"]
        order = jnp.bitwise_xor(jnp.asarray(row_order(bits[:1] + order), jnp.int32), lax.axis_index("dp"))
        turned.append(jnp.take(one, order, axis=0).reshape(2 * rows, wide))
    value = jnp.stack(turned)
    return (value[:, :rows], value[:, rows:])


def put_stage(value, way, refs, whole_refs):
    if way is None:
        refs[0][...] = value
    elif way == "mp":
        refs[0][...] = value[0:1].astype(BF)
        refs[1][...] = value[1:2].astype(BF)
    else:
        rows = value.shape[1] // 2
        refs[0][...] = value[:, :rows].astype(BF)
        refs[1][...] = value[:, rows:].astype(BF)


def stage_kernel(ways, keep_first, got_first, keep_second, got_second, *refs):
    per = len(refs) // 2
    for k, (keep, got) in enumerate(((keep_first, got_first), (keep_second, got_second))):
        value = keep[...].astype(F32) + got[...].astype(F32)
        put_stage(value, ways[k], refs[per * k : per * (k + 1)], None)


def core_stage_kernel(ways, keep_own, got_own, keep_other, got_other, *refs):
    for k in range(2):
        parts = [
            keep[k : k + 1].astype(F32) + got[k : k + 1].astype(F32)
            for keep, got in ((keep_own, got_own), (keep_other, got_other))
        ]
        for part, at in zip(parts, range(2)):
            if ways[k] == "mp":
                refs[2 * k + at][...] = part.astype(BF)
                continue
            rows = part.shape[1] // 2
            refs[2 * k][at : at + 1] = part[:, :rows].astype(BF)
            refs[2 * k + 1][at : at + 1] = part[:, rows:].astype(BF)


class Reduction:
    def __init__(self, name, ways, keep_own, send_own, keep_other, send_other):
        size = lax.axis_size("dp")
        self.name = name
        self.bits = bits_of(size)
        self.aligned = (2 * keep_own.shape[1] // size) % 16 == 0
        if not self.aligned:
            keep_own, send_own = reorder(ways, keep_own, send_own)
            keep_other, send_other = reorder(ways, keep_other, send_other)
        self.ways = ways(self.bits[1:])
        self.steps = len(self.ways[0])
        self.at = 0
        self.keep = (keep_own, keep_other)
        self.got = tuple(flip(send, self.bits[0]) for send in (send_own, send_other))

    def ways_at(self, at):
        return tuple(ways[at] if at < self.steps else None for ways in self.ways)

    def outs(self, shapes, ways):
        made = []
        for (parts, rows, wide), way in zip(shapes, ways):
            if way is None:
                made.append(shape_of((parts, rows, wide), F32))
            elif way == "mp":
                made += [shape_of((1, rows, wide), BF)] * 2
            else:
                made += [shape_of((parts, rows // 2, wide), BF)] * 2
        return made

    def call(self, kernel, args, shapes, ways, deps, cost):
        if not self.aligned:
            refs = [Box(out) for out in self.outs(shapes, ways)]
            kernel(ways, *args, *refs)
            return [ref.value for ref in refs]
        made = self.outs(shapes, ways)
        wide = made[0].shape[2]
        chunk = 384

        def spec(value):
            return pl.BlockSpec(value.shape[:2] + (chunk,), lambda j, *_: (0, 0, j))

        return run(
            functools.partial(kernel, ways),
            self.name + str(self.at),
            args,
            made,
            grid=(wide // chunk,),
            specs={k: spec(value) for k, value in enumerate(args)},
            out_specs={k: spec(value) for k, value in enumerate(made)},
            deps=deps,
            cost=cost,
        )

    def take(self, made):
        per = len(made) // 2
        self.value = [made[per * k : per * (k + 1)] for k in range(2)]

    def cores(self, *deps, cost=0):
        own, other = self.keep
        _, rows, wide = own.shape
        args = (own, self.got[0], other, self.got[1])
        self.take(self.call(core_stage_kernel, args, [(2, rows, wide)] * 2, self.ways_at(0), deps, cost))
        self.at = 0
        self.send()

    def send(self):
        self.got = []
        for (_, send), way in zip(self.value, self.ways_at(self.at)):
            self.got.append(swap(send) if way == "mp" else flip(send, way))

    def ready(self):
        return tuple(one for values in self.value for one in values)

    def step(self, *deps, cost=0):
        args = (self.value[0][0], self.got[0], self.value[1][0], self.got[1])
        shapes = [value[0].shape for value in self.value]
        self.at += 1
        self.take(self.call(stage_kernel, args, shapes, self.ways_at(self.at), deps, cost))
        if self.at < self.steps:
            self.send()


class Box:
    def __init__(self, out):
        self.value = jnp.zeros(out.shape, out.dtype)

    def __setitem__(self, at, value):
        self.value = value if at is Ellipsis else self.value.at[at].set(value)


def on_device(
    tokens,
    captions,
    clip_groups,
    caption_groups,
    msg_weight,
    msg_gain,
    msg_in,
    msg_out,
    frame_gain,
    frame_in,
    frame_out,
    mlp_gain,
    up_weight,
    down_weight,
    proj_weight,
    out_cot,
):
    clips, frames, patches, width = tokens.shape
    assert clips == 1 and frames == 8 and lax.axis_size("mp") == 2
    size = lax.axis_size("dp")
    valid = patches + 1
    seq = -(-valid // 16) * 16
    half = frames // 2
    rows = half * seq
    share = width // size
    aligned = share % 16 == 0
    count = len(bits_of(size)) - 1 if aligned else None
    h_half = frame_in.shape[2]
    f_half = up_weight.shape[1]
    embed = proj_weight.shape[1]
    me_dp, me_mp = (lax.axis_index("dp"), lax.axis_index("mp"))
    place = jnp.stack([me_mp, me_dp, clip_groups[0], caption_groups[0]]).astype(jnp.int32)
    msg_gain, frame_gain, mlp_gain = (gain.reshape(1, width) for gain in (msg_gain, frame_gain, mlp_gain))
    tokens_t, cot_t = (jnp.transpose(value, (0, 2, 1, 3)) for value in (tokens, out_cot))
    class_spec = pl.BlockSpec((1, 1, frames, width), lambda *_: (0, 0, 0, 0))

    def mine(value, axis=1):
        return lax.dynamic_slice_in_dim(value, me_dp * share, share, axis)

    devices = size if aligned else 16
    each = width // devices

    def packed(up, down):
        up = up.reshape(-1, each, f_half // width, width).transpose(0, 2, 1, 3).reshape(-1, f_half // devices, width)
        return jnp.concatenate([up, down.reshape(-1, f_half // devices, width)], axis=1)

    if aligned:
        down_share = lax.dynamic_slice_in_dim(down_weight, me_dp * (f_half // size), f_half // size, 0)
        mlp_share = swap(packed(mine(up_weight, 0), down_share))
    else:
        mlp_other = packed(swap(up_weight), swap(down_weight))

    message, early, msg_qkv, msg_part = run(
        functools.partial(message_forward_kernel, HEADS),
        "message_forward",
        (place, tokens_t, captions, msg_weight, msg_gain, msg_in, msg_out),
        (
            shape_of((frames, width), F32),
            shape_of((16, 2 * width + h_half), BF),
            shape_of((frames, 3 * h_half), BF),
            shape_of((frames, width), F32),
        ),
        prefetch=1,
        specs={0: class_spec},
    )
    msg_other = swap(msg_part)
    if aligned:
        mlp_other = lax.all_gather(after(mlp_share, msg_part), "dp", axis=0, tiled=True)

    def half_rows(value, axis):
        rows_half = value.shape[axis] // 2
        return lax.dynamic_slice_in_dim(value, (me_dp % 2) * rows_half, rows_half, axis)

    in_mine = swap(after(half_rows(frame_in, 1), msg_other))

    one_frame = lambda wide, first=0: pl.BlockSpec((1, seq, wide), lambda f, *_: (f + first, 0, 0))
    whole_wide = pltpu.VMEM((width // 128, patches * frames, 128), F32)
    stream, frame_low, qkv_own, context_own = run(
        functools.partial(frame_first_kernel, HEADS, half),
        "frame_first",
        (place, tokens_t.reshape(patches, frames, width), message, msg_part, msg_other, frame_gain, frame_in),
        (
            shape_of((half, seq, width), F32),
            shape_of((half, seq, width), BF),
            shape_of((half, seq, 3 * h_half), BF),
            shape_of((half, seq, h_half), BF),
        ),
        grid=(half,),
        prefetch=1,
        out_specs={0: one_frame(width), 1: one_frame(width), 2: one_frame(3 * h_half), 3: one_frame(h_half)},
        scratch=[whole_wide],
    )
    in_theirs = flip(after(in_mine, stream), 1)
    out_mine = swap(after(half_rows(frame_out, 0), stream))
    bits = gather_bits()

    def hop(value, k, *deps):
        return jnp.concatenate([value, after(flip(value, bits[k]), *deps)], axis=0)

    early_all = hop(after(early[None], stream), 0)
    chunk = 512
    grad, dact_own = run(
        functools.partial(cotangent_kernel, half),
        "cotangent",
        (place, cot_t.reshape(patches, frames, width), down_weight),
        (shape_of((rows, width), BF), shape_of((rows, f_half), BF)),
        grid=(f_half // chunk,),
        prefetch=1,
        specs={1: pl.BlockSpec((chunk, width), lambda j, *_: (j, 0))},
        out_specs={1: pl.BlockSpec((rows, chunk), lambda j, *_: (0, j))},
        scratch=[whole_wide],
        deps=(stream,),
    )
    qkv_other, context_other, in_other = run(
        functools.partial(frame_second_kernel, HEADS, valid),
        "frame_second",
        (place, frame_low, in_mine, in_theirs),
        (shape_of((half, seq, 3 * h_half), BF), shape_of((half, seq, h_half), BF), shape_of(frame_in.shape, BF)),
        grid=(half,),
        prefetch=1,
        specs={0: one_frame(width)},
        out_specs={0: one_frame(3 * h_half), 1: one_frame(h_half)},
        deps=(grad,),
    )
    out_theirs = flip(out_mine, 1)
    early_all = hop(after(early_all, context_other), 1)

    steps = f_half // chunk
    up_spec = pl.BlockSpec((width, chunk), lambda j, *_: (0, j))
    down_spec = pl.BlockSpec((chunk, width), lambda j, *_: (j, 0))
    unit_spec = pl.BlockSpec((rows, chunk), lambda j, *_: (0, j))
    units = shape_of((rows, f_half), BF)
    wide_rows = shape_of((rows, width), F32)
    context_own2, context_other2 = (v.reshape(rows, h_half) for v in (context_own, context_other))
    (
        middle, mlp_low, activ_own, dhid_own, slope_cls_own, total, back, cls_low, cls_total, out_other,
    ) = run(
        functools.partial(mlp_first_kernel, half),
        "mlp_first",
        (
            place, stream.reshape(rows, width), context_own2, context_other2, frame_out, out_mine, out_theirs, mlp_gain,
            up_weight, down_weight, dact_own,
        ),
        (
            wide_rows, shape_of((rows, width), BF), units, units, shape_of((16, f_half), F32), wide_rows, wide_rows,
            shape_of((16, width), BF), shape_of((16, width), F32), shape_of(frame_out.shape, BF),
        ),
        grid=(steps,),
        prefetch=1,
        specs={7: up_spec, 8: down_spec, 9: unit_spec},
        out_specs={2: unit_spec, 3: unit_spec, 4: pl.BlockSpec((16, chunk), lambda j, *_: (0, j))},
    )

    part = f_half // 4
    per = width // part

    def up_other_spec(first):
        return pl.BlockSpec((devices, each, part), lambda j, *_: (0, (j + first) // per, (j + first) % per))

    def down_other_spec(first):
        return pl.BlockSpec((devices // 4, f_half // devices, width), lambda j, *_: (j + first, 1, 0))

    def part_spec(first=0):
        return pl.BlockSpec((rows, part), lambda j, *_: (0, j + first))

    (pooled_part,) = run(
        functools.partial(class_forward_kernel, half),
        "class_forward",
        (cls_low, cls_total, mlp_other, mlp_other),
        (shape_of((1, width), F32),),
        grid=(4,),
        specs={2: up_other_spec(0), 3: down_other_spec(0)},
        scratch=[pltpu.VMEM((16, width), F32)],
    )
    pooled_low = ((pooled_part + swap(pooled_part)) / frames).astype(BF)
    for k in range(2, len(bits)):
        early_all = hop(after(early_all, pooled_part), k)
    stages = [pooled_low]
    for bit in bits:
        stages.append(jnp.concatenate([stages[-1], flip(stages[-1], bit)], axis=0))
    pooled_all = stages[-1]
    anywhere = pl.BlockSpec(memory_space=pl.ANY)
    activ_2, slope_2, total = run(
        functools.partial(mlp_second_kernel, half),
        "mlp_second",
        (total, mlp_low, mlp_other, mlp_other),
        (units, units, wide_rows),
        grid=(2,),
        specs={2: up_other_spec(0), 3: down_other_spec(0)},
        out_specs={0: part_spec(), 1: part_spec()},
        deps=(stages[0],),
    )
    activ_other, slope_other, result_own = run(
        functools.partial(mlp_third_kernel, half),
        "mlp_third",
        (total, mlp_low, mlp_other, mlp_other, activ_2, slope_2),
        (units, units, shape_of((rows, width), BF)),
        grid=(2,),
        specs={2: up_other_spec(2), 3: down_other_spec(2), 4: anywhere, 5: anywhere},
        out_specs={0: part_spec(2), 1: part_spec(2)},
        scratch=[pltpu.VMEM((rows, width), F32)],
        aliases={4: 0, 5: 1},
        deps=(stages[1],),
    )
    result_other = swap(result_own)

    def hidden_backward(name, back, first, deps, *made):
        return run(
            hidden_backward_kernel,
            name,
            (back, grad, slope_other, mlp_other, mlp_other, *made),
            (units, wide_rows),
            grid=(2,),
            specs={2: part_spec(first), 3: up_other_spec(first), 4: down_other_spec(first), 5: anywhere},
            out_specs={0: part_spec(first)},
            aliases={5: 0} if made else None,
            deps=deps,
        )

    dhid_2, back = hidden_backward("hidden_backward_a", back, 0, (stages[2], result_own))
    dhid_other, back = hidden_backward("hidden_backward_b", back, 2, (stages[3],), dhid_2)
    class_picks = [slope_other[f * seq : f * seq + 1] for f in range(half)]
    slope_cls_other = jnp.concatenate(class_picks + [jnp.zeros((16 - half, f_half), BF)], axis=0).astype(F32)

    text_all = early_all[:, frames, :width]
    loss, caption_grad, embed_grad, pooled_all, pooled_grad = run(
        functools.partial(loss_kernel, bits, frames),
        "contrast",
        (place, pooled_all, text_all, proj_weight),
        (
            shape_of((1, 1), F32),
            shape_of((1, embed), F32),
            shape_of((size, embed), BF),
            shape_of((size, width), BF),
            shape_of((1, width), F32),
        ),
        prefetch=1,
        deps=(back,),
    )

    part_cols = lambda n: pl.BlockSpec((n, part), lambda j, *_: (0, j))
    cls_units = shape_of((16, f_half), BF)
    grad_cls, dhid_cls_own, dhid_cls_other, back_cls = run(
        functools.partial(class_backward_kernel, half),
        "class_backward",
        (place, cot_t, pooled_grad, slope_cls_own, slope_cls_other, up_weight, down_weight, mlp_other, mlp_other),
        (shape_of((16, width), BF), cls_units, cls_units, shape_of((16, width), F32)),
        grid=(4,),
        prefetch=1,
        specs={
            0: class_spec,
            2: part_cols(16),
            3: part_cols(16),
            4: part_cols(width),
            5: pl.BlockSpec((part, width), lambda j, *_: (j, 0)),
            6: up_other_spec(0),
            7: down_other_spec(0),
        },
        out_specs={1: part_cols(16), 2: part_cols(16)},
    )
    weights = shape_of((2, width // 2, f_half), BF)
    weights_spec = pl.BlockSpec((2, width // 2, chunk), lambda j, *_: (0, 0, j))
    turned = shape_of((width, rows), BF)
    cls_spec = pl.BlockSpec((16, chunk), lambda j, *_: (0, j))
    keep_other, send_other, grad_t, low_t = run(
        functools.partial(mlp_weight_first_kernel, half, count),
        "mlp_weight_first",
        (place, grad, grad_cls, mlp_low, activ_other, dhid_other, dhid_cls_other),
        (weights, weights, turned, turned),
        grid=(steps,),
        prefetch=1,
        specs={3: unit_spec, 4: unit_spec, 5: cls_spec},
        out_specs={0: weights_spec, 1: weights_spec},
        scratch=[pltpu.VMEM((rows, chunk), BF), pltpu.VMEM((rows, width), BF)],
    )
    keep_own, send_own = run(
        functools.partial(mlp_weight_second_kernel, half, count),
        "mlp_weight_second",
        (place, grad_t, low_t, activ_own, dhid_own, dhid_cls_own),
        (weights, weights),
        grid=(steps,),
        prefetch=1,
        specs={2: unit_spec, 3: unit_spec, 4: cls_spec},
        out_specs={0: weights_spec, 1: weights_spec},
        scratch=[pltpu.VMEM((rows, chunk), BF)],
        deps=(result_other,),
    )
    frame_spec2 = pl.BlockSpec((seq, width), lambda f: (f, 0))
    middle_grad, mlp_gain_grad = run(
        functools.partial(mlp_norm_kernel, half),
        "mlp_norm",
        (back, back_cls, grad, grad_cls, middle, mlp_gain),
        (wide_rows, shape_of((1, width), F32)),
        grid=(half,),
        specs={0: frame_spec2, 2: frame_spec2, 4: frame_spec2},
        out_specs={0: frame_spec2},
        deps=(keep_own,),
    )
    mlp_stages = Reduction("mlp_stage", mlp_ways, keep_own, send_own, keep_other, send_other)
    mlp_stages.cores(middle_grad)

    in_shape = shape_of((half, seq, 3 * h_half), BF)
    made = (
        shape_of((half, seq, width), BF), in_shape, in_shape, shape_of((half // 2, seq, width), BF), shape_of((16, width), F32),
    )

    def frame_backward(name, first, middle_grad, before, deps=()):
        tensors = (
            middle_grad.reshape(half, seq, width), qkv_own, qkv_other, stream, frame_gain, frame_out, out_other,
            frame_in, in_other, mlp_gain_grad, *before,
        )
        specs = {
            0: one_frame(width, first),
            1: one_frame(3 * h_half, first),
            2: one_frame(3 * h_half, first),
            3: one_frame(width, first),
        }
        specs.update({10 + k: anywhere for k in range(3 if before else 0)})
        return run(
            functools.partial(frame_backward_kernel, HEADS, valid, half, first),
            name,
            tensors,
            made,
            grid=(half // 2,),
            specs=specs,
            out_specs={
                0: one_frame(width, first),
                1: one_frame(3 * h_half, first),
                2: one_frame(3 * h_half, first),
                3: one_frame(width),
            },
            aliases={10 + k: k for k in range(3)} if before else None,
            deps=deps,
        )

    before = frame_backward("frame_backward_a", 0, middle_grad, (), mlp_stages.ready())
    token_first = before[3]
    token_first_other = swap(token_first)
    middle_low, dqkv_own, dqkv_other, token_second, edges = frame_backward(
        "frame_backward_b", half // 2, middle_grad, (before[0], before[1], before[2], before[4])
    )
    edges_other = swap(edges)
    mlp_stages.step(edges)

    next_grad, next_low, msg_dqkv, msg_normed = run(
        functools.partial(message_backward_kernel, HEADS),
        "message_backward",
        (place, edges, edges_other, msg_qkv, msg_out, msg_in),
        (
            shape_of((frames, width), F32),
            shape_of((frames, width), BF),
            shape_of((frames, 3 * h_half), BF),
            shape_of((frames, width), F32),
        ),
        prefetch=1,
        deps=mlp_stages.ready(),
    )
    msg_normed_other = swap(msg_normed)
    grads = shape_of((2, width // 2, 2 * h_half), BF)

    def share_spec(first):
        def index(t, *_):
            k = jnp.clip(t - first, 0, 3)
            return (k // 2, 0, k % 2)

        return pl.BlockSpec((1, width // 2, h_half), index)

    def column_spec(first):
        return pl.BlockSpec((rows, h_half), lambda t, *_: (0, jnp.clip(t - first, 0, 2)))

    keep_own, send_own, keep_other, send_other = run(
        functools.partial(frame_weight_kernel, count),
        "frame_weights",
        (
            place, frame_low.reshape(rows, width), middle_low.reshape(rows, width),
            dqkv_own.reshape(rows, 3 * h_half), dqkv_other.reshape(rows, 3 * h_half), context_own2, context_other2,
        ),
        (grads,) * 4,
        grid=(8,),
        prefetch=1,
        specs={2: column_spec(4), 3: column_spec(0)},
        out_specs={0: share_spec(4), 1: share_spec(4), 2: share_spec(0), 3: share_spec(0)},
        scratch=[pltpu.VMEM((width, rows), BF), pltpu.VMEM((width, rows), BF)],
        deps=(next_grad, token_first_other),
    )
    frame_stages = Reduction("frame_stage", frame_ways, keep_own, send_own, keep_other, send_other)

    late, cls_rows = run(
        message_last_kernel,
        "message_last",
        (
            place, edges, edges_other, next_grad, next_low, msg_dqkv, msg_normed,
            msg_normed_other, message, msg_gain, msg_weight,
        ),
        (shape_of((frames, 2 * width + 6 * h_half), BF), shape_of((frames, width), BF)),
        prefetch=1,
        deps=(keep_own,),
    )
    frame_stages.cores(late)
    cores_ready = frame_stages.ready()
    late_all = hop(late[None], 0, *cores_ready)
    for k in range(1, len(bits)):
        frame_stages.step()
        if k == 1:
            token_second_other = swap(after(token_second, *frame_stages.ready()))
        late_all = hop(late_all, k, *frame_stages.ready())
        mlp_stages.step(*frame_stages.ready())
    frame_stages.step()
    (up_grad,), (down_grad,) = mlp_stages.value
    up_grad, down_grad = (up_grad[0], down_grad[0].T)
    (first,), (second,) = frame_stages.value
    first, second = (first[0], second[0])
    in_grad = jnp.stack([first[:, :h_half], first[:, h_half:], second[:, :h_half]])
    out_grad = second[:, h_half:].T

    def both(name, own, other, extra=(), deps=()):
        tile = 64
        parts = own + other
        (out,) = run(
            functools.partial(assemble_kernel, len(own)),
            name,
            (place, *parts, *extra),
            (shape_of((patches, frames, width), BF),),
            grid=(-(-patches // tile),),
            prefetch=1,
            specs={
                k: pl.BlockSpec((part.shape[0], tile, width), lambda t, s: (0, t, 0)) for k, part in enumerate(parts)
            },
            out_specs={0: pl.BlockSpec((tile, frames, width), lambda t, s: (t, 0, 0))},
            scratch=[pltpu.VMEM((width // 128, tile * frames, 128), F32)],
            deps=deps,
        )
        return jnp.transpose(out[None], (0, 2, 1, 3))

    result_own, result_other = (value.reshape(half, seq, width) for value in (result_own, result_other))
    layer_out = both("assemble_out", (result_own,), (result_other,), deps=cores_ready)
    token_grad = both(
        "assemble_grad", (token_first, token_second), (token_first_other, token_second_other), (cls_rows,)
    )

    msg_weight_share, msg_in_share, msg_out_share, proj_share, gains = run(
        functools.partial(factor_kernel, frames),
        "factors",
        (place, early_all, late_all, pooled_all, embed_grad),
        (
            shape_of((share, width), F32),
            shape_of((3, share, h_half), F32),
            shape_of((share, h_half), F32),
            shape_of((share, embed), F32),
            shape_of((3, width), F32),
        ),
        prefetch=1,
    )
    msg_out_share = msg_out_share.T
    gains = mine(gains)
    return (
        layer_out,
        loss[0, 0],
        token_grad,
        caption_grad,
        msg_weight_share,
        gains[2],
        msg_in_share,
        msg_out_share,
        gains[1],
        in_grad,
        out_grad,
        gains[0],
        up_grad,
        down_grad,
        proj_share,
    )


def solution(mesh):
    in_specs = (
        P("dp", None, None, None),
        P("dp", None),
        P("dp"),
        P("dp"),
        P(),
        P(),
        P(None, None, "mp"),
        P("mp", None),
        P(),
        P(None, None, "mp"),
        P("mp", None),
        P(),
        P(None, "mp"),
        P("mp", None),
        P(),
        P("dp", None, None, None),
    )
    out_specs = (
        P("dp", None, None, None),
        P(),
        P("dp", None, None, None),
        P("dp", None),
        P("dp", None),
        P("dp"),
        P(None, "dp", "mp"),
        P("mp", "dp"),
        P("dp"),
        P(None, "dp", "mp"),
        P("mp", "dp"),
        P("dp"),
        P("dp", "mp"),
        P("mp", "dp"),
        P("dp", None),
    )
    return jax.shard_map(
        on_device, mesh=mesh, in_specs=in_specs, out_specs=out_specs, check_vma=False
    )
```

```python
import functools

import jax
import jax.numpy as jnp
from jax import lax
from jax.experimental import pallas as pl
from jax.experimental.pallas import tpu as pltpu
from jax.sharding import PartitionSpec as P

HEADS = 12
SHARPNESS = 50.0
LOWEST = -1e30
BF = jnp.bfloat16
F32 = jnp.float32
VMEM_BYTES = 52 * 1024 * 1024
KERNEL_US = {
    "frame_first": 7,
    "cotangent": 4,
    "frame_second": 6,
    "mlp_first": 16,
    "mlp_second": 5,
    "mlp_third": 5,
    "hidden_backward_a": 5,
    "hidden_backward_b": 5,
    "class_backward": 5,
    "mlp_weights": 15,
    "frame_backward_a": 14,
    "frame_backward_b": 14,
    "frame_weights": 11,
}


def swap(value):
    return lax.ppermute(value, "mp", [(0, 1), (1, 0)])


def flip(value, bit):
    size = lax.axis_size("dp")
    return lax.ppermute(value, "dp", [(i, i ^ bit) for i in range(size)])


def after(value, *deps):
    return lax.optimization_barrier((value,) + deps)[0]


def bits_of(size):
    return [1 << k for k in range(size.bit_length() - 1)]


def row_order(bits):
    order = [0]
    for bit in reversed(bits):
        order = order + [mask | bit for mask in order]
    return order


def mlp_ways(bits):
    return (bits[:1] + ["mp"] + bits[1:], bits[1:] + bits[:1] + ["mp"])


def frame_ways(bits):
    return (bits[:1] + ["mp"] + bits[1:], ["mp"] + bits)


def gather_bits():
    bits = bits_of(lax.axis_size("dp"))
    return bits[:0:-1] + bits[:1]


def gather(value):
    for bit in gather_bits():
        value = jnp.concatenate([value, flip(value, bit)], axis=0)
    return value


def dot(a, b):
    return jnp.dot(a, b, preferred_element_type=F32)


def dot_nt(a, b):
    return lax.dot_general(a, b, (((1,), (1,)), ((), ())), preferred_element_type=F32)


def dot_tn(a, b):
    return lax.dot_general(a, b, (((0,), (0,)), ((), ())), preferred_element_type=F32)


def standardized(value):
    centered = value - jnp.mean(value, axis=-1, keepdims=True)
    rstd = lax.rsqrt(jnp.mean(centered * centered, axis=-1, keepdims=True) + 1e-05)
    return (centered * rstd, rstd)


def spread(rstd):
    return jnp.broadcast_to(rstd, (rstd.shape[0], 128))


def norm_backward(grad, gain, normal, rstd):
    scaled = grad * gain
    inner = (
        scaled
        - jnp.mean(scaled, axis=-1, keepdims=True)
        - normal * jnp.mean(scaled * normal, axis=-1, keepdims=True)
    )
    return (rstd * inner, jnp.sum(grad * normal, axis=0, keepdims=True))


def lane_half(rows, pair, which):
    lane = lax.broadcasted_iota(jnp.int32, (rows, pair), 1)
    return (lane < pair // 2) if which == 0 else (lane >= pair // 2)


def only(value, which):
    return jnp.where(lane_half(*value.shape, which), value, jnp.zeros_like(value))


def attend_pair(query, keys, values, valid):
    rows, pair = query.shape
    out = None
    sums = []
    for which in range(2):
        scores = dot_nt(only(query, which), keys)
        if valid < rows:
            key = lax.broadcasted_iota(jnp.int32, scores.shape, 1)
            scores = jnp.where(key < valid, scores, LOWEST)
        top = jnp.max(scores, axis=1, keepdims=True)
        each = jnp.exp(scores - top)
        total = jnp.sum(each, axis=1, keepdims=True)
        sums.append(top + jnp.log(total))
        part = dot(each.astype(BF), only(values, which)) * (1.0 / total)
        out = part if out is None else out + part
    return (out, sums)


def attend_pair_kept(query, keys, values, grad, logsums, inners, valid, scale):
    rows, _ = query.shape
    sums = [None, None, None]
    edge = valid // 16 * 16
    for which in range(2):
        query_own, key_own, grad_own = (only(query, which), only(keys, which), only(grad, which))
        weights = jnp.exp(dot_nt(keys, query_own) - logsums[which])
        tail = weights[edge:]
        row = lax.broadcasted_iota(jnp.int32, tail.shape, 0)
        weights = jnp.concatenate([weights[:edge], jnp.where(row < valid - edge, tail, 0.0)], axis=0)
        weight_grad = dot_nt(values, grad_own)
        value_grad = dot(weights.astype(BF), grad_own)
        score_grad = (weights * (weight_grad - inners[which])).astype(BF)
        key_grad = dot(score_grad, query_own)
        query_grad = dot_tn(score_grad, key_own) * scale
        parts = (query_grad, key_grad, value_grad)
        sums = [part if one is None else one + part for one, part in zip(sums, parts)]
    return [one.astype(BF) for one in sums]


def head_sums(value, size):
    head = lax.broadcasted_iota(jnp.int32, (16, value.shape[1]), 1) // size
    pick = (head == lax.broadcasted_iota(jnp.int32, head.shape, 0)).astype(F32).astype(BF)
    high = value.astype(BF)
    return dot_nt(pick, high) + dot_nt(pick, (value - high.astype(F32)).astype(BF))


def attend_pair_backward(query, keys, values, grad, valid, scale):
    rows, _ = query.shape
    sums = [None, None, None]
    for which in range(2):
        query_own, key_own, grad_own = (only(query, which), only(keys, which), only(grad, which))
        scores = dot_nt(keys, query_own)
        if valid < rows:
            key = lax.broadcasted_iota(jnp.int32, scores.shape, 0)
            scores = jnp.where(key < valid, scores, LOWEST)
        top = jnp.max(scores, axis=0, keepdims=True)
        each = jnp.exp(scores - top)
        weights = each * (1.0 / jnp.sum(each, axis=0, keepdims=True))
        weight_grad = dot_nt(values, grad_own)
        value_grad = dot(weights.astype(BF), grad_own)
        inner = jnp.sum(weights * weight_grad, axis=0, keepdims=True)
        score_grad = (weights * (weight_grad - inner)).astype(BF)
        key_grad = dot(score_grad, query_own)
        query_grad = dot_tn(score_grad, key_own) * scale
        parts = (query_grad, key_grad, value_grad)
        sums = [part if one is None else one + part for one, part in zip(sums, parts)]
    return [one.astype(BF) for one in sums]


def project(normed, in_ref, scale):
    wide = in_ref.shape[2]
    query = dot(normed, in_ref[0]).astype(BF) * jnp.asarray(scale, BF)
    keys = dot(normed, in_ref[1]).astype(BF)
    values = dot(normed, in_ref[2]).astype(BF)
    return (query, keys, values, wide)


def turn_rows(ways, count, which, to_ref, from_ref, place_ref):
    rows = to_ref.shape[0]
    pairs = 8 if count is None else 1 << count
    block = rows // (2 * pairs)
    turned = from_ref[...].T
    me = place_ref[1]
    for j in range(2 * pairs):
        if count is None:
            spot = j // 2 + (j % 2) * pairs
        else:
            mask = (me >> 1) ^ (j >> 1)
            order = [k for k in ways(list(range(count)))[which] if k != "mp"]
            spot = sum(((mask >> k) & 1) << (count - 1 - i) for i, k in enumerate(order))
            spot = spot + ((me ^ j) & 1) * pairs
        to_ref[pl.ds(pl.multiple_of(spot * block, 16), block), :] = turned[block * j : block * (j + 1)]


def put_product(keep_ref, send_ref, lead, turned_ref, value):
    rows = keep_ref.shape[1]
    keep_ref[lead] = dot(turned_ref[:rows], value).astype(BF)
    send_ref[lead] = dot(turned_ref[rows:], value).astype(BF)


def frame_rows(wide_ref, frame, patches):
    at = pl.ds(frame, patches, stride=8)
    return jnp.concatenate([wide_ref[j, at, :] for j in range(wide_ref.shape[0])], axis=1)


def widen(wide_ref, from_ref):
    for j in range(wide_ref.shape[0]):
        value = from_ref[:, :, 128 * j : 128 * (j + 1)].astype(F32)
        wide_ref[j] = value.reshape(wide_ref.shape[1:])


def put_class_rows(to_ref, rows_ref, half):
    seq = to_ref.shape[0] // half
    for f in range(half):
        old = to_ref[f * seq : f * seq + 16, :].astype(F32)
        row = lax.broadcasted_iota(jnp.int32, old.shape, 0)
        new = jnp.where(row == 0, rows_ref[f : f + 1, :].astype(F32), old)
        to_ref[f * seq : f * seq + 16, :] = new.astype(to_ref.dtype)


def class_rows(from_ref, half, dtype, count):
    seq = from_ref.shape[0] // half
    rows = [from_ref[f * seq : f * seq + 16, :].astype(F32)[0:1] for f in range(half)]
    rows.append(jnp.zeros((count - half, from_ref.shape[1]), F32))
    return jnp.concatenate(rows, axis=0).astype(dtype)


def message_forward_kernel(
    heads, place_ref, tok_ref, captions_ref, w_ref, gain_ref, in_ref, out_ref, message_ref, early_ref, qkv_ref, part_ref
):
    cls = tok_ref[0, 0]
    frames, width = cls.shape
    message = dot(cls, w_ref[...])
    message_ref[...] = message
    normal, _ = standardized(message)
    low = (normal * gain_ref[...]).astype(BF)
    size = width // heads
    query, keys, values, wide = project(low, in_ref, size**-0.5)
    contexts = []
    for j in range(wide // (2 * size)):
        at = slice(2 * size * j, 2 * size * (j + 1))
        contexts.append(attend_pair(query[:, at], keys[:, at], values[:, at], frames)[0])
    context = jnp.concatenate(contexts, axis=1).astype(BF)
    part_ref[...] = dot(context, out_ref[...])
    qkv_ref[:, :wide] = query
    qkv_ref[:, wide : 2 * wide] = keys
    qkv_ref[:, 2 * wide :] = values

    def padded(value):
        value = value.astype(F32)
        return jnp.concatenate([value, jnp.zeros((16 - value.shape[0], value.shape[1]), F32)], axis=0)

    early_ref[:, width : 2 * width] = padded(low).astype(BF)
    early_ref[:, 2 * width :] = padded(context).astype(BF)
    embed = captions_ref.shape[1]
    lane = lax.broadcasted_iota(jnp.int32, (1, width - embed), 1)
    ids = jnp.where(lane == 0, place_ref[2], jnp.where(lane == 1, place_ref[3], 0)).astype(F32)
    text = jnp.concatenate([captions_ref[...].astype(F32), ids], axis=1)
    row = lax.broadcasted_iota(jnp.int32, (8, width), 0)
    text = jnp.where(row == 0, text, 0.0)
    early_ref[:, :width] = jnp.concatenate([cls.astype(F32), text], axis=0).astype(BF)


def frame_attention(heads, valid, low, in_ref, qkv_ref, context_ref, logsum_ref):
    size = low.shape[1] // heads
    wide = in_ref.shape[2]
    for k in range(3):
        value = dot(low, in_ref[k]).astype(BF)
        if k == 0:
            value = value * jnp.asarray(size**-0.5, BF)
        qkv_ref[0, :, wide * k : wide * (k + 1)] = value
    lane = lax.broadcasted_iota(jnp.int32, (low.shape[0], 128), 1)
    logsums = jnp.zeros(lane.shape, F32)
    for j in range(wide // (2 * size)):
        query, keys, values = (
            qkv_ref[0, :, wide * k + 2 * size * j : wide * k + 2 * size * (j + 1)] for k in range(3)
        )
        context, sums = attend_pair(query, keys, values, valid)
        context_ref[0, :, 2 * size * j : 2 * size * (j + 1)] = context.astype(BF)
        for which, one in enumerate(sums):
            logsums = jnp.where(lane == 2 * j + which, one, logsums)
    logsum_ref[0] = logsums


def frame_first_kernel(
    heads, half, place_ref, tok_ref, message_ref, part_ref, other_ref, gain_ref, in_ref,
    stream_ref, low_ref, qkv_ref, context_ref, rstd_ref, logsum_ref, wide_ref, rows_ref,
):
    patches, frames, width = tok_ref.shape
    seq = stream_ref.shape[1]
    frame = place_ref[0] * half + pl.program_id(0)

    @pl.when(pl.program_id(0) == 0)
    def _():
        widen(wide_ref, tok_ref)

    at = pl.ds(frame, 1)
    message = message_ref[at, :] + (part_ref[at, :] + other_ref[at, :])
    edge = patches // 8 * 8
    rows_ref[edge:seq, :] = jnp.zeros((seq - edge, width), F32)
    rows_ref[0:patches, :] = frame_rows(wide_ref, frame, patches)
    rows_ref[patches : patches + 1, :] = message
    stream_ref[0] = rows_ref[...].astype(BF)
    normal, rstd = standardized(rows_ref[...])
    rstd_ref[0] = spread(rstd)
    low = (normal * gain_ref[...]).astype(BF)
    low_ref[0] = low
    frame_attention(heads, patches + 1, low, in_ref, qkv_ref, context_ref, logsum_ref)


def joined(place_ref, to_ref, mine_ref, theirs_ref, axis):
    rows = mine_ref.shape[axis]
    core = place_ref[1] & 1
    lead = (slice(None),) * axis
    to_ref[lead + (pl.ds(pl.multiple_of(core * rows, 16), rows),)] = mine_ref[...]
    to_ref[lead + (pl.ds(pl.multiple_of((1 - core) * rows, 16), rows),)] = theirs_ref[...]


def frame_second_kernel(
    heads, valid, place_ref, low_ref, mine_ref, theirs_ref, qkv_ref, context_ref, in_ref, logsum_ref
):
    @pl.when(pl.program_id(0) == 0)
    def _():
        joined(place_ref, in_ref, mine_ref, theirs_ref, 1)

    frame_attention(heads, valid, low_ref[0], in_ref, qkv_ref, context_ref, logsum_ref)


def cotangent_kernel(half, place_ref, cot_ref, down_ref, grad_ref, dact_ref, wide_ref):
    patches, frames, width = cot_ref.shape
    seq = grad_ref.shape[0] // half

    @pl.when(pl.program_id(0) == 0)
    def _():
        widen(wide_ref, cot_ref)
        edge = patches // 16 * 16
        for f in range(half):
            value = frame_rows(wide_ref, place_ref[0] * half + f, patches)
            tail = jnp.concatenate([value[edge:], jnp.zeros((seq - patches, width), F32)], axis=0)
            grad_ref[f * seq : f * seq + edge, :] = value[:edge].astype(BF)
            grad_ref[f * seq + edge : (f + 1) * seq, :] = tail.astype(BF)

    dact_ref[...] = dot_nt(grad_ref[...], down_ref[...]).astype(BF)


def gate(hidden):
    sigmo = 1.0 / (1.0 + jnp.exp(-1.702 * hidden))
    gated = hidden * sigmo
    return (gated, sigmo + 1.702 * gated * (1.0 - sigmo))


def up_block(ref):
    return ref[...].reshape(ref.shape[0] * ref.shape[1], ref.shape[2])


def mlp_first_kernel(
    half, stream_ref, own_ref, other_ref, out_own_ref, out_other_ref, gain_ref, up_ref, down_ref, dact_ref,
    rstd_ref, low_ref, activ_ref, dhid_ref, slope_ref, total_ref, back_ref, cls_low_ref, cls_total_ref,
):
    step = pl.program_id(0)

    @pl.when(step == 0)
    def _():
        branch = dot(own_ref[...], out_own_ref[...]) + dot(other_ref[...], out_other_ref[...])
        middle = stream_ref[...].astype(F32) + branch
        normal, rstd = standardized(middle)
        rstd_ref[...] = spread(rstd)
        low_ref[...] = (normal * gain_ref[...]).astype(BF)
        total_ref[...] = middle
        back_ref[...] = jnp.zeros_like(back_ref)
        cls_low_ref[...] = class_rows(low_ref, half, BF, 16)

    seq = low_ref.shape[0] // half
    activ, slope = gate(dot(low_ref[...], up_ref[...]))
    activ_ref[...] = activ.astype(BF)
    dhid_ref[...] = (dact_ref[...].astype(F32) * slope).astype(BF)
    rows = [slope[f * seq : f * seq + 1] for f in range(half)]
    slope_ref[...] = jnp.concatenate(rows + [jnp.zeros((16 - half, slope.shape[1]), F32)], axis=0)
    total_ref[...] += dot(activ_ref[...], down_ref[...])
    back_ref[...] += dot_nt(dhid_ref[...], up_ref[...])

    @pl.when(step == pl.num_programs(0) - 1)
    def _():
        cls_total_ref[...] = class_rows(total_ref, half, F32, 16)


def class_forward_kernel(half, low_ref, start_ref, up_ref, down_ref, pooled_ref, total_ref):
    step = pl.program_id(0)

    @pl.when(step == 0)
    def _():
        total_ref[...] = start_ref[...]

    activ, _ = gate(dot(low_ref[...], up_block(up_ref)))
    total_ref[...] += dot(activ.astype(BF), up_block(down_ref))

    @pl.when(step == pl.num_programs(0) - 1)
    def _():
        pooled_ref[...] = jnp.sum(total_ref[0:half, :], axis=0, keepdims=True)


def mlp_second_kernel(half, start_ref, low_ref, up_ref, down_ref, activ_ref, slope_ref, total_ref):
    @pl.when(pl.program_id(0) == 0)
    def _():
        total_ref[...] = start_ref[...]

    activ, slope = gate(dot(low_ref[...], up_block(up_ref)))
    activ_ref[...] = activ.astype(BF)
    slope_ref[...] = slope.astype(BF)
    total_ref[...] += dot(activ_ref[...], up_block(down_ref))


def mlp_third_kernel(half, start_ref, low_ref, up_ref, down_ref, _, __, activ_ref, slope_ref, result_ref, total_ref):
    mlp_second_kernel(half, start_ref, low_ref, up_ref, down_ref, activ_ref, slope_ref, total_ref)

    @pl.when(pl.program_id(0) == pl.num_programs(0) - 1)
    def _():
        result_ref[...] = total_ref[...].astype(BF)


def hidden_backward_kernel(start_ref, grad_ref, slope_ref, up_ref, down_ref, *refs):
    dhid_ref, back_ref = refs[-2:]

    @pl.when(pl.program_id(0) == 0)
    def _():
        back_ref[...] = start_ref[...]

    dact = dot_nt(grad_ref[...], up_block(down_ref))
    dhid_ref[...] = (dact * slope_ref[...].astype(F32)).astype(BF)
    back_ref[...] += dot_nt(dhid_ref[...], up_block(up_ref))


def loss_kernel(
    order, frames, place_ref, early_ref, proj_ref,
    loss_ref, caption_grad_ref, embed_grad_ref, pooled_all_ref, pooled_grad_ref,
):
    clips = early_ref.shape[0]
    width, wide = proj_ref.shape
    me = place_ref[1]
    early = early_ref[...].astype(F32)[:, frames, :].astype(BF)
    block = lax.broadcasted_iota(jnp.int32, (clips, clips), 1)
    mask = jnp.zeros_like(block)
    for k, bit in enumerate(order):
        mask = mask + ((block >> k) & 1) * bit
    row = lax.broadcasted_iota(jnp.int32, (clips, clips), 0)
    pick = (row == jnp.bitwise_xor(mask, me)).astype(F32).astype(BF)
    text = dot(pick, early[:, :width]).astype(BF)
    pooled = dot(pick, early[:, width : 2 * width]).astype(BF)
    pooled_all_ref[...] = pooled
    embed = dot(pooled, proj_ref[...])
    embed_rinv = lax.rsqrt(jnp.sum(embed * embed, axis=-1, keepdims=True) + 1e-06)
    embed_low = (embed * embed_rinv).astype(BF)
    caption_f = text[:, :wide].astype(F32)
    caption_rinv = lax.rsqrt(jnp.sum(caption_f * caption_f, axis=-1, keepdims=True) + 1e-06)
    caption_low = (caption_f * caption_rinv).astype(BF)
    scores = SHARPNESS * dot_nt(embed_low, caption_low)
    lane = lax.broadcasted_iota(jnp.int32, (8, text.shape[1] - wide), 1)
    pick_id = (lane == 1).astype(F32).astype(BF)
    caption_ids = dot_nt(pick_id, text[:, wide:])[0:1, :]
    clip_ids = text[:, wide:].astype(F32)[:, 0:1]
    positive = clip_ids == caption_ids
    masked = jnp.where(positive, scores, LOWEST)

    def side(axis):
        top = jnp.max(scores, axis=axis, keepdims=True)
        each = jnp.exp(scores - top)
        total = jnp.sum(each, axis=axis, keepdims=True)
        pos_top = jnp.max(masked, axis=axis, keepdims=True)
        pos_each = jnp.where(positive, jnp.exp(masked - pos_top), 0.0)
        pos_total = jnp.sum(pos_each, axis=axis, keepdims=True)
        part = jnp.sum(top + jnp.log(total) - pos_top - jnp.log(pos_total), axis=1 - axis, keepdims=True)
        return (part, each / total - pos_each / pos_total)

    row_loss, row_grad = side(1)
    column_loss, column_grad = side(0)
    loss_ref[...] = 0.5 * (row_loss + column_loss)
    dscore = 0.5 * (row_grad + column_grad)
    embed_grad = SHARPNESS * dot(dscore.astype(BF), caption_low)
    caps_grad = SHARPNESS * dot_tn(dscore.astype(BF), embed_low)
    caption_grad = caption_rinv * caps_grad - caption_f * (
        caption_rinv * caption_rinv * caption_rinv * jnp.sum(caption_f * caps_grad, axis=-1, keepdims=True)
    )
    embed_diff = embed_rinv * embed_grad - embed * (
        embed_rinv * embed_rinv * embed_rinv * jnp.sum(embed * embed_grad, axis=-1, keepdims=True)
    )
    embed_diff = embed_diff.astype(BF)
    embed_grad_ref[...] = embed_diff
    grads = dot_nt(embed_diff, proj_ref[...])

    def own_row(value):
        own = lax.broadcasted_iota(jnp.int32, value.shape, 0) == me
        return jnp.sum(jnp.where(own, value, 0.0), axis=0, keepdims=True)

    caption_grad_ref[...] = own_row(caption_grad)
    pooled_grad_ref[...] = own_row(grads) / frames


def class_backward_kernel(
    half, place_ref, cot_ref, pooled_ref, slope_own_ref, slope_other_ref, up_own_ref, down_own_ref, up_ref, down_ref,
    grad_ref, dhid_own_ref, dhid_other_ref, back_ref,
):
    @pl.when(pl.program_id(0) == 0)
    def _():
        cot = cot_ref[0, 0].astype(F32)
        cot = jnp.where(place_ref[0] == 0, cot[:half], cot[half:]) + pooled_ref[...]
        grad_ref[...] = jnp.concatenate([cot, jnp.zeros((16 - half, cot.shape[1]), F32)], axis=0).astype(BF)
        back_ref[...] = jnp.zeros_like(back_ref)

    grad = grad_ref[...]
    dhid_own_ref[...] = (dot_nt(grad, down_own_ref[...]) * slope_own_ref[...]).astype(BF)
    dhid_other_ref[...] = (dot_nt(grad, up_block(down_ref)) * slope_other_ref[...]).astype(BF)
    back_ref[...] += dot_nt(dhid_own_ref[...], up_own_ref[...]) + dot_nt(dhid_other_ref[...], up_block(up_ref))


def mlp_weight_kernel(
    half, count, place_ref, grad_ref, grad_cls_ref, low_ref, activ_own_ref, dhid_own_ref, dhid_cls_own_ref,
    activ_other_ref, dhid_other_ref, dhid_cls_other_ref,
    keep_own_ref, send_own_ref, keep_other_ref, send_other_ref, grad_t_ref, low_t_ref, fixed_ref, rows_ref,
):
    step = pl.program_id(0)
    steps = pl.num_programs(0) // 2

    @pl.when(step == 0)
    def _():
        rows_ref[...] = grad_ref[...]
        put_class_rows(rows_ref, grad_cls_ref, half)
        turn_rows(mlp_ways, count, 0, low_t_ref, low_ref, place_ref)
        turn_rows(mlp_ways, count, 1, grad_t_ref, rows_ref, place_ref)

    def part(activ_ref, dhid_ref, dhid_cls_ref, keep_ref, send_ref):
        fixed_ref[...] = dhid_ref[...]
        put_class_rows(fixed_ref, dhid_cls_ref, half)
        put_product(keep_ref, send_ref, 0, low_t_ref, fixed_ref[...])
        put_product(keep_ref, send_ref, 1, grad_t_ref, activ_ref[...])

    @pl.when(step < steps)
    def _():
        part(activ_other_ref, dhid_other_ref, dhid_cls_other_ref, keep_other_ref, send_other_ref)

    @pl.when(step >= steps)
    def _():
        part(activ_own_ref, dhid_own_ref, dhid_cls_own_ref, keep_own_ref, send_own_ref)


def frame_backward_kernel(
    heads, valid, half, first, back_ref, grad_in_ref, mid_ref, mid_rstd_ref, own_ref, other_ref, low_in_ref, rstd_ref,
    context_own_ref, context_other_ref, logsum_own_ref, logsum_other_ref,
    back_cls_ref, grad_cls_ref, mlp_gain_ref, gain_ref, out_own_ref, out_other_ref, in_own_ref, in_other_ref, *refs,
):
    low_ref, down_ref, dother_ref, token_ref, edge_ref = refs[-5:]
    step = pl.program_id(0)
    f = first + step
    width = back_ref.shape[1]
    size = width // heads
    scale = size**-0.5
    row = lax.broadcasted_iota(jnp.int32, back_ref.shape, 0)
    at = pl.ds(f, 1)
    back = jnp.where(row == 0, back_cls_ref[at, :], back_ref[...])
    cls = jnp.zeros((1, width), F32)
    for k in range(half):
        cls = jnp.where(f == k, grad_cls_ref[...].astype(F32)[k : k + 1], cls)
    grad = jnp.where(row == 0, cls, grad_in_ref[...].astype(F32))
    normal = mid_ref[...].astype(F32) * (1.0 / mlp_gain_ref[...])
    part, mlp_gain_grad = norm_backward(back, mlp_gain_ref[...], normal, mid_rstd_ref[:, 0:1])
    grad = grad + part
    low = grad.astype(BF)
    low_ref[0] = low
    normed_grad = None
    for qkv_ref, context_ref, logsum_ref, out_ref, in_ref, to_ref in (
        (own_ref, context_own_ref, logsum_own_ref, out_own_ref, in_own_ref, down_ref),
        (other_ref, context_other_ref, logsum_other_ref, out_other_ref, in_other_ref, dother_ref),
    ):
        wide = in_ref.shape[2]
        context_grad = dot_nt(low, out_ref[...]).astype(BF)
        inners = head_sums(context_grad.astype(F32) * context_ref[0].astype(F32), size)
        logsums = logsum_ref[0].T
        for j in range(wide // (2 * size)):
            query, keys, values = (
                qkv_ref[0, :, wide * k + 2 * size * j : wide * k + 2 * size * (j + 1)] for k in range(3)
            )
            grads = attend_pair_kept(
                query,
                keys,
                values,
                context_grad[:, 2 * size * j : 2 * size * (j + 1)],
                [logsums[2 * j + which : 2 * j + which + 1] for which in range(2)],
                [inners[2 * j + which : 2 * j + which + 1] for which in range(2)],
                valid,
                scale,
            )
            for k in range(3):
                to_ref[0, :, wide * k + 2 * size * j : wide * k + 2 * size * (j + 1)] = grads[k]
        for k in range(3):
            part = dot_nt(to_ref[0, :, wide * k : wide * (k + 1)], in_ref[k])
            normed_grad = part if normed_grad is None else normed_grad + part
    normal = low_in_ref[0].astype(F32) * (1.0 / gain_ref[...])
    part, gain_grad = norm_backward(normed_grad, gain_ref[...], normal, rstd_ref[0, :, 0:1])
    total = grad + part
    token_ref[0] = total.astype(BF)

    @pl.when(step == 0)
    def _():
        if first == 0:
            edge_ref[...] = jnp.zeros_like(edge_ref)
        else:
            edge_ref[...] = refs[3][...]

    edge_ref[pl.ds(f, 1), :] = total[0:1]
    edge_ref[pl.ds(half + f, 1), :] = total[valid - 1 : valid]
    edge_ref[2 * half : 2 * half + 1, :] += gain_grad
    edge_ref[2 * half + 1 : 2 * half + 2, :] += mlp_gain_grad


def frame_weight_kernel(
    count, place_ref, low_ref, grad_ref, down_ref, dother_ref, own_ref, other_ref,
    keep_own_ref, send_own_ref, keep_other_ref, send_other_ref, low_t_ref, grad_t_ref,
):
    step = pl.program_id(0)

    @pl.when(step == 0)
    def _():
        turn_rows(frame_ways, count, 0, low_t_ref, low_ref, place_ref)
        turn_rows(frame_ways, count, 0, grad_t_ref, grad_ref, place_ref)

    for first, dqkv_ref, context_ref, keep_ref, send_ref in (
        (0, dother_ref, other_ref, keep_other_ref, send_other_ref),
        (4, down_ref, own_ref, keep_own_ref, send_own_ref),
    ):

        @pl.when((step >= first) & (step < first + 3))
        def _(dqkv_ref=dqkv_ref, keep_ref=keep_ref, send_ref=send_ref):
            put_product(keep_ref, send_ref, 0, low_t_ref, dqkv_ref[...])

        @pl.when(step == first + 3)
        def _(context_ref=context_ref, keep_ref=keep_ref, send_ref=send_ref):
            put_product(keep_ref, send_ref, 0, grad_t_ref, context_ref[...])


def both_halves(place, own, other):
    return jnp.concatenate(
        [jnp.where(place == 0, own, other), jnp.where(place == 0, other, own)], axis=0
    )


def message_backward_kernel(
    heads, place_ref, own_ref, other_ref, qkv_ref, out_ref, in_ref, next_ref, low_ref, dqkv_ref, part_ref
):
    frames, width = next_ref.shape
    half = frames // 2
    at = slice(half, 2 * half)
    grad = both_halves(place_ref[0], own_ref[at, :], other_ref[at, :])
    next_ref[...] = grad
    low = grad.astype(BF)
    low_ref[...] = low
    size = width // heads
    scale = size**-0.5
    wide = in_ref.shape[2]
    context_grad = dot_nt(low, out_ref[...]).astype(BF)
    for j in range(wide // (2 * size)):
        query, keys, values = (
            qkv_ref[:, wide * k + 2 * size * j : wide * k + 2 * size * (j + 1)] for k in range(3)
        )
        grads = attend_pair_backward(
            query, keys, values, context_grad[:, 2 * size * j : 2 * size * (j + 1)], frames, scale
        )
        for k in range(3):
            dqkv_ref[:, wide * k + 2 * size * j : wide * k + 2 * size * (j + 1)] = grads[k]
    total = None
    for k in range(3):
        part = dot_nt(dqkv_ref[:, wide * k : wide * (k + 1)], in_ref[k])
        total = part if total is None else total + part
    part_ref[...] = total


def message_last_kernel(
    place_ref, own_ref, other_ref, next_ref, low_ref, dqkv_ref, part_ref, part_other_ref, message_ref, gain_ref, w_ref,
    late_ref, cls_ref,
):
    frames, width = next_ref.shape
    half = frames // 2
    normal, rstd = standardized(message_ref[...])
    part, gain_grad = norm_backward(part_ref[...] + part_other_ref[...], gain_ref[...], normal, rstd)
    message_low = (next_ref[...] + part).astype(BF)
    cls = both_halves(place_ref[0], own_ref[0:half, :], other_ref[0:half, :])
    cls_ref[...] = (cls + dot_nt(message_low, w_ref[...])).astype(BF)
    wide = dqkv_ref.shape[1]
    late_ref[0:frames, 0:width] = low_ref[...]
    late_ref[0:frames, width : 2 * width] = message_low
    late_ref[0:frames, 2 * width : 2 * width + wide] = dqkv_ref[...]
    both = own_ref[2 * half : 2 * half + 2, :] + other_ref[2 * half : 2 * half + 2, :]
    gains = jnp.concatenate([both[1:2], both[0:1], gain_grad], axis=1)
    room = late_ref.shape[1] - 2 * width - wide
    gains = jnp.concatenate([gains, jnp.zeros((1, frames * room - 3 * width), F32)], axis=1)
    gains = jnp.concatenate([gains[:, room * r : room * (r + 1)] for r in range(frames)], axis=0)
    late_ref[:, 2 * width + wide :] = gains.astype(BF)


def assemble_kernel(pieces, place_ref, *refs):
    out_ref, wide_ref = refs[-2:]
    tile, frames, width = out_ref.shape
    half = frames // 2
    for side in range(2):
        mp = place_ref[0] if side == 0 else 1 - place_ref[0]
        for k in range(half):
            per = half // pieces
            value = refs[side * pieces + k // per][k % per].astype(F32)
            for j in range(width // 128):
                wide_ref[j, pl.ds(mp * half + k, tile, stride=8), :] = value[:, 128 * j : 128 * (j + 1)]
    for j in range(width // 128):
        out_ref[:, :, 128 * j : 128 * (j + 1)] = wide_ref[j].reshape(tile, frames, 128).astype(BF)
    if len(refs) > 2 * pieces + 2:

        @pl.when(pl.program_id(0) == 0)
        def _():
            out_ref[0] = refs[2 * pieces][...]


def factor_kernel(
    frames, place_ref, early_ref, late_ref, pooled_ref, embed_ref,
    weight_ref, in_ref, out_ref, proj_ref, gains_ref,
):
    size = early_ref.shape[0]
    share, width = weight_ref.shape
    wide = out_ref.shape[1]
    column = lax.broadcasted_iota(jnp.int32, (share, width), 1)
    row = lax.broadcasted_iota(jnp.int32, (share, width), 0)
    pick = (column == place_ref[1] * share + row).astype(F32).astype(BF)

    def early(first, wide):
        value = early_ref[:, :, first : first + wide].astype(F32)[:, :frames]
        return value.reshape(size * frames, wide).astype(BF)

    def late(first, wide):
        return late_ref[:, :, first : first + wide].astype(F32).reshape(size * frames, wide).astype(BF)

    def own(value):
        return dot_nt(pick, value).astype(BF)

    weight_ref[...] = dot(own(early(0, width)), late(width, width))
    product = dot(own(early(width, width)), late(2 * width, 3 * wide))
    for k in range(3):
        in_ref[k] = product[:, wide * k : wide * (k + 1)]
    out_ref[...] = dot(own(late(0, width)), early(2 * width, wide))
    proj_ref[...] = dot(own(pooled_ref[...]), embed_ref[...])
    room = late_ref.shape[2] - 2 * width - 3 * wide
    gains = jnp.sum(late_ref[:, :, 2 * width + 3 * wide :].astype(F32), axis=0)
    gains = jnp.concatenate([gains[r : r + 1, :] for r in range(frames)], axis=1)
    for k in range(3):
        gains_ref[k : k + 1, :] = gains[:, width * k : width * (k + 1)]


def whole(shape):
    return pl.BlockSpec(tuple(shape), lambda *_: (0,) * len(shape))


def run(kernel, name, args, outs, grid=(1,), prefetch=0, specs=None, out_specs=None, scratch=(), aliases=None, deps=(), cost=2):
    specs = specs or {}
    out_specs = out_specs or {}
    tensors = args[prefetch:]
    taken = len(args)

    def body(*refs):
        kernel(*refs[:taken], *refs[taken + len(deps) :])

    return pl.pallas_call(
        body,
        out_shape=list(outs),
        grid_spec=pltpu.PrefetchScalarGridSpec(
            num_scalar_prefetch=prefetch,
            grid=grid,
            in_specs=[specs.get(k, whole(t.shape)) for k, t in enumerate(tensors)]
            + [pl.BlockSpec(memory_space=pl.ANY)] * len(deps),
            out_specs=[out_specs.get(k, whole(o.shape)) for k, o in enumerate(outs)],
            scratch_shapes=list(scratch),
        ),
        compiler_params=pltpu.CompilerParams(
            dimension_semantics=("arbitrary",) * len(grid), vmem_limit_bytes=VMEM_BYTES
        ),
        cost_estimate=pl.CostEstimate(flops=round(KERNEL_US.get(name, cost) * 2.3e9), bytes_accessed=0, transcendentals=0),
        input_output_aliases={prefetch + k: out for k, out in (aliases or {}).items()},
        name=name,
    )(*args, *deps)


def shape_of(shape, dtype):
    return jax.ShapeDtypeStruct(tuple(shape), dtype)


def plus(a, b, dtype=BF):
    return (a.astype(F32) + b.astype(F32)).astype(dtype)


def reorder(ways, keep, send):
    size = lax.axis_size("dp")
    bits = bits_of(size)
    lead, rows, wide = keep.shape
    block = 2 * rows // 16
    value = jnp.stack([keep.reshape(lead, 8, block, wide), send.reshape(lead, 8, block, wide)], axis=2)
    value = value.reshape(lead, size, 2 * rows // size, wide)
    turned = []
    for one, order in zip(value, ways(bits[1:])):
        order = [bit for bit in order if bit != "mp"]
        order = jnp.bitwise_xor(jnp.asarray(row_order(bits[:1] + order), jnp.int32), lax.axis_index("dp"))
        turned.append(jnp.take(one, order, axis=0).reshape(2 * rows, wide))
    value = jnp.stack(turned)
    return (value[:, :rows], value[:, rows:])


def joint(ways):
    return ways[0] == ways[1] and ways[0] not in (None, "mp")


def stage_values(keep_first, keep_second, *got):
    parts = keep_first.shape[0]
    came = (got[0][:parts], got[0][parts:]) if len(got) == 1 else (got[0][...], got[1][...])
    return [keep[...].astype(F32) + one.astype(F32) for keep, one in zip((keep_first, keep_second), came)]


def stage_kernel(ways, came, *refs):
    values = stage_values(*refs[: 2 + came])
    refs = refs[2 + came :]
    if joint(ways):
        at = 0
        for k, value in enumerate(values):
            parts, rows, _ = value.shape
            refs[k][...] = value[:, : rows // 2].astype(BF)
            refs[2][at : at + parts] = value[:, rows // 2 :].astype(BF)
            at += parts
        return
    per = len(refs) // 2
    for k, (value, way) in enumerate(zip(values, ways)):
        keep, send = (refs[per * k], refs[per * (k + 1) - 1])
        if way is None:
            keep[...] = value
        elif way == "mp":
            keep[...] = value[0:1].astype(BF)
            send[...] = value[1:2].astype(BF)
        else:
            rows = value.shape[1] // 2
            keep[...] = value[:, :rows].astype(BF)
            send[...] = value[:, rows:].astype(BF)


def frame_final_kernel(keep_first, keep_second, got, in_ref, out_ref):
    first, second = stage_values(keep_first, keep_second, got)
    wide = out_ref.shape[1]
    in_ref[0] = first[0][:, :wide]
    in_ref[1] = first[0][:, wide:]
    in_ref[2] = second[0][:, :wide]
    out_ref[...] = second[0][:, wide:]


def core_stage_kernel(ways, keep_own, got_own, keep_other, got_other, *refs):
    for k in range(2):
        parts = [
            keep[k : k + 1].astype(F32) + got[k : k + 1].astype(F32)
            for keep, got in ((keep_own, got_own), (keep_other, got_other))
        ]
        for part, at in zip(parts, range(2)):
            if ways[k] == "mp":
                refs[2 * k + at][...] = part.astype(BF)
                continue
            rows = part.shape[1] // 2
            refs[2 * k][at : at + 1] = part[:, :rows].astype(BF)
            refs[2 * k + 1][at : at + 1] = part[:, rows:].astype(BF)


class Reduction:
    def __init__(self, name, ways, keep_own, send_own, keep_other, send_other):
        size = lax.axis_size("dp")
        self.name = name
        self.bits = bits_of(size)
        self.aligned = (2 * keep_own.shape[1] // size) % 16 == 0
        if not self.aligned:
            keep_own, send_own = reorder(ways, keep_own, send_own)
            keep_other, send_other = reorder(ways, keep_other, send_other)
        self.ways = ways(self.bits[1:])
        self.steps = len(self.ways[0])
        self.at = 0
        self.keep = (keep_own, keep_other)
        self.got = tuple(flip(send, self.bits[0]) for send in (send_own, send_other))

    def ways_at(self, at):
        return tuple(ways[at] if at < self.steps else None for ways in self.ways)

    def outs(self, shapes, ways):
        made = []
        if joint(ways):
            parts = [shape[0] for shape in shapes]
            _, rows, wide = shapes[0]
            return [shape_of((count, rows // 2, wide), BF) for count in parts + [sum(parts)]]
        for (parts, rows, wide), way in zip(shapes, ways):
            if way is None:
                made.append(shape_of((parts, rows, wide), F32))
            elif way == "mp":
                made += [shape_of((1, rows, wide), BF)] * 2
            else:
                made += [shape_of((parts, rows // 2, wide), BF)] * 2
        return made

    def call(self, kernel, args, shapes, ways, deps, cost):
        if not self.aligned:
            refs = [Box(out) for out in self.outs(shapes, ways)]
            kernel(ways, *args, *refs)
            return [ref.value for ref in refs]
        made = self.outs(shapes, ways)
        wide = made[0].shape[2]
        chunk = 384

        def spec(value):
            return pl.BlockSpec(value.shape[:2] + (chunk,), lambda j, *_: (0, 0, j))

        return run(
            functools.partial(kernel, ways),
            self.name + str(self.at),
            args,
            made,
            grid=(wide // chunk,),
            specs={k: spec(value) for k, value in enumerate(args)},
            out_specs={k: spec(value) for k, value in enumerate(made)},
            deps=deps,
            cost=cost,
        )

    def take(self, made):
        self.joined = made[2:] if len(made) == 3 else []
        per = (len(made) - len(self.joined)) // 2
        self.value = [made[per * k : per * (k + 1)] for k in range(2)]

    def cores(self, *deps, cost=0):
        own, other = self.keep
        _, rows, wide = own.shape
        args = (own, self.got[0], other, self.got[1])
        self.take(self.call(core_stage_kernel, args, [(2, rows, wide)] * 2, self.ways_at(0), deps, cost))
        self.at = 0
        self.send()

    def send(self):
        ways = self.ways_at(self.at)
        if self.joined:
            self.got = [flip(self.joined[0], ways[0])]
            return
        self.got = []
        for (_, send), way in zip(self.value, ways):
            self.got.append(swap(send) if way == "mp" else flip(send, way))

    def ready(self):
        return tuple(one for values in self.value for one in values)

    def parts(self):
        return (self.value[0][0], self.value[1][0], *self.got)

    def step(self, *deps, cost=0):
        args = self.parts()
        shapes = [value[0].shape for value in self.value]
        self.at += 1
        kernel = lambda ways, *refs: stage_kernel(ways, len(args) - 2, *refs)
        self.take(self.call(kernel, args, shapes, self.ways_at(self.at), deps, cost))
        if self.at < self.steps:
            self.send()


class Box:
    def __init__(self, out):
        self.value = jnp.zeros(out.shape, out.dtype)

    def __setitem__(self, at, value):
        self.value = value if at is Ellipsis else self.value.at[at].set(value)


def on_device(
    tokens,
    captions,
    clip_groups,
    caption_groups,
    msg_weight,
    msg_gain,
    msg_in,
    msg_out,
    frame_gain,
    frame_in,
    frame_out,
    mlp_gain,
    up_weight,
    down_weight,
    proj_weight,
    out_cot,
):
    clips, frames, patches, width = tokens.shape
    assert clips == 1 and frames == 8 and lax.axis_size("mp") == 2
    size = lax.axis_size("dp")
    valid = patches + 1
    seq = -(-valid // 16) * 16
    half = frames // 2
    rows = half * seq
    share = width // size
    aligned = share % 16 == 0
    count = len(bits_of(size)) - 1 if aligned else None
    h_half = frame_in.shape[2]
    f_half = up_weight.shape[1]
    embed = proj_weight.shape[1]
    me_dp, me_mp = (lax.axis_index("dp"), lax.axis_index("mp"))
    place = jnp.stack([me_mp, me_dp, clip_groups[0], caption_groups[0]]).astype(jnp.int32)
    msg_gain, frame_gain, mlp_gain = (gain.reshape(1, width) for gain in (msg_gain, frame_gain, mlp_gain))
    tokens_t, cot_t = (jnp.transpose(value, (0, 2, 1, 3)) for value in (tokens, out_cot))
    class_spec = pl.BlockSpec((1, 1, frames, width), lambda *_: (0, 0, 0, 0))

    def mine(value, axis=1):
        return lax.dynamic_slice_in_dim(value, me_dp * share, share, axis)

    devices = size if aligned else 16
    each = width // devices

    def packed(up, down):
        up = up.reshape(-1, each, f_half // width, width).transpose(0, 2, 1, 3).reshape(-1, f_half // devices, width)
        return jnp.concatenate([up, down.reshape(-1, f_half // devices, width)], axis=1)

    if aligned:
        down_share = lax.dynamic_slice_in_dim(down_weight, me_dp * (f_half // size), f_half // size, 0)
        mlp_share = swap(packed(mine(up_weight, 0), down_share))
    else:
        mlp_other = packed(swap(up_weight), swap(down_weight))

    message, early, msg_qkv, msg_part = run(
        functools.partial(message_forward_kernel, HEADS),
        "message_forward",
        (place, tokens_t, captions, msg_weight, msg_gain, msg_in, msg_out),
        (
            shape_of((frames, width), F32),
            shape_of((16, 2 * width + h_half), BF),
            shape_of((frames, 3 * h_half), BF),
            shape_of((frames, width), F32),
        ),
        prefetch=1,
        specs={0: class_spec},
    )
    msg_other = swap(msg_part)
    if aligned:
        mlp_other = lax.all_gather(after(mlp_share, msg_part), "dp", axis=0, tiled=True)

    def half_rows(value, axis):
        rows_half = value.shape[axis] // 2
        return lax.dynamic_slice_in_dim(value, (me_dp % 2) * rows_half, rows_half, axis)

    in_mine = swap(after(half_rows(frame_in, 1), msg_part))

    one_frame = lambda wide, first=0: pl.BlockSpec((1, seq, wide), lambda f, *_: (f + first, 0, 0))
    whole_wide = pltpu.VMEM((width // 128, patches * frames, 128), F32)
    chunk = 512
    grad, dact_own = run(
        functools.partial(cotangent_kernel, half),
        "cotangent",
        (place, cot_t.reshape(patches, frames, width), down_weight),
        (shape_of((rows, width), BF), shape_of((rows, f_half), BF)),
        grid=(f_half // chunk,),
        prefetch=1,
        specs={1: pl.BlockSpec((chunk, width), lambda j, *_: (j, 0))},
        out_specs={1: pl.BlockSpec((rows, chunk), lambda j, *_: (0, j))},
        scratch=[whole_wide],
        deps=(msg_part,),
    )
    stream, frame_low, qkv_own, context_own, frame_rstd, logsum_own = run(
        functools.partial(frame_first_kernel, HEADS, half),
        "frame_first",
        (place, tokens_t.reshape(patches, frames, width), message, msg_part, msg_other, frame_gain, frame_in),
        (
            shape_of((half, seq, width), BF),
            shape_of((half, seq, width), BF),
            shape_of((half, seq, 3 * h_half), BF),
            shape_of((half, seq, h_half), BF),
            shape_of((half, seq, 128), F32),
            shape_of((half, seq, 128), F32),
        ),
        grid=(half,),
        prefetch=1,
        out_specs={
            0: one_frame(width),
            1: one_frame(width),
            2: one_frame(3 * h_half),
            3: one_frame(h_half),
            4: one_frame(128),
            5: one_frame(128),
        },
        scratch=[whole_wide, pltpu.VMEM((seq, width), F32)],
        deps=(grad,),
    )
    in_theirs = flip(after(in_mine, stream), 1)
    out_other = swap(after(frame_out, grad))
    bits = gather_bits()

    def hop(value, k, *deps):
        return jnp.concatenate([value, after(flip(value, bits[k]), *deps)], axis=0)

    qkv_other, context_other, in_other, logsum_other = run(
        functools.partial(frame_second_kernel, HEADS, valid),
        "frame_second",
        (place, frame_low, in_mine, in_theirs),
        (
            shape_of((half, seq, 3 * h_half), BF),
            shape_of((half, seq, h_half), BF),
            shape_of(frame_in.shape, BF),
            shape_of((half, seq, 128), F32),
        ),
        grid=(half,),
        prefetch=1,
        specs={0: one_frame(width)},
        out_specs={0: one_frame(3 * h_half), 1: one_frame(h_half), 3: one_frame(128)},
    )

    steps = f_half // chunk
    up_spec = pl.BlockSpec((width, chunk), lambda j, *_: (0, j))
    down_spec = pl.BlockSpec((chunk, width), lambda j, *_: (j, 0))
    unit_spec = pl.BlockSpec((rows, chunk), lambda j, *_: (0, j))
    units = shape_of((rows, f_half), BF)
    wide_rows = shape_of((rows, width), F32)
    context_own2, context_other2 = (v.reshape(rows, h_half) for v in (context_own, context_other))
    (
        mlp_rstd, mlp_low, activ_own, dhid_own, slope_cls_own, total, back, cls_low, cls_total,
    ) = run(
        functools.partial(mlp_first_kernel, half),
        "mlp_first",
        (
            stream.reshape(rows, width), context_own2, context_other2, frame_out, out_other, mlp_gain,
            up_weight, down_weight, dact_own,
        ),
        (
            shape_of((rows, 128), F32), shape_of((rows, width), BF), units, units, shape_of((16, f_half), F32), wide_rows,
            wide_rows,
            shape_of((16, width), BF), shape_of((16, width), F32),
        ),
        grid=(steps,),
        specs={6: up_spec, 7: down_spec, 8: unit_spec},
        out_specs={2: unit_spec, 3: unit_spec, 4: pl.BlockSpec((16, chunk), lambda j, *_: (0, j))},
    )

    part = f_half // 4
    per = width // part

    def up_other_spec(first):
        return pl.BlockSpec((devices, each, part), lambda j, *_: (0, (j + first) // per, (j + first) % per))

    def down_other_spec(first):
        return pl.BlockSpec((devices // 4, f_half // devices, width), lambda j, *_: (j + first, 1, 0))

    def part_spec(first=0):
        return pl.BlockSpec((rows, part), lambda j, *_: (0, j + first))

    (pooled_part,) = run(
        functools.partial(class_forward_kernel, half),
        "class_forward",
        (cls_low, cls_total, mlp_other, mlp_other),
        (shape_of((1, width), F32),),
        grid=(4,),
        specs={2: up_other_spec(0), 3: down_other_spec(0)},
        scratch=[pltpu.VMEM((16, width), F32)],
    )
    pooled_low = ((pooled_part + swap(pooled_part)) / frames).astype(BF)
    stages = [early.at[frames : frames + 1, width : 2 * width].set(pooled_low)[None]]
    for k in range(len(bits)):
        stages.append(hop(stages[-1], k))
    early_all = stages[-1]
    anywhere = pl.BlockSpec(memory_space=pl.ANY)
    activ_2, slope_2, total = run(
        functools.partial(mlp_second_kernel, half),
        "mlp_second",
        (total, mlp_low, mlp_other, mlp_other),
        (units, units, wide_rows),
        grid=(2,),
        specs={2: up_other_spec(0), 3: down_other_spec(0)},
        out_specs={0: part_spec(), 1: part_spec()},
        deps=(stages[0],),
    )
    activ_other, slope_other, result_own = run(
        functools.partial(mlp_third_kernel, half),
        "mlp_third",
        (total, mlp_low, mlp_other, mlp_other, activ_2, slope_2),
        (units, units, shape_of((rows, width), BF)),
        grid=(2,),
        specs={2: up_other_spec(2), 3: down_other_spec(2), 4: anywhere, 5: anywhere},
        out_specs={0: part_spec(2), 1: part_spec(2)},
        scratch=[pltpu.VMEM((rows, width), F32)],
        aliases={4: 0, 5: 1},
        deps=(stages[1],),
    )
    result_other = swap(result_own)

    def hidden_backward(name, back, first, deps, *made):
        return run(
            hidden_backward_kernel,
            name,
            (back, grad, slope_other, mlp_other, mlp_other, *made),
            (units, wide_rows),
            grid=(2,),
            specs={2: part_spec(first), 3: up_other_spec(first), 4: down_other_spec(first), 5: anywhere},
            out_specs={0: part_spec(first)},
            aliases={5: 0} if made else None,
            deps=deps,
        )

    dhid_2, back = hidden_backward("hidden_backward_a", back, 0, (stages[2], result_own))
    dhid_other, back = hidden_backward("hidden_backward_b", back, 2, (stages[3],), dhid_2)
    class_picks = [slope_other[f * seq : f * seq + 1] for f in range(half)]
    slope_cls_other = jnp.concatenate(class_picks + [jnp.zeros((16 - half, f_half), BF)], axis=0).astype(F32)

    loss, caption_grad, embed_grad, pooled_all, pooled_grad = run(
        functools.partial(loss_kernel, bits, frames),
        "contrast",
        (place, early_all, proj_weight),
        (
            shape_of((1, 1), F32),
            shape_of((1, embed), F32),
            shape_of((size, embed), BF),
            shape_of((size, width), BF),
            shape_of((1, width), F32),
        ),
        prefetch=1,
        deps=(back,),
    )

    part_cols = lambda n: pl.BlockSpec((n, part), lambda j, *_: (0, j))
    cls_units = shape_of((16, f_half), BF)
    grad_cls, dhid_cls_own, dhid_cls_other, back_cls = run(
        functools.partial(class_backward_kernel, half),
        "class_backward",
        (place, cot_t, pooled_grad, slope_cls_own, slope_cls_other, up_weight, down_weight, mlp_other, mlp_other),
        (shape_of((16, width), BF), cls_units, cls_units, shape_of((16, width), F32)),
        grid=(4,),
        prefetch=1,
        specs={
            0: class_spec,
            2: part_cols(16),
            3: part_cols(16),
            4: part_cols(width),
            5: pl.BlockSpec((part, width), lambda j, *_: (j, 0)),
            6: up_other_spec(0),
            7: down_other_spec(0),
        },
        out_specs={1: part_cols(16), 2: part_cols(16)},
    )
    weights = shape_of((2, width // 2, f_half), BF)
    def unit_part(first, lead):
        return pl.BlockSpec(lead + (chunk,), lambda t, *_: (0,) * len(lead) + (jnp.clip(t - first, 0, steps - 1),))

    keep_own, send_own, keep_other, send_other = run(
        functools.partial(mlp_weight_kernel, half, count),
        "mlp_weights",
        (
            place, grad, grad_cls, mlp_low, activ_own, dhid_own, dhid_cls_own, activ_other, dhid_other, dhid_cls_other,
        ),
        (weights,) * 4,
        grid=(2 * steps,),
        prefetch=1,
        specs={
            3: unit_part(steps, (rows,)),
            4: unit_part(steps, (rows,)),
            5: unit_part(steps, (16,)),
            6: unit_part(0, (rows,)),
            7: unit_part(0, (rows,)),
            8: unit_part(0, (16,)),
        },
        out_specs={k: unit_part(steps if k < 2 else 0, (2, width // 2)) for k in range(4)},
        scratch=[
            pltpu.VMEM((width, rows), BF),
            pltpu.VMEM((width, rows), BF),
            pltpu.VMEM((rows, chunk), BF),
            pltpu.VMEM((rows, width), BF),
        ],
        deps=(result_other,),
    )
    mlp_stages = Reduction("mlp_stage", mlp_ways, keep_own, send_own, keep_other, send_other)

    in_shape = shape_of((half, seq, 3 * h_half), BF)
    made = (
        shape_of((half, seq, width), BF), in_shape, in_shape, shape_of((half // 2, seq, width), BF), shape_of((16, width), F32),
    )

    def frame_backward(name, first, before, deps=()):
        tensors = (
            back, grad, mlp_low, mlp_rstd, qkv_own, qkv_other, frame_low, frame_rstd, context_own, context_other,
            logsum_own, logsum_other, back_cls, grad_cls, mlp_gain,
            frame_gain, frame_out, out_other, frame_in, in_other, *before,
        )
        flat_frame = lambda wide: pl.BlockSpec((seq, wide), lambda f, *_: (f + first, 0))
        specs = {
            0: flat_frame(width),
            1: flat_frame(width),
            2: flat_frame(width),
            3: flat_frame(128),
            4: one_frame(3 * h_half, first),
            5: one_frame(3 * h_half, first),
            6: one_frame(width, first),
            7: one_frame(128, first),
            8: one_frame(h_half, first),
            9: one_frame(h_half, first),
            10: one_frame(128, first),
            11: one_frame(128, first),
        }
        specs.update({20 + k: anywhere for k in range(3 if before else 0)})
        return run(
            functools.partial(frame_backward_kernel, HEADS, valid, half, first),
            name,
            tensors,
            made,
            grid=(half // 2,),
            specs=specs,
            out_specs={
                0: one_frame(width, first),
                1: one_frame(3 * h_half, first),
                2: one_frame(3 * h_half, first),
                3: one_frame(width),
            },
            aliases={20 + k: k for k in range(3)} if before else None,
            deps=deps,
        )

    before = frame_backward("frame_backward_a", 0, (), (keep_own,))
    mlp_stages.cores(before[0])
    token_first = before[3]
    token_first_other = swap(token_first)
    middle_low, dqkv_own, dqkv_other, token_second, edges = frame_backward(
        "frame_backward_b", half // 2, (before[0], before[1], before[2], before[4]), mlp_stages.ready()
    )
    edges_other = swap(edges)

    next_grad, next_low, msg_dqkv, msg_normed = run(
        functools.partial(message_backward_kernel, HEADS),
        "message_backward",
        (place, edges, edges_other, msg_qkv, msg_out, msg_in),
        (
            shape_of((frames, width), F32),
            shape_of((frames, width), BF),
            shape_of((frames, 3 * h_half), BF),
            shape_of((frames, width), F32),
        ),
        prefetch=1,
    )
    msg_normed_other = swap(msg_normed)
    mlp_stages.step(next_grad)
    grads = shape_of((2, width // 2, 2 * h_half), BF)

    def share_spec(first):
        def index(t, *_):
            k = jnp.clip(t - first, 0, 3)
            return (k // 2, 0, k % 2)

        return pl.BlockSpec((1, width // 2, h_half), index)

    def column_spec(first):
        return pl.BlockSpec((rows, h_half), lambda t, *_: (0, jnp.clip(t - first, 0, 2)))

    keep_own, send_own, keep_other, send_other = run(
        functools.partial(frame_weight_kernel, count),
        "frame_weights",
        (
            place, frame_low.reshape(rows, width), middle_low.reshape(rows, width),
            dqkv_own.reshape(rows, 3 * h_half), dqkv_other.reshape(rows, 3 * h_half), context_own2, context_other2,
        ),
        (grads,) * 4,
        grid=(8,),
        prefetch=1,
        specs={2: column_spec(4), 3: column_spec(0)},
        out_specs={0: share_spec(4), 1: share_spec(4), 2: share_spec(0), 3: share_spec(0)},
        scratch=[pltpu.VMEM((width, rows), BF), pltpu.VMEM((width, rows), BF)],
        deps=(*mlp_stages.ready(), token_first_other),
    )
    frame_stages = Reduction("frame_stage", frame_ways, keep_own, send_own, keep_other, send_other)

    late, cls_rows = run(
        message_last_kernel,
        "message_last",
        (
            place, edges, edges_other, next_grad, next_low, msg_dqkv, msg_normed,
            msg_normed_other, message, msg_gain, msg_weight,
        ),
        (shape_of((frames, 2 * width + 6 * h_half), BF), shape_of((frames, width), BF)),
        prefetch=1,
        deps=(keep_own,),
    )
    frame_stages.cores(late)
    cores_ready = frame_stages.ready()
    for k in range(1, len(bits)):
        last = mlp_stages.at == mlp_stages.steps - 1
        mlp_stages.step(*frame_stages.ready())
        if k == 1:
            late_all = hop(late[None], 0, *mlp_stages.ready())
        frame_stages.step(*((mlp_stages.value[0][0],) if last else mlp_stages.ready()))
        if k == 1:
            token_second_other = swap(after(token_second, *frame_stages.ready()))
        late_all = hop(late_all, k, *(frame_stages.ready() if k < 3 else ()))

    def both(name, own, other, extra=(), deps=()):
        tile = 64
        parts = own + other
        (out,) = run(
            functools.partial(assemble_kernel, len(own)),
            name,
            (place, *parts, *extra),
            (shape_of((patches, frames, width), BF),),
            grid=(-(-patches // tile),),
            prefetch=1,
            specs={
                k: pl.BlockSpec((part.shape[0], tile, width), lambda t, s: (0, t, 0)) for k, part in enumerate(parts)
            },
            out_specs={0: pl.BlockSpec((tile, frames, width), lambda t, s: (t, 0, 0))},
            scratch=[pltpu.VMEM((width // 128, tile * frames, 128), F32)],
            deps=deps,
        )
        return out

    def whole_of(value):
        return jnp.transpose(value[None], (0, 2, 1, 3))

    result_own, result_other = (value.reshape(half, seq, width) for value in (result_own, result_other))
    layer_out = whole_of(both("assemble_out", (result_own,), (result_other,), deps=cores_ready))
    token_parts = both(
        "assemble_grad", (token_first, token_second), (token_first_other, token_second_other), (cls_rows,)
    )

    msg_weight_share, msg_in_share, msg_out_share, proj_share, gains = run(
        functools.partial(factor_kernel, frames),
        "factors",
        (place, early_all, late_all, pooled_all, embed_grad),
        (
            shape_of((share, width), F32),
            shape_of((3, share, h_half), F32),
            shape_of((share, h_half), F32),
            shape_of((share, embed), F32),
            shape_of((3, width), F32),
        ),
        prefetch=1,
    )
    if aligned:
        in_grad, out_grad = run(
            frame_final_kernel,
            "frame_final",
            frame_stages.parts(),
            (shape_of((3, share, h_half), F32), shape_of((share, h_half), F32)),
            deps=(token_parts, gains),
        )
        out_grad = out_grad.T
    else:
        frame_stages.step(token_parts, gains)
        (first,), (second,) = frame_stages.value
        first, second = first[0], second[0]
        in_grad = jnp.stack([first[:, :h_half], first[:, h_half:], second[:, :h_half]])
        out_grad = second[:, h_half:].T
    token_grad = whole_of(token_parts)
    (up_grad,), (down_grad,) = mlp_stages.value
    up_grad, down_grad = (up_grad[0], down_grad[0].T)
    msg_out_share = msg_out_share.T
    gains = mine(gains)
    return (
        layer_out,
        loss[0, 0],
        token_grad,
        caption_grad,
        msg_weight_share,
        gains[2],
        msg_in_share,
        msg_out_share,
        gains[1],
        in_grad,
        out_grad,
        gains[0],
        up_grad,
        down_grad,
        proj_share,
    )


def solution(mesh):
    in_specs = (
        P("dp", None, None, None),
        P("dp", None),
        P("dp"),
        P("dp"),
        P(),
        P(),
        P(None, None, "mp"),
        P("mp", None),
        P(),
        P(None, None, "mp"),
        P("mp", None),
        P(),
        P(None, "mp"),
        P("mp", None),
        P(),
        P("dp", None, None, None),
    )
    out_specs = (
        P("dp", None, None, None),
        P(),
        P("dp", None, None, None),
        P("dp", None),
        P("dp", None),
        P("dp"),
        P(None, "dp", "mp"),
        P("mp", "dp"),
        P("dp"),
        P(None, "dp", "mp"),
        P("mp", "dp"),
        P("dp"),
        P("dp", "mp"),
        P("mp", "dp"),
        P("dp", None),
    )
    return jax.shard_map(
        on_device, mesh=mesh, in_specs=in_specs, out_specs=out_specs, check_vma=False
    )
```

```python
import functools

import jax
import jax.numpy as jnp
from jax import lax
from jax.experimental import pallas as pl
from jax.experimental.pallas import tpu as pltpu
from jax.sharding import PartitionSpec as P

HEADS = 12
SHARPNESS = 50.0
LOWEST = -1e30
BF = jnp.bfloat16
F32 = jnp.float32
KERNEL_MIB = {
    "frame_first": 52,
    "cotangent": 52,
    "frame_second": 52,
    "mlp_first": 52,
    "mlp_second": 52,
    "mlp_third": 52,
    "hidden_backward_a": 52,
    "hidden_backward_b": 52,
    "mlp_weights": 52,
    "frame_backward_a": 52,
    "frame_backward_b": 52,
    "frame_weights": 52,
    "contrast": 52,
    "class_backward": 52,
    "class_forward": 52,
}
KERNEL_US = {
    "frame_first": 7,
    "cotangent": 4,
    "frame_second": 6,
    "mlp_first": 16,
    "mlp_second": 5,
    "mlp_third": 5,
    "hidden_backward_a": 5,
    "hidden_backward_b": 5,
    "class_backward": 5,
    "mlp_weights": 15,
    "frame_backward_a": 14,
    "frame_backward_b": 14,
    "frame_weights": 11,
}


def swap(value):
    return lax.ppermute(value, "mp", [(0, 1), (1, 0)])


def flip(value, bit):
    size = lax.axis_size("dp")
    return lax.ppermute(value, "dp", [(i, i ^ bit) for i in range(size)])


def after(value, *deps):
    return lax.optimization_barrier((value,) + deps)[0]


def bits_of(size):
    return [1 << k for k in range(size.bit_length() - 1)]


def row_order(bits):
    order = [0]
    for bit in reversed(bits):
        order = order + [mask | bit for mask in order]
    return order


def mlp_ways(bits):
    return (bits[:1] + ["mp"] + bits[1:], bits[1:] + bits[:1] + ["mp"])


def frame_ways(bits):
    return (bits[:1] + ["mp"] + bits[1:], ["mp"] + bits)


def gather_bits():
    bits = bits_of(lax.axis_size("dp"))
    return bits[:0:-1] + bits[:1]


def gather(value):
    for bit in gather_bits():
        value = jnp.concatenate([value, flip(value, bit)], axis=0)
    return value


def dot(a, b):
    return jnp.dot(a, b, preferred_element_type=F32)


def dot_nt(a, b):
    return lax.dot_general(a, b, (((1,), (1,)), ((), ())), preferred_element_type=F32)


def dot_tn(a, b):
    return lax.dot_general(a, b, (((0,), (0,)), ((), ())), preferred_element_type=F32)


def standardized(value):
    centered = value - jnp.mean(value, axis=-1, keepdims=True)
    rstd = lax.rsqrt(jnp.mean(centered * centered, axis=-1, keepdims=True) + 1e-05)
    return (centered * rstd, rstd)


def spread(rstd):
    return jnp.broadcast_to(rstd, (rstd.shape[0], 128))


def norm_backward(grad, gain, normal, rstd):
    scaled = grad * gain
    inner = (
        scaled
        - jnp.mean(scaled, axis=-1, keepdims=True)
        - normal * jnp.mean(scaled * normal, axis=-1, keepdims=True)
    )
    return (rstd * inner, jnp.sum(grad * normal, axis=0, keepdims=True))


def lane_half(rows, pair, which):
    lane = lax.broadcasted_iota(jnp.int32, (rows, pair), 1)
    return (lane < pair // 2) if which == 0 else (lane >= pair // 2)


def only(value, which):
    return jnp.where(lane_half(*value.shape, which), value, jnp.zeros_like(value))


def attend_pair(query, keys, values, valid):
    rows, pair = query.shape
    out = None
    sums = []
    for which in range(2):
        scores = dot_nt(only(query, which), keys)
        if valid < rows:
            key = lax.broadcasted_iota(jnp.int32, scores.shape, 1)
            scores = jnp.where(key < valid, scores, LOWEST)
        top = jnp.max(scores, axis=1, keepdims=True)
        each = jnp.exp(scores - top)
        total = jnp.sum(each, axis=1, keepdims=True)
        sums.append(top + jnp.log(total))
        part = dot(each.astype(BF), only(values, which)) * (1.0 / total)
        out = part if out is None else out + part
    return (out, sums)


def attend_pair_kept(query, keys, values, grad, logsums, inners, valid, scale):
    rows, pair = query.shape
    size = pair // 2
    edge = valid // 16 * 16
    lane = lax.broadcasted_iota(jnp.int32, (1, pair), 1)
    keys_t = keys.T
    turned, both = ([], [])
    for which in range(2):
        head = (lane // size == which).astype(F32).astype(BF)
        weights = jnp.exp(dot_nt(keys, query * head) - logsums[which])
        tail = weights[edge:]
        row = lax.broadcasted_iota(jnp.int32, tail.shape, 0)
        weights = jnp.concatenate([weights[:edge], jnp.where(row < valid - edge, tail, 0.0)], axis=0)
        weight_grad = dot_nt(values, grad * head)
        value_grad = dot(weights.astype(BF), grad)
        score_grad = (weights * (weight_grad - inners[which])).astype(BF)
        key_grad = dot(score_grad, query)
        turned.append(dot(keys_t[size * which : size * (which + 1)], score_grad))
        both.append((key_grad, value_grad))
    query_grad = (jnp.concatenate(turned, axis=0) * scale).astype(BF).T
    first = lane_half(rows, pair, 0)
    key_grad, value_grad = (jnp.where(first, one, two).astype(BF) for one, two in zip(*both))
    return [query_grad, key_grad, value_grad]


def head_sums(value, size):
    head = lax.broadcasted_iota(jnp.int32, (16, value.shape[1]), 1) // size
    pick = (head == lax.broadcasted_iota(jnp.int32, head.shape, 0)).astype(F32).astype(BF)
    high = value.astype(BF)
    return dot_nt(pick, high) + dot_nt(pick, (value - high.astype(F32)).astype(BF))


def attend_pair_backward(query, keys, values, grad, valid, scale):
    rows, _ = query.shape
    sums = [None, None, None]
    for which in range(2):
        query_own, key_own, grad_own = (only(query, which), only(keys, which), only(grad, which))
        scores = dot_nt(keys, query_own)
        if valid < rows:
            key = lax.broadcasted_iota(jnp.int32, scores.shape, 0)
            scores = jnp.where(key < valid, scores, LOWEST)
        top = jnp.max(scores, axis=0, keepdims=True)
        each = jnp.exp(scores - top)
        weights = each * (1.0 / jnp.sum(each, axis=0, keepdims=True))
        weight_grad = dot_nt(values, grad_own)
        value_grad = dot(weights.astype(BF), grad_own)
        inner = jnp.sum(weights * weight_grad, axis=0, keepdims=True)
        score_grad = (weights * (weight_grad - inner)).astype(BF)
        key_grad = dot(score_grad, query_own)
        query_grad = dot_tn(score_grad, key_own) * scale
        parts = (query_grad, key_grad, value_grad)
        sums = [part if one is None else one + part for one, part in zip(sums, parts)]
    return [one.astype(BF) for one in sums]


def project(normed, in_ref, scale):
    wide = in_ref.shape[2]
    query = dot(normed, in_ref[0]).astype(BF) * jnp.asarray(scale, BF)
    keys = dot(normed, in_ref[1]).astype(BF)
    values = dot(normed, in_ref[2]).astype(BF)
    return (query, keys, values, wide)


def turn_rows(ways, count, which, to_ref, from_ref, place_ref):
    rows = to_ref.shape[0]
    pairs = 8 if count is None else 1 << count
    block = rows // (2 * pairs)
    turned = from_ref[...].T
    me = place_ref[1]
    for j in range(2 * pairs):
        if count is None:
            spot = j // 2 + (j % 2) * pairs
        else:
            mask = (me >> 1) ^ (j >> 1)
            order = [k for k in ways(list(range(count)))[which] if k != "mp"]
            spot = sum(((mask >> k) & 1) << (count - 1 - i) for i, k in enumerate(order))
            spot = spot + ((me ^ j) & 1) * pairs
        to_ref[pl.ds(pl.multiple_of(spot * block, 16), block), :] = turned[block * j : block * (j + 1)]


def put_product(keep_ref, send_ref, lead, turned_ref, value, lanes=slice(None)):
    rows = keep_ref.shape[1]
    keep_ref[lead, :, lanes] = dot(turned_ref[:rows], value).astype(BF)
    send_ref[lead, :, lanes] = dot(turned_ref[rows:], value).astype(BF)


def frame_rows(wide_ref, frame, patches):
    at = pl.ds(frame, patches, stride=8)
    return jnp.concatenate([wide_ref[j, at, :] for j in range(wide_ref.shape[0])], axis=1)


def widen(wide_ref, from_ref):
    for j in range(wide_ref.shape[0]):
        value = from_ref[:, :, 128 * j : 128 * (j + 1)].astype(F32)
        wide_ref[j] = value.reshape(wide_ref.shape[1:])


def put_class_rows(to_ref, rows_ref, half):
    seq = to_ref.shape[0] // half
    for f in range(half):
        old = to_ref[f * seq : f * seq + 16, :].astype(F32)
        row = lax.broadcasted_iota(jnp.int32, old.shape, 0)
        new = jnp.where(row == 0, rows_ref[f : f + 1, :].astype(F32), old)
        to_ref[f * seq : f * seq + 16, :] = new.astype(to_ref.dtype)


def class_rows(from_ref, half, dtype, count):
    seq = from_ref.shape[0] // half
    rows = [from_ref[f * seq : f * seq + 16, :].astype(F32)[0:1] for f in range(half)]
    rows.append(jnp.zeros((count - half, from_ref.shape[1]), F32))
    return jnp.concatenate(rows, axis=0).astype(dtype)


def message_forward_kernel(
    heads, place_ref, tok_ref, captions_ref, w_ref, gain_ref, in_ref, out_ref, message_ref, early_ref, qkv_ref, part_ref
):
    cls = tok_ref[0, 0]
    frames, width = cls.shape
    message = dot(cls, w_ref[...])
    message_ref[...] = message
    normal, _ = standardized(message)
    low = (normal * gain_ref[...]).astype(BF)
    size = width // heads
    query, keys, values, wide = project(low, in_ref, size**-0.5)
    contexts = []
    for j in range(wide // (2 * size)):
        at = slice(2 * size * j, 2 * size * (j + 1))
        contexts.append(attend_pair(query[:, at], keys[:, at], values[:, at], frames)[0])
    context = jnp.concatenate(contexts, axis=1).astype(BF)
    part_ref[...] = dot(context, out_ref[...])
    qkv_ref[:, :wide] = query
    qkv_ref[:, wide : 2 * wide] = keys
    qkv_ref[:, 2 * wide :] = values

    def padded(value):
        value = value.astype(F32)
        return jnp.concatenate([value, jnp.zeros((16 - value.shape[0], value.shape[1]), F32)], axis=0)

    early_ref[:, width : 2 * width] = padded(low).astype(BF)
    early_ref[:, 2 * width :] = padded(context).astype(BF)
    embed = captions_ref.shape[1]
    lane = lax.broadcasted_iota(jnp.int32, (1, width - embed), 1)
    ids = jnp.where(lane == 0, place_ref[2], jnp.where(lane == 1, place_ref[3], 0)).astype(F32)
    text = jnp.concatenate([captions_ref[...].astype(F32), ids], axis=1)
    row = lax.broadcasted_iota(jnp.int32, (8, width), 0)
    text = jnp.where(row == 0, text, 0.0)
    early_ref[:, :width] = jnp.concatenate([cls.astype(F32), text], axis=0).astype(BF)


def frame_attention(heads, valid, low, in_ref, qkv_ref, context_ref, logsum_ref):
    size = low.shape[1] // heads
    wide = in_ref.shape[2]
    for k in range(3):
        value = dot(low, in_ref[k]).astype(BF)
        if k == 0:
            value = value * jnp.asarray(size**-0.5, BF)
        qkv_ref[0, :, wide * k : wide * (k + 1)] = value
    lane = lax.broadcasted_iota(jnp.int32, (low.shape[0], 128), 1)
    logsums = jnp.zeros(lane.shape, F32)
    for j in range(wide // (2 * size)):
        query, keys, values = (
            qkv_ref[0, :, wide * k + 2 * size * j : wide * k + 2 * size * (j + 1)] for k in range(3)
        )
        context, sums = attend_pair(query, keys, values, valid)
        context_ref[0, :, 2 * size * j : 2 * size * (j + 1)] = context.astype(BF)
        for which, one in enumerate(sums):
            logsums = jnp.where(lane == 2 * j + which, one, logsums)
    logsum_ref[0] = logsums


def frame_first_kernel(
    heads, half, place_ref, tok_ref, message_ref, part_ref, other_ref, gain_ref, in_ref,
    stream_ref, low_ref, qkv_ref, context_ref, rstd_ref, logsum_ref, wide_ref, rows_ref,
):
    patches, frames, width = tok_ref.shape
    seq = stream_ref.shape[1]
    frame = place_ref[0] * half + pl.program_id(0)

    @pl.when(pl.program_id(0) == 0)
    def _():
        widen(wide_ref, tok_ref)

    at = pl.ds(frame, 1)
    message = message_ref[at, :] + (part_ref[at, :] + other_ref[at, :])
    edge = patches // 8 * 8
    rows_ref[edge:seq, :] = jnp.zeros((seq - edge, width), F32)
    rows_ref[0:patches, :] = frame_rows(wide_ref, frame, patches)
    rows_ref[patches : patches + 1, :] = message
    stream_ref[0] = rows_ref[...].astype(BF)
    normal, rstd = standardized(rows_ref[...])
    rstd_ref[0] = spread(rstd)
    low = (normal * gain_ref[...]).astype(BF)
    low_ref[0] = low
    frame_attention(heads, patches + 1, low, in_ref, qkv_ref, context_ref, logsum_ref)


def joined(place_ref, to_ref, mine_ref, theirs_ref, axis):
    rows = mine_ref.shape[axis]
    core = place_ref[1] & 1
    lead = (slice(None),) * axis
    to_ref[lead + (pl.ds(pl.multiple_of(core * rows, 16), rows),)] = mine_ref[...]
    to_ref[lead + (pl.ds(pl.multiple_of((1 - core) * rows, 16), rows),)] = theirs_ref[...]


def frame_second_kernel(
    heads, valid, place_ref, low_ref, mine_ref, theirs_ref, qkv_ref, context_ref, in_ref, logsum_ref
):
    @pl.when(pl.program_id(0) == 0)
    def _():
        joined(place_ref, in_ref, mine_ref, theirs_ref, 1)

    frame_attention(heads, valid, low_ref[0], in_ref, qkv_ref, context_ref, logsum_ref)


def cotangent_kernel(half, place_ref, cot_ref, down_ref, grad_ref, dact_ref, wide_ref):
    patches, frames, width = cot_ref.shape
    seq = grad_ref.shape[0] // half

    @pl.when(pl.program_id(0) == 0)
    def _():
        widen(wide_ref, cot_ref)
        edge = patches // 16 * 16
        for f in range(half):
            value = frame_rows(wide_ref, place_ref[0] * half + f, patches)
            tail = jnp.concatenate([value[edge:], jnp.zeros((seq - patches, width), F32)], axis=0)
            grad_ref[f * seq : f * seq + edge, :] = value[:edge].astype(BF)
            grad_ref[f * seq + edge : (f + 1) * seq, :] = tail.astype(BF)

    dact_ref[...] = dot_nt(grad_ref[...], down_ref[...]).astype(BF)


def gate(hidden):
    sigmo = 1.0 / (1.0 + jnp.exp(-1.702 * hidden))
    gated = hidden * sigmo
    return (gated, sigmo + 1.702 * gated * (1.0 - sigmo))


def up_block(ref):
    return ref[...].reshape(ref.shape[0] * ref.shape[1], ref.shape[2])


def mlp_first_kernel(
    half, stream_ref, own_ref, other_ref, out_own_ref, out_other_ref, gain_ref, up_ref, down_ref, dact_ref,
    rstd_ref, low_ref, activ_ref, dhid_ref, slope_ref, total_ref, back_ref, cls_low_ref, cls_total_ref,
):
    step = pl.program_id(0)

    @pl.when(step == 0)
    def _():
        branch = dot(own_ref[...], out_own_ref[...]) + dot(other_ref[...], out_other_ref[...])
        middle = stream_ref[...].astype(F32) + branch
        normal, rstd = standardized(middle)
        rstd_ref[...] = spread(rstd)
        low_ref[...] = (normal * gain_ref[...]).astype(BF)
        total_ref[...] = middle
        back_ref[...] = jnp.zeros_like(back_ref)
        cls_low_ref[...] = class_rows(low_ref, half, BF, 16)

    seq = low_ref.shape[0] // half
    activ, slope = gate(dot(low_ref[...], up_ref[...]))
    activ_ref[...] = activ.astype(BF)
    dhid_ref[...] = (dact_ref[...].astype(F32) * slope).astype(BF)
    rows = [slope[f * seq : f * seq + 1] for f in range(half)]
    slope_ref[...] = jnp.concatenate(rows + [jnp.zeros((16 - half, slope.shape[1]), F32)], axis=0)
    total_ref[...] += dot(activ_ref[...], down_ref[...])
    back_ref[...] += dot_nt(dhid_ref[...], up_ref[...])

    @pl.when(step == pl.num_programs(0) - 1)
    def _():
        cls_total_ref[...] = class_rows(total_ref, half, F32, 16)


def class_forward_kernel(half, low_ref, start_ref, up_ref, down_ref, pooled_ref, total_ref):
    step = pl.program_id(0)

    @pl.when(step == 0)
    def _():
        total_ref[...] = start_ref[...]

    activ, _ = gate(dot(low_ref[...], up_block(up_ref)))
    total_ref[...] += dot(activ.astype(BF), up_block(down_ref))

    @pl.when(step == pl.num_programs(0) - 1)
    def _():
        pooled_ref[...] = jnp.sum(total_ref[0:half, :], axis=0, keepdims=True)


def mlp_second_kernel(half, start_ref, low_ref, up_ref, down_ref, activ_ref, slope_ref, total_ref):
    @pl.when(pl.program_id(0) == 0)
    def _():
        total_ref[...] = start_ref[...]

    activ, slope = gate(dot(low_ref[...], up_block(up_ref)))
    activ_ref[...] = activ.astype(BF)
    slope_ref[...] = slope.astype(BF)
    total_ref[...] += dot(activ_ref[...], up_block(down_ref))


def mlp_third_kernel(half, start_ref, low_ref, up_ref, down_ref, _, __, activ_ref, slope_ref, result_ref, total_ref):
    mlp_second_kernel(half, start_ref, low_ref, up_ref, down_ref, activ_ref, slope_ref, total_ref)

    @pl.when(pl.program_id(0) == pl.num_programs(0) - 1)
    def _():
        result_ref[...] = total_ref[...].astype(BF)


def hidden_backward_kernel(start_ref, grad_ref, slope_ref, up_ref, down_ref, *refs):
    dhid_ref, back_ref = refs[-2:]

    @pl.when(pl.program_id(0) == 0)
    def _():
        back_ref[...] = start_ref[...]

    dact = dot_nt(grad_ref[...], up_block(down_ref))
    dhid_ref[...] = (dact * slope_ref[...].astype(F32)).astype(BF)
    back_ref[...] += dot_nt(dhid_ref[...], up_block(up_ref))


def loss_kernel(
    order, frames, place_ref, early_ref, proj_ref,
    loss_ref, caption_grad_ref, embed_grad_ref, pooled_all_ref, pooled_grad_ref,
):
    clips = early_ref.shape[0]
    width, wide = proj_ref.shape
    me = place_ref[1]
    early = early_ref[...].astype(F32)[:, frames, :].astype(BF)
    block = lax.broadcasted_iota(jnp.int32, (clips, clips), 1)
    mask = jnp.zeros_like(block)
    for k, bit in enumerate(order):
        mask = mask + ((block >> k) & 1) * bit
    row = lax.broadcasted_iota(jnp.int32, (clips, clips), 0)
    pick = (row == jnp.bitwise_xor(mask, me)).astype(F32).astype(BF)
    text = dot(pick, early[:, :width]).astype(BF)
    pooled = dot(pick, early[:, width : 2 * width]).astype(BF)
    pooled_all_ref[...] = pooled
    embed = dot(pooled, proj_ref[...])
    embed_rinv = lax.rsqrt(jnp.sum(embed * embed, axis=-1, keepdims=True) + 1e-06)
    embed_low = (embed * embed_rinv).astype(BF)
    caption_f = text[:, :wide].astype(F32)
    caption_rinv = lax.rsqrt(jnp.sum(caption_f * caption_f, axis=-1, keepdims=True) + 1e-06)
    caption_low = (caption_f * caption_rinv).astype(BF)
    scores = SHARPNESS * dot_nt(embed_low, caption_low)
    lane = lax.broadcasted_iota(jnp.int32, (8, text.shape[1] - wide), 1)
    pick_id = (lane == 1).astype(F32).astype(BF)
    caption_ids = dot_nt(pick_id, text[:, wide:])[0:1, :]
    clip_ids = text[:, wide:].astype(F32)[:, 0:1]
    positive = clip_ids == caption_ids
    masked = jnp.where(positive, scores, LOWEST)

    def side(axis):
        top = jnp.max(scores, axis=axis, keepdims=True)
        each = jnp.exp(scores - top)
        total = jnp.sum(each, axis=axis, keepdims=True)
        pos_top = jnp.max(masked, axis=axis, keepdims=True)
        pos_each = jnp.where(positive, jnp.exp(masked - pos_top), 0.0)
        pos_total = jnp.sum(pos_each, axis=axis, keepdims=True)
        part = jnp.sum(top + jnp.log(total) - pos_top - jnp.log(pos_total), axis=1 - axis, keepdims=True)
        return (part, each / total - pos_each / pos_total)

    row_loss, row_grad = side(1)
    column_loss, column_grad = side(0)
    loss_ref[...] = 0.5 * (row_loss + column_loss)
    dscore = 0.5 * (row_grad + column_grad)
    embed_grad = SHARPNESS * dot(dscore.astype(BF), caption_low)
    caps_grad = SHARPNESS * dot_tn(dscore.astype(BF), embed_low)
    caption_grad = caption_rinv * caps_grad - caption_f * (
        caption_rinv * caption_rinv * caption_rinv * jnp.sum(caption_f * caps_grad, axis=-1, keepdims=True)
    )
    embed_diff = embed_rinv * embed_grad - embed * (
        embed_rinv * embed_rinv * embed_rinv * jnp.sum(embed * embed_grad, axis=-1, keepdims=True)
    )
    embed_diff = embed_diff.astype(BF)
    embed_grad_ref[...] = embed_diff
    grads = dot_nt(embed_diff, proj_ref[...])

    def own_row(value):
        own = lax.broadcasted_iota(jnp.int32, value.shape, 0) == me
        return jnp.sum(jnp.where(own, value, 0.0), axis=0, keepdims=True)

    caption_grad_ref[...] = own_row(caption_grad)
    pooled_grad_ref[...] = own_row(grads) / frames


def class_backward_kernel(
    half, place_ref, cot_ref, pooled_ref, slope_own_ref, slope_other_ref, up_own_ref, down_own_ref, up_ref, down_ref,
    grad_ref, dhid_own_ref, dhid_other_ref, back_ref,
):
    @pl.when(pl.program_id(0) == 0)
    def _():
        cot = cot_ref[0, 0].astype(F32)
        cot = jnp.where(place_ref[0] == 0, cot[:half], cot[half:]) + pooled_ref[...]
        grad_ref[...] = jnp.concatenate([cot, jnp.zeros((16 - half, cot.shape[1]), F32)], axis=0).astype(BF)
        back_ref[...] = jnp.zeros_like(back_ref)

    grad = grad_ref[...]
    dhid_own_ref[...] = (dot_nt(grad, down_own_ref[...]) * slope_own_ref[...]).astype(BF)
    dhid_other_ref[...] = (dot_nt(grad, up_block(down_ref)) * slope_other_ref[...]).astype(BF)
    back_ref[...] += dot_nt(dhid_own_ref[...], up_own_ref[...]) + dot_nt(dhid_other_ref[...], up_block(up_ref))


def mlp_weight_kernel(
    half, count, place_ref, grad_ref, grad_cls_ref, low_ref, activ_own_ref, dhid_own_ref, dhid_cls_own_ref,
    activ_other_ref, dhid_other_ref, dhid_cls_other_ref,
    keep_own_ref, send_own_ref, keep_other_ref, send_other_ref, grad_t_ref, low_t_ref, fixed_ref, rows_ref,
):
    step = pl.program_id(0)
    steps = pl.num_programs(0) // 2

    @pl.when(step == 0)
    def _():
        rows_ref[...] = grad_ref[...]
        put_class_rows(rows_ref, grad_cls_ref, half)
        turn_rows(mlp_ways, count, 0, low_t_ref, low_ref, place_ref)
        turn_rows(mlp_ways, count, 1, grad_t_ref, rows_ref, place_ref)

    def part(activ_ref, dhid_ref, dhid_cls_ref, keep_ref, send_ref):
        fixed_ref[...] = dhid_ref[...]
        put_class_rows(fixed_ref, dhid_cls_ref, half)
        put_product(keep_ref, send_ref, 0, low_t_ref, fixed_ref[...])
        put_product(keep_ref, send_ref, 1, grad_t_ref, activ_ref[...])

    @pl.when(step < steps)
    def _():
        part(activ_other_ref, dhid_other_ref, dhid_cls_other_ref, keep_other_ref, send_other_ref)

    @pl.when(step >= steps)
    def _():
        part(activ_own_ref, dhid_own_ref, dhid_cls_own_ref, keep_own_ref, send_own_ref)


def frame_backward_kernel(
    heads, valid, half, first, back_ref, grad_in_ref, mid_ref, mid_rstd_ref, own_ref, other_ref, low_in_ref, rstd_ref,
    context_own_ref, context_other_ref, logsum_own_ref, logsum_other_ref,
    back_cls_ref, grad_cls_ref, mlp_gain_ref, gain_ref, out_own_ref, out_other_ref, in_own_ref, in_other_ref, *refs,
):
    low_ref, down_ref, dother_ref, token_ref, edge_ref = refs[-5:]
    step = pl.program_id(0)
    f = first + step
    width = back_ref.shape[1]
    size = width // heads
    scale = size**-0.5
    row = lax.broadcasted_iota(jnp.int32, back_ref.shape, 0)
    at = pl.ds(f, 1)
    back = jnp.where(row == 0, back_cls_ref[at, :], back_ref[...])
    cls = jnp.zeros((1, width), F32)
    for k in range(half):
        cls = jnp.where(f == k, grad_cls_ref[...].astype(F32)[k : k + 1], cls)
    grad = jnp.where(row == 0, cls, grad_in_ref[...].astype(F32))
    normal = mid_ref[...].astype(F32) * (1.0 / mlp_gain_ref[...])
    part, mlp_gain_grad = norm_backward(back, mlp_gain_ref[...], normal, mid_rstd_ref[:, 0:1])
    grad = grad + part
    low = grad.astype(BF)
    low_ref[0] = low
    normed_grad = None
    for qkv_ref, context_ref, logsum_ref, out_ref, in_ref, to_ref in (
        (own_ref, context_own_ref, logsum_own_ref, out_own_ref, in_own_ref, down_ref),
        (other_ref, context_other_ref, logsum_other_ref, out_other_ref, in_other_ref, dother_ref),
    ):
        wide = in_ref.shape[2]
        context_grad = dot_nt(low, out_ref[...]).astype(BF)
        inners = head_sums(context_grad.astype(F32) * context_ref[0].astype(F32), size)
        logsums = logsum_ref[0].T
        for j in range(wide // (2 * size)):
            query, keys, values = (
                qkv_ref[0, :, wide * k + 2 * size * j : wide * k + 2 * size * (j + 1)] for k in range(3)
            )
            grads = attend_pair_kept(
                query,
                keys,
                values,
                context_grad[:, 2 * size * j : 2 * size * (j + 1)],
                [logsums[2 * j + which : 2 * j + which + 1] for which in range(2)],
                [inners[2 * j + which : 2 * j + which + 1] for which in range(2)],
                valid,
                scale,
            )
            for k in range(3):
                to_ref[0, :, wide * k + 2 * size * j : wide * k + 2 * size * (j + 1)] = grads[k]
        for k in range(3):
            part = dot_nt(to_ref[0, :, wide * k : wide * (k + 1)], in_ref[k])
            normed_grad = part if normed_grad is None else normed_grad + part
    normal = low_in_ref[0].astype(F32) * (1.0 / gain_ref[...])
    part, gain_grad = norm_backward(normed_grad, gain_ref[...], normal, rstd_ref[0, :, 0:1])
    total = grad + part
    token_ref[0] = total.astype(BF)

    @pl.when(step == 0)
    def _():
        if first == 0:
            edge_ref[...] = jnp.zeros_like(edge_ref)
        else:
            edge_ref[...] = refs[3][...]

    edge_ref[pl.ds(f, 1), :] = total[0:1]
    edge_ref[pl.ds(half + f, 1), :] = total[valid - 1 : valid]
    edge_ref[2 * half : 2 * half + 1, :] += gain_grad
    edge_ref[2 * half + 1 : 2 * half + 2, :] += mlp_gain_grad


def frame_weight_kernel(
    count, place_ref, low_ref, grad_ref, down_ref, dother_ref, own_ref, other_ref,
    keep_own_ref, send_own_ref, keep_other_ref, send_other_ref, low_t_ref, grad_t_ref,
):
    step = pl.program_id(0)

    @pl.when(step == 0)
    def _():
        turn_rows(frame_ways, count, 0, low_t_ref, low_ref, place_ref)
        turn_rows(frame_ways, count, 0, grad_t_ref, grad_ref, place_ref)

    wide = own_ref.shape[1]
    for first, dqkv_ref, context_ref, keep_ref, send_ref in (
        (0, dother_ref, other_ref, keep_other_ref, send_other_ref),
        (2, down_ref, own_ref, keep_own_ref, send_own_ref),
    ):

        @pl.when(step == first)
        def _(dqkv_ref=dqkv_ref, keep_ref=keep_ref, send_ref=send_ref):
            put_product(keep_ref, send_ref, 0, low_t_ref, dqkv_ref[...])

        @pl.when(step == first + 1)
        def _(dqkv_ref=dqkv_ref, context_ref=context_ref, keep_ref=keep_ref, send_ref=send_ref):
            put_product(keep_ref, send_ref, 0, low_t_ref, dqkv_ref[:, :wide], slice(0, wide))
            put_product(keep_ref, send_ref, 0, grad_t_ref, context_ref[...], slice(wide, 2 * wide))


def both_halves(place, own, other):
    return jnp.concatenate(
        [jnp.where(place == 0, own, other), jnp.where(place == 0, other, own)], axis=0
    )


def message_backward_kernel(
    heads, place_ref, own_ref, other_ref, qkv_ref, out_ref, in_ref, next_ref, low_ref, dqkv_ref, part_ref
):
    frames, width = next_ref.shape
    half = frames // 2
    at = slice(half, 2 * half)
    grad = both_halves(place_ref[0], own_ref[at, :], other_ref[at, :])
    next_ref[...] = grad
    low = grad.astype(BF)
    low_ref[...] = low
    size = width // heads
    scale = size**-0.5
    wide = in_ref.shape[2]
    context_grad = dot_nt(low, out_ref[...]).astype(BF)
    for j in range(wide // (2 * size)):
        query, keys, values = (
            qkv_ref[:, wide * k + 2 * size * j : wide * k + 2 * size * (j + 1)] for k in range(3)
        )
        grads = attend_pair_backward(
            query, keys, values, context_grad[:, 2 * size * j : 2 * size * (j + 1)], frames, scale
        )
        for k in range(3):
            dqkv_ref[:, wide * k + 2 * size * j : wide * k + 2 * size * (j + 1)] = grads[k]
    total = None
    for k in range(3):
        part = dot_nt(dqkv_ref[:, wide * k : wide * (k + 1)], in_ref[k])
        total = part if total is None else total + part
    part_ref[...] = total


def message_last_kernel(
    place_ref, own_ref, other_ref, next_ref, low_ref, dqkv_ref, part_ref, part_other_ref, message_ref, gain_ref, w_ref,
    late_ref, cls_ref,
):
    frames, width = next_ref.shape
    half = frames // 2
    normal, rstd = standardized(message_ref[...])
    part, gain_grad = norm_backward(part_ref[...] + part_other_ref[...], gain_ref[...], normal, rstd)
    message_low = (next_ref[...] + part).astype(BF)
    cls = both_halves(place_ref[0], own_ref[0:half, :], other_ref[0:half, :])
    cls_ref[...] = (cls + dot_nt(message_low, w_ref[...])).astype(BF)
    wide = dqkv_ref.shape[1]
    late_ref[0:frames, 0:width] = low_ref[...]
    late_ref[0:frames, width : 2 * width] = message_low
    late_ref[0:frames, 2 * width : 2 * width + wide] = dqkv_ref[...]
    both = own_ref[2 * half : 2 * half + 2, :] + other_ref[2 * half : 2 * half + 2, :]
    gains = jnp.concatenate([both[1:2], both[0:1], gain_grad], axis=1)
    room = late_ref.shape[1] - 2 * width - wide
    gains = jnp.concatenate([gains, jnp.zeros((1, frames * room - 3 * width), F32)], axis=1)
    gains = jnp.concatenate([gains[:, room * r : room * (r + 1)] for r in range(frames)], axis=0)
    late_ref[:, 2 * width + wide :] = gains.astype(BF)


def assemble_kernel(pieces, place_ref, *refs):
    out_ref, wide_ref = refs[-2:]
    tile, frames, width = out_ref.shape
    half = frames // 2
    for side in range(2):
        mp = place_ref[0] if side == 0 else 1 - place_ref[0]
        for k in range(half):
            per = half // pieces
            value = refs[side * pieces + k // per][k % per].astype(F32)
            for j in range(width // 128):
                wide_ref[j, pl.ds(mp * half + k, tile, stride=8), :] = value[:, 128 * j : 128 * (j + 1)]
    for j in range(width // 128):
        out_ref[:, :, 128 * j : 128 * (j + 1)] = wide_ref[j].reshape(tile, frames, 128).astype(BF)
    if len(refs) > 2 * pieces + 2:

        @pl.when(pl.program_id(0) == 0)
        def _():
            out_ref[0] = refs[2 * pieces][...]


def factor_kernel(
    frames, place_ref, early_ref, late_ref, pooled_ref, embed_ref,
    weight_ref, in_ref, out_ref, proj_ref, gains_ref,
):
    size = early_ref.shape[0]
    share, width = weight_ref.shape
    wide = out_ref.shape[1]
    column = lax.broadcasted_iota(jnp.int32, (share, width), 1)
    row = lax.broadcasted_iota(jnp.int32, (share, width), 0)
    pick = (column == place_ref[1] * share + row).astype(F32).astype(BF)

    def early(first, wide):
        value = early_ref[:, :, first : first + wide].astype(F32)[:, :frames]
        return value.reshape(size * frames, wide).astype(BF)

    def late(first, wide):
        return late_ref[:, :, first : first + wide].astype(F32).reshape(size * frames, wide).astype(BF)

    def own(value):
        return dot_nt(pick, value).astype(BF)

    weight_ref[...] = dot(own(early(0, width)), late(width, width))
    product = dot(own(early(width, width)), late(2 * width, 3 * wide))
    for k in range(3):
        in_ref[k] = product[:, wide * k : wide * (k + 1)]
    out_ref[...] = dot(own(late(0, width)), early(2 * width, wide))
    proj_ref[...] = dot(own(pooled_ref[...]), embed_ref[...])
    room = late_ref.shape[2] - 2 * width - 3 * wide
    gains = jnp.sum(late_ref[:, :, 2 * width + 3 * wide :].astype(F32), axis=0)
    gains = jnp.concatenate([gains[r : r + 1, :] for r in range(frames)], axis=1)
    for k in range(3):
        gains_ref[k : k + 1, :] = gains[:, width * k : width * (k + 1)]


def whole(shape):
    return pl.BlockSpec(tuple(shape), lambda *_: (0,) * len(shape))


def run(kernel, name, args, outs, grid=(1,), prefetch=0, specs=None, out_specs=None, scratch=(), aliases=None, deps=(), cost=2):
    specs = specs or {}
    out_specs = out_specs or {}
    tensors = args[prefetch:]
    taken = len(args)

    def body(*refs):
        kernel(*refs[:taken], *refs[taken + len(deps) :])

    return pl.pallas_call(
        body,
        out_shape=list(outs),
        grid_spec=pltpu.PrefetchScalarGridSpec(
            num_scalar_prefetch=prefetch,
            grid=grid,
            in_specs=[specs.get(k, whole(t.shape)) for k, t in enumerate(tensors)]
            + [pl.BlockSpec(memory_space=pl.ANY)] * len(deps),
            out_specs=[out_specs.get(k, whole(o.shape)) for k, o in enumerate(outs)],
            scratch_shapes=list(scratch),
        ),
        compiler_params=pltpu.CompilerParams(
            dimension_semantics=("arbitrary",) * len(grid), vmem_limit_bytes=KERNEL_MIB.get(name, 16) * 1024 * 1024
        ),
        cost_estimate=pl.CostEstimate(flops=round(KERNEL_US.get(name, cost) * 2.3e9), bytes_accessed=0, transcendentals=0),
        input_output_aliases={prefetch + k: out for k, out in (aliases or {}).items()},
        name=name,
    )(*args, *deps)


def shape_of(shape, dtype):
    return jax.ShapeDtypeStruct(tuple(shape), dtype)


def plus(a, b, dtype=BF):
    return (a.astype(F32) + b.astype(F32)).astype(dtype)


def reorder(ways, keep, send):
    size = lax.axis_size("dp")
    bits = bits_of(size)
    lead, rows, wide = keep.shape
    block = 2 * rows // 16
    value = jnp.stack([keep.reshape(lead, 8, block, wide), send.reshape(lead, 8, block, wide)], axis=2)
    value = value.reshape(lead, size, 2 * rows // size, wide)
    turned = []
    for one, order in zip(value, ways(bits[1:])):
        order = [bit for bit in order if bit != "mp"]
        order = jnp.bitwise_xor(jnp.asarray(row_order(bits[:1] + order), jnp.int32), lax.axis_index("dp"))
        turned.append(jnp.take(one, order, axis=0).reshape(2 * rows, wide))
    value = jnp.stack(turned)
    return (value[:, :rows], value[:, rows:])


def joint(ways):
    return ways[0] == ways[1] and ways[0] not in (None, "mp")


def stage_values(keep_first, keep_second, *got):
    parts = keep_first.shape[0]
    came = (got[0][:parts], got[0][parts:]) if len(got) == 1 else (got[0][...], got[1][...])
    return [keep[...].astype(F32) + one.astype(F32) for keep, one in zip((keep_first, keep_second), came)]


def stage_kernel(ways, came, *refs):
    values = stage_values(*refs[: 2 + came])
    refs = refs[2 + came :]
    if joint(ways):
        at = 0
        for k, value in enumerate(values):
            parts, rows, _ = value.shape
            refs[k][...] = value[:, : rows // 2].astype(BF)
            refs[2][at : at + parts] = value[:, rows // 2 :].astype(BF)
            at += parts
        return
    per = len(refs) // 2
    for k, (value, way) in enumerate(zip(values, ways)):
        keep, send = (refs[per * k], refs[per * (k + 1) - 1])
        if way is None:
            keep[...] = value
        elif way == "mp":
            keep[...] = value[0:1].astype(BF)
            send[...] = value[1:2].astype(BF)
        else:
            rows = value.shape[1] // 2
            keep[...] = value[:, :rows].astype(BF)
            send[...] = value[:, rows:].astype(BF)


def frame_final_kernel(keep_first, keep_second, got, in_ref, out_ref):
    first, second = stage_values(keep_first, keep_second, got)
    wide = out_ref.shape[1]
    in_ref[0] = first[0][:, :wide]
    in_ref[1] = first[0][:, wide:]
    in_ref[2] = second[0][:, :wide]
    out_ref[...] = second[0][:, wide:]


def core_stage_kernel(ways, keep_own, got_own, keep_other, got_other, *refs):
    for k in range(2):
        parts = [
            keep[k : k + 1].astype(F32) + got[k : k + 1].astype(F32)
            for keep, got in ((keep_own, got_own), (keep_other, got_other))
        ]
        for part, at in zip(parts, range(2)):
            if ways[k] == "mp":
                refs[2 * k + at][...] = part.astype(BF)
                continue
            rows = part.shape[1] // 2
            refs[2 * k][at : at + 1] = part[:, :rows].astype(BF)
            refs[2 * k + 1][at : at + 1] = part[:, rows:].astype(BF)


class Reduction:
    def __init__(self, name, ways, keep_own, send_own, keep_other, send_other):
        size = lax.axis_size("dp")
        self.name = name
        self.bits = bits_of(size)
        self.aligned = (2 * keep_own.shape[1] // size) % 16 == 0
        if not self.aligned:
            keep_own, send_own = reorder(ways, keep_own, send_own)
            keep_other, send_other = reorder(ways, keep_other, send_other)
        self.ways = ways(self.bits[1:])
        self.steps = len(self.ways[0])
        self.at = 0
        self.keep = (keep_own, keep_other)
        self.got = tuple(flip(send, self.bits[0]) for send in (send_own, send_other))

    def ways_at(self, at):
        return tuple(ways[at] if at < self.steps else None for ways in self.ways)

    def outs(self, shapes, ways):
        made = []
        if joint(ways):
            parts = [shape[0] for shape in shapes]
            _, rows, wide = shapes[0]
            return [shape_of((count, rows // 2, wide), BF) for count in parts + [sum(parts)]]
        for (parts, rows, wide), way in zip(shapes, ways):
            if way is None:
                made.append(shape_of((parts, rows, wide), F32))
            elif way == "mp":
                made += [shape_of((1, rows, wide), BF)] * 2
            else:
                made += [shape_of((parts, rows // 2, wide), BF)] * 2
        return made

    def call(self, kernel, args, shapes, ways, deps, cost):
        if not self.aligned:
            refs = [Box(out) for out in self.outs(shapes, ways)]
            kernel(ways, *args, *refs)
            return [ref.value for ref in refs]
        made = self.outs(shapes, ways)
        wide = made[0].shape[2]
        chunk = 384

        def spec(value):
            return pl.BlockSpec(value.shape[:2] + (chunk,), lambda j, *_: (0, 0, j))

        return run(
            functools.partial(kernel, ways),
            self.name + str(self.at),
            args,
            made,
            grid=(wide // chunk,),
            specs={k: spec(value) for k, value in enumerate(args)},
            out_specs={k: spec(value) for k, value in enumerate(made)},
            deps=deps,
            cost=cost,
        )

    def take(self, made):
        self.joined = made[2:] if len(made) == 3 else []
        per = (len(made) - len(self.joined)) // 2
        self.value = [made[per * k : per * (k + 1)] for k in range(2)]

    def cores(self, *deps, cost=0):
        own, other = self.keep
        _, rows, wide = own.shape
        args = (own, self.got[0], other, self.got[1])
        self.take(self.call(core_stage_kernel, args, [(2, rows, wide)] * 2, self.ways_at(0), deps, cost))
        self.at = 0
        self.send()

    def send(self):
        ways = self.ways_at(self.at)
        if self.joined:
            self.got = [flip(self.joined[0], ways[0])]
            return
        self.got = []
        for (_, send), way in zip(self.value, ways):
            self.got.append(swap(send) if way == "mp" else flip(send, way))

    def ready(self):
        return tuple(one for values in self.value for one in values)

    def parts(self):
        return (self.value[0][0], self.value[1][0], *self.got)

    def step(self, *deps, cost=0):
        args = self.parts()
        shapes = [value[0].shape for value in self.value]
        self.at += 1
        kernel = lambda ways, *refs: stage_kernel(ways, len(args) - 2, *refs)
        self.take(self.call(kernel, args, shapes, self.ways_at(self.at), deps, cost))
        if self.at < self.steps:
            self.send()


class Box:
    def __init__(self, out):
        self.value = jnp.zeros(out.shape, out.dtype)

    def __setitem__(self, at, value):
        self.value = value if at is Ellipsis else self.value.at[at].set(value)


def on_device(
    tokens,
    captions,
    clip_groups,
    caption_groups,
    msg_weight,
    msg_gain,
    msg_in,
    msg_out,
    frame_gain,
    frame_in,
    frame_out,
    mlp_gain,
    up_weight,
    down_weight,
    proj_weight,
    out_cot,
):
    clips, frames, patches, width = tokens.shape
    assert clips == 1 and frames == 8 and lax.axis_size("mp") == 2
    size = lax.axis_size("dp")
    valid = patches + 1
    seq = -(-valid // 16) * 16
    half = frames // 2
    rows = half * seq
    share = width // size
    aligned = share % 16 == 0
    count = len(bits_of(size)) - 1 if aligned else None
    h_half = frame_in.shape[2]
    f_half = up_weight.shape[1]
    embed = proj_weight.shape[1]
    me_dp, me_mp = (lax.axis_index("dp"), lax.axis_index("mp"))
    place = jnp.stack([me_mp, me_dp, clip_groups[0], caption_groups[0]]).astype(jnp.int32)
    msg_gain, frame_gain, mlp_gain = (gain.reshape(1, width) for gain in (msg_gain, frame_gain, mlp_gain))
    tokens_t, cot_t = (jnp.transpose(value, (0, 2, 1, 3)) for value in (tokens, out_cot))
    class_spec = pl.BlockSpec((1, 1, frames, width), lambda *_: (0, 0, 0, 0))

    def mine(value, axis=1):
        return lax.dynamic_slice_in_dim(value, me_dp * share, share, axis)

    devices = size if aligned else 16
    each = width // devices

    def packed(up, down):
        up = up.reshape(-1, each, f_half // width, width).transpose(0, 2, 1, 3).reshape(-1, f_half // devices, width)
        return jnp.concatenate([up, down.reshape(-1, f_half // devices, width)], axis=1)

    if aligned:
        down_share = lax.dynamic_slice_in_dim(down_weight, me_dp * (f_half // size), f_half // size, 0)
        mlp_share = swap(packed(mine(up_weight, 0), down_share))
    else:
        mlp_other = packed(swap(up_weight), swap(down_weight))

    message, early, msg_qkv, msg_part = run(
        functools.partial(message_forward_kernel, HEADS),
        "message_forward",
        (place, tokens_t, captions, msg_weight, msg_gain, msg_in, msg_out),
        (
            shape_of((frames, width), F32),
            shape_of((16, 2 * width + h_half), BF),
            shape_of((frames, 3 * h_half), BF),
            shape_of((frames, width), F32),
        ),
        prefetch=1,
        specs={0: class_spec},
    )
    msg_other = swap(msg_part)
    if aligned:
        mlp_other = lax.all_gather(after(mlp_share, msg_part), "dp", axis=0, tiled=True)

    def half_rows(value, axis):
        rows_half = value.shape[axis] // 2
        return lax.dynamic_slice_in_dim(value, (me_dp % 2) * rows_half, rows_half, axis)

    in_mine = swap(after(half_rows(frame_in, 1), msg_part))

    one_frame = lambda wide, first=0: pl.BlockSpec((1, seq, wide), lambda f, *_: (f + first, 0, 0))
    whole_wide = pltpu.VMEM((width // 128, patches * frames, 128), F32)
    chunk = 512
    grad, dact_own = run(
        functools.partial(cotangent_kernel, half),
        "cotangent",
        (place, cot_t.reshape(patches, frames, width), down_weight),
        (shape_of((rows, width), BF), shape_of((rows, f_half), BF)),
        grid=(f_half // chunk,),
        prefetch=1,
        specs={1: pl.BlockSpec((chunk, width), lambda j, *_: (j, 0))},
        out_specs={1: pl.BlockSpec((rows, chunk), lambda j, *_: (0, j))},
        scratch=[whole_wide],
        deps=(msg_part,),
    )
    stream, frame_low, qkv_own, context_own, frame_rstd, logsum_own = run(
        functools.partial(frame_first_kernel, HEADS, half),
        "frame_first",
        (place, tokens_t.reshape(patches, frames, width), message, msg_part, msg_other, frame_gain, frame_in),
        (
            shape_of((half, seq, width), BF),
            shape_of((half, seq, width), BF),
            shape_of((half, seq, 3 * h_half), BF),
            shape_of((half, seq, h_half), BF),
            shape_of((half, seq, 128), F32),
            shape_of((half, seq, 128), F32),
        ),
        grid=(half,),
        prefetch=1,
        out_specs={
            0: one_frame(width),
            1: one_frame(width),
            2: one_frame(3 * h_half),
            3: one_frame(h_half),
            4: one_frame(128),
            5: one_frame(128),
        },
        scratch=[whole_wide, pltpu.VMEM((seq, width), F32)],
        deps=(grad,),
    )
    in_theirs = flip(after(in_mine, stream), 1)
    out_other = swap(after(frame_out, grad))
    bits = gather_bits()

    def hop(value, k, *deps):
        return jnp.concatenate([value, after(flip(value, bits[k]), *deps)], axis=0)

    qkv_other, context_other, in_other, logsum_other = run(
        functools.partial(frame_second_kernel, HEADS, valid),
        "frame_second",
        (place, frame_low, in_mine, in_theirs),
        (
            shape_of((half, seq, 3 * h_half), BF),
            shape_of((half, seq, h_half), BF),
            shape_of(frame_in.shape, BF),
            shape_of((half, seq, 128), F32),
        ),
        grid=(half,),
        prefetch=1,
        specs={0: one_frame(width)},
        out_specs={0: one_frame(3 * h_half), 1: one_frame(h_half), 3: one_frame(128)},
    )

    steps = f_half // chunk
    up_spec = pl.BlockSpec((width, chunk), lambda j, *_: (0, j))
    down_spec = pl.BlockSpec((chunk, width), lambda j, *_: (j, 0))
    unit_spec = pl.BlockSpec((rows, chunk), lambda j, *_: (0, j))
    units = shape_of((rows, f_half), BF)
    wide_rows = shape_of((rows, width), F32)
    context_own2, context_other2 = (v.reshape(rows, h_half) for v in (context_own, context_other))
    (
        mlp_rstd, mlp_low, activ_own, dhid_own, slope_cls_own, total, back, cls_low, cls_total,
    ) = run(
        functools.partial(mlp_first_kernel, half),
        "mlp_first",
        (
            stream.reshape(rows, width), context_own2, context_other2, frame_out, out_other, mlp_gain,
            up_weight, down_weight, dact_own,
        ),
        (
            shape_of((rows, 128), F32), shape_of((rows, width), BF), units, units, shape_of((16, f_half), F32), wide_rows,
            wide_rows,
            shape_of((16, width), BF), shape_of((16, width), F32),
        ),
        grid=(steps,),
        specs={6: up_spec, 7: down_spec, 8: unit_spec},
        out_specs={2: unit_spec, 3: unit_spec, 4: pl.BlockSpec((16, chunk), lambda j, *_: (0, j))},
    )

    part = f_half // 4
    per = width // part

    def up_other_spec(first):
        return pl.BlockSpec((devices, each, part), lambda j, *_: (0, (j + first) // per, (j + first) % per))

    def down_other_spec(first):
        return pl.BlockSpec((devices // 4, f_half // devices, width), lambda j, *_: (j + first, 1, 0))

    def part_spec(first=0):
        return pl.BlockSpec((rows, part), lambda j, *_: (0, j + first))

    (pooled_part,) = run(
        functools.partial(class_forward_kernel, half),
        "class_forward",
        (cls_low, cls_total, mlp_other, mlp_other),
        (shape_of((1, width), F32),),
        grid=(4,),
        specs={2: up_other_spec(0), 3: down_other_spec(0)},
        scratch=[pltpu.VMEM((16, width), F32)],
    )
    pooled_low = ((pooled_part + swap(pooled_part)) / frames).astype(BF)
    stages = [early.at[frames : frames + 1, width : 2 * width].set(pooled_low)[None]]
    for k in range(len(bits)):
        stages.append(hop(stages[-1], k))
    early_all = stages[-1]
    anywhere = pl.BlockSpec(memory_space=pl.ANY)
    activ_2, slope_2, total = run(
        functools.partial(mlp_second_kernel, half),
        "mlp_second",
        (total, mlp_low, mlp_other, mlp_other),
        (units, units, wide_rows),
        grid=(2,),
        specs={2: up_other_spec(0), 3: down_other_spec(0)},
        out_specs={0: part_spec(), 1: part_spec()},
        deps=(stages[0],),
    )
    activ_other, slope_other, result_own = run(
        functools.partial(mlp_third_kernel, half),
        "mlp_third",
        (total, mlp_low, mlp_other, mlp_other, activ_2, slope_2),
        (units, units, shape_of((rows, width), BF)),
        grid=(2,),
        specs={2: up_other_spec(2), 3: down_other_spec(2), 4: anywhere, 5: anywhere},
        out_specs={0: part_spec(2), 1: part_spec(2)},
        scratch=[pltpu.VMEM((rows, width), F32)],
        aliases={4: 0, 5: 1},
        deps=(stages[1],),
    )
    result_other = swap(result_own)

    def hidden_backward(name, back, first, deps, *made):
        return run(
            hidden_backward_kernel,
            name,
            (back, grad, slope_other, mlp_other, mlp_other, *made),
            (units, wide_rows),
            grid=(2,),
            specs={2: part_spec(first), 3: up_other_spec(first), 4: down_other_spec(first), 5: anywhere},
            out_specs={0: part_spec(first)},
            aliases={5: 0} if made else None,
            deps=deps,
        )

    dhid_2, back = hidden_backward("hidden_backward_a", back, 0, (stages[2], result_own))
    dhid_other, back = hidden_backward("hidden_backward_b", back, 2, (stages[3],), dhid_2)
    class_picks = [slope_other[f * seq : f * seq + 1] for f in range(half)]
    slope_cls_other = jnp.concatenate(class_picks + [jnp.zeros((16 - half, f_half), BF)], axis=0).astype(F32)

    loss, caption_grad, embed_grad, pooled_all, pooled_grad = run(
        functools.partial(loss_kernel, bits, frames),
        "contrast",
        (place, early_all, proj_weight),
        (
            shape_of((1, 1), F32),
            shape_of((1, embed), F32),
            shape_of((size, embed), BF),
            shape_of((size, width), BF),
            shape_of((1, width), F32),
        ),
        prefetch=1,
        deps=(back,),
    )

    part_cols = lambda n: pl.BlockSpec((n, part), lambda j, *_: (0, j))
    cls_units = shape_of((16, f_half), BF)
    grad_cls, dhid_cls_own, dhid_cls_other, back_cls = run(
        functools.partial(class_backward_kernel, half),
        "class_backward",
        (place, cot_t, pooled_grad, slope_cls_own, slope_cls_other, up_weight, down_weight, mlp_other, mlp_other),
        (shape_of((16, width), BF), cls_units, cls_units, shape_of((16, width), F32)),
        grid=(4,),
        prefetch=1,
        specs={
            0: class_spec,
            2: part_cols(16),
            3: part_cols(16),
            4: part_cols(width),
            5: pl.BlockSpec((part, width), lambda j, *_: (j, 0)),
            6: up_other_spec(0),
            7: down_other_spec(0),
        },
        out_specs={1: part_cols(16), 2: part_cols(16)},
    )
    weights = shape_of((2, width // 2, f_half), BF)
    wide_steps = f_half // width

    def unit_part(first, lead):
        return pl.BlockSpec(lead + (width,), lambda t, *_: (0,) * len(lead) + (jnp.clip(t - first, 0, wide_steps - 1),))

    keep_own, send_own, keep_other, send_other = run(
        functools.partial(mlp_weight_kernel, half, count),
        "mlp_weights",
        (
            place, grad, grad_cls, mlp_low, activ_own, dhid_own, dhid_cls_own, activ_other, dhid_other, dhid_cls_other,
        ),
        (weights,) * 4,
        grid=(2 * wide_steps,),
        prefetch=1,
        specs={
            3: unit_part(wide_steps, (rows,)),
            4: unit_part(wide_steps, (rows,)),
            5: unit_part(wide_steps, (16,)),
            6: unit_part(0, (rows,)),
            7: unit_part(0, (rows,)),
            8: unit_part(0, (16,)),
        },
        out_specs={k: unit_part(wide_steps if k < 2 else 0, (2, width // 2)) for k in range(4)},
        scratch=[
            pltpu.VMEM((width, rows), BF),
            pltpu.VMEM((width, rows), BF),
            pltpu.VMEM((rows, width), BF),
            pltpu.VMEM((rows, width), BF),
        ],
        deps=(result_other,),
    )
    mlp_stages = Reduction("mlp_stage", mlp_ways, keep_own, send_own, keep_other, send_other)

    in_shape = shape_of((half, seq, 3 * h_half), BF)
    made = (
        shape_of((half, seq, width), BF), in_shape, in_shape, shape_of((half // 2, seq, width), BF), shape_of((16, width), F32),
    )

    def frame_backward(name, first, before, deps=()):
        tensors = (
            back, grad, mlp_low, mlp_rstd, qkv_own, qkv_other, frame_low, frame_rstd, context_own, context_other,
            logsum_own, logsum_other, back_cls, grad_cls, mlp_gain,
            frame_gain, frame_out, out_other, frame_in, in_other, *before,
        )
        flat_frame = lambda wide: pl.BlockSpec((seq, wide), lambda f, *_: (f + first, 0))
        specs = {
            0: flat_frame(width),
            1: flat_frame(width),
            2: flat_frame(width),
            3: flat_frame(128),
            4: one_frame(3 * h_half, first),
            5: one_frame(3 * h_half, first),
            6: one_frame(width, first),
            7: one_frame(128, first),
            8: one_frame(h_half, first),
            9: one_frame(h_half, first),
            10: one_frame(128, first),
            11: one_frame(128, first),
        }
        specs.update({20 + k: anywhere for k in range(3 if before else 0)})
        return run(
            functools.partial(frame_backward_kernel, HEADS, valid, half, first),
            name,
            tensors,
            made,
            grid=(half // 2,),
            specs=specs,
            out_specs={
                0: one_frame(width, first),
                1: one_frame(3 * h_half, first),
                2: one_frame(3 * h_half, first),
                3: one_frame(width),
            },
            aliases={20 + k: k for k in range(3)} if before else None,
            deps=deps,
        )

    before = frame_backward("frame_backward_a", 0, (), (keep_own,))
    mlp_stages.cores(before[0])
    token_first = before[3]
    token_first_other = swap(token_first)
    middle_low, dqkv_own, dqkv_other, token_second, edges = frame_backward(
        "frame_backward_b", half // 2, (before[0], before[1], before[2], before[4]), mlp_stages.ready()
    )
    edges_other = swap(edges)

    next_grad, next_low, msg_dqkv, msg_normed = run(
        functools.partial(message_backward_kernel, HEADS),
        "message_backward",
        (place, edges, edges_other, msg_qkv, msg_out, msg_in),
        (
            shape_of((frames, width), F32),
            shape_of((frames, width), BF),
            shape_of((frames, 3 * h_half), BF),
            shape_of((frames, width), F32),
        ),
        prefetch=1,
    )
    msg_normed_other = swap(msg_normed)
    mlp_stages.step(next_grad)
    grads = shape_of((2, width // 2, 2 * h_half), BF)

    def share_spec(first):
        return pl.BlockSpec((1, width // 2, 2 * h_half), lambda t, *_: (jnp.clip(t - first, 0, 1), 0, 0))

    def column_spec(first):
        return pl.BlockSpec((rows, 2 * h_half), lambda t, *_: (0, jnp.clip(t - first, 0, 1)))

    keep_own, send_own, keep_other, send_other = run(
        functools.partial(frame_weight_kernel, count),
        "frame_weights",
        (
            place, frame_low.reshape(rows, width), middle_low.reshape(rows, width),
            dqkv_own.reshape(rows, 3 * h_half), dqkv_other.reshape(rows, 3 * h_half), context_own2, context_other2,
        ),
        (grads,) * 4,
        grid=(4,),
        prefetch=1,
        specs={2: column_spec(2), 3: column_spec(0)},
        out_specs={0: share_spec(2), 1: share_spec(2), 2: share_spec(0), 3: share_spec(0)},
        scratch=[pltpu.VMEM((width, rows), BF), pltpu.VMEM((width, rows), BF)],
        deps=(*mlp_stages.ready(), token_first_other),
    )
    frame_stages = Reduction("frame_stage", frame_ways, keep_own, send_own, keep_other, send_other)

    late, cls_rows = run(
        message_last_kernel,
        "message_last",
        (
            place, edges, edges_other, next_grad, next_low, msg_dqkv, msg_normed,
            msg_normed_other, message, msg_gain, msg_weight,
        ),
        (shape_of((frames, 2 * width + 6 * h_half), BF), shape_of((frames, width), BF)),
        prefetch=1,
        deps=(keep_own,),
    )
    frame_stages.cores(late)
    cores_ready = frame_stages.ready()
    def both(name, own, other, extra=(), deps=()):
        tile = 64
        parts = own + other
        (out,) = run(
            functools.partial(assemble_kernel, len(own)),
            name,
            (place, *parts, *extra),
            (shape_of((patches, frames, width), BF),),
            grid=(-(-patches // tile),),
            prefetch=1,
            specs={
                k: pl.BlockSpec((part.shape[0], tile, width), lambda t, s: (0, t, 0)) for k, part in enumerate(parts)
            },
            out_specs={0: pl.BlockSpec((tile, frames, width), lambda t, s: (t, 0, 0))},
            scratch=[pltpu.VMEM((width // 128, tile * frames, 128), F32)],
            deps=deps,
        )
        return out

    def whole_of(value):
        return jnp.transpose(value[None], (0, 2, 1, 3))

    result_own, result_other = (value.reshape(half, seq, width) for value in (result_own, result_other))
    for k in range(1, len(bits)):
        extra = ()
        if k == 2:
            layer_parts = both("assemble_out", (result_own,), (result_other,), deps=frame_stages.ready())
            extra = (layer_parts,)
        last = mlp_stages.at == mlp_stages.steps - 1
        mlp_stages.step(*frame_stages.ready())
        if k == 1:
            late_all = hop(late[None], 0, *mlp_stages.ready())
        frame_stages.step(*extra, *((mlp_stages.value[0][0],) if last else mlp_stages.ready()))
        if k == 1:
            token_second_other = swap(after(token_second, *frame_stages.ready()))
        late_all = hop(late_all, k, *(frame_stages.ready() if k < 3 else ()))

    layer_out = whole_of(layer_parts)
    token_parts = both(
        "assemble_grad", (token_first, token_second), (token_first_other, token_second_other), (cls_rows,)
    )

    msg_weight_share, msg_in_share, msg_out_share, proj_share, gains = run(
        functools.partial(factor_kernel, frames),
        "factors",
        (place, early_all, late_all, pooled_all, embed_grad),
        (
            shape_of((share, width), F32),
            shape_of((3, share, h_half), F32),
            shape_of((share, h_half), F32),
            shape_of((share, embed), F32),
            shape_of((3, width), F32),
        ),
        prefetch=1,
    )
    if aligned:
        in_grad, out_grad = run(
            frame_final_kernel,
            "frame_final",
            frame_stages.parts(),
            (shape_of((3, share, h_half), F32), shape_of((share, h_half), F32)),
            deps=(token_parts, gains),
        )
        out_grad = out_grad.T
    else:
        frame_stages.step(token_parts, gains)
        (first,), (second,) = frame_stages.value
        first, second = first[0], second[0]
        in_grad = jnp.stack([first[:, :h_half], first[:, h_half:], second[:, :h_half]])
        out_grad = second[:, h_half:].T
    token_grad = whole_of(token_parts)
    (up_grad,), (down_grad,) = mlp_stages.value
    up_grad, down_grad = (up_grad[0], down_grad[0].T)
    msg_out_share = msg_out_share.T
    gains = mine(gains)
    return (
        layer_out,
        loss[0, 0],
        token_grad,
        caption_grad,
        msg_weight_share,
        gains[2],
        msg_in_share,
        msg_out_share,
        gains[1],
        in_grad,
        out_grad,
        gains[0],
        up_grad,
        down_grad,
        proj_share,
    )


def solution(mesh):
    in_specs = (
        P("dp", None, None, None),
        P("dp", None),
        P("dp"),
        P("dp"),
        P(),
        P(),
        P(None, None, "mp"),
        P("mp", None),
        P(),
        P(None, None, "mp"),
        P("mp", None),
        P(),
        P(None, "mp"),
        P("mp", None),
        P(),
        P("dp", None, None, None),
    )
    out_specs = (
        P("dp", None, None, None),
        P(),
        P("dp", None, None, None),
        P("dp", None),
        P("dp", None),
        P("dp"),
        P(None, "dp", "mp"),
        P("mp", "dp"),
        P("dp"),
        P(None, "dp", "mp"),
        P("mp", "dp"),
        P("dp"),
        P("dp", "mp"),
        P("mp", "dp"),
        P("dp", None),
    )
    return jax.shard_map(
        on_device, mesh=mesh, in_specs=in_specs, out_specs=out_specs, check_vma=False
    )
```

```python
import functools

import jax
import jax.numpy as jnp
from jax import lax
from jax.experimental import pallas as pl
from jax.experimental.pallas import tpu as pltpu
from jax.sharding import PartitionSpec as P

HEADS = 12
SHARPNESS = 50.0
LOWEST = -1e30
BF = jnp.bfloat16
F32 = jnp.float32
KERNEL_MIB = {
    "frame_first": 52,
    "cotangent": 52,
    "frame_second": 52,
    "mlp_first": 52,
    "mlp_second": 52,
    "mlp_third": 52,
    "hidden_backward_a": 52,
    "hidden_backward_b": 52,
    "mlp_weights": 52,
    "frame_backward_a": 52,
    "frame_backward_b": 52,
    "frame_weights": 52,
    "contrast": 52,
    "class_backward": 52,
    "class_forward": 52,
}
KERNEL_US = {
    "frame_first": 7,
    "cotangent": 4,
    "frame_second": 6,
    "mlp_first": 16,
    "mlp_second": 5,
    "mlp_third": 5,
    "hidden_backward_a": 5,
    "hidden_backward_b": 5,
    "class_backward": 5,
    "mlp_weights": 15,
    "frame_backward_a": 14,
    "frame_backward_b": 14,
    "frame_weights": 11,
}


def swap(value):
    return lax.ppermute(value, "mp", [(0, 1), (1, 0)])


def flip(value, bit):
    size = lax.axis_size("dp")
    return lax.ppermute(value, "dp", [(i, i ^ bit) for i in range(size)])


def after(value, *deps):
    return lax.optimization_barrier((value,) + deps)[0]


def bits_of(size):
    return [1 << k for k in range(size.bit_length() - 1)]


def row_order(bits):
    order = [0]
    for bit in reversed(bits):
        order = order + [mask | bit for mask in order]
    return order


def mlp_ways(bits):
    return (bits[:1] + ["mp"] + bits[1:], bits[1:] + bits[:1] + ["mp"])


def frame_ways(bits):
    return (bits[:1] + ["mp"] + bits[1:], ["mp"] + bits)


def gather_bits():
    bits = bits_of(lax.axis_size("dp"))
    return bits[:0:-1] + bits[:1]


def gather(value):
    for bit in gather_bits():
        value = jnp.concatenate([value, flip(value, bit)], axis=0)
    return value


def dot(a, b):
    return jnp.dot(a, b, preferred_element_type=F32)


def dot_nt(a, b):
    return lax.dot_general(a, b, (((1,), (1,)), ((), ())), preferred_element_type=F32)


def dot_tn(a, b):
    return lax.dot_general(a, b, (((0,), (0,)), ((), ())), preferred_element_type=F32)


def standardized(value):
    centered = value - jnp.mean(value, axis=-1, keepdims=True)
    rstd = lax.rsqrt(jnp.mean(centered * centered, axis=-1, keepdims=True) + 1e-05)
    return (centered * rstd, rstd)


def spread(rstd):
    return jnp.broadcast_to(rstd, (rstd.shape[0], 128))


def norm_backward(grad, gain, normal, rstd):
    scaled = grad * gain
    inner = (
        scaled
        - jnp.mean(scaled, axis=-1, keepdims=True)
        - normal * jnp.mean(scaled * normal, axis=-1, keepdims=True)
    )
    return (rstd * inner, jnp.sum(grad * normal, axis=0, keepdims=True))


def lane_half(rows, pair, which):
    lane = lax.broadcasted_iota(jnp.int32, (rows, pair), 1)
    return (lane < pair // 2) if which == 0 else (lane >= pair // 2)


def only(value, which):
    return jnp.where(lane_half(*value.shape, which), value, jnp.zeros_like(value))


def attend_pair(query, keys, values, valid):
    rows, pair = query.shape
    out = None
    sums = []
    for which in range(2):
        scores = dot_nt(only(query, which), keys)
        if valid < rows:
            key = lax.broadcasted_iota(jnp.int32, scores.shape, 1)
            scores = jnp.where(key < valid, scores, LOWEST)
        top = jnp.max(scores, axis=1, keepdims=True)
        each = jnp.exp(scores - top)
        total = jnp.sum(each, axis=1, keepdims=True)
        sums.append(top + jnp.log(total))
        part = dot(each.astype(BF), only(values, which)) * (1.0 / total)
        out = part if out is None else out + part
    return (out, sums)


def attend_pair_kept(query, keys, values, grad, logsums, inners, valid, scale):
    rows, pair = query.shape
    size = pair // 2
    edge = valid // 16 * 16
    lane = lax.broadcasted_iota(jnp.int32, (1, pair), 1)
    keys_t = keys.T
    turned, both = ([], [])
    for which in range(2):
        head = (lane // size == which).astype(F32).astype(BF)
        weights = jnp.exp(dot_nt(keys, query * head) - logsums[which])
        tail = weights[edge:]
        row = lax.broadcasted_iota(jnp.int32, tail.shape, 0)
        weights = jnp.concatenate([weights[:edge], jnp.where(row < valid - edge, tail, 0.0)], axis=0)
        weight_grad = dot_nt(values, grad * head)
        value_grad = dot(weights.astype(BF), grad)
        score_grad = (weights * (weight_grad - inners[which])).astype(BF)
        key_grad = dot(score_grad, query)
        turned.append(dot(keys_t[size * which : size * (which + 1)], score_grad))
        both.append((key_grad, value_grad))
    query_grad = (jnp.concatenate(turned, axis=0) * scale).astype(BF).T
    first = lane_half(rows, pair, 0)
    key_grad, value_grad = (jnp.where(first, one, two).astype(BF) for one, two in zip(*both))
    return [query_grad, key_grad, value_grad]


def head_sums(value, size):
    head = lax.broadcasted_iota(jnp.int32, (16, value.shape[1]), 1) // size
    pick = (head == lax.broadcasted_iota(jnp.int32, head.shape, 0)).astype(F32).astype(BF)
    high = value.astype(BF)
    return dot_nt(pick, high) + dot_nt(pick, (value - high.astype(F32)).astype(BF))


def attend_pair_backward(query, keys, values, grad, valid, scale):
    rows, _ = query.shape
    sums = [None, None, None]
    for which in range(2):
        query_own, key_own, grad_own = (only(query, which), only(keys, which), only(grad, which))
        scores = dot_nt(keys, query_own)
        if valid < rows:
            key = lax.broadcasted_iota(jnp.int32, scores.shape, 0)
            scores = jnp.where(key < valid, scores, LOWEST)
        top = jnp.max(scores, axis=0, keepdims=True)
        each = jnp.exp(scores - top)
        weights = each * (1.0 / jnp.sum(each, axis=0, keepdims=True))
        weight_grad = dot_nt(values, grad_own)
        value_grad = dot(weights.astype(BF), grad_own)
        inner = jnp.sum(weights * weight_grad, axis=0, keepdims=True)
        score_grad = (weights * (weight_grad - inner)).astype(BF)
        key_grad = dot(score_grad, query_own)
        query_grad = dot_tn(score_grad, key_own) * scale
        parts = (query_grad, key_grad, value_grad)
        sums = [part if one is None else one + part for one, part in zip(sums, parts)]
    return [one.astype(BF) for one in sums]


def project(normed, in_ref, scale):
    wide = in_ref.shape[2]
    query = dot(normed, in_ref[0]).astype(BF) * jnp.asarray(scale, BF)
    keys = dot(normed, in_ref[1]).astype(BF)
    values = dot(normed, in_ref[2]).astype(BF)
    return (query, keys, values, wide)


def turn_rows(ways, count, which, to_ref, from_ref, place_ref):
    rows = to_ref.shape[0]
    pairs = 8 if count is None else 1 << count
    block = rows // (2 * pairs)
    turned = from_ref[...].T
    me = place_ref[1]
    for j in range(2 * pairs):
        if count is None:
            spot = j // 2 + (j % 2) * pairs
        else:
            mask = (me >> 1) ^ (j >> 1)
            order = [k for k in ways(list(range(count)))[which] if k != "mp"]
            spot = sum(((mask >> k) & 1) << (count - 1 - i) for i, k in enumerate(order))
            spot = spot + ((me ^ j) & 1) * pairs
        to_ref[pl.ds(pl.multiple_of(spot * block, 16), block), :] = turned[block * j : block * (j + 1)]


def put_product(keep_ref, send_ref, lead, turned_ref, value, lanes=slice(None)):
    rows = keep_ref.shape[1]
    keep_ref[lead, :, lanes] = dot(turned_ref[:rows], value).astype(BF)
    send_ref[lead, :, lanes] = dot(turned_ref[rows:], value).astype(BF)


def frame_rows(wide_ref, frame, patches):
    at = pl.ds(frame, patches, stride=8)
    return jnp.concatenate([wide_ref[j, at, :] for j in range(wide_ref.shape[0])], axis=1)


def widen(wide_ref, from_ref):
    for j in range(wide_ref.shape[0]):
        value = from_ref[:, :, 128 * j : 128 * (j + 1)].astype(F32)
        wide_ref[j] = value.reshape(wide_ref.shape[1:])


def put_class_rows(to_ref, rows_ref, half):
    seq = to_ref.shape[0] // half
    for f in range(half):
        old = to_ref[f * seq : f * seq + 16, :].astype(F32)
        row = lax.broadcasted_iota(jnp.int32, old.shape, 0)
        new = jnp.where(row == 0, rows_ref[f : f + 1, :].astype(F32), old)
        to_ref[f * seq : f * seq + 16, :] = new.astype(to_ref.dtype)


def class_rows(from_ref, half, dtype, count):
    seq = from_ref.shape[0] // half
    rows = [from_ref[f * seq : f * seq + 16, :].astype(F32)[0:1] for f in range(half)]
    rows.append(jnp.zeros((count - half, from_ref.shape[1]), F32))
    return jnp.concatenate(rows, axis=0).astype(dtype)


def message_forward_kernel(
    heads, place_ref, tok_ref, captions_ref, w_ref, gain_ref, in_ref, out_ref, message_ref, early_ref, qkv_ref, part_ref
):
    cls = tok_ref[0, 0]
    frames, width = cls.shape
    message = dot(cls, w_ref[...])
    message_ref[...] = message
    normal, _ = standardized(message)
    low = (normal * gain_ref[...]).astype(BF)
    size = width // heads
    query, keys, values, wide = project(low, in_ref, size**-0.5)
    contexts = []
    for j in range(wide // (2 * size)):
        at = slice(2 * size * j, 2 * size * (j + 1))
        contexts.append(attend_pair(query[:, at], keys[:, at], values[:, at], frames)[0])
    context = jnp.concatenate(contexts, axis=1).astype(BF)
    part_ref[...] = dot(context, out_ref[...])
    qkv_ref[:, :wide] = query
    qkv_ref[:, wide : 2 * wide] = keys
    qkv_ref[:, 2 * wide :] = values

    def padded(value):
        value = value.astype(F32)
        return jnp.concatenate([value, jnp.zeros((16 - value.shape[0], value.shape[1]), F32)], axis=0)

    early_ref[:, width : 2 * width] = padded(low).astype(BF)
    early_ref[:, 2 * width :] = padded(context).astype(BF)
    embed = captions_ref.shape[1]
    lane = lax.broadcasted_iota(jnp.int32, (1, width - embed), 1)
    ids = jnp.where(lane == 0, place_ref[2], jnp.where(lane == 1, place_ref[3], 0)).astype(F32)
    text = jnp.concatenate([captions_ref[...].astype(F32), ids], axis=1)
    row = lax.broadcasted_iota(jnp.int32, (8, width), 0)
    text = jnp.where(row == 0, text, 0.0)
    early_ref[:, :width] = jnp.concatenate([cls.astype(F32), text], axis=0).astype(BF)


def frame_attention(heads, valid, low, in_ref, qkv_ref, context_ref, logsum_ref):
    size = low.shape[1] // heads
    wide = in_ref.shape[2]
    for k in range(3):
        value = dot(low, in_ref[k]).astype(BF)
        if k == 0:
            value = value * jnp.asarray(size**-0.5, BF)
        qkv_ref[0, :, wide * k : wide * (k + 1)] = value
    lane = lax.broadcasted_iota(jnp.int32, (low.shape[0], 128), 1)
    logsums = jnp.zeros(lane.shape, F32)
    for j in range(wide // (2 * size)):
        query, keys, values = (
            qkv_ref[0, :, wide * k + 2 * size * j : wide * k + 2 * size * (j + 1)] for k in range(3)
        )
        context, sums = attend_pair(query, keys, values, valid)
        context_ref[0, :, 2 * size * j : 2 * size * (j + 1)] = context.astype(BF)
        for which, one in enumerate(sums):
            logsums = jnp.where(lane == 2 * j + which, one, logsums)
    logsum_ref[0] = logsums


def frame_first_kernel(
    heads, half, place_ref, tok_ref, message_ref, part_ref, other_ref, gain_ref, in_ref,
    stream_ref, low_ref, qkv_ref, context_ref, rstd_ref, logsum_ref, wide_ref, rows_ref,
):
    patches, frames, width = tok_ref.shape
    seq = stream_ref.shape[1]
    frame = place_ref[0] * half + pl.program_id(0)

    @pl.when(pl.program_id(0) == 0)
    def _():
        widen(wide_ref, tok_ref)

    at = pl.ds(frame, 1)
    message = message_ref[at, :] + (part_ref[at, :] + other_ref[at, :])
    edge = patches // 8 * 8
    rows_ref[edge:seq, :] = jnp.zeros((seq - edge, width), F32)
    rows_ref[0:patches, :] = frame_rows(wide_ref, frame, patches)
    rows_ref[patches : patches + 1, :] = message
    stream_ref[0] = rows_ref[...].astype(BF)
    normal, rstd = standardized(rows_ref[...])
    rstd_ref[0] = spread(rstd)
    low = (normal * gain_ref[...]).astype(BF)
    low_ref[0] = low
    frame_attention(heads, patches + 1, low, in_ref, qkv_ref, context_ref, logsum_ref)


def joined(place_ref, to_ref, mine_ref, theirs_ref, axis):
    rows = mine_ref.shape[axis]
    core = place_ref[1] & 1
    lead = (slice(None),) * axis
    to_ref[lead + (pl.ds(pl.multiple_of(core * rows, 16), rows),)] = mine_ref[...]
    to_ref[lead + (pl.ds(pl.multiple_of((1 - core) * rows, 16), rows),)] = theirs_ref[...]


def frame_second_kernel(
    heads, valid, place_ref, low_ref, mine_ref, theirs_ref, qkv_ref, context_ref, in_ref, logsum_ref
):
    @pl.when(pl.program_id(0) == 0)
    def _():
        joined(place_ref, in_ref, mine_ref, theirs_ref, 1)

    frame_attention(heads, valid, low_ref[0], in_ref, qkv_ref, context_ref, logsum_ref)


def cotangent_kernel(half, place_ref, cot_ref, down_ref, grad_ref, dact_ref, wide_ref):
    patches, frames, width = cot_ref.shape
    seq = grad_ref.shape[0] // half

    @pl.when(pl.program_id(0) == 0)
    def _():
        widen(wide_ref, cot_ref)
        edge = patches // 16 * 16
        for f in range(half):
            value = frame_rows(wide_ref, place_ref[0] * half + f, patches)
            tail = jnp.concatenate([value[edge:], jnp.zeros((seq - patches, width), F32)], axis=0)
            grad_ref[f * seq : f * seq + edge, :] = value[:edge].astype(BF)
            grad_ref[f * seq + edge : (f + 1) * seq, :] = tail.astype(BF)

    dact_ref[...] = dot_nt(grad_ref[...], down_ref[...]).astype(BF)


def gate(hidden):
    sigmo = 1.0 / (1.0 + jnp.exp(-1.702 * hidden))
    gated = hidden * sigmo
    return (gated, sigmo + 1.702 * gated * (1.0 - sigmo))


def up_block(ref):
    return ref[...].reshape(ref.shape[0] * ref.shape[1], ref.shape[2])


def mlp_first_kernel(
    half, stream_ref, own_ref, other_ref, out_own_ref, out_other_ref, gain_ref, up_ref, down_ref, dact_ref,
    rstd_ref, low_ref, activ_ref, dhid_ref, slope_ref, total_ref, back_ref, cls_low_ref, cls_total_ref,
):
    step = pl.program_id(0)

    @pl.when(step == 0)
    def _():
        branch = dot(own_ref[...], out_own_ref[...]) + dot(other_ref[...], out_other_ref[...])
        middle = stream_ref[...].astype(F32) + branch
        normal, rstd = standardized(middle)
        rstd_ref[...] = spread(rstd)
        low_ref[...] = (normal * gain_ref[...]).astype(BF)
        total_ref[...] = middle
        back_ref[...] = jnp.zeros_like(back_ref)
        cls_low_ref[...] = class_rows(low_ref, half, BF, 16)

    seq = low_ref.shape[0] // half
    activ, slope = gate(dot(low_ref[...], up_ref[...]))
    activ_ref[...] = activ.astype(BF)
    dhid_ref[...] = (dact_ref[...].astype(F32) * slope).astype(BF)
    rows = [slope[f * seq : f * seq + 1] for f in range(half)]
    slope_ref[...] = jnp.concatenate(rows + [jnp.zeros((16 - half, slope.shape[1]), F32)], axis=0)
    total_ref[...] += dot(activ_ref[...], down_ref[...])
    back_ref[...] += dot_nt(dhid_ref[...], up_ref[...])

    @pl.when(step == pl.num_programs(0) - 1)
    def _():
        cls_total_ref[...] = class_rows(total_ref, half, F32, 16)


def class_forward_kernel(half, low_ref, start_ref, up_ref, down_ref, pooled_ref, total_ref):
    step = pl.program_id(0)

    @pl.when(step == 0)
    def _():
        total_ref[...] = start_ref[...]

    activ, _ = gate(dot(low_ref[...], up_block(up_ref)))
    total_ref[...] += dot(activ.astype(BF), up_block(down_ref))

    @pl.when(step == pl.num_programs(0) - 1)
    def _():
        pooled_ref[...] = jnp.sum(total_ref[0:half, :], axis=0, keepdims=True)


def mlp_second_kernel(half, start_ref, low_ref, up_ref, down_ref, activ_ref, slope_ref, total_ref):
    @pl.when(pl.program_id(0) == 0)
    def _():
        total_ref[...] = start_ref[...]

    activ, slope = gate(dot(low_ref[...], up_block(up_ref)))
    activ_ref[...] = activ.astype(BF)
    slope_ref[...] = slope.astype(BF)
    total_ref[...] += dot(activ_ref[...], up_block(down_ref))


def mlp_third_kernel(half, start_ref, low_ref, up_ref, down_ref, _, __, activ_ref, slope_ref, result_ref, total_ref):
    mlp_second_kernel(half, start_ref, low_ref, up_ref, down_ref, activ_ref, slope_ref, total_ref)

    @pl.when(pl.program_id(0) == pl.num_programs(0) - 1)
    def _():
        result_ref[...] = total_ref[...].astype(BF)


def hidden_backward_kernel(start_ref, grad_ref, slope_ref, up_ref, down_ref, *refs):
    dhid_ref, back_ref = refs[-2:]

    @pl.when(pl.program_id(0) == 0)
    def _():
        back_ref[...] = start_ref[...]

    dact = dot_nt(grad_ref[...], up_block(down_ref))
    dhid_ref[...] = (dact * slope_ref[...].astype(F32)).astype(BF)
    back_ref[...] += dot_nt(dhid_ref[...], up_block(up_ref))


def loss_kernel(
    order, frames, place_ref, early_ref, proj_ref,
    loss_ref, caption_grad_ref, embed_grad_ref, pooled_all_ref, pooled_grad_ref,
):
    clips = early_ref.shape[0]
    width, wide = proj_ref.shape
    me = place_ref[1]
    early = early_ref[...].astype(F32)[:, frames, :].astype(BF)
    block = lax.broadcasted_iota(jnp.int32, (clips, clips), 1)
    mask = jnp.zeros_like(block)
    for k, bit in enumerate(order):
        mask = mask + ((block >> k) & 1) * bit
    row = lax.broadcasted_iota(jnp.int32, (clips, clips), 0)
    pick = (row == jnp.bitwise_xor(mask, me)).astype(F32).astype(BF)
    text = dot(pick, early[:, :width]).astype(BF)
    pooled = dot(pick, early[:, width : 2 * width]).astype(BF)
    pooled_all_ref[...] = pooled
    embed = dot(pooled, proj_ref[...])
    embed_rinv = lax.rsqrt(jnp.sum(embed * embed, axis=-1, keepdims=True) + 1e-06)
    embed_low = (embed * embed_rinv).astype(BF)
    caption_f = text[:, :wide].astype(F32)
    caption_rinv = lax.rsqrt(jnp.sum(caption_f * caption_f, axis=-1, keepdims=True) + 1e-06)
    caption_low = (caption_f * caption_rinv).astype(BF)
    scores = SHARPNESS * dot_nt(embed_low, caption_low)
    lane = lax.broadcasted_iota(jnp.int32, (8, text.shape[1] - wide), 1)
    pick_id = (lane == 1).astype(F32).astype(BF)
    caption_ids = dot_nt(pick_id, text[:, wide:])[0:1, :]
    clip_ids = text[:, wide:].astype(F32)[:, 0:1]
    positive = clip_ids == caption_ids
    masked = jnp.where(positive, scores, LOWEST)

    def side(axis):
        top = jnp.max(scores, axis=axis, keepdims=True)
        each = jnp.exp(scores - top)
        total = jnp.sum(each, axis=axis, keepdims=True)
        pos_top = jnp.max(masked, axis=axis, keepdims=True)
        pos_each = jnp.where(positive, jnp.exp(masked - pos_top), 0.0)
        pos_total = jnp.sum(pos_each, axis=axis, keepdims=True)
        part = jnp.sum(top + jnp.log(total) - pos_top - jnp.log(pos_total), axis=1 - axis, keepdims=True)
        return (part, each / total - pos_each / pos_total)

    row_loss, row_grad = side(1)
    column_loss, column_grad = side(0)
    loss_ref[...] = 0.5 * (row_loss + column_loss)
    dscore = 0.5 * (row_grad + column_grad)
    embed_grad = SHARPNESS * dot(dscore.astype(BF), caption_low)
    caps_grad = SHARPNESS * dot_tn(dscore.astype(BF), embed_low)
    caption_grad = caption_rinv * caps_grad - caption_f * (
        caption_rinv * caption_rinv * caption_rinv * jnp.sum(caption_f * caps_grad, axis=-1, keepdims=True)
    )
    embed_diff = embed_rinv * embed_grad - embed * (
        embed_rinv * embed_rinv * embed_rinv * jnp.sum(embed * embed_grad, axis=-1, keepdims=True)
    )
    embed_diff = embed_diff.astype(BF)
    embed_grad_ref[...] = embed_diff
    grads = dot_nt(embed_diff, proj_ref[...])

    def own_row(value):
        own = lax.broadcasted_iota(jnp.int32, value.shape, 0) == me
        return jnp.sum(jnp.where(own, value, 0.0), axis=0, keepdims=True)

    caption_grad_ref[...] = own_row(caption_grad)
    pooled_grad_ref[...] = own_row(grads) / frames


def class_backward_kernel(
    half, place_ref, cot_ref, pooled_ref, slope_own_ref, slope_other_ref, up_own_ref, down_own_ref, up_ref, down_ref,
    grad_ref, dhid_own_ref, dhid_other_ref, back_ref,
):
    @pl.when(pl.program_id(0) == 0)
    def _():
        cot = cot_ref[0, 0].astype(F32)
        cot = jnp.where(place_ref[0] == 0, cot[:half], cot[half:]) + pooled_ref[...]
        grad_ref[...] = jnp.concatenate([cot, jnp.zeros((16 - half, cot.shape[1]), F32)], axis=0).astype(BF)
        back_ref[...] = jnp.zeros_like(back_ref)

    grad = grad_ref[...]
    dhid_own_ref[...] = (dot_nt(grad, down_own_ref[...]) * slope_own_ref[...]).astype(BF)
    dhid_other_ref[...] = (dot_nt(grad, up_block(down_ref)) * slope_other_ref[...]).astype(BF)
    back_ref[...] += dot_nt(dhid_own_ref[...], up_own_ref[...]) + dot_nt(dhid_other_ref[...], up_block(up_ref))


def mlp_weight_kernel(
    half, count, place_ref, grad_ref, grad_cls_ref, low_ref, activ_own_ref, dhid_own_ref, dhid_cls_own_ref,
    activ_other_ref, dhid_other_ref, dhid_cls_other_ref,
    keep_own_ref, send_own_ref, keep_other_ref, send_other_ref, grad_t_ref, low_t_ref, fixed_ref, rows_ref,
):
    step = pl.program_id(0)
    steps = pl.num_programs(0) // 2

    @pl.when(step == 0)
    def _():
        rows_ref[...] = grad_ref[...]
        put_class_rows(rows_ref, grad_cls_ref, half)
        turn_rows(mlp_ways, count, 0, low_t_ref, low_ref, place_ref)
        turn_rows(mlp_ways, count, 1, grad_t_ref, rows_ref, place_ref)

    def part(activ_ref, dhid_ref, dhid_cls_ref, keep_ref, send_ref):
        fixed_ref[...] = dhid_ref[...]
        put_class_rows(fixed_ref, dhid_cls_ref, half)
        put_product(keep_ref, send_ref, 0, low_t_ref, fixed_ref[...])
        put_product(keep_ref, send_ref, 1, grad_t_ref, activ_ref[...])

    @pl.when(step < steps)
    def _():
        part(activ_other_ref, dhid_other_ref, dhid_cls_other_ref, keep_other_ref, send_other_ref)

    @pl.when(step >= steps)
    def _():
        part(activ_own_ref, dhid_own_ref, dhid_cls_own_ref, keep_own_ref, send_own_ref)


def frame_backward_kernel(
    heads, valid, half, first, back_ref, grad_in_ref, mid_ref, mid_rstd_ref, own_ref, other_ref, low_in_ref, rstd_ref,
    context_own_ref, context_other_ref, logsum_own_ref, logsum_other_ref,
    back_cls_ref, grad_cls_ref, mlp_gain_ref, gain_ref, out_own_ref, out_other_ref, in_own_ref, in_other_ref, *refs,
):
    low_ref, down_ref, dother_ref, token_ref, edge_ref = refs[-5:]
    step = pl.program_id(0)
    f = first + step
    width = back_ref.shape[1]
    size = width // heads
    scale = size**-0.5
    row = lax.broadcasted_iota(jnp.int32, back_ref.shape, 0)
    at = pl.ds(f, 1)
    back = jnp.where(row == 0, back_cls_ref[at, :], back_ref[...])
    cls = jnp.zeros((1, width), F32)
    for k in range(half):
        cls = jnp.where(f == k, grad_cls_ref[...].astype(F32)[k : k + 1], cls)
    grad = jnp.where(row == 0, cls, grad_in_ref[...].astype(F32))
    normal = mid_ref[...].astype(F32) * (1.0 / mlp_gain_ref[...])
    part, mlp_gain_grad = norm_backward(back, mlp_gain_ref[...], normal, mid_rstd_ref[:, 0:1])
    grad = grad + part
    low = grad.astype(BF)
    low_ref[0] = low
    normed_grad = None
    for qkv_ref, context_ref, logsum_ref, out_ref, in_ref, to_ref in (
        (own_ref, context_own_ref, logsum_own_ref, out_own_ref, in_own_ref, down_ref),
        (other_ref, context_other_ref, logsum_other_ref, out_other_ref, in_other_ref, dother_ref),
    ):
        wide = in_ref.shape[2]
        context_grad = dot_nt(low, out_ref[...]).astype(BF)
        inners = head_sums(context_grad.astype(F32) * context_ref[0].astype(F32), size)
        logsums = logsum_ref[0].T
        for j in range(wide // (2 * size)):
            query, keys, values = (
                qkv_ref[0, :, wide * k + 2 * size * j : wide * k + 2 * size * (j + 1)] for k in range(3)
            )
            grads = attend_pair_kept(
                query,
                keys,
                values,
                context_grad[:, 2 * size * j : 2 * size * (j + 1)],
                [logsums[2 * j + which : 2 * j + which + 1] for which in range(2)],
                [inners[2 * j + which : 2 * j + which + 1] for which in range(2)],
                valid,
                scale,
            )
            for k in range(3):
                to_ref[0, :, wide * k + 2 * size * j : wide * k + 2 * size * (j + 1)] = grads[k]
        for k in range(3):
            part = dot_nt(to_ref[0, :, wide * k : wide * (k + 1)], in_ref[k])
            normed_grad = part if normed_grad is None else normed_grad + part
    normal = low_in_ref[0].astype(F32) * (1.0 / gain_ref[...])
    part, gain_grad = norm_backward(normed_grad, gain_ref[...], normal, rstd_ref[0, :, 0:1])
    total = grad + part
    token_ref[0] = total.astype(BF)

    @pl.when(step == 0)
    def _():
        if first == 0:
            edge_ref[...] = jnp.zeros_like(edge_ref)
        else:
            edge_ref[...] = refs[3][...]

    edge_ref[pl.ds(f, 1), :] = total[0:1]
    edge_ref[pl.ds(half + f, 1), :] = total[valid - 1 : valid]
    edge_ref[2 * half : 2 * half + 1, :] += gain_grad
    edge_ref[2 * half + 1 : 2 * half + 2, :] += mlp_gain_grad


def frame_weight_kernel(
    count, place_ref, low_ref, grad_ref, down_ref, dother_ref, own_ref, other_ref,
    keep_own_ref, send_own_ref, keep_other_ref, send_other_ref, low_t_ref, grad_t_ref,
):
    step = pl.program_id(0)

    @pl.when(step == 0)
    def _():
        turn_rows(frame_ways, count, 0, low_t_ref, low_ref, place_ref)
        turn_rows(frame_ways, count, 0, grad_t_ref, grad_ref, place_ref)

    wide = own_ref.shape[1]
    for first, dqkv_ref, context_ref, keep_ref, send_ref in (
        (0, dother_ref, other_ref, keep_other_ref, send_other_ref),
        (2, down_ref, own_ref, keep_own_ref, send_own_ref),
    ):

        @pl.when(step == first)
        def _(dqkv_ref=dqkv_ref, keep_ref=keep_ref, send_ref=send_ref):
            put_product(keep_ref, send_ref, 0, low_t_ref, dqkv_ref[...])

        @pl.when(step == first + 1)
        def _(dqkv_ref=dqkv_ref, context_ref=context_ref, keep_ref=keep_ref, send_ref=send_ref):
            put_product(keep_ref, send_ref, 0, low_t_ref, dqkv_ref[:, :wide], slice(0, wide))
            put_product(keep_ref, send_ref, 0, grad_t_ref, context_ref[...], slice(wide, 2 * wide))


def both_halves(place, own, other):
    return jnp.concatenate(
        [jnp.where(place == 0, own, other), jnp.where(place == 0, other, own)], axis=0
    )


def message_backward_kernel(
    heads, place_ref, own_ref, other_ref, qkv_ref, out_ref, in_ref, next_ref, low_ref, dqkv_ref, part_ref
):
    frames, width = next_ref.shape
    half = frames // 2
    at = slice(half, 2 * half)
    grad = both_halves(place_ref[0], own_ref[at, :], other_ref[at, :])
    next_ref[...] = grad
    low = grad.astype(BF)
    low_ref[...] = low
    size = width // heads
    scale = size**-0.5
    wide = in_ref.shape[2]
    context_grad = dot_nt(low, out_ref[...]).astype(BF)
    for j in range(wide // (2 * size)):
        query, keys, values = (
            qkv_ref[:, wide * k + 2 * size * j : wide * k + 2 * size * (j + 1)] for k in range(3)
        )
        grads = attend_pair_backward(
            query, keys, values, context_grad[:, 2 * size * j : 2 * size * (j + 1)], frames, scale
        )
        for k in range(3):
            dqkv_ref[:, wide * k + 2 * size * j : wide * k + 2 * size * (j + 1)] = grads[k]
    total = None
    for k in range(3):
        part = dot_nt(dqkv_ref[:, wide * k : wide * (k + 1)], in_ref[k])
        total = part if total is None else total + part
    part_ref[...] = total


def message_last_kernel(
    place_ref, own_ref, other_ref, next_ref, low_ref, dqkv_ref, part_ref, part_other_ref, message_ref, gain_ref, w_ref,
    late_ref, cls_ref,
):
    frames, width = next_ref.shape
    half = frames // 2
    normal, rstd = standardized(message_ref[...])
    part, gain_grad = norm_backward(part_ref[...] + part_other_ref[...], gain_ref[...], normal, rstd)
    message_low = (next_ref[...] + part).astype(BF)
    cls = both_halves(place_ref[0], own_ref[0:half, :], other_ref[0:half, :])
    cls_ref[...] = (cls + dot_nt(message_low, w_ref[...])).astype(BF)
    wide = dqkv_ref.shape[1]
    late_ref[0:frames, 0:width] = low_ref[...]
    late_ref[0:frames, width : 2 * width] = message_low
    late_ref[0:frames, 2 * width : 2 * width + wide] = dqkv_ref[...]
    both = own_ref[2 * half : 2 * half + 2, :] + other_ref[2 * half : 2 * half + 2, :]
    gains = jnp.concatenate([both[1:2], both[0:1], gain_grad], axis=1)
    room = late_ref.shape[1] - 2 * width - wide
    gains = jnp.concatenate([gains, jnp.zeros((1, frames * room - 3 * width), F32)], axis=1)
    gains = jnp.concatenate([gains[:, room * r : room * (r + 1)] for r in range(frames)], axis=0)
    late_ref[:, 2 * width + wide :] = gains.astype(BF)


def assemble_kernel(pieces, place_ref, *refs):
    out_ref, wide_ref = refs[-2:]
    tile, frames, width = out_ref.shape
    half = frames // 2
    for side in range(2):
        mp = place_ref[0] if side == 0 else 1 - place_ref[0]
        for k in range(half):
            per = half // pieces
            value = refs[side * pieces + k // per][k % per].astype(F32)
            for j in range(width // 128):
                wide_ref[j, pl.ds(mp * half + k, tile, stride=8), :] = value[:, 128 * j : 128 * (j + 1)]
    for j in range(width // 128):
        out_ref[:, :, 128 * j : 128 * (j + 1)] = wide_ref[j].reshape(tile, frames, 128).astype(BF)
    if len(refs) > 2 * pieces + 2:

        @pl.when(pl.program_id(0) == 0)
        def _():
            out_ref[0] = refs[2 * pieces][...]


def factor_kernel(
    frames, place_ref, early_ref, late_ref, pooled_ref, embed_ref,
    weight_ref, in_ref, out_ref, proj_ref, gains_ref,
):
    size = early_ref.shape[0]
    share, width = weight_ref.shape
    wide = out_ref.shape[1]
    column = lax.broadcasted_iota(jnp.int32, (share, width), 1)
    row = lax.broadcasted_iota(jnp.int32, (share, width), 0)
    pick = (column == place_ref[1] * share + row).astype(F32).astype(BF)

    def early(first, wide):
        value = early_ref[:, :, first : first + wide].astype(F32)[:, :frames]
        return value.reshape(size * frames, wide).astype(BF)

    def late(first, wide):
        return late_ref[:, :, first : first + wide].astype(F32).reshape(size * frames, wide).astype(BF)

    def own(value):
        return dot_nt(pick, value).astype(BF)

    weight_ref[...] = dot(own(early(0, width)), late(width, width))
    product = dot(own(early(width, width)), late(2 * width, 3 * wide))
    for k in range(3):
        in_ref[k] = product[:, wide * k : wide * (k + 1)]
    out_ref[...] = dot(own(late(0, width)), early(2 * width, wide))
    proj_ref[...] = dot(own(pooled_ref[...]), embed_ref[...])
    room = late_ref.shape[2] - 2 * width - 3 * wide
    gains = jnp.sum(late_ref[:, :, 2 * width + 3 * wide :].astype(F32), axis=0)
    gains = jnp.concatenate([gains[r : r + 1, :] for r in range(frames)], axis=1)
    for k in range(3):
        gains_ref[k : k + 1, :] = gains[:, width * k : width * (k + 1)]


def whole(shape):
    return pl.BlockSpec(tuple(shape), lambda *_: (0,) * len(shape))


def run(kernel, name, args, outs, grid=(1,), prefetch=0, specs=None, out_specs=None, scratch=(), aliases=None, deps=(), cost=2):
    specs = specs or {}
    out_specs = out_specs or {}
    tensors = args[prefetch:]
    taken = len(args)

    def body(*refs):
        kernel(*refs[:taken], *refs[taken + len(deps) :])

    return pl.pallas_call(
        body,
        out_shape=list(outs),
        grid_spec=pltpu.PrefetchScalarGridSpec(
            num_scalar_prefetch=prefetch,
            grid=grid,
            in_specs=[specs.get(k, whole(t.shape)) for k, t in enumerate(tensors)]
            + [pl.BlockSpec(memory_space=pl.ANY)] * len(deps),
            out_specs=[out_specs.get(k, whole(o.shape)) for k, o in enumerate(outs)],
            scratch_shapes=list(scratch),
        ),
        compiler_params=pltpu.CompilerParams(
            dimension_semantics=("arbitrary",) * len(grid), vmem_limit_bytes=KERNEL_MIB.get(name, 16) * 1024 * 1024
        ),
        cost_estimate=pl.CostEstimate(flops=round(KERNEL_US.get(name, cost) * 2.3e9), bytes_accessed=0, transcendentals=0),
        input_output_aliases={prefetch + k: out for k, out in (aliases or {}).items()},
        name=name,
    )(*args, *deps)


def shape_of(shape, dtype):
    return jax.ShapeDtypeStruct(tuple(shape), dtype)


def plus(a, b, dtype=BF):
    return (a.astype(F32) + b.astype(F32)).astype(dtype)


def reorder(ways, keep, send):
    size = lax.axis_size("dp")
    bits = bits_of(size)
    lead, rows, wide = keep.shape
    block = 2 * rows // 16
    value = jnp.stack([keep.reshape(lead, 8, block, wide), send.reshape(lead, 8, block, wide)], axis=2)
    value = value.reshape(lead, size, 2 * rows // size, wide)
    turned = []
    for one, order in zip(value, ways(bits[1:])):
        order = [bit for bit in order if bit != "mp"]
        order = jnp.bitwise_xor(jnp.asarray(row_order(bits[:1] + order), jnp.int32), lax.axis_index("dp"))
        turned.append(jnp.take(one, order, axis=0).reshape(2 * rows, wide))
    value = jnp.stack(turned)
    return (value[:, :rows], value[:, rows:])


def joint(ways):
    return ways[0] == ways[1] and ways[0] not in (None, "mp")


def stage_values(keep_first, keep_second, *got):
    parts = keep_first.shape[0]
    came = (got[0][:parts], got[0][parts:]) if len(got) == 1 else (got[0][...], got[1][...])
    return [keep[...].astype(F32) + one.astype(F32) for keep, one in zip((keep_first, keep_second), came)]


def stage_kernel(ways, came, *refs):
    values = stage_values(*refs[: 2 + came])
    refs = refs[2 + came :]
    if joint(ways):
        at = 0
        for k, value in enumerate(values):
            parts, rows, _ = value.shape
            refs[k][...] = value[:, : rows // 2].astype(BF)
            refs[2][at : at + parts] = value[:, rows // 2 :].astype(BF)
            at += parts
        return
    per = len(refs) // 2
    for k, (value, way) in enumerate(zip(values, ways)):
        keep, send = (refs[per * k], refs[per * (k + 1) - 1])
        if way is None:
            keep[...] = value
        elif way == "mp":
            keep[...] = value[0:1].astype(BF)
            send[...] = value[1:2].astype(BF)
        else:
            rows = value.shape[1] // 2
            keep[...] = value[:, :rows].astype(BF)
            send[...] = value[:, rows:].astype(BF)


def frame_final_kernel(keep_first, keep_second, got, in_ref, out_ref):
    first, second = stage_values(keep_first, keep_second, got)
    wide = out_ref.shape[1]
    in_ref[0] = first[0][:, :wide]
    in_ref[1] = first[0][:, wide:]
    in_ref[2] = second[0][:, :wide]
    out_ref[...] = second[0][:, wide:]


def core_stage_kernel(ways, keep_own, got_own, keep_other, got_other, *refs):
    for k in range(2):
        parts = [
            keep[k : k + 1].astype(F32) + got[k : k + 1].astype(F32)
            for keep, got in ((keep_own, got_own), (keep_other, got_other))
        ]
        for part, at in zip(parts, range(2)):
            if ways[k] == "mp":
                refs[2 * k + at][...] = part.astype(BF)
                continue
            rows = part.shape[1] // 2
            refs[2 * k][at : at + 1] = part[:, :rows].astype(BF)
            refs[2 * k + 1][at : at + 1] = part[:, rows:].astype(BF)


class Reduction:
    def __init__(self, name, ways, keep_own, send_own, keep_other, send_other):
        size = lax.axis_size("dp")
        self.name = name
        self.bits = bits_of(size)
        self.aligned = (2 * keep_own.shape[1] // size) % 16 == 0
        if not self.aligned:
            keep_own, send_own = reorder(ways, keep_own, send_own)
            keep_other, send_other = reorder(ways, keep_other, send_other)
        self.ways = ways(self.bits[1:])
        self.steps = len(self.ways[0])
        self.at = 0
        self.keep = (keep_own, keep_other)
        self.got = tuple(flip(send, self.bits[0]) for send in (send_own, send_other))

    def ways_at(self, at):
        return tuple(ways[at] if at < self.steps else None for ways in self.ways)

    def outs(self, shapes, ways):
        made = []
        if joint(ways):
            parts = [shape[0] for shape in shapes]
            _, rows, wide = shapes[0]
            return [shape_of((count, rows // 2, wide), BF) for count in parts + [sum(parts)]]
        for (parts, rows, wide), way in zip(shapes, ways):
            if way is None:
                made.append(shape_of((parts, rows, wide), F32))
            elif way == "mp":
                made += [shape_of((1, rows, wide), BF)] * 2
            else:
                made += [shape_of((parts, rows // 2, wide), BF)] * 2
        return made

    def call(self, kernel, args, shapes, ways, deps, cost):
        if not self.aligned:
            refs = [Box(out) for out in self.outs(shapes, ways)]
            kernel(ways, *args, *refs)
            return [ref.value for ref in refs]
        made = self.outs(shapes, ways)
        wide = made[0].shape[2]
        chunk = 384

        def spec(value):
            return pl.BlockSpec(value.shape[:2] + (chunk,), lambda j, *_: (0, 0, j))

        return run(
            functools.partial(kernel, ways),
            self.name + str(self.at),
            args,
            made,
            grid=(wide // chunk,),
            specs={k: spec(value) for k, value in enumerate(args)},
            out_specs={k: spec(value) for k, value in enumerate(made)},
            deps=deps,
            cost=cost,
        )

    def take(self, made):
        self.joined = made[2:] if len(made) == 3 else []
        per = (len(made) - len(self.joined)) // 2
        self.value = [made[per * k : per * (k + 1)] for k in range(2)]

    def cores(self, *deps, cost=0):
        own, other = self.keep
        _, rows, wide = own.shape
        args = (own, self.got[0], other, self.got[1])
        self.take(self.call(core_stage_kernel, args, [(2, rows, wide)] * 2, self.ways_at(0), deps, cost))
        self.at = 0
        self.send()

    def send(self):
        ways = self.ways_at(self.at)
        if self.joined:
            self.got = [flip(self.joined[0], ways[0])]
            return
        self.got = []
        for (_, send), way in zip(self.value, ways):
            self.got.append(swap(send) if way == "mp" else flip(send, way))

    def ready(self):
        return tuple(one for values in self.value for one in values)

    def parts(self):
        return (self.value[0][0], self.value[1][0], *self.got)

    def step(self, *deps, cost=0):
        args = self.parts()
        shapes = [value[0].shape for value in self.value]
        self.at += 1
        kernel = lambda ways, *refs: stage_kernel(ways, len(args) - 2, *refs)
        self.take(self.call(kernel, args, shapes, self.ways_at(self.at), deps, cost))
        if self.at < self.steps:
            self.send()


class Box:
    def __init__(self, out):
        self.value = jnp.zeros(out.shape, out.dtype)

    def __setitem__(self, at, value):
        self.value = value if at is Ellipsis else self.value.at[at].set(value)


def on_device(
    tokens,
    captions,
    clip_groups,
    caption_groups,
    msg_weight,
    msg_gain,
    msg_in,
    msg_out,
    frame_gain,
    frame_in,
    frame_out,
    mlp_gain,
    up_weight,
    down_weight,
    proj_weight,
    out_cot,
):
    clips, frames, patches, width = tokens.shape
    assert clips == 1 and frames == 8 and lax.axis_size("mp") == 2
    size = lax.axis_size("dp")
    valid = patches + 1
    seq = -(-valid // 16) * 16
    half = frames // 2
    rows = half * seq
    share = width // size
    aligned = share % 16 == 0
    count = len(bits_of(size)) - 1 if aligned else None
    h_half = frame_in.shape[2]
    f_half = up_weight.shape[1]
    embed = proj_weight.shape[1]
    me_dp, me_mp = (lax.axis_index("dp"), lax.axis_index("mp"))
    place = jnp.stack([me_mp, me_dp, clip_groups[0], caption_groups[0]]).astype(jnp.int32)
    msg_gain, frame_gain, mlp_gain = (gain.reshape(1, width) for gain in (msg_gain, frame_gain, mlp_gain))
    tokens_t, cot_t = (jnp.transpose(value, (0, 2, 1, 3)) for value in (tokens, out_cot))
    class_spec = pl.BlockSpec((1, 1, frames, width), lambda *_: (0, 0, 0, 0))

    def mine(value, axis=1):
        return lax.dynamic_slice_in_dim(value, me_dp * share, share, axis)

    devices = size if aligned else 16
    each = width // devices

    def packed(up, down):
        up = up.reshape(-1, each, f_half // width, width).transpose(0, 2, 1, 3).reshape(-1, f_half // devices, width)
        return jnp.concatenate([up, down.reshape(-1, f_half // devices, width)], axis=1)

    if aligned:
        down_share = lax.dynamic_slice_in_dim(down_weight, me_dp * (f_half // size), f_half // size, 0)
        mlp_share = swap(packed(mine(up_weight, 0), down_share))
    else:
        mlp_other = packed(swap(up_weight), swap(down_weight))

    message, early, msg_qkv, msg_part = run(
        functools.partial(message_forward_kernel, HEADS),
        "message_forward",
        (place, tokens_t, captions, msg_weight, msg_gain, msg_in, msg_out),
        (
            shape_of((frames, width), F32),
            shape_of((16, 2 * width + h_half), BF),
            shape_of((frames, 3 * h_half), BF),
            shape_of((frames, width), F32),
        ),
        prefetch=1,
        specs={0: class_spec},
    )
    msg_other = swap(msg_part)
    if aligned:
        mlp_other = lax.all_gather(after(mlp_share, msg_part), "dp", axis=0, tiled=True)

    def half_rows(value, axis):
        rows_half = value.shape[axis] // 2
        return lax.dynamic_slice_in_dim(value, (me_dp % 2) * rows_half, rows_half, axis)

    in_mine = swap(after(half_rows(frame_in, 1), msg_part))

    one_frame = lambda wide, first=0: pl.BlockSpec((1, seq, wide), lambda f, *_: (f + first, 0, 0))
    whole_wide = pltpu.VMEM((width // 128, patches * frames, 128), F32)
    chunk = 512
    grad, dact_own = run(
        functools.partial(cotangent_kernel, half),
        "cotangent",
        (place, cot_t.reshape(patches, frames, width), down_weight),
        (shape_of((rows, width), BF), shape_of((rows, f_half), BF)),
        grid=(f_half // chunk,),
        prefetch=1,
        specs={1: pl.BlockSpec((chunk, width), lambda j, *_: (j, 0))},
        out_specs={1: pl.BlockSpec((rows, chunk), lambda j, *_: (0, j))},
        scratch=[whole_wide],
        deps=(msg_part,),
    )
    stream, frame_low, qkv_own, context_own, frame_rstd, logsum_own = run(
        functools.partial(frame_first_kernel, HEADS, half),
        "frame_first",
        (place, tokens_t.reshape(patches, frames, width), message, msg_part, msg_other, frame_gain, frame_in),
        (
            shape_of((half, seq, width), BF),
            shape_of((half, seq, width), BF),
            shape_of((half, seq, 3 * h_half), BF),
            shape_of((half, seq, h_half), BF),
            shape_of((half, seq, 128), F32),
            shape_of((half, seq, 128), F32),
        ),
        grid=(half,),
        prefetch=1,
        out_specs={
            0: one_frame(width),
            1: one_frame(width),
            2: one_frame(3 * h_half),
            3: one_frame(h_half),
            4: one_frame(128),
            5: one_frame(128),
        },
        scratch=[whole_wide, pltpu.VMEM((seq, width), F32)],
        deps=(grad,),
    )
    in_theirs = flip(after(in_mine, stream), 1)
    out_other = swap(after(frame_out, grad))
    bits = gather_bits()

    def hop(value, k, *deps):
        return jnp.concatenate([value, after(flip(value, bits[k]), *deps)], axis=0)

    qkv_other, context_other, in_other, logsum_other = run(
        functools.partial(frame_second_kernel, HEADS, valid),
        "frame_second",
        (place, frame_low, in_mine, in_theirs),
        (
            shape_of((half, seq, 3 * h_half), BF),
            shape_of((half, seq, h_half), BF),
            shape_of(frame_in.shape, BF),
            shape_of((half, seq, 128), F32),
        ),
        grid=(half,),
        prefetch=1,
        specs={0: one_frame(width)},
        out_specs={0: one_frame(3 * h_half), 1: one_frame(h_half), 3: one_frame(128)},
    )

    steps = f_half // chunk
    up_spec = pl.BlockSpec((width, chunk), lambda j, *_: (0, j))
    down_spec = pl.BlockSpec((chunk, width), lambda j, *_: (j, 0))
    unit_spec = pl.BlockSpec((rows, chunk), lambda j, *_: (0, j))
    units = shape_of((rows, f_half), BF)
    wide_rows = shape_of((rows, width), F32)
    context_own2, context_other2 = (v.reshape(rows, h_half) for v in (context_own, context_other))
    (
        mlp_rstd, mlp_low, activ_own, dhid_own, slope_cls_own, total, back, cls_low, cls_total,
    ) = run(
        functools.partial(mlp_first_kernel, half),
        "mlp_first",
        (
            stream.reshape(rows, width), context_own2, context_other2, frame_out, out_other, mlp_gain,
            up_weight, down_weight, dact_own,
        ),
        (
            shape_of((rows, 128), F32), shape_of((rows, width), BF), units, units, shape_of((16, f_half), F32), wide_rows,
            wide_rows,
            shape_of((16, width), BF), shape_of((16, width), F32),
        ),
        grid=(steps,),
        specs={6: up_spec, 7: down_spec, 8: unit_spec},
        out_specs={2: unit_spec, 3: unit_spec, 4: pl.BlockSpec((16, chunk), lambda j, *_: (0, j))},
    )

    part = f_half // 4
    per = width // part

    def up_other_spec(first):
        return pl.BlockSpec((devices, each, part), lambda j, *_: (0, (j + first) // per, (j + first) % per))

    def down_other_spec(first):
        return pl.BlockSpec((devices // 4, f_half // devices, width), lambda j, *_: (j + first, 1, 0))

    def part_spec(first=0):
        return pl.BlockSpec((rows, part), lambda j, *_: (0, j + first))

    (pooled_part,) = run(
        functools.partial(class_forward_kernel, half),
        "class_forward",
        (cls_low, cls_total, mlp_other, mlp_other),
        (shape_of((1, width), F32),),
        grid=(4,),
        specs={2: up_other_spec(0), 3: down_other_spec(0)},
        scratch=[pltpu.VMEM((16, width), F32)],
    )
    pooled_low = ((pooled_part + swap(pooled_part)) / frames).astype(BF)
    stages = [early.at[frames : frames + 1, width : 2 * width].set(pooled_low)[None]]
    for k in range(len(bits)):
        stages.append(hop(stages[-1], k))
    early_all = stages[-1]
    anywhere = pl.BlockSpec(memory_space=pl.ANY)
    activ_2, slope_2, total = run(
        functools.partial(mlp_second_kernel, half),
        "mlp_second",
        (total, mlp_low, mlp_other, mlp_other),
        (units, units, wide_rows),
        grid=(2,),
        specs={2: up_other_spec(0), 3: down_other_spec(0)},
        out_specs={0: part_spec(), 1: part_spec()},
        deps=(stages[0],),
    )
    activ_other, slope_other, result_own = run(
        functools.partial(mlp_third_kernel, half),
        "mlp_third",
        (total, mlp_low, mlp_other, mlp_other, activ_2, slope_2),
        (units, units, shape_of((rows, width), BF)),
        grid=(2,),
        specs={2: up_other_spec(2), 3: down_other_spec(2), 4: anywhere, 5: anywhere},
        out_specs={0: part_spec(2), 1: part_spec(2)},
        scratch=[pltpu.VMEM((rows, width), F32)],
        aliases={4: 0, 5: 1},
        deps=(stages[1],),
    )
    result_other = swap(result_own)

    def hidden_backward(name, back, first, deps, *made):
        return run(
            hidden_backward_kernel,
            name,
            (back, grad, slope_other, mlp_other, mlp_other, *made),
            (units, wide_rows),
            grid=(2,),
            specs={2: part_spec(first), 3: up_other_spec(first), 4: down_other_spec(first), 5: anywhere},
            out_specs={0: part_spec(first)},
            aliases={5: 0} if made else None,
            deps=deps,
        )

    dhid_2, back = hidden_backward("hidden_backward_a", back, 0, (stages[2], result_own))
    dhid_other, back = hidden_backward("hidden_backward_b", back, 2, (stages[3],), dhid_2)
    class_picks = [slope_other[f * seq : f * seq + 1] for f in range(half)]
    slope_cls_other = jnp.concatenate(class_picks + [jnp.zeros((16 - half, f_half), BF)], axis=0).astype(F32)

    loss, caption_grad, embed_grad, pooled_all, pooled_grad = run(
        functools.partial(loss_kernel, bits, frames),
        "contrast",
        (place, early_all, proj_weight),
        (
            shape_of((1, 1), F32),
            shape_of((1, embed), F32),
            shape_of((size, embed), BF),
            shape_of((size, width), BF),
            shape_of((1, width), F32),
        ),
        prefetch=1,
        deps=(back,),
    )

    part_cols = lambda n: pl.BlockSpec((n, part), lambda j, *_: (0, j))
    cls_units = shape_of((16, f_half), BF)
    grad_cls, dhid_cls_own, dhid_cls_other, back_cls = run(
        functools.partial(class_backward_kernel, half),
        "class_backward",
        (place, cot_t, pooled_grad, slope_cls_own, slope_cls_other, up_weight, down_weight, mlp_other, mlp_other),
        (shape_of((16, width), BF), cls_units, cls_units, shape_of((16, width), F32)),
        grid=(4,),
        prefetch=1,
        specs={
            0: class_spec,
            2: part_cols(16),
            3: part_cols(16),
            4: part_cols(width),
            5: pl.BlockSpec((part, width), lambda j, *_: (j, 0)),
            6: up_other_spec(0),
            7: down_other_spec(0),
        },
        out_specs={1: part_cols(16), 2: part_cols(16)},
    )
    weights = shape_of((2, width // 2, f_half), BF)
    wide_steps = f_half // width

    def unit_part(first, lead):
        return pl.BlockSpec(lead + (width,), lambda t, *_: (0,) * len(lead) + (jnp.clip(t - first, 0, wide_steps - 1),))

    keep_own, send_own, keep_other, send_other = run(
        functools.partial(mlp_weight_kernel, half, count),
        "mlp_weights",
        (
            place, grad, grad_cls, mlp_low, activ_own, dhid_own, dhid_cls_own, activ_other, dhid_other, dhid_cls_other,
        ),
        (weights,) * 4,
        grid=(2 * wide_steps,),
        prefetch=1,
        specs={
            3: unit_part(wide_steps, (rows,)),
            4: unit_part(wide_steps, (rows,)),
            5: unit_part(wide_steps, (16,)),
            6: unit_part(0, (rows,)),
            7: unit_part(0, (rows,)),
            8: unit_part(0, (16,)),
        },
        out_specs={k: unit_part(wide_steps if k < 2 else 0, (2, width // 2)) for k in range(4)},
        scratch=[
            pltpu.VMEM((width, rows), BF),
            pltpu.VMEM((width, rows), BF),
            pltpu.VMEM((rows, width), BF),
            pltpu.VMEM((rows, width), BF),
        ],
        deps=(result_other,),
    )
    mlp_stages = Reduction("mlp_stage", mlp_ways, keep_own, send_own, keep_other, send_other)

    in_shape = shape_of((half, seq, 3 * h_half), BF)
    made = (
        shape_of((half, seq, width), BF), in_shape, in_shape, shape_of((half // 2, seq, width), BF), shape_of((16, width), F32),
    )

    def frame_backward(name, first, before, deps=()):
        tensors = (
            back, grad, mlp_low, mlp_rstd, qkv_own, qkv_other, frame_low, frame_rstd, context_own, context_other,
            logsum_own, logsum_other, back_cls, grad_cls, mlp_gain,
            frame_gain, frame_out, out_other, frame_in, in_other, *before,
        )
        flat_frame = lambda wide: pl.BlockSpec((seq, wide), lambda f, *_: (f + first, 0))
        specs = {
            0: flat_frame(width),
            1: flat_frame(width),
            2: flat_frame(width),
            3: flat_frame(128),
            4: one_frame(3 * h_half, first),
            5: one_frame(3 * h_half, first),
            6: one_frame(width, first),
            7: one_frame(128, first),
            8: one_frame(h_half, first),
            9: one_frame(h_half, first),
            10: one_frame(128, first),
            11: one_frame(128, first),
        }
        specs.update({20 + k: anywhere for k in range(3 if before else 0)})
        return run(
            functools.partial(frame_backward_kernel, HEADS, valid, half, first),
            name,
            tensors,
            made,
            grid=(half // 2,),
            specs=specs,
            out_specs={
                0: one_frame(width, first),
                1: one_frame(3 * h_half, first),
                2: one_frame(3 * h_half, first),
                3: one_frame(width),
            },
            aliases={20 + k: k for k in range(3)} if before else None,
            deps=deps,
        )

    before = frame_backward("frame_backward_a", 0, (), (keep_own,))
    mlp_stages.cores(before[0])
    token_first = before[3]
    token_first_other = swap(token_first)
    middle_low, dqkv_own, dqkv_other, token_second, edges = frame_backward(
        "frame_backward_b", half // 2, (before[0], before[1], before[2], before[4]), mlp_stages.ready()
    )
    edges_other = swap(edges)

    next_grad, next_low, msg_dqkv, msg_normed = run(
        functools.partial(message_backward_kernel, HEADS),
        "message_backward",
        (place, edges, edges_other, msg_qkv, msg_out, msg_in),
        (
            shape_of((frames, width), F32),
            shape_of((frames, width), BF),
            shape_of((frames, 3 * h_half), BF),
            shape_of((frames, width), F32),
        ),
        prefetch=1,
    )
    msg_normed_other = swap(msg_normed)
    mlp_stages.step(next_grad)
    grads = shape_of((2, width // 2, 2 * h_half), BF)

    def share_spec(first):
        return pl.BlockSpec((1, width // 2, 2 * h_half), lambda t, *_: (jnp.clip(t - first, 0, 1), 0, 0))

    def column_spec(first):
        return pl.BlockSpec((rows, 2 * h_half), lambda t, *_: (0, jnp.clip(t - first, 0, 1)))

    keep_own, send_own, keep_other, send_other = run(
        functools.partial(frame_weight_kernel, count),
        "frame_weights",
        (
            place, frame_low.reshape(rows, width), middle_low.reshape(rows, width),
            dqkv_own.reshape(rows, 3 * h_half), dqkv_other.reshape(rows, 3 * h_half), context_own2, context_other2,
        ),
        (grads,) * 4,
        grid=(4,),
        prefetch=1,
        specs={2: column_spec(2), 3: column_spec(0)},
        out_specs={0: share_spec(2), 1: share_spec(2), 2: share_spec(0), 3: share_spec(0)},
        scratch=[pltpu.VMEM((width, rows), BF), pltpu.VMEM((width, rows), BF)],
        deps=(*mlp_stages.ready(), token_first_other),
    )
    frame_stages = Reduction("frame_stage", frame_ways, keep_own, send_own, keep_other, send_other)

    late, cls_rows = run(
        message_last_kernel,
        "message_last",
        (
            place, edges, edges_other, next_grad, next_low, msg_dqkv, msg_normed,
            msg_normed_other, message, msg_gain, msg_weight,
        ),
        (shape_of((frames, 2 * width + 6 * h_half), BF), shape_of((frames, width), BF)),
        prefetch=1,
        deps=(keep_own,),
    )
    frame_stages.cores(late)
    cores_ready = frame_stages.ready()
    def both(name, own, other, extra=(), deps=()):
        tile = 64
        parts = own + other
        (out,) = run(
            functools.partial(assemble_kernel, len(own)),
            name,
            (place, *parts, *extra),
            (shape_of((patches, frames, width), BF),),
            grid=(-(-patches // tile),),
            prefetch=1,
            specs={
                k: pl.BlockSpec((part.shape[0], tile, width), lambda t, s: (0, t, 0)) for k, part in enumerate(parts)
            },
            out_specs={0: pl.BlockSpec((tile, frames, width), lambda t, s: (t, 0, 0))},
            scratch=[pltpu.VMEM((width // 128, tile * frames, 128), F32)],
            deps=deps,
        )
        return out

    def whole_of(value):
        return jnp.transpose(value[None], (0, 2, 1, 3))

    result_own, result_other = (value.reshape(half, seq, width) for value in (result_own, result_other))
    for k in range(1, len(bits)):
        extra = ()
        if k == 1:
            layer_parts = both("assemble_out", (result_own,), (result_other,), deps=frame_stages.ready())
            extra = (layer_parts,)
        last = mlp_stages.at == mlp_stages.steps - 1
        mlp_stages.step(*extra, *frame_stages.ready())
        if k == 1:
            late_all = hop(late[None], 0, *mlp_stages.ready())
        frame_stages.step(*((mlp_stages.value[0][0],) if last else mlp_stages.ready()))
        if k == 1:
            token_second_other = swap(after(token_second, *frame_stages.ready()))
        late_all = hop(late_all, k, *(frame_stages.ready() if k < 3 else ()))

    layer_out = whole_of(layer_parts)
    token_parts = both(
        "assemble_grad", (token_first, token_second), (token_first_other, token_second_other), (cls_rows,)
    )

    msg_weight_share, msg_in_share, msg_out_share, proj_share, gains = run(
        functools.partial(factor_kernel, frames),
        "factors",
        (place, early_all, late_all, pooled_all, embed_grad),
        (
            shape_of((share, width), F32),
            shape_of((3, share, h_half), F32),
            shape_of((share, h_half), F32),
            shape_of((share, embed), F32),
            shape_of((3, width), F32),
        ),
        prefetch=1,
    )
    if aligned:
        in_grad, out_grad = run(
            frame_final_kernel,
            "frame_final",
            frame_stages.parts(),
            (shape_of((3, share, h_half), F32), shape_of((share, h_half), F32)),
            deps=(token_parts, gains),
        )
        out_grad = out_grad.T
    else:
        frame_stages.step(token_parts, gains)
        (first,), (second,) = frame_stages.value
        first, second = first[0], second[0]
        in_grad = jnp.stack([first[:, :h_half], first[:, h_half:], second[:, :h_half]])
        out_grad = second[:, h_half:].T
    token_grad = whole_of(token_parts)
    (up_grad,), (down_grad,) = mlp_stages.value
    up_grad, down_grad = (up_grad[0], down_grad[0].T)
    msg_out_share = msg_out_share.T
    gains = mine(gains)
    return (
        layer_out,
        loss[0, 0],
        token_grad,
        caption_grad,
        msg_weight_share,
        gains[2],
        msg_in_share,
        msg_out_share,
        gains[1],
        in_grad,
        out_grad,
        gains[0],
        up_grad,
        down_grad,
        proj_share,
    )


def solution(mesh):
    in_specs = (
        P("dp", None, None, None),
        P("dp", None),
        P("dp"),
        P("dp"),
        P(),
        P(),
        P(None, None, "mp"),
        P("mp", None),
        P(),
        P(None, None, "mp"),
        P("mp", None),
        P(),
        P(None, "mp"),
        P("mp", None),
        P(),
        P("dp", None, None, None),
    )
    out_specs = (
        P("dp", None, None, None),
        P(),
        P("dp", None, None, None),
        P("dp", None),
        P("dp", None),
        P("dp"),
        P(None, "dp", "mp"),
        P("mp", "dp"),
        P("dp"),
        P(None, "dp", "mp"),
        P("mp", "dp"),
        P("dp"),
        P("dp", "mp"),
        P("mp", "dp"),
        P("dp", None),
    )
    return jax.shard_map(
        on_device, mesh=mesh, in_specs=in_specs, out_specs=out_specs, check_vma=False
    )
```

```python
import functools

import jax
import jax.numpy as jnp
from jax import lax
from jax.experimental import pallas as pl
from jax.experimental.pallas import tpu as pltpu
from jax.sharding import PartitionSpec as P

HEADS = 12
SHARPNESS = 50.0
LOWEST = -1e30
BF = jnp.bfloat16
F32 = jnp.float32
KERNEL_MIB = {
    "frame_first": 52,
    "cotangent": 52,
    "frame_second": 52,
    "mlp_first": 52,
    "mlp_second": 52,
    "mlp_third": 52,
    "hidden_backward_a": 52,
    "hidden_backward_b": 52,
    "mlp_weights": 52,
    "frame_backward_a": 52,
    "frame_backward_b": 52,
    "frame_weights": 52,
    "contrast": 52,
    "class_backward": 52,
    "class_forward": 52,
}
KERNEL_US = {
    "frame_first": 7,
    "cotangent": 4,
    "frame_second": 6,
    "mlp_first": 16,
    "mlp_second": 5,
    "mlp_third": 5,
    "hidden_backward_a": 5,
    "hidden_backward_b": 5,
    "class_backward": 5,
    "mlp_weights": 15,
    "frame_backward_a": 14,
    "frame_backward_b": 14,
    "frame_weights": 11,
}


def swap(value):
    return lax.ppermute(value, "mp", [(0, 1), (1, 0)])


def flip(value, bit):
    size = lax.axis_size("dp")
    return lax.ppermute(value, "dp", [(i, i ^ bit) for i in range(size)])


def after(value, *deps):
    return lax.optimization_barrier((value,) + deps)[0]


def bits_of(size):
    return [1 << k for k in range(size.bit_length() - 1)]


def row_order(bits):
    order = [0]
    for bit in reversed(bits):
        order = order + [mask | bit for mask in order]
    return order


def mlp_ways(bits):
    return (bits[:1] + ["mp"] + bits[1:], bits[1:] + bits[:1] + ["mp"])


def frame_ways(bits):
    return (bits[:1] + ["mp"] + bits[1:], ["mp"] + bits)


def gather_bits():
    bits = bits_of(lax.axis_size("dp"))
    return bits[:0:-1] + bits[:1]


def gather(value):
    for bit in gather_bits():
        value = jnp.concatenate([value, flip(value, bit)], axis=0)
    return value


def dot(a, b):
    return jnp.dot(a, b, preferred_element_type=F32)


def dot_nt(a, b):
    return lax.dot_general(a, b, (((1,), (1,)), ((), ())), preferred_element_type=F32)


def dot_tn(a, b):
    return lax.dot_general(a, b, (((0,), (0,)), ((), ())), preferred_element_type=F32)


def standardized(value):
    centered = value - jnp.mean(value, axis=-1, keepdims=True)
    rstd = lax.rsqrt(jnp.mean(centered * centered, axis=-1, keepdims=True) + 1e-05)
    return (centered * rstd, rstd)


def spread(rstd):
    return jnp.broadcast_to(rstd, (rstd.shape[0], 128))


def norm_backward(grad, gain, normal, rstd):
    scaled = grad * gain
    inner = (
        scaled
        - jnp.mean(scaled, axis=-1, keepdims=True)
        - normal * jnp.mean(scaled * normal, axis=-1, keepdims=True)
    )
    return (rstd * inner, jnp.sum(grad * normal, axis=0, keepdims=True))


def lane_half(rows, pair, which):
    lane = lax.broadcasted_iota(jnp.int32, (rows, pair), 1)
    return (lane < pair // 2) if which == 0 else (lane >= pair // 2)


def only(value, which):
    return jnp.where(lane_half(*value.shape, which), value, jnp.zeros_like(value))


def attend_pair(query, keys, values, valid):
    rows, pair = query.shape
    out = None
    sums = []
    for which in range(2):
        scores = dot_nt(only(query, which), keys)
        if valid < rows:
            key = lax.broadcasted_iota(jnp.int32, scores.shape, 1)
            scores = jnp.where(key < valid, scores, LOWEST)
        top = jnp.max(scores, axis=1, keepdims=True)
        each = jnp.exp(scores - top)
        total = jnp.sum(each, axis=1, keepdims=True)
        sums.append(top + jnp.log(total))
        part = dot(each.astype(BF), only(values, which)) * (1.0 / total)
        out = part if out is None else out + part
    return (out, sums)


def attend_pair_kept(query, keys, values, grad, logsums, inners, valid, scale):
    rows, pair = query.shape
    size = pair // 2
    edge = valid // 16 * 16
    lane = lax.broadcasted_iota(jnp.int32, (1, pair), 1)
    keys_t = keys.T
    turned, both = ([], [])
    for which in range(2):
        head = (lane // size == which).astype(F32).astype(BF)
        weights = jnp.exp(dot_nt(keys, query * head) - logsums[which])
        tail = weights[edge:]
        row = lax.broadcasted_iota(jnp.int32, tail.shape, 0)
        weights = jnp.concatenate([weights[:edge], jnp.where(row < valid - edge, tail, 0.0)], axis=0)
        weight_grad = dot_nt(values, grad * head)
        value_grad = dot(weights.astype(BF), grad)
        score_grad = (weights * (weight_grad - inners[which])).astype(BF)
        key_grad = dot(score_grad, query)
        turned.append(dot(keys_t[size * which : size * (which + 1)], score_grad))
        both.append((key_grad, value_grad))
    query_grad = (jnp.concatenate(turned, axis=0) * scale).astype(BF).T
    first = lane_half(rows, pair, 0)
    key_grad, value_grad = (jnp.where(first, one, two).astype(BF) for one, two in zip(*both))
    return [query_grad, key_grad, value_grad]


def head_sums(value, size):
    head = lax.broadcasted_iota(jnp.int32, (16, value.shape[1]), 1) // size
    pick = (head == lax.broadcasted_iota(jnp.int32, head.shape, 0)).astype(F32).astype(BF)
    high = value.astype(BF)
    return dot_nt(pick, high) + dot_nt(pick, (value - high.astype(F32)).astype(BF))


def attend_pair_backward(query, keys, values, grad, valid, scale):
    rows, _ = query.shape
    sums = [None, None, None]
    for which in range(2):
        query_own, key_own, grad_own = (only(query, which), only(keys, which), only(grad, which))
        scores = dot_nt(keys, query_own)
        if valid < rows:
            key = lax.broadcasted_iota(jnp.int32, scores.shape, 0)
            scores = jnp.where(key < valid, scores, LOWEST)
        top = jnp.max(scores, axis=0, keepdims=True)
        each = jnp.exp(scores - top)
        weights = each * (1.0 / jnp.sum(each, axis=0, keepdims=True))
        weight_grad = dot_nt(values, grad_own)
        value_grad = dot(weights.astype(BF), grad_own)
        inner = jnp.sum(weights * weight_grad, axis=0, keepdims=True)
        score_grad = (weights * (weight_grad - inner)).astype(BF)
        key_grad = dot(score_grad, query_own)
        query_grad = dot_tn(score_grad, key_own) * scale
        parts = (query_grad, key_grad, value_grad)
        sums = [part if one is None else one + part for one, part in zip(sums, parts)]
    return [one.astype(BF) for one in sums]


def project(normed, in_ref, scale):
    wide = in_ref.shape[2]
    query = dot(normed, in_ref[0]).astype(BF) * jnp.asarray(scale, BF)
    keys = dot(normed, in_ref[1]).astype(BF)
    values = dot(normed, in_ref[2]).astype(BF)
    return (query, keys, values, wide)


def turn_rows(ways, count, which, to_ref, from_ref, place_ref):
    rows = to_ref.shape[0]
    pairs = 8 if count is None else 1 << count
    block = rows // (2 * pairs)
    turned = from_ref[...].T
    me = place_ref[1]
    for j in range(2 * pairs):
        if count is None:
            spot = j // 2 + (j % 2) * pairs
        else:
            mask = (me >> 1) ^ (j >> 1)
            order = [k for k in ways(list(range(count)))[which] if k != "mp"]
            spot = sum(((mask >> k) & 1) << (count - 1 - i) for i, k in enumerate(order))
            spot = spot + ((me ^ j) & 1) * pairs
        to_ref[pl.ds(pl.multiple_of(spot * block, 16), block), :] = turned[block * j : block * (j + 1)]


def put_product(keep_ref, send_ref, lead, turned_ref, value, lanes=slice(None)):
    rows = keep_ref.shape[1]
    keep_ref[lead, :, lanes] = dot(turned_ref[:rows], value).astype(BF)
    send_ref[lead, :, lanes] = dot(turned_ref[rows:], value).astype(BF)


def frame_rows(wide_ref, frame, patches):
    at = pl.ds(frame, patches, stride=8)
    return jnp.concatenate([wide_ref[j, at, :] for j in range(wide_ref.shape[0])], axis=1)


def widen(wide_ref, from_ref):
    for j in range(wide_ref.shape[0]):
        value = from_ref[:, :, 128 * j : 128 * (j + 1)].astype(F32)
        wide_ref[j] = value.reshape(wide_ref.shape[1:])


def put_class_rows(to_ref, rows_ref, half):
    seq = to_ref.shape[0] // half
    for f in range(half):
        old = to_ref[f * seq : f * seq + 16, :].astype(F32)
        row = lax.broadcasted_iota(jnp.int32, old.shape, 0)
        new = jnp.where(row == 0, rows_ref[f : f + 1, :].astype(F32), old)
        to_ref[f * seq : f * seq + 16, :] = new.astype(to_ref.dtype)


def class_rows(from_ref, half, dtype, count):
    seq = from_ref.shape[0] // half
    rows = [from_ref[f * seq : f * seq + 16, :].astype(F32)[0:1] for f in range(half)]
    rows.append(jnp.zeros((count - half, from_ref.shape[1]), F32))
    return jnp.concatenate(rows, axis=0).astype(dtype)


def message_forward_kernel(
    heads, place_ref, tok_ref, captions_ref, w_ref, gain_ref, in_ref, out_ref, message_ref, early_ref, qkv_ref, part_ref
):
    cls = tok_ref[0, 0]
    frames, width = cls.shape
    message = dot(cls, w_ref[...])
    message_ref[...] = message
    normal, _ = standardized(message)
    low = (normal * gain_ref[...]).astype(BF)
    size = width // heads
    query, keys, values, wide = project(low, in_ref, size**-0.5)
    contexts = []
    for j in range(wide // (2 * size)):
        at = slice(2 * size * j, 2 * size * (j + 1))
        contexts.append(attend_pair(query[:, at], keys[:, at], values[:, at], frames)[0])
    context = jnp.concatenate(contexts, axis=1).astype(BF)
    part_ref[...] = dot(context, out_ref[...])
    qkv_ref[:, :wide] = query
    qkv_ref[:, wide : 2 * wide] = keys
    qkv_ref[:, 2 * wide :] = values

    def padded(value):
        value = value.astype(F32)
        return jnp.concatenate([value, jnp.zeros((16 - value.shape[0], value.shape[1]), F32)], axis=0)

    early_ref[:, width : 2 * width] = padded(low).astype(BF)
    early_ref[:, 2 * width :] = padded(context).astype(BF)
    embed = captions_ref.shape[1]
    lane = lax.broadcasted_iota(jnp.int32, (1, width - embed), 1)
    ids = jnp.where(lane == 0, place_ref[2], jnp.where(lane == 1, place_ref[3], 0)).astype(F32)
    text = jnp.concatenate([captions_ref[...].astype(F32), ids], axis=1)
    row = lax.broadcasted_iota(jnp.int32, (8, width), 0)
    text = jnp.where(row == 0, text, 0.0)
    early_ref[:, :width] = jnp.concatenate([cls.astype(F32), text], axis=0).astype(BF)


def frame_attention(heads, valid, low, in_ref, qkv_ref, context_ref, logsum_ref):
    size = low.shape[1] // heads
    wide = in_ref.shape[2]
    for k in range(3):
        value = dot(low, in_ref[k]).astype(BF)
        if k == 0:
            value = value * jnp.asarray(size**-0.5, BF)
        qkv_ref[0, :, wide * k : wide * (k + 1)] = value
    lane = lax.broadcasted_iota(jnp.int32, (low.shape[0], 128), 1)
    logsums = jnp.zeros(lane.shape, F32)
    for j in range(wide // (2 * size)):
        query, keys, values = (
            qkv_ref[0, :, wide * k + 2 * size * j : wide * k + 2 * size * (j + 1)] for k in range(3)
        )
        context, sums = attend_pair(query, keys, values, valid)
        context_ref[0, :, 2 * size * j : 2 * size * (j + 1)] = context.astype(BF)
        for which, one in enumerate(sums):
            logsums = jnp.where(lane == 2 * j + which, one, logsums)
    logsum_ref[0] = logsums


def frame_first_kernel(
    heads, half, place_ref, tok_ref, message_ref, part_ref, other_ref, gain_ref, in_ref,
    stream_ref, low_ref, qkv_ref, context_ref, rstd_ref, logsum_ref, wide_ref, rows_ref,
):
    patches, frames, width = tok_ref.shape
    seq = stream_ref.shape[1]
    frame = place_ref[0] * half + pl.program_id(0)

    @pl.when(pl.program_id(0) == 0)
    def _():
        widen(wide_ref, tok_ref)

    at = pl.ds(frame, 1)
    message = message_ref[at, :] + (part_ref[at, :] + other_ref[at, :])
    edge = patches // 8 * 8
    rows_ref[edge:seq, :] = jnp.zeros((seq - edge, width), F32)
    rows_ref[0:patches, :] = frame_rows(wide_ref, frame, patches)
    rows_ref[patches : patches + 1, :] = message
    stream_ref[0] = rows_ref[...].astype(BF)
    normal, rstd = standardized(rows_ref[...])
    rstd_ref[0] = spread(rstd)
    low = (normal * gain_ref[...]).astype(BF)
    low_ref[0] = low
    frame_attention(heads, patches + 1, low, in_ref, qkv_ref, context_ref, logsum_ref)


def joined(place_ref, to_ref, mine_ref, theirs_ref, axis):
    rows = mine_ref.shape[axis]
    core = place_ref[1] & 1
    lead = (slice(None),) * axis
    to_ref[lead + (pl.ds(pl.multiple_of(core * rows, 16), rows),)] = mine_ref[...]
    to_ref[lead + (pl.ds(pl.multiple_of((1 - core) * rows, 16), rows),)] = theirs_ref[...]


def frame_second_kernel(
    heads, valid, place_ref, low_ref, mine_ref, theirs_ref, qkv_ref, context_ref, in_ref, logsum_ref
):
    @pl.when(pl.program_id(0) == 0)
    def _():
        joined(place_ref, in_ref, mine_ref, theirs_ref, 1)

    frame_attention(heads, valid, low_ref[0], in_ref, qkv_ref, context_ref, logsum_ref)


def cotangent_kernel(half, place_ref, cot_ref, down_ref, grad_ref, dact_ref, wide_ref):
    patches, frames, width = cot_ref.shape
    seq = grad_ref.shape[0] // half

    @pl.when(pl.program_id(0) == 0)
    def _():
        widen(wide_ref, cot_ref)
        edge = patches // 16 * 16
        for f in range(half):
            value = frame_rows(wide_ref, place_ref[0] * half + f, patches)
            tail = jnp.concatenate([value[edge:], jnp.zeros((seq - patches, width), F32)], axis=0)
            grad_ref[f * seq : f * seq + edge, :] = value[:edge].astype(BF)
            grad_ref[f * seq + edge : (f + 1) * seq, :] = tail.astype(BF)

    dact_ref[...] = dot_nt(grad_ref[...], down_ref[...]).astype(BF)


def gate(hidden):
    sigmo = 1.0 / (1.0 + jnp.exp(-1.702 * hidden))
    gated = hidden * sigmo
    return (gated, sigmo + 1.702 * gated * (1.0 - sigmo))


def up_block(ref):
    return ref[...].reshape(ref.shape[0] * ref.shape[1], ref.shape[2])


def mlp_first_kernel(
    half, stream_ref, own_ref, other_ref, out_own_ref, out_other_ref, gain_ref, up_ref, down_ref, dact_ref,
    rstd_ref, low_ref, activ_ref, dhid_ref, slope_ref, total_ref, back_ref, cls_low_ref, cls_total_ref,
):
    step = pl.program_id(0)

    @pl.when(step == 0)
    def _():
        branch = dot(own_ref[...], out_own_ref[...]) + dot(other_ref[...], out_other_ref[...])
        middle = stream_ref[...].astype(F32) + branch
        normal, rstd = standardized(middle)
        rstd_ref[...] = spread(rstd)
        low_ref[...] = (normal * gain_ref[...]).astype(BF)
        total_ref[...] = middle
        back_ref[...] = jnp.zeros_like(back_ref)
        cls_low_ref[...] = class_rows(low_ref, half, BF, 16)

    seq = low_ref.shape[0] // half
    activ, slope = gate(dot(low_ref[...], up_ref[...]))
    activ_ref[...] = activ.astype(BF)
    dhid_ref[...] = (dact_ref[...].astype(F32) * slope).astype(BF)
    rows = [slope[f * seq : f * seq + 1] for f in range(half)]
    slope_ref[...] = jnp.concatenate(rows + [jnp.zeros((16 - half, slope.shape[1]), F32)], axis=0)
    total_ref[...] += dot(activ_ref[...], down_ref[...])
    back_ref[...] += dot_nt(dhid_ref[...], up_ref[...])

    @pl.when(step == pl.num_programs(0) - 1)
    def _():
        cls_total_ref[...] = class_rows(total_ref, half, F32, 16)


def class_forward_kernel(half, low_ref, start_ref, up_ref, down_ref, pooled_ref, total_ref):
    step = pl.program_id(0)

    @pl.when(step == 0)
    def _():
        total_ref[...] = start_ref[...]

    activ, _ = gate(dot(low_ref[...], up_block(up_ref)))
    total_ref[...] += dot(activ.astype(BF), up_block(down_ref))

    @pl.when(step == pl.num_programs(0) - 1)
    def _():
        pooled_ref[...] = jnp.sum(total_ref[0:half, :], axis=0, keepdims=True)


def mlp_second_kernel(half, start_ref, low_ref, up_ref, down_ref, activ_ref, slope_ref, total_ref):
    @pl.when(pl.program_id(0) == 0)
    def _():
        total_ref[...] = start_ref[...]

    activ, slope = gate(dot(low_ref[...], up_block(up_ref)))
    activ_ref[...] = activ.astype(BF)
    slope_ref[...] = slope.astype(BF)
    total_ref[...] += dot(activ_ref[...], up_block(down_ref))


def mlp_third_kernel(half, start_ref, low_ref, up_ref, down_ref, _, __, activ_ref, slope_ref, result_ref, total_ref):
    mlp_second_kernel(half, start_ref, low_ref, up_ref, down_ref, activ_ref, slope_ref, total_ref)

    @pl.when(pl.program_id(0) == pl.num_programs(0) - 1)
    def _():
        result_ref[...] = total_ref[...].astype(BF)


def hidden_backward_kernel(start_ref, grad_ref, slope_ref, up_ref, down_ref, *refs):
    dhid_ref, back_ref = refs[-2:]

    @pl.when(pl.program_id(0) == 0)
    def _():
        back_ref[...] = start_ref[...]

    dact = dot_nt(grad_ref[...], up_block(down_ref))
    dhid_ref[...] = (dact * slope_ref[...].astype(F32)).astype(BF)
    back_ref[...] += dot_nt(dhid_ref[...], up_block(up_ref))


def loss_kernel(
    order, frames, place_ref, early_ref, proj_ref,
    loss_ref, caption_grad_ref, embed_grad_ref, pooled_all_ref, pooled_grad_ref,
):
    clips = early_ref.shape[0]
    width, wide = proj_ref.shape
    me = place_ref[1]
    early = early_ref[...].astype(F32)[:, frames, :].astype(BF)
    block = lax.broadcasted_iota(jnp.int32, (clips, clips), 1)
    mask = jnp.zeros_like(block)
    for k, bit in enumerate(order):
        mask = mask + ((block >> k) & 1) * bit
    row = lax.broadcasted_iota(jnp.int32, (clips, clips), 0)
    pick = (row == jnp.bitwise_xor(mask, me)).astype(F32).astype(BF)
    text = dot(pick, early[:, :width]).astype(BF)
    pooled = dot(pick, early[:, width : 2 * width]).astype(BF)
    pooled_all_ref[...] = pooled
    embed = dot(pooled, proj_ref[...])
    embed_rinv = lax.rsqrt(jnp.sum(embed * embed, axis=-1, keepdims=True) + 1e-06)
    embed_low = (embed * embed_rinv).astype(BF)
    caption_f = text[:, :wide].astype(F32)
    caption_rinv = lax.rsqrt(jnp.sum(caption_f * caption_f, axis=-1, keepdims=True) + 1e-06)
    caption_low = (caption_f * caption_rinv).astype(BF)
    scores = SHARPNESS * dot_nt(embed_low, caption_low)
    lane = lax.broadcasted_iota(jnp.int32, (8, text.shape[1] - wide), 1)
    pick_id = (lane == 1).astype(F32).astype(BF)
    caption_ids = dot_nt(pick_id, text[:, wide:])[0:1, :]
    clip_ids = text[:, wide:].astype(F32)[:, 0:1]
    positive = clip_ids == caption_ids
    masked = jnp.where(positive, scores, LOWEST)

    def side(axis):
        top = jnp.max(scores, axis=axis, keepdims=True)
        each = jnp.exp(scores - top)
        total = jnp.sum(each, axis=axis, keepdims=True)
        pos_top = jnp.max(masked, axis=axis, keepdims=True)
        pos_each = jnp.where(positive, jnp.exp(masked - pos_top), 0.0)
        pos_total = jnp.sum(pos_each, axis=axis, keepdims=True)
        part = jnp.sum(top + jnp.log(total) - pos_top - jnp.log(pos_total), axis=1 - axis, keepdims=True)
        return (part, each / total - pos_each / pos_total)

    row_loss, row_grad = side(1)
    column_loss, column_grad = side(0)
    loss_ref[...] = 0.5 * (row_loss + column_loss)
    dscore = 0.5 * (row_grad + column_grad)
    embed_grad = SHARPNESS * dot(dscore.astype(BF), caption_low)
    caps_grad = SHARPNESS * dot_tn(dscore.astype(BF), embed_low)
    caption_grad = caption_rinv * caps_grad - caption_f * (
        caption_rinv * caption_rinv * caption_rinv * jnp.sum(caption_f * caps_grad, axis=-1, keepdims=True)
    )
    embed_diff = embed_rinv * embed_grad - embed * (
        embed_rinv * embed_rinv * embed_rinv * jnp.sum(embed * embed_grad, axis=-1, keepdims=True)
    )
    embed_diff = embed_diff.astype(BF)
    embed_grad_ref[...] = embed_diff
    grads = dot_nt(embed_diff, proj_ref[...])

    def own_row(value):
        own = lax.broadcasted_iota(jnp.int32, value.shape, 0) == me
        return jnp.sum(jnp.where(own, value, 0.0), axis=0, keepdims=True)

    caption_grad_ref[...] = own_row(caption_grad)
    pooled_grad_ref[...] = own_row(grads) / frames


def class_backward_kernel(
    half, place_ref, cot_ref, pooled_ref, slope_own_ref, slope_other_ref, up_own_ref, down_own_ref, up_ref, down_ref,
    grad_ref, dhid_own_ref, dhid_other_ref, back_ref,
):
    @pl.when(pl.program_id(0) == 0)
    def _():
        cot = cot_ref[0, 0].astype(F32)
        cot = jnp.where(place_ref[0] == 0, cot[:half], cot[half:]) + pooled_ref[...]
        grad_ref[...] = jnp.concatenate([cot, jnp.zeros((16 - half, cot.shape[1]), F32)], axis=0).astype(BF)
        back_ref[...] = jnp.zeros_like(back_ref)

    grad = grad_ref[...]
    dhid_own_ref[...] = (dot_nt(grad, down_own_ref[...]) * slope_own_ref[...]).astype(BF)
    dhid_other_ref[...] = (dot_nt(grad, up_block(down_ref)) * slope_other_ref[...]).astype(BF)
    back_ref[...] += dot_nt(dhid_own_ref[...], up_own_ref[...]) + dot_nt(dhid_other_ref[...], up_block(up_ref))


def mlp_weight_kernel(
    half, count, place_ref, grad_ref, grad_cls_ref, low_ref, activ_own_ref, dhid_own_ref, dhid_cls_own_ref,
    activ_other_ref, dhid_other_ref, dhid_cls_other_ref,
    keep_own_ref, send_own_ref, keep_other_ref, send_other_ref, grad_t_ref, low_t_ref, fixed_ref, rows_ref,
):
    step = pl.program_id(0)
    steps = pl.num_programs(0) // 2

    @pl.when(step == 0)
    def _():
        rows_ref[...] = grad_ref[...]
        put_class_rows(rows_ref, grad_cls_ref, half)
        turn_rows(mlp_ways, count, 0, low_t_ref, low_ref, place_ref)
        turn_rows(mlp_ways, count, 1, grad_t_ref, rows_ref, place_ref)

    def part(activ_ref, dhid_ref, dhid_cls_ref, keep_ref, send_ref):
        fixed_ref[...] = dhid_ref[...]
        put_class_rows(fixed_ref, dhid_cls_ref, half)
        put_product(keep_ref, send_ref, 0, low_t_ref, fixed_ref[...])
        put_product(keep_ref, send_ref, 1, grad_t_ref, activ_ref[...])

    @pl.when(step < steps)
    def _():
        part(activ_other_ref, dhid_other_ref, dhid_cls_other_ref, keep_other_ref, send_other_ref)

    @pl.when(step >= steps)
    def _():
        part(activ_own_ref, dhid_own_ref, dhid_cls_own_ref, keep_own_ref, send_own_ref)


def frame_backward_kernel(
    heads, valid, half, first, back_ref, grad_in_ref, mid_ref, mid_rstd_ref, own_ref, other_ref, low_in_ref, rstd_ref,
    context_own_ref, context_other_ref, logsum_own_ref, logsum_other_ref,
    back_cls_ref, grad_cls_ref, mlp_gain_ref, gain_ref, out_own_ref, out_other_ref, in_own_ref, in_other_ref, *refs,
):
    low_ref, down_ref, dother_ref, token_ref, edge_ref = refs[-5:]
    step = pl.program_id(0)
    f = first + step
    width = back_ref.shape[1]
    size = width // heads
    scale = size**-0.5
    row = lax.broadcasted_iota(jnp.int32, back_ref.shape, 0)
    at = pl.ds(f, 1)
    back = jnp.where(row == 0, back_cls_ref[at, :], back_ref[...])
    cls = jnp.zeros((1, width), F32)
    for k in range(half):
        cls = jnp.where(f == k, grad_cls_ref[...].astype(F32)[k : k + 1], cls)
    grad = jnp.where(row == 0, cls, grad_in_ref[...].astype(F32))
    normal = mid_ref[...].astype(F32) * (1.0 / mlp_gain_ref[...])
    part, mlp_gain_grad = norm_backward(back, mlp_gain_ref[...], normal, mid_rstd_ref[:, 0:1])
    grad = grad + part
    low = grad.astype(BF)
    low_ref[0] = low
    normed_grad = None
    for qkv_ref, context_ref, logsum_ref, out_ref, in_ref, to_ref in (
        (own_ref, context_own_ref, logsum_own_ref, out_own_ref, in_own_ref, down_ref),
        (other_ref, context_other_ref, logsum_other_ref, out_other_ref, in_other_ref, dother_ref),
    ):
        wide = in_ref.shape[2]
        context_grad = dot_nt(low, out_ref[...]).astype(BF)
        inners = head_sums(context_grad.astype(F32) * context_ref[0].astype(F32), size)
        logsums = logsum_ref[0].T
        for j in range(wide // (2 * size)):
            query, keys, values = (
                qkv_ref[0, :, wide * k + 2 * size * j : wide * k + 2 * size * (j + 1)] for k in range(3)
            )
            grads = attend_pair_kept(
                query,
                keys,
                values,
                context_grad[:, 2 * size * j : 2 * size * (j + 1)],
                [logsums[2 * j + which : 2 * j + which + 1] for which in range(2)],
                [inners[2 * j + which : 2 * j + which + 1] for which in range(2)],
                valid,
                scale,
            )
            for k in range(3):
                to_ref[0, :, wide * k + 2 * size * j : wide * k + 2 * size * (j + 1)] = grads[k]
        for k in range(3):
            part = dot_nt(to_ref[0, :, wide * k : wide * (k + 1)], in_ref[k])
            normed_grad = part if normed_grad is None else normed_grad + part
    normal = low_in_ref[0].astype(F32) * (1.0 / gain_ref[...])
    part, gain_grad = norm_backward(normed_grad, gain_ref[...], normal, rstd_ref[0, :, 0:1])
    total = grad + part
    token_ref[0] = total.astype(BF)

    @pl.when(step == 0)
    def _():
        if first == 0:
            edge_ref[...] = jnp.zeros_like(edge_ref)
        else:
            edge_ref[...] = refs[3][...]

    edge_ref[pl.ds(f, 1), :] = total[0:1]
    edge_ref[pl.ds(half + f, 1), :] = total[valid - 1 : valid]
    edge_ref[2 * half : 2 * half + 1, :] += gain_grad
    edge_ref[2 * half + 1 : 2 * half + 2, :] += mlp_gain_grad


def frame_weight_kernel(
    count, place_ref, low_ref, grad_ref, down_ref, dother_ref, own_ref, other_ref,
    keep_own_ref, send_own_ref, keep_other_ref, send_other_ref, low_t_ref, grad_t_ref,
):
    step = pl.program_id(0)

    @pl.when(step == 0)
    def _():
        turn_rows(frame_ways, count, 0, low_t_ref, low_ref, place_ref)
        turn_rows(frame_ways, count, 0, grad_t_ref, grad_ref, place_ref)

    wide = own_ref.shape[1]
    for first, dqkv_ref, context_ref, keep_ref, send_ref in (
        (0, dother_ref, other_ref, keep_other_ref, send_other_ref),
        (2, down_ref, own_ref, keep_own_ref, send_own_ref),
    ):

        @pl.when(step == first)
        def _(dqkv_ref=dqkv_ref, keep_ref=keep_ref, send_ref=send_ref):
            put_product(keep_ref, send_ref, 0, low_t_ref, dqkv_ref[...])

        @pl.when(step == first + 1)
        def _(dqkv_ref=dqkv_ref, context_ref=context_ref, keep_ref=keep_ref, send_ref=send_ref):
            put_product(keep_ref, send_ref, 0, low_t_ref, dqkv_ref[:, :wide], slice(0, wide))
            put_product(keep_ref, send_ref, 0, grad_t_ref, context_ref[...], slice(wide, 2 * wide))


def both_halves(place, own, other):
    return jnp.concatenate(
        [jnp.where(place == 0, own, other), jnp.where(place == 0, other, own)], axis=0
    )


def message_backward_kernel(
    heads, place_ref, own_ref, other_ref, qkv_ref, out_ref, in_ref, next_ref, low_ref, dqkv_ref, part_ref
):
    frames, width = next_ref.shape
    half = frames // 2
    at = slice(half, 2 * half)
    grad = both_halves(place_ref[0], own_ref[at, :], other_ref[at, :])
    next_ref[...] = grad
    low = grad.astype(BF)
    low_ref[...] = low
    size = width // heads
    scale = size**-0.5
    wide = in_ref.shape[2]
    context_grad = dot_nt(low, out_ref[...]).astype(BF)
    for j in range(wide // (2 * size)):
        query, keys, values = (
            qkv_ref[:, wide * k + 2 * size * j : wide * k + 2 * size * (j + 1)] for k in range(3)
        )
        grads = attend_pair_backward(
            query, keys, values, context_grad[:, 2 * size * j : 2 * size * (j + 1)], frames, scale
        )
        for k in range(3):
            dqkv_ref[:, wide * k + 2 * size * j : wide * k + 2 * size * (j + 1)] = grads[k]
    total = None
    for k in range(3):
        part = dot_nt(dqkv_ref[:, wide * k : wide * (k + 1)], in_ref[k])
        total = part if total is None else total + part
    part_ref[...] = total


def message_last_kernel(
    place_ref, own_ref, other_ref, next_ref, low_ref, dqkv_ref, part_ref, part_other_ref, message_ref, gain_ref, w_ref,
    late_ref, cls_ref,
):
    frames, width = next_ref.shape
    half = frames // 2
    normal, rstd = standardized(message_ref[...])
    part, gain_grad = norm_backward(part_ref[...] + part_other_ref[...], gain_ref[...], normal, rstd)
    message_low = (next_ref[...] + part).astype(BF)
    cls = both_halves(place_ref[0], own_ref[0:half, :], other_ref[0:half, :])
    cls_ref[...] = (cls + dot_nt(message_low, w_ref[...])).astype(BF)
    wide = dqkv_ref.shape[1]
    late_ref[0:frames, 0:width] = low_ref[...]
    late_ref[0:frames, width : 2 * width] = message_low
    late_ref[0:frames, 2 * width : 2 * width + wide] = dqkv_ref[...]
    both = own_ref[2 * half : 2 * half + 2, :] + other_ref[2 * half : 2 * half + 2, :]
    gains = jnp.concatenate([both[1:2], both[0:1], gain_grad], axis=1)
    room = late_ref.shape[1] - 2 * width - wide
    gains = jnp.concatenate([gains, jnp.zeros((1, frames * room - 3 * width), F32)], axis=1)
    gains = jnp.concatenate([gains[:, room * r : room * (r + 1)] for r in range(frames)], axis=0)
    late_ref[:, 2 * width + wide :] = gains.astype(BF)


def assemble_kernel(pieces, place_ref, *refs):
    out_ref, wide_ref = refs[-2:]
    tile, frames, width = out_ref.shape
    half = frames // 2
    for side in range(2):
        mp = place_ref[0] if side == 0 else 1 - place_ref[0]
        for k in range(half):
            per = half // pieces
            value = refs[side * pieces + k // per][k % per].astype(F32)
            for j in range(width // 128):
                wide_ref[j, pl.ds(mp * half + k, tile, stride=8), :] = value[:, 128 * j : 128 * (j + 1)]
    for j in range(width // 128):
        out_ref[:, :, 128 * j : 128 * (j + 1)] = wide_ref[j].reshape(tile, frames, 128).astype(BF)
    if len(refs) > 2 * pieces + 2:

        @pl.when(pl.program_id(0) == 0)
        def _():
            out_ref[0] = refs[2 * pieces][...]


def factor_kernel(
    frames, place_ref, early_ref, late_ref, pooled_ref, embed_ref,
    weight_ref, in_ref, out_ref, proj_ref, gains_ref,
):
    size = early_ref.shape[0]
    share, width = weight_ref.shape
    wide = out_ref.shape[1]
    column = lax.broadcasted_iota(jnp.int32, (share, width), 1)
    row = lax.broadcasted_iota(jnp.int32, (share, width), 0)
    pick = (column == place_ref[1] * share + row).astype(F32).astype(BF)

    def early(first, wide):
        value = early_ref[:, :, first : first + wide].astype(F32)[:, :frames]
        return value.reshape(size * frames, wide).astype(BF)

    def late(first, wide):
        return late_ref[:, :, first : first + wide].astype(F32).reshape(size * frames, wide).astype(BF)

    def own(value):
        return dot_nt(pick, value).astype(BF)

    weight_ref[...] = dot(own(early(0, width)), late(width, width))
    product = dot(own(early(width, width)), late(2 * width, 3 * wide))
    for k in range(3):
        in_ref[k] = product[:, wide * k : wide * (k + 1)]
    out_ref[...] = dot(own(late(0, width)), early(2 * width, wide))
    proj_ref[...] = dot(own(pooled_ref[...]), embed_ref[...])
    room = late_ref.shape[2] - 2 * width - 3 * wide
    gains = jnp.sum(late_ref[:, :, 2 * width + 3 * wide :].astype(F32), axis=0)
    gains = jnp.concatenate([gains[r : r + 1, :] for r in range(frames)], axis=1)
    for k in range(3):
        gains_ref[k : k + 1, :] = gains[:, width * k : width * (k + 1)]


def whole(shape):
    return pl.BlockSpec(tuple(shape), lambda *_: (0,) * len(shape))


def run(kernel, name, args, outs, grid=(1,), prefetch=0, specs=None, out_specs=None, scratch=(), aliases=None, deps=(), cost=2):
    specs = specs or {}
    out_specs = out_specs or {}
    tensors = args[prefetch:]
    taken = len(args)

    def body(*refs):
        kernel(*refs[:taken], *refs[taken + len(deps) :])

    return pl.pallas_call(
        body,
        out_shape=list(outs),
        grid_spec=pltpu.PrefetchScalarGridSpec(
            num_scalar_prefetch=prefetch,
            grid=grid,
            in_specs=[specs.get(k, whole(t.shape)) for k, t in enumerate(tensors)]
            + [pl.BlockSpec(memory_space=pl.ANY)] * len(deps),
            out_specs=[out_specs.get(k, whole(o.shape)) for k, o in enumerate(outs)],
            scratch_shapes=list(scratch),
        ),
        compiler_params=pltpu.CompilerParams(
            dimension_semantics=("arbitrary",) * len(grid), vmem_limit_bytes=KERNEL_MIB.get(name, 16) * 1024 * 1024
        ),
        cost_estimate=pl.CostEstimate(flops=round(KERNEL_US.get(name, cost) * 2.3e9), bytes_accessed=0, transcendentals=0),
        input_output_aliases={prefetch + k: out for k, out in (aliases or {}).items()},
        name=name,
    )(*args, *deps)


def shape_of(shape, dtype):
    return jax.ShapeDtypeStruct(tuple(shape), dtype)


def plus(a, b, dtype=BF):
    return (a.astype(F32) + b.astype(F32)).astype(dtype)


def reorder(ways, keep, send):
    size = lax.axis_size("dp")
    bits = bits_of(size)
    lead, rows, wide = keep.shape
    block = 2 * rows // 16
    value = jnp.stack([keep.reshape(lead, 8, block, wide), send.reshape(lead, 8, block, wide)], axis=2)
    value = value.reshape(lead, size, 2 * rows // size, wide)
    turned = []
    for one, order in zip(value, ways(bits[1:])):
        order = [bit for bit in order if bit != "mp"]
        order = jnp.bitwise_xor(jnp.asarray(row_order(bits[:1] + order), jnp.int32), lax.axis_index("dp"))
        turned.append(jnp.take(one, order, axis=0).reshape(2 * rows, wide))
    value = jnp.stack(turned)
    return (value[:, :rows], value[:, rows:])


def joint(ways):
    return ways[0] == ways[1] and ways[0] not in (None, "mp")


def stage_values(keep_first, keep_second, *got):
    parts = keep_first.shape[0]
    came = (got[0][:parts], got[0][parts:]) if len(got) == 1 else (got[0][...], got[1][...])
    return [keep[...].astype(F32) + one.astype(F32) for keep, one in zip((keep_first, keep_second), came)]


def stage_kernel(ways, came, *refs):
    values = stage_values(*refs[: 2 + came])
    refs = refs[2 + came :]
    if joint(ways):
        at = 0
        for k, value in enumerate(values):
            parts, rows, _ = value.shape
            refs[k][...] = value[:, : rows // 2].astype(BF)
            refs[2][at : at + parts] = value[:, rows // 2 :].astype(BF)
            at += parts
        return
    per = len(refs) // 2
    for k, (value, way) in enumerate(zip(values, ways)):
        keep, send = (refs[per * k], refs[per * (k + 1) - 1])
        if way is None:
            keep[...] = value
        elif way == "mp":
            keep[...] = value[0:1].astype(BF)
            send[...] = value[1:2].astype(BF)
        else:
            rows = value.shape[1] // 2
            keep[...] = value[:, :rows].astype(BF)
            send[...] = value[:, rows:].astype(BF)


def frame_final_kernel(keep_first, keep_second, got, in_ref, out_ref):
    first, second = stage_values(keep_first, keep_second, got)
    wide = out_ref.shape[1]
    in_ref[0] = first[0][:, :wide]
    in_ref[1] = first[0][:, wide:]
    in_ref[2] = second[0][:, :wide]
    out_ref[...] = second[0][:, wide:]


def core_stage_kernel(ways, keep_own, got_own, keep_other, got_other, *refs):
    for k in range(2):
        parts = [
            keep[k : k + 1].astype(F32) + got[k : k + 1].astype(F32)
            for keep, got in ((keep_own, got_own), (keep_other, got_other))
        ]
        for part, at in zip(parts, range(2)):
            if ways[k] == "mp":
                refs[2 * k + at][...] = part.astype(BF)
                continue
            rows = part.shape[1] // 2
            refs[2 * k][at : at + 1] = part[:, :rows].astype(BF)
            refs[2 * k + 1][at : at + 1] = part[:, rows:].astype(BF)


class Reduction:
    def __init__(self, name, ways, keep_own, send_own, keep_other, send_other):
        size = lax.axis_size("dp")
        self.name = name
        self.bits = bits_of(size)
        self.aligned = (2 * keep_own.shape[1] // size) % 16 == 0
        if not self.aligned:
            keep_own, send_own = reorder(ways, keep_own, send_own)
            keep_other, send_other = reorder(ways, keep_other, send_other)
        self.ways = ways(self.bits[1:])
        self.steps = len(self.ways[0])
        self.at = 0
        self.keep = (keep_own, keep_other)
        self.got = tuple(flip(send, self.bits[0]) for send in (send_own, send_other))

    def ways_at(self, at):
        return tuple(ways[at] if at < self.steps else None for ways in self.ways)

    def outs(self, shapes, ways):
        made = []
        if joint(ways):
            parts = [shape[0] for shape in shapes]
            _, rows, wide = shapes[0]
            return [shape_of((count, rows // 2, wide), BF) for count in parts + [sum(parts)]]
        for (parts, rows, wide), way in zip(shapes, ways):
            if way is None:
                made.append(shape_of((parts, rows, wide), F32))
            elif way == "mp":
                made += [shape_of((1, rows, wide), BF)] * 2
            else:
                made += [shape_of((parts, rows // 2, wide), BF)] * 2
        return made

    def call(self, kernel, args, shapes, ways, deps, cost):
        if not self.aligned:
            refs = [Box(out) for out in self.outs(shapes, ways)]
            kernel(ways, *args, *refs)
            return [ref.value for ref in refs]
        made = self.outs(shapes, ways)
        wide = made[0].shape[2]
        chunk = 384

        def spec(value):
            return pl.BlockSpec(value.shape[:2] + (chunk,), lambda j, *_: (0, 0, j))

        return run(
            functools.partial(kernel, ways),
            self.name + str(self.at),
            args,
            made,
            grid=(wide // chunk,),
            specs={k: spec(value) for k, value in enumerate(args)},
            out_specs={k: spec(value) for k, value in enumerate(made)},
            deps=deps,
            cost=cost,
        )

    def take(self, made):
        self.joined = made[2:] if len(made) == 3 else []
        per = (len(made) - len(self.joined)) // 2
        self.value = [made[per * k : per * (k + 1)] for k in range(2)]

    def cores(self, *deps, cost=0):
        own, other = self.keep
        _, rows, wide = own.shape
        args = (own, self.got[0], other, self.got[1])
        self.take(self.call(core_stage_kernel, args, [(2, rows, wide)] * 2, self.ways_at(0), deps, cost))
        self.at = 0
        self.send()

    def send(self):
        ways = self.ways_at(self.at)
        if self.joined:
            self.got = [flip(self.joined[0], ways[0])]
            return
        self.got = []
        for (_, send), way in zip(self.value, ways):
            self.got.append(swap(send) if way == "mp" else flip(send, way))

    def ready(self):
        return tuple(one for values in self.value for one in values)

    def parts(self):
        return (self.value[0][0], self.value[1][0], *self.got)

    def step(self, *deps, cost=0):
        args = self.parts()
        shapes = [value[0].shape for value in self.value]
        self.at += 1
        kernel = lambda ways, *refs: stage_kernel(ways, len(args) - 2, *refs)
        self.take(self.call(kernel, args, shapes, self.ways_at(self.at), deps, cost))
        if self.at < self.steps:
            self.send()


class Box:
    def __init__(self, out):
        self.value = jnp.zeros(out.shape, out.dtype)

    def __setitem__(self, at, value):
        self.value = value if at is Ellipsis else self.value.at[at].set(value)


def on_device(
    tokens,
    captions,
    clip_groups,
    caption_groups,
    msg_weight,
    msg_gain,
    msg_in,
    msg_out,
    frame_gain,
    frame_in,
    frame_out,
    mlp_gain,
    up_weight,
    down_weight,
    proj_weight,
    out_cot,
):
    clips, frames, patches, width = tokens.shape
    assert clips == 1 and frames == 8 and lax.axis_size("mp") == 2
    size = lax.axis_size("dp")
    valid = patches + 1
    seq = -(-valid // 16) * 16
    half = frames // 2
    rows = half * seq
    share = width // size
    aligned = share % 16 == 0
    count = len(bits_of(size)) - 1 if aligned else None
    h_half = frame_in.shape[2]
    f_half = up_weight.shape[1]
    embed = proj_weight.shape[1]
    me_dp, me_mp = (lax.axis_index("dp"), lax.axis_index("mp"))
    place = jnp.stack([me_mp, me_dp, clip_groups[0], caption_groups[0]]).astype(jnp.int32)
    msg_gain, frame_gain, mlp_gain = (gain.reshape(1, width) for gain in (msg_gain, frame_gain, mlp_gain))
    tokens_t, cot_t = (jnp.transpose(value, (0, 2, 1, 3)) for value in (tokens, out_cot))
    class_spec = pl.BlockSpec((1, 1, frames, width), lambda *_: (0, 0, 0, 0))

    def mine(value, axis=1):
        return lax.dynamic_slice_in_dim(value, me_dp * share, share, axis)

    devices = size if aligned else 16
    each = width // devices

    def packed(up, down):
        up = up.reshape(-1, each, f_half // width, width).transpose(0, 2, 1, 3).reshape(-1, f_half // devices, width)
        return jnp.concatenate([up, down.reshape(-1, f_half // devices, width)], axis=1)

    if aligned:
        down_share = lax.dynamic_slice_in_dim(down_weight, me_dp * (f_half // size), f_half // size, 0)
        mlp_share = swap(packed(mine(up_weight, 0), down_share))
    else:
        mlp_other = packed(swap(up_weight), swap(down_weight))

    message, early, msg_qkv, msg_part = run(
        functools.partial(message_forward_kernel, HEADS),
        "message_forward",
        (place, tokens_t, captions, msg_weight, msg_gain, msg_in, msg_out),
        (
            shape_of((frames, width), F32),
            shape_of((16, 2 * width + h_half), BF),
            shape_of((frames, 3 * h_half), BF),
            shape_of((frames, width), F32),
        ),
        prefetch=1,
        specs={0: class_spec},
    )
    msg_other = swap(msg_part)
    if aligned:
        mlp_other = lax.all_gather(after(mlp_share, msg_part), "dp", axis=0, tiled=True)

    def half_rows(value, axis):
        rows_half = value.shape[axis] // 2
        return lax.dynamic_slice_in_dim(value, (me_dp % 2) * rows_half, rows_half, axis)

    in_mine = swap(after(half_rows(frame_in, 1), msg_part))

    one_frame = lambda wide, first=0: pl.BlockSpec((1, seq, wide), lambda f, *_: (f + first, 0, 0))
    whole_wide = pltpu.VMEM((width // 128, patches * frames, 128), F32)
    chunk = 512
    grad, dact_own = run(
        functools.partial(cotangent_kernel, half),
        "cotangent",
        (place, cot_t.reshape(patches, frames, width), down_weight),
        (shape_of((rows, width), BF), shape_of((rows, f_half), BF)),
        grid=(f_half // chunk,),
        prefetch=1,
        specs={1: pl.BlockSpec((chunk, width), lambda j, *_: (j, 0))},
        out_specs={1: pl.BlockSpec((rows, chunk), lambda j, *_: (0, j))},
        scratch=[whole_wide],
        deps=(msg_part,),
    )
    stream, frame_low, qkv_own, context_own, frame_rstd, logsum_own = run(
        functools.partial(frame_first_kernel, HEADS, half),
        "frame_first",
        (place, tokens_t.reshape(patches, frames, width), message, msg_part, msg_other, frame_gain, frame_in),
        (
            shape_of((half, seq, width), BF),
            shape_of((half, seq, width), BF),
            shape_of((half, seq, 3 * h_half), BF),
            shape_of((half, seq, h_half), BF),
            shape_of((half, seq, 128), F32),
            shape_of((half, seq, 128), F32),
        ),
        grid=(half,),
        prefetch=1,
        out_specs={
            0: one_frame(width),
            1: one_frame(width),
            2: one_frame(3 * h_half),
            3: one_frame(h_half),
            4: one_frame(128),
            5: one_frame(128),
        },
        scratch=[whole_wide, pltpu.VMEM((seq, width), F32)],
        deps=(grad,),
    )
    in_theirs = flip(after(in_mine, stream), 1)
    out_other = swap(after(frame_out, grad))
    bits = gather_bits()

    def hop(value, k, *deps):
        return jnp.concatenate([value, after(flip(value, bits[k]), *deps)], axis=0)

    qkv_other, context_other, in_other, logsum_other = run(
        functools.partial(frame_second_kernel, HEADS, valid),
        "frame_second",
        (place, frame_low, in_mine, in_theirs),
        (
            shape_of((half, seq, 3 * h_half), BF),
            shape_of((half, seq, h_half), BF),
            shape_of(frame_in.shape, BF),
            shape_of((half, seq, 128), F32),
        ),
        grid=(half,),
        prefetch=1,
        specs={0: one_frame(width)},
        out_specs={0: one_frame(3 * h_half), 1: one_frame(h_half), 3: one_frame(128)},
    )

    steps = f_half // chunk
    up_spec = pl.BlockSpec((width, chunk), lambda j, *_: (0, j))
    down_spec = pl.BlockSpec((chunk, width), lambda j, *_: (j, 0))
    unit_spec = pl.BlockSpec((rows, chunk), lambda j, *_: (0, j))
    units = shape_of((rows, f_half), BF)
    wide_rows = shape_of((rows, width), F32)
    context_own2, context_other2 = (v.reshape(rows, h_half) for v in (context_own, context_other))
    (
        mlp_rstd, mlp_low, activ_own, dhid_own, slope_cls_own, total, back, cls_low, cls_total,
    ) = run(
        functools.partial(mlp_first_kernel, half),
        "mlp_first",
        (
            stream.reshape(rows, width), context_own2, context_other2, frame_out, out_other, mlp_gain,
            up_weight, down_weight, dact_own,
        ),
        (
            shape_of((rows, 128), F32), shape_of((rows, width), BF), units, units, shape_of((16, f_half), F32), wide_rows,
            wide_rows,
            shape_of((16, width), BF), shape_of((16, width), F32),
        ),
        grid=(steps,),
        specs={6: up_spec, 7: down_spec, 8: unit_spec},
        out_specs={2: unit_spec, 3: unit_spec, 4: pl.BlockSpec((16, chunk), lambda j, *_: (0, j))},
    )

    part = f_half // 4
    per = width // part

    def up_other_spec(first):
        return pl.BlockSpec((devices, each, part), lambda j, *_: (0, (j + first) // per, (j + first) % per))

    def down_other_spec(first):
        return pl.BlockSpec((devices // 4, f_half // devices, width), lambda j, *_: (j + first, 1, 0))

    def part_spec(first=0):
        return pl.BlockSpec((rows, part), lambda j, *_: (0, j + first))

    (pooled_part,) = run(
        functools.partial(class_forward_kernel, half),
        "class_forward",
        (cls_low, cls_total, mlp_other, mlp_other),
        (shape_of((1, width), F32),),
        grid=(4,),
        specs={2: up_other_spec(0), 3: down_other_spec(0)},
        scratch=[pltpu.VMEM((16, width), F32)],
    )
    pooled_low = ((pooled_part + swap(pooled_part)) / frames).astype(BF)
    stages = [early.at[frames : frames + 1, width : 2 * width].set(pooled_low)[None]]
    for k in range(len(bits)):
        stages.append(hop(stages[-1], k))
    early_all = stages[-1]
    anywhere = pl.BlockSpec(memory_space=pl.ANY)
    activ_2, slope_2, total = run(
        functools.partial(mlp_second_kernel, half),
        "mlp_second",
        (total, mlp_low, mlp_other, mlp_other),
        (units, units, wide_rows),
        grid=(2,),
        specs={2: up_other_spec(0), 3: down_other_spec(0)},
        out_specs={0: part_spec(), 1: part_spec()},
        deps=(pooled_part,),
    )
    activ_other, slope_other, result_own = run(
        functools.partial(mlp_third_kernel, half),
        "mlp_third",
        (total, mlp_low, mlp_other, mlp_other, activ_2, slope_2),
        (units, units, shape_of((rows, width), BF)),
        grid=(2,),
        specs={2: up_other_spec(2), 3: down_other_spec(2), 4: anywhere, 5: anywhere},
        out_specs={0: part_spec(2), 1: part_spec(2)},
        scratch=[pltpu.VMEM((rows, width), F32)],
        aliases={4: 0, 5: 1},
        deps=(stages[0],),
    )
    result_other = swap(result_own)

    def hidden_backward(name, back, first, deps, *made):
        return run(
            hidden_backward_kernel,
            name,
            (back, grad, slope_other, mlp_other, mlp_other, *made),
            (units, wide_rows),
            grid=(2,),
            specs={2: part_spec(first), 3: up_other_spec(first), 4: down_other_spec(first), 5: anywhere},
            out_specs={0: part_spec(first)},
            aliases={5: 0} if made else None,
            deps=deps,
        )

    dhid_2, back = hidden_backward("hidden_backward_a", back, 0, (stages[1], result_own))
    dhid_other, back = hidden_backward("hidden_backward_b", back, 2, (stages[2],), dhid_2)
    class_picks = [slope_other[f * seq : f * seq + 1] for f in range(half)]
    slope_cls_other = jnp.concatenate(class_picks + [jnp.zeros((16 - half, f_half), BF)], axis=0).astype(F32)

    loss, caption_grad, embed_grad, pooled_all, pooled_grad = run(
        functools.partial(loss_kernel, bits, frames),
        "contrast",
        (place, early_all, proj_weight),
        (
            shape_of((1, 1), F32),
            shape_of((1, embed), F32),
            shape_of((size, embed), BF),
            shape_of((size, width), BF),
            shape_of((1, width), F32),
        ),
        prefetch=1,
        deps=(back,),
    )

    part_cols = lambda n: pl.BlockSpec((n, part), lambda j, *_: (0, j))
    cls_units = shape_of((16, f_half), BF)
    grad_cls, dhid_cls_own, dhid_cls_other, back_cls = run(
        functools.partial(class_backward_kernel, half),
        "class_backward",
        (place, cot_t, pooled_grad, slope_cls_own, slope_cls_other, up_weight, down_weight, mlp_other, mlp_other),
        (shape_of((16, width), BF), cls_units, cls_units, shape_of((16, width), F32)),
        grid=(4,),
        prefetch=1,
        specs={
            0: class_spec,
            2: part_cols(16),
            3: part_cols(16),
            4: part_cols(width),
            5: pl.BlockSpec((part, width), lambda j, *_: (j, 0)),
            6: up_other_spec(0),
            7: down_other_spec(0),
        },
        out_specs={1: part_cols(16), 2: part_cols(16)},
    )
    weights = shape_of((2, width // 2, f_half), BF)
    wide_steps = f_half // width

    def unit_part(first, lead):
        return pl.BlockSpec(lead + (width,), lambda t, *_: (0,) * len(lead) + (jnp.clip(t - first, 0, wide_steps - 1),))

    keep_own, send_own, keep_other, send_other = run(
        functools.partial(mlp_weight_kernel, half, count),
        "mlp_weights",
        (
            place, grad, grad_cls, mlp_low, activ_own, dhid_own, dhid_cls_own, activ_other, dhid_other, dhid_cls_other,
        ),
        (weights,) * 4,
        grid=(2 * wide_steps,),
        prefetch=1,
        specs={
            3: unit_part(wide_steps, (rows,)),
            4: unit_part(wide_steps, (rows,)),
            5: unit_part(wide_steps, (16,)),
            6: unit_part(0, (rows,)),
            7: unit_part(0, (rows,)),
            8: unit_part(0, (16,)),
        },
        out_specs={k: unit_part(wide_steps if k < 2 else 0, (2, width // 2)) for k in range(4)},
        scratch=[
            pltpu.VMEM((width, rows), BF),
            pltpu.VMEM((width, rows), BF),
            pltpu.VMEM((rows, width), BF),
            pltpu.VMEM((rows, width), BF),
        ],
        deps=(result_other,),
    )
    mlp_stages = Reduction("mlp_stage", mlp_ways, keep_own, send_own, keep_other, send_other)

    in_shape = shape_of((half, seq, 3 * h_half), BF)
    made = (
        shape_of((half, seq, width), BF), in_shape, in_shape, shape_of((half // 2, seq, width), BF), shape_of((16, width), F32),
    )

    def frame_backward(name, first, before, deps=()):
        tensors = (
            back, grad, mlp_low, mlp_rstd, qkv_own, qkv_other, frame_low, frame_rstd, context_own, context_other,
            logsum_own, logsum_other, back_cls, grad_cls, mlp_gain,
            frame_gain, frame_out, out_other, frame_in, in_other, *before,
        )
        flat_frame = lambda wide: pl.BlockSpec((seq, wide), lambda f, *_: (f + first, 0))
        specs = {
            0: flat_frame(width),
            1: flat_frame(width),
            2: flat_frame(width),
            3: flat_frame(128),
            4: one_frame(3 * h_half, first),
            5: one_frame(3 * h_half, first),
            6: one_frame(width, first),
            7: one_frame(128, first),
            8: one_frame(h_half, first),
            9: one_frame(h_half, first),
            10: one_frame(128, first),
            11: one_frame(128, first),
        }
        specs.update({20 + k: anywhere for k in range(3 if before else 0)})
        return run(
            functools.partial(frame_backward_kernel, HEADS, valid, half, first),
            name,
            tensors,
            made,
            grid=(half // 2,),
            specs=specs,
            out_specs={
                0: one_frame(width, first),
                1: one_frame(3 * h_half, first),
                2: one_frame(3 * h_half, first),
                3: one_frame(width),
            },
            aliases={20 + k: k for k in range(3)} if before else None,
            deps=deps,
        )

    before = frame_backward("frame_backward_a", 0, (), (keep_own,))
    mlp_stages.cores(before[0])
    token_first = before[3]
    token_first_other = swap(token_first)
    middle_low, dqkv_own, dqkv_other, token_second, edges = frame_backward(
        "frame_backward_b", half // 2, (before[0], before[1], before[2], before[4]), mlp_stages.ready()
    )
    edges_other = swap(edges)

    next_grad, next_low, msg_dqkv, msg_normed = run(
        functools.partial(message_backward_kernel, HEADS),
        "message_backward",
        (place, edges, edges_other, msg_qkv, msg_out, msg_in),
        (
            shape_of((frames, width), F32),
            shape_of((frames, width), BF),
            shape_of((frames, 3 * h_half), BF),
            shape_of((frames, width), F32),
        ),
        prefetch=1,
    )
    msg_normed_other = swap(msg_normed)
    mlp_stages.step(next_grad)
    grads = shape_of((2, width // 2, 2 * h_half), BF)

    def share_spec(first):
        return pl.BlockSpec((1, width // 2, 2 * h_half), lambda t, *_: (jnp.clip(t - first, 0, 1), 0, 0))

    def column_spec(first):
        return pl.BlockSpec((rows, 2 * h_half), lambda t, *_: (0, jnp.clip(t - first, 0, 1)))

    keep_own, send_own, keep_other, send_other = run(
        functools.partial(frame_weight_kernel, count),
        "frame_weights",
        (
            place, frame_low.reshape(rows, width), middle_low.reshape(rows, width),
            dqkv_own.reshape(rows, 3 * h_half), dqkv_other.reshape(rows, 3 * h_half), context_own2, context_other2,
        ),
        (grads,) * 4,
        grid=(4,),
        prefetch=1,
        specs={2: column_spec(2), 3: column_spec(0)},
        out_specs={0: share_spec(2), 1: share_spec(2), 2: share_spec(0), 3: share_spec(0)},
        scratch=[pltpu.VMEM((width, rows), BF), pltpu.VMEM((width, rows), BF)],
        deps=(*mlp_stages.ready(), token_first_other),
    )
    frame_stages = Reduction("frame_stage", frame_ways, keep_own, send_own, keep_other, send_other)

    late, cls_rows = run(
        message_last_kernel,
        "message_last",
        (
            place, edges, edges_other, next_grad, next_low, msg_dqkv, msg_normed,
            msg_normed_other, message, msg_gain, msg_weight,
        ),
        (shape_of((frames, 2 * width + 6 * h_half), BF), shape_of((frames, width), BF)),
        prefetch=1,
        deps=(keep_own,),
    )
    frame_stages.cores(late)
    cores_ready = frame_stages.ready()
    def both(name, own, other, extra=(), deps=()):
        tile = 64
        parts = own + other
        (out,) = run(
            functools.partial(assemble_kernel, len(own)),
            name,
            (place, *parts, *extra),
            (shape_of((patches, frames, width), BF),),
            grid=(-(-patches // tile),),
            prefetch=1,
            specs={
                k: pl.BlockSpec((part.shape[0], tile, width), lambda t, s: (0, t, 0)) for k, part in enumerate(parts)
            },
            out_specs={0: pl.BlockSpec((tile, frames, width), lambda t, s: (t, 0, 0))},
            scratch=[pltpu.VMEM((width // 128, tile * frames, 128), F32)],
            deps=deps,
        )
        return out

    def whole_of(value):
        return jnp.transpose(value[None], (0, 2, 1, 3))

    result_own, result_other = (value.reshape(half, seq, width) for value in (result_own, result_other))
    for k in range(1, len(bits)):
        extra = ()
        if k == 1:
            layer_parts = both("assemble_out", (result_own,), (result_other,), deps=frame_stages.ready())
            extra = (layer_parts,)
        last = mlp_stages.at == mlp_stages.steps - 1
        mlp_stages.step(*extra, *frame_stages.ready())
        if k == 1:
            late_all = hop(late[None], 0, *mlp_stages.ready())
        frame_stages.step(*((mlp_stages.value[0][0],) if last else mlp_stages.ready()))
        if k == 1:
            token_second_other = swap(after(token_second, *frame_stages.ready()))
        late_all = hop(late_all, k, *(frame_stages.ready() if k < 3 else ()))

    layer_out = whole_of(layer_parts)
    token_parts = both(
        "assemble_grad", (token_first, token_second), (token_first_other, token_second_other), (cls_rows,)
    )

    msg_weight_share, msg_in_share, msg_out_share, proj_share, gains = run(
        functools.partial(factor_kernel, frames),
        "factors",
        (place, early_all, late_all, pooled_all, embed_grad),
        (
            shape_of((share, width), F32),
            shape_of((3, share, h_half), F32),
            shape_of((share, h_half), F32),
            shape_of((share, embed), F32),
            shape_of((3, width), F32),
        ),
        prefetch=1,
    )
    if aligned:
        in_grad, out_grad = run(
            frame_final_kernel,
            "frame_final",
            frame_stages.parts(),
            (shape_of((3, share, h_half), F32), shape_of((share, h_half), F32)),
            deps=(token_parts, gains),
        )
        out_grad = out_grad.T
    else:
        frame_stages.step(token_parts, gains)
        (first,), (second,) = frame_stages.value
        first, second = first[0], second[0]
        in_grad = jnp.stack([first[:, :h_half], first[:, h_half:], second[:, :h_half]])
        out_grad = second[:, h_half:].T
    token_grad = whole_of(token_parts)
    (up_grad,), (down_grad,) = mlp_stages.value
    up_grad, down_grad = (up_grad[0], down_grad[0].T)
    msg_out_share = msg_out_share.T
    gains = mine(gains)
    return (
        layer_out,
        loss[0, 0],
        token_grad,
        caption_grad,
        msg_weight_share,
        gains[2],
        msg_in_share,
        msg_out_share,
        gains[1],
        in_grad,
        out_grad,
        gains[0],
        up_grad,
        down_grad,
        proj_share,
    )


def solution(mesh):
    in_specs = (
        P("dp", None, None, None),
        P("dp", None),
        P("dp"),
        P("dp"),
        P(),
        P(),
        P(None, None, "mp"),
        P("mp", None),
        P(),
        P(None, None, "mp"),
        P("mp", None),
        P(),
        P(None, "mp"),
        P("mp", None),
        P(),
        P("dp", None, None, None),
    )
    out_specs = (
        P("dp", None, None, None),
        P(),
        P("dp", None, None, None),
        P("dp", None),
        P("dp", None),
        P("dp"),
        P(None, "dp", "mp"),
        P("mp", "dp"),
        P("dp"),
        P(None, "dp", "mp"),
        P("mp", "dp"),
        P("dp"),
        P("dp", "mp"),
        P("mp", "dp"),
        P("dp", None),
    )
    return jax.shard_map(
        on_device, mesh=mesh, in_specs=in_specs, out_specs=out_specs, check_vma=False
    )
```

```python
import functools

import jax
import jax.numpy as jnp
from jax import lax
from jax.experimental import pallas as pl
from jax.experimental.pallas import tpu as pltpu
from jax.sharding import PartitionSpec as P

HEADS = 12
SHARPNESS = 50.0
LOWEST = -1e30
BF = jnp.bfloat16
F32 = jnp.float32
KERNEL_MIB = {
    "frame_first": 52,
    "cotangent": 52,
    "frame_second": 52,
    "mlp_first": 52,
    "mlp_second": 52,
    "mlp_third": 52,
    "hidden_backward_a": 52,
    "hidden_backward_b": 52,
    "mlp_weights": 52,
    "frame_backward_a": 52,
    "frame_backward_b": 52,
    "frame_weights": 52,
    "contrast": 52,
    "class_backward": 52,
    "class_forward": 52,
}
KERNEL_US = {
    "frame_first": 7,
    "cotangent": 4,
    "frame_second": 6,
    "mlp_first": 16,
    "mlp_second": 5,
    "mlp_third": 5,
    "hidden_backward_a": 5,
    "hidden_backward_b": 5,
    "class_backward": 5,
    "mlp_weights": 15,
    "frame_backward_a": 14,
    "frame_backward_b": 14,
    "frame_weights": 11,
}


def swap(value):
    return lax.ppermute(value, "mp", [(0, 1), (1, 0)])


def flip(value, bit):
    size = lax.axis_size("dp")
    return lax.ppermute(value, "dp", [(i, i ^ bit) for i in range(size)])


def after(value, *deps):
    return lax.optimization_barrier((value,) + deps)[0]


def bits_of(size):
    return [1 << k for k in range(size.bit_length() - 1)]


def row_order(bits):
    order = [0]
    for bit in reversed(bits):
        order = order + [mask | bit for mask in order]
    return order


def mlp_ways(bits):
    return (bits[:1] + ["mp"] + bits[1:], bits[1:] + bits[:1] + ["mp"])


def frame_ways(bits):
    return (bits[:1] + ["mp"] + bits[1:], ["mp"] + bits)


def gather_bits():
    bits = bits_of(lax.axis_size("dp"))
    return bits[:0:-1] + bits[:1]


def gather(value):
    for bit in gather_bits():
        value = jnp.concatenate([value, flip(value, bit)], axis=0)
    return value


def dot(a, b):
    return jnp.dot(a, b, preferred_element_type=F32)


def dot_nt(a, b):
    return lax.dot_general(a, b, (((1,), (1,)), ((), ())), preferred_element_type=F32)


def dot_tn(a, b):
    return lax.dot_general(a, b, (((0,), (0,)), ((), ())), preferred_element_type=F32)


def standardized(value):
    centered = value - jnp.mean(value, axis=-1, keepdims=True)
    rstd = lax.rsqrt(jnp.mean(centered * centered, axis=-1, keepdims=True) + 1e-05)
    return (centered * rstd, rstd)


def spread(rstd):
    return jnp.broadcast_to(rstd, (rstd.shape[0], 128))


def norm_backward(grad, gain, normal, rstd):
    scaled = grad * gain
    inner = (
        scaled
        - jnp.mean(scaled, axis=-1, keepdims=True)
        - normal * jnp.mean(scaled * normal, axis=-1, keepdims=True)
    )
    return (rstd * inner, jnp.sum(grad * normal, axis=0, keepdims=True))


def lane_half(rows, pair, which):
    lane = lax.broadcasted_iota(jnp.int32, (rows, pair), 1)
    return (lane < pair // 2) if which == 0 else (lane >= pair // 2)


def only(value, which):
    return jnp.where(lane_half(*value.shape, which), value, jnp.zeros_like(value))


def attend_pair(query, keys, values, valid):
    rows, pair = query.shape
    out = None
    sums = []
    for which in range(2):
        scores = dot_nt(only(query, which), keys)
        if valid < rows:
            key = lax.broadcasted_iota(jnp.int32, scores.shape, 1)
            scores = jnp.where(key < valid, scores, LOWEST)
        top = jnp.max(scores, axis=1, keepdims=True)
        each = jnp.exp(scores - top)
        total = jnp.sum(each, axis=1, keepdims=True)
        sums.append(top + jnp.log(total))
        part = dot(each.astype(BF), only(values, which)) * (1.0 / total)
        out = part if out is None else out + part
    return (out, sums)


def attend_pair_kept(query, keys, values, grad, logsums, inners, valid, scale):
    rows, pair = query.shape
    size = pair // 2
    edge = valid // 16 * 16
    lane = lax.broadcasted_iota(jnp.int32, (1, pair), 1)
    keys_t = keys.T
    turned, both = ([], [])
    for which in range(2):
        head = (lane // size == which).astype(F32).astype(BF)
        weights = jnp.exp(dot_nt(keys, query * head) - logsums[which])
        tail = weights[edge:]
        row = lax.broadcasted_iota(jnp.int32, tail.shape, 0)
        weights = jnp.concatenate([weights[:edge], jnp.where(row < valid - edge, tail, 0.0)], axis=0)
        weight_grad = dot_nt(values, grad * head)
        value_grad = dot(weights.astype(BF), grad)
        score_grad = (weights * (weight_grad - inners[which])).astype(BF)
        key_grad = dot(score_grad, query)
        turned.append(dot(keys_t[size * which : size * (which + 1)], score_grad))
        both.append((key_grad, value_grad))
    query_grad = (jnp.concatenate(turned, axis=0) * scale).astype(BF).T
    first = lane_half(rows, pair, 0)
    key_grad, value_grad = (jnp.where(first, one, two).astype(BF) for one, two in zip(*both))
    return [query_grad, key_grad, value_grad]


def head_sums(value, size):
    head = lax.broadcasted_iota(jnp.int32, (16, value.shape[1]), 1) // size
    pick = (head == lax.broadcasted_iota(jnp.int32, head.shape, 0)).astype(F32).astype(BF)
    high = value.astype(BF)
    return dot_nt(pick, high) + dot_nt(pick, (value - high.astype(F32)).astype(BF))


def attend_pair_backward(query, keys, values, grad, valid, scale):
    rows, _ = query.shape
    sums = [None, None, None]
    for which in range(2):
        query_own, key_own, grad_own = (only(query, which), only(keys, which), only(grad, which))
        scores = dot_nt(keys, query_own)
        if valid < rows:
            key = lax.broadcasted_iota(jnp.int32, scores.shape, 0)
            scores = jnp.where(key < valid, scores, LOWEST)
        top = jnp.max(scores, axis=0, keepdims=True)
        each = jnp.exp(scores - top)
        weights = each * (1.0 / jnp.sum(each, axis=0, keepdims=True))
        weight_grad = dot_nt(values, grad_own)
        value_grad = dot(weights.astype(BF), grad_own)
        inner = jnp.sum(weights * weight_grad, axis=0, keepdims=True)
        score_grad = (weights * (weight_grad - inner)).astype(BF)
        key_grad = dot(score_grad, query_own)
        query_grad = dot_tn(score_grad, key_own) * scale
        parts = (query_grad, key_grad, value_grad)
        sums = [part if one is None else one + part for one, part in zip(sums, parts)]
    return [one.astype(BF) for one in sums]


def project(normed, in_ref, scale):
    wide = in_ref.shape[2]
    query = dot(normed, in_ref[0]).astype(BF) * jnp.asarray(scale, BF)
    keys = dot(normed, in_ref[1]).astype(BF)
    values = dot(normed, in_ref[2]).astype(BF)
    return (query, keys, values, wide)


def turn_rows(ways, count, which, to_ref, from_ref, place_ref):
    rows = to_ref.shape[0]
    pairs = 8 if count is None else 1 << count
    block = rows // (2 * pairs)
    turned = from_ref[...].T
    me = place_ref[1]
    for j in range(2 * pairs):
        if count is None:
            spot = j // 2 + (j % 2) * pairs
        else:
            mask = (me >> 1) ^ (j >> 1)
            order = [k for k in ways(list(range(count)))[which] if k != "mp"]
            spot = sum(((mask >> k) & 1) << (count - 1 - i) for i, k in enumerate(order))
            spot = spot + ((me ^ j) & 1) * pairs
        to_ref[pl.ds(pl.multiple_of(spot * block, 16), block), :] = turned[block * j : block * (j + 1)]


def put_product(keep_ref, send_ref, lead, turned_ref, value, lanes=slice(None)):
    rows = keep_ref.shape[1]
    keep_ref[lead, :, lanes] = dot(turned_ref[:rows], value).astype(BF)
    send_ref[lead, :, lanes] = dot(turned_ref[rows:], value).astype(BF)


def frame_rows(wide_ref, frame, patches):
    at = pl.ds(frame, patches, stride=8)
    return jnp.concatenate([wide_ref[j, at, :] for j in range(wide_ref.shape[0])], axis=1)


def widen(wide_ref, from_ref):
    for j in range(wide_ref.shape[0]):
        value = from_ref[:, :, 128 * j : 128 * (j + 1)].astype(F32)
        wide_ref[j] = value.reshape(wide_ref.shape[1:])


def put_class_rows(to_ref, rows_ref, half):
    seq = to_ref.shape[0] // half
    for f in range(half):
        old = to_ref[f * seq : f * seq + 16, :].astype(F32)
        row = lax.broadcasted_iota(jnp.int32, old.shape, 0)
        new = jnp.where(row == 0, rows_ref[f : f + 1, :].astype(F32), old)
        to_ref[f * seq : f * seq + 16, :] = new.astype(to_ref.dtype)


def class_rows(from_ref, half, dtype, count):
    seq = from_ref.shape[0] // half
    rows = [from_ref[f * seq : f * seq + 16, :].astype(F32)[0:1] for f in range(half)]
    rows.append(jnp.zeros((count - half, from_ref.shape[1]), F32))
    return jnp.concatenate(rows, axis=0).astype(dtype)


def message_forward_kernel(
    heads, place_ref, tok_ref, captions_ref, w_ref, gain_ref, in_ref, out_ref, message_ref, early_ref, qkv_ref, part_ref
):
    cls = tok_ref[0, 0]
    frames, width = cls.shape
    message = dot(cls, w_ref[...])
    message_ref[...] = message
    normal, _ = standardized(message)
    low = (normal * gain_ref[...]).astype(BF)
    size = width // heads
    query, keys, values, wide = project(low, in_ref, size**-0.5)
    contexts = []
    for j in range(wide // (2 * size)):
        at = slice(2 * size * j, 2 * size * (j + 1))
        contexts.append(attend_pair(query[:, at], keys[:, at], values[:, at], frames)[0])
    context = jnp.concatenate(contexts, axis=1).astype(BF)
    part_ref[...] = dot(context, out_ref[...])
    qkv_ref[:, :wide] = query
    qkv_ref[:, wide : 2 * wide] = keys
    qkv_ref[:, 2 * wide :] = values

    def padded(value):
        value = value.astype(F32)
        return jnp.concatenate([value, jnp.zeros((16 - value.shape[0], value.shape[1]), F32)], axis=0)

    early_ref[:, width : 2 * width] = padded(low).astype(BF)
    early_ref[:, 2 * width :] = padded(context).astype(BF)
    embed = captions_ref.shape[1]
    lane = lax.broadcasted_iota(jnp.int32, (1, width - embed), 1)
    ids = jnp.where(lane == 0, place_ref[2], jnp.where(lane == 1, place_ref[3], 0)).astype(F32)
    text = jnp.concatenate([captions_ref[...].astype(F32), ids], axis=1)
    row = lax.broadcasted_iota(jnp.int32, (8, width), 0)
    text = jnp.where(row == 0, text, 0.0)
    early_ref[:, :width] = jnp.concatenate([cls.astype(F32), text], axis=0).astype(BF)


def frame_attention(heads, valid, low, in_ref, qkv_ref, context_ref, logsum_ref):
    size = low.shape[1] // heads
    wide = in_ref.shape[2]
    for k in range(3):
        value = dot(low, in_ref[k]).astype(BF)
        if k == 0:
            value = value * jnp.asarray(size**-0.5, BF)
        qkv_ref[0, :, wide * k : wide * (k + 1)] = value
    lane = lax.broadcasted_iota(jnp.int32, (low.shape[0], 128), 1)
    logsums = jnp.zeros(lane.shape, F32)
    for j in range(wide // (2 * size)):
        query, keys, values = (
            qkv_ref[0, :, wide * k + 2 * size * j : wide * k + 2 * size * (j + 1)] for k in range(3)
        )
        context, sums = attend_pair(query, keys, values, valid)
        context_ref[0, :, 2 * size * j : 2 * size * (j + 1)] = context.astype(BF)
        for which, one in enumerate(sums):
            logsums = jnp.where(lane == 2 * j + which, one, logsums)
    logsum_ref[0] = logsums


def frame_first_kernel(
    heads, half, place_ref, tok_ref, message_ref, part_ref, other_ref, gain_ref, in_ref,
    stream_ref, low_ref, qkv_ref, context_ref, rstd_ref, logsum_ref, wide_ref, rows_ref,
):
    patches, frames, width = tok_ref.shape
    seq = stream_ref.shape[1]
    frame = place_ref[0] * half + pl.program_id(0)

    @pl.when(pl.program_id(0) == 0)
    def _():
        widen(wide_ref, tok_ref)

    at = pl.ds(frame, 1)
    message = message_ref[at, :] + (part_ref[at, :] + other_ref[at, :])
    edge = patches // 8 * 8
    rows_ref[edge:seq, :] = jnp.zeros((seq - edge, width), F32)
    rows_ref[0:patches, :] = frame_rows(wide_ref, frame, patches)
    rows_ref[patches : patches + 1, :] = message
    stream_ref[0] = rows_ref[...].astype(BF)
    normal, rstd = standardized(rows_ref[...])
    rstd_ref[0] = spread(rstd)
    low = (normal * gain_ref[...]).astype(BF)
    low_ref[0] = low
    frame_attention(heads, patches + 1, low, in_ref, qkv_ref, context_ref, logsum_ref)


def joined(place_ref, to_ref, mine_ref, theirs_ref, axis):
    rows = mine_ref.shape[axis]
    core = place_ref[1] & 1
    lead = (slice(None),) * axis
    to_ref[lead + (pl.ds(pl.multiple_of(core * rows, 16), rows),)] = mine_ref[...]
    to_ref[lead + (pl.ds(pl.multiple_of((1 - core) * rows, 16), rows),)] = theirs_ref[...]


def frame_second_kernel(
    heads, valid, place_ref, low_ref, mine_ref, theirs_ref, qkv_ref, context_ref, in_ref, logsum_ref
):
    @pl.when(pl.program_id(0) == 0)
    def _():
        joined(place_ref, in_ref, mine_ref, theirs_ref, 1)

    frame_attention(heads, valid, low_ref[0], in_ref, qkv_ref, context_ref, logsum_ref)


def cotangent_kernel(half, place_ref, cot_ref, down_ref, grad_ref, dact_ref, wide_ref):
    patches, frames, width = cot_ref.shape
    seq = grad_ref.shape[0] // half

    @pl.when(pl.program_id(0) == 0)
    def _():
        widen(wide_ref, cot_ref)
        edge = patches // 16 * 16
        for f in range(half):
            value = frame_rows(wide_ref, place_ref[0] * half + f, patches)
            tail = jnp.concatenate([value[edge:], jnp.zeros((seq - patches, width), F32)], axis=0)
            grad_ref[f * seq : f * seq + edge, :] = value[:edge].astype(BF)
            grad_ref[f * seq + edge : (f + 1) * seq, :] = tail.astype(BF)

    dact_ref[...] = dot_nt(grad_ref[...], down_ref[...]).astype(BF)


def gate(hidden):
    sigmo = 1.0 / (1.0 + jnp.exp(-1.702 * hidden))
    gated = hidden * sigmo
    return (gated, sigmo + 1.702 * gated * (1.0 - sigmo))


def up_block(ref):
    return ref[...].reshape(ref.shape[0] * ref.shape[1], ref.shape[2])


def mlp_first_kernel(
    half, stream_ref, own_ref, other_ref, out_own_ref, out_other_ref, gain_ref, up_ref, down_ref, dact_ref,
    rstd_ref, low_ref, activ_ref, dhid_ref, slope_ref, total_ref, back_ref, cls_low_ref, cls_total_ref,
):
    step = pl.program_id(0)

    @pl.when(step == 0)
    def _():
        branch = dot(own_ref[...], out_own_ref[...]) + dot(other_ref[...], out_other_ref[...])
        middle = stream_ref[...].astype(F32) + branch
        normal, rstd = standardized(middle)
        rstd_ref[...] = spread(rstd)
        low_ref[...] = (normal * gain_ref[...]).astype(BF)
        total_ref[...] = middle
        back_ref[...] = jnp.zeros_like(back_ref)
        cls_low_ref[...] = class_rows(low_ref, half, BF, 16)

    seq = low_ref.shape[0] // half
    activ, slope = gate(dot(low_ref[...], up_ref[...]))
    activ_ref[...] = activ.astype(BF)
    dhid_ref[...] = (dact_ref[...].astype(F32) * slope).astype(BF)
    rows = [slope[f * seq : f * seq + 1] for f in range(half)]
    slope_ref[...] = jnp.concatenate(rows + [jnp.zeros((16 - half, slope.shape[1]), F32)], axis=0)
    total_ref[...] += dot(activ_ref[...], down_ref[...])
    back_ref[...] += dot_nt(dhid_ref[...], up_ref[...])

    @pl.when(step == pl.num_programs(0) - 1)
    def _():
        cls_total_ref[...] = class_rows(total_ref, half, F32, 16)


def class_forward_kernel(half, low_ref, start_ref, up_ref, down_ref, pooled_ref, total_ref):
    step = pl.program_id(0)

    @pl.when(step == 0)
    def _():
        total_ref[...] = start_ref[...]

    activ, _ = gate(dot(low_ref[...], up_block(up_ref)))
    total_ref[...] += dot(activ.astype(BF), up_block(down_ref))

    @pl.when(step == pl.num_programs(0) - 1)
    def _():
        pooled_ref[...] = jnp.sum(total_ref[0:half, :], axis=0, keepdims=True)


def mlp_second_kernel(half, start_ref, low_ref, up_ref, down_ref, activ_ref, slope_ref, total_ref):
    @pl.when(pl.program_id(0) == 0)
    def _():
        total_ref[...] = start_ref[...]

    activ, slope = gate(dot(low_ref[...], up_block(up_ref)))
    activ_ref[...] = activ.astype(BF)
    slope_ref[...] = slope.astype(BF)
    total_ref[...] += dot(activ_ref[...], up_block(down_ref))


def mlp_third_kernel(half, start_ref, low_ref, up_ref, down_ref, _, __, activ_ref, slope_ref, result_ref, total_ref):
    mlp_second_kernel(half, start_ref, low_ref, up_ref, down_ref, activ_ref, slope_ref, total_ref)

    @pl.when(pl.program_id(0) == pl.num_programs(0) - 1)
    def _():
        result_ref[...] = total_ref[...].astype(BF)


def hidden_backward_kernel(start_ref, grad_ref, slope_ref, up_ref, down_ref, *refs):
    dhid_ref, back_ref = refs[-2:]

    @pl.when(pl.program_id(0) == 0)
    def _():
        back_ref[...] = start_ref[...]

    dact = dot_nt(grad_ref[...], up_block(down_ref))
    dhid_ref[...] = (dact * slope_ref[...].astype(F32)).astype(BF)
    back_ref[...] += dot_nt(dhid_ref[...], up_block(up_ref))


def loss_kernel(
    order, frames, place_ref, early_ref, proj_ref,
    loss_ref, caption_grad_ref, embed_grad_ref, pooled_all_ref, pooled_grad_ref,
):
    clips = early_ref.shape[0]
    width, wide = proj_ref.shape
    me = place_ref[1]
    early = early_ref[...].astype(F32)[:, frames, :].astype(BF)
    block = lax.broadcasted_iota(jnp.int32, (clips, clips), 1)
    mask = jnp.zeros_like(block)
    for k, bit in enumerate(order):
        mask = mask + ((block >> k) & 1) * bit
    row = lax.broadcasted_iota(jnp.int32, (clips, clips), 0)
    pick = (row == jnp.bitwise_xor(mask, me)).astype(F32).astype(BF)
    text = dot(pick, early[:, :width]).astype(BF)
    pooled = dot(pick, early[:, width : 2 * width]).astype(BF)
    pooled_all_ref[...] = pooled
    embed = dot(pooled, proj_ref[...])
    embed_rinv = lax.rsqrt(jnp.sum(embed * embed, axis=-1, keepdims=True) + 1e-06)
    embed_low = (embed * embed_rinv).astype(BF)
    caption_f = text[:, :wide].astype(F32)
    caption_rinv = lax.rsqrt(jnp.sum(caption_f * caption_f, axis=-1, keepdims=True) + 1e-06)
    caption_low = (caption_f * caption_rinv).astype(BF)
    scores = SHARPNESS * dot_nt(embed_low, caption_low)
    lane = lax.broadcasted_iota(jnp.int32, (8, text.shape[1] - wide), 1)
    pick_id = (lane == 1).astype(F32).astype(BF)
    caption_ids = dot_nt(pick_id, text[:, wide:])[0:1, :]
    clip_ids = text[:, wide:].astype(F32)[:, 0:1]
    positive = clip_ids == caption_ids
    masked = jnp.where(positive, scores, LOWEST)

    def side(axis):
        top = jnp.max(scores, axis=axis, keepdims=True)
        each = jnp.exp(scores - top)
        total = jnp.sum(each, axis=axis, keepdims=True)
        pos_top = jnp.max(masked, axis=axis, keepdims=True)
        pos_each = jnp.where(positive, jnp.exp(masked - pos_top), 0.0)
        pos_total = jnp.sum(pos_each, axis=axis, keepdims=True)
        part = jnp.sum(top + jnp.log(total) - pos_top - jnp.log(pos_total), axis=1 - axis, keepdims=True)
        return (part, each / total - pos_each / pos_total)

    row_loss, row_grad = side(1)
    column_loss, column_grad = side(0)
    loss_ref[...] = 0.5 * (row_loss + column_loss)
    dscore = 0.5 * (row_grad + column_grad)
    embed_grad = SHARPNESS * dot(dscore.astype(BF), caption_low)
    caps_grad = SHARPNESS * dot_tn(dscore.astype(BF), embed_low)
    caption_grad = caption_rinv * caps_grad - caption_f * (
        caption_rinv * caption_rinv * caption_rinv * jnp.sum(caption_f * caps_grad, axis=-1, keepdims=True)
    )
    embed_diff = embed_rinv * embed_grad - embed * (
        embed_rinv * embed_rinv * embed_rinv * jnp.sum(embed * embed_grad, axis=-1, keepdims=True)
    )
    embed_diff = embed_diff.astype(BF)
    embed_grad_ref[...] = embed_diff
    grads = dot_nt(embed_diff, proj_ref[...])

    def own_row(value):
        own = lax.broadcasted_iota(jnp.int32, value.shape, 0) == me
        return jnp.sum(jnp.where(own, value, 0.0), axis=0, keepdims=True)

    caption_grad_ref[...] = own_row(caption_grad)
    pooled_grad_ref[...] = own_row(grads) / frames


def class_backward_kernel(
    half, place_ref, cot_ref, pooled_ref, slope_own_ref, slope_other_ref, up_own_ref, down_own_ref, up_ref, down_ref,
    grad_ref, dhid_own_ref, dhid_other_ref, back_ref,
):
    @pl.when(pl.program_id(0) == 0)
    def _():
        cot = cot_ref[0, 0].astype(F32)
        cot = jnp.where(place_ref[0] == 0, cot[:half], cot[half:]) + pooled_ref[...]
        grad_ref[...] = jnp.concatenate([cot, jnp.zeros((16 - half, cot.shape[1]), F32)], axis=0).astype(BF)
        back_ref[...] = jnp.zeros_like(back_ref)

    grad = grad_ref[...]
    dhid_own_ref[...] = (dot_nt(grad, down_own_ref[...]) * slope_own_ref[...]).astype(BF)
    dhid_other_ref[...] = (dot_nt(grad, up_block(down_ref)) * slope_other_ref[...]).astype(BF)
    back_ref[...] += dot_nt(dhid_own_ref[...], up_own_ref[...]) + dot_nt(dhid_other_ref[...], up_block(up_ref))


def mlp_weight_kernel(
    half, count, place_ref, grad_ref, grad_cls_ref, low_ref, activ_own_ref, dhid_own_ref, dhid_cls_own_ref,
    activ_other_ref, dhid_other_ref, dhid_cls_other_ref,
    keep_own_ref, send_own_ref, keep_other_ref, send_other_ref, grad_t_ref, low_t_ref, fixed_ref, rows_ref,
):
    step = pl.program_id(0)
    steps = pl.num_programs(0) // 2

    @pl.when(step == 0)
    def _():
        rows_ref[...] = grad_ref[...]
        put_class_rows(rows_ref, grad_cls_ref, half)
        turn_rows(mlp_ways, count, 0, low_t_ref, low_ref, place_ref)
        turn_rows(mlp_ways, count, 1, grad_t_ref, rows_ref, place_ref)

    def part(activ_ref, dhid_ref, dhid_cls_ref, keep_ref, send_ref):
        fixed_ref[...] = dhid_ref[...]
        put_class_rows(fixed_ref, dhid_cls_ref, half)
        put_product(keep_ref, send_ref, 0, low_t_ref, fixed_ref[...])
        put_product(keep_ref, send_ref, 1, grad_t_ref, activ_ref[...])

    @pl.when(step < steps)
    def _():
        part(activ_other_ref, dhid_other_ref, dhid_cls_other_ref, keep_other_ref, send_other_ref)

    @pl.when(step >= steps)
    def _():
        part(activ_own_ref, dhid_own_ref, dhid_cls_own_ref, keep_own_ref, send_own_ref)


def frame_backward_kernel(
    heads, valid, half, first, back_ref, grad_in_ref, mid_ref, mid_rstd_ref, own_ref, other_ref, low_in_ref, rstd_ref,
    context_own_ref, context_other_ref, logsum_own_ref, logsum_other_ref,
    back_cls_ref, grad_cls_ref, mlp_gain_ref, gain_ref, out_own_ref, out_other_ref, in_own_ref, in_other_ref, *refs,
):
    low_ref, down_ref, dother_ref, token_ref, edge_ref = refs[-5:]
    step = pl.program_id(0)
    f = first + step
    width = back_ref.shape[1]
    size = width // heads
    scale = size**-0.5
    row = lax.broadcasted_iota(jnp.int32, back_ref.shape, 0)
    at = pl.ds(f, 1)
    back = jnp.where(row == 0, back_cls_ref[at, :], back_ref[...])
    cls = jnp.zeros((1, width), F32)
    for k in range(half):
        cls = jnp.where(f == k, grad_cls_ref[...].astype(F32)[k : k + 1], cls)
    grad = jnp.where(row == 0, cls, grad_in_ref[...].astype(F32))
    normal = mid_ref[...].astype(F32) * (1.0 / mlp_gain_ref[...])
    part, mlp_gain_grad = norm_backward(back, mlp_gain_ref[...], normal, mid_rstd_ref[:, 0:1])
    grad = grad + part
    low = grad.astype(BF)
    low_ref[0] = low
    normed_grad = None
    for qkv_ref, context_ref, logsum_ref, out_ref, in_ref, to_ref in (
        (own_ref, context_own_ref, logsum_own_ref, out_own_ref, in_own_ref, down_ref),
        (other_ref, context_other_ref, logsum_other_ref, out_other_ref, in_other_ref, dother_ref),
    ):
        wide = in_ref.shape[2]
        context_grad = dot_nt(low, out_ref[...]).astype(BF)
        inners = head_sums(context_grad.astype(F32) * context_ref[0].astype(F32), size)
        logsums = logsum_ref[0].T
        for j in range(wide // (2 * size)):
            query, keys, values = (
                qkv_ref[0, :, wide * k + 2 * size * j : wide * k + 2 * size * (j + 1)] for k in range(3)
            )
            grads = attend_pair_kept(
                query,
                keys,
                values,
                context_grad[:, 2 * size * j : 2 * size * (j + 1)],
                [logsums[2 * j + which : 2 * j + which + 1] for which in range(2)],
                [inners[2 * j + which : 2 * j + which + 1] for which in range(2)],
                valid,
                scale,
            )
            for k in range(3):
                to_ref[0, :, wide * k + 2 * size * j : wide * k + 2 * size * (j + 1)] = grads[k]
        for k in range(3):
            part = dot_nt(to_ref[0, :, wide * k : wide * (k + 1)], in_ref[k])
            normed_grad = part if normed_grad is None else normed_grad + part
    normal = low_in_ref[0].astype(F32) * (1.0 / gain_ref[...])
    part, gain_grad = norm_backward(normed_grad, gain_ref[...], normal, rstd_ref[0, :, 0:1])
    total = grad + part
    token_ref[0] = total.astype(BF)

    @pl.when(step == 0)
    def _():
        if first == 0:
            edge_ref[...] = jnp.zeros_like(edge_ref)
        else:
            edge_ref[...] = refs[3][...]

    edge_ref[pl.ds(f, 1), :] = total[0:1]
    edge_ref[pl.ds(half + f, 1), :] = total[valid - 1 : valid]
    edge_ref[2 * half : 2 * half + 1, :] += gain_grad
    edge_ref[2 * half + 1 : 2 * half + 2, :] += mlp_gain_grad


def frame_weight_kernel(
    count, place_ref, low_ref, grad_ref, down_ref, dother_ref, own_ref, other_ref,
    keep_own_ref, send_own_ref, keep_other_ref, send_other_ref, low_t_ref, grad_t_ref,
):
    step = pl.program_id(0)

    @pl.when(step == 0)
    def _():
        turn_rows(frame_ways, count, 0, low_t_ref, low_ref, place_ref)
        turn_rows(frame_ways, count, 0, grad_t_ref, grad_ref, place_ref)

    wide = own_ref.shape[1]
    for first, dqkv_ref, context_ref, keep_ref, send_ref in (
        (0, dother_ref, other_ref, keep_other_ref, send_other_ref),
        (2, down_ref, own_ref, keep_own_ref, send_own_ref),
    ):

        @pl.when(step == first)
        def _(dqkv_ref=dqkv_ref, keep_ref=keep_ref, send_ref=send_ref):
            put_product(keep_ref, send_ref, 0, low_t_ref, dqkv_ref[...])

        @pl.when(step == first + 1)
        def _(dqkv_ref=dqkv_ref, context_ref=context_ref, keep_ref=keep_ref, send_ref=send_ref):
            put_product(keep_ref, send_ref, 0, low_t_ref, dqkv_ref[:, :wide], slice(0, wide))
            put_product(keep_ref, send_ref, 0, grad_t_ref, context_ref[...], slice(wide, 2 * wide))


def both_halves(place, own, other):
    return jnp.concatenate(
        [jnp.where(place == 0, own, other), jnp.where(place == 0, other, own)], axis=0
    )


def message_backward_kernel(
    heads, place_ref, own_ref, other_ref, qkv_ref, out_ref, in_ref, next_ref, low_ref, dqkv_ref, part_ref
):
    frames, width = next_ref.shape
    half = frames // 2
    at = slice(half, 2 * half)
    grad = both_halves(place_ref[0], own_ref[at, :], other_ref[at, :])
    next_ref[...] = grad
    low = grad.astype(BF)
    low_ref[...] = low
    size = width // heads
    scale = size**-0.5
    wide = in_ref.shape[2]
    context_grad = dot_nt(low, out_ref[...]).astype(BF)
    for j in range(wide // (2 * size)):
        query, keys, values = (
            qkv_ref[:, wide * k + 2 * size * j : wide * k + 2 * size * (j + 1)] for k in range(3)
        )
        grads = attend_pair_backward(
            query, keys, values, context_grad[:, 2 * size * j : 2 * size * (j + 1)], frames, scale
        )
        for k in range(3):
            dqkv_ref[:, wide * k + 2 * size * j : wide * k + 2 * size * (j + 1)] = grads[k]
    total = None
    for k in range(3):
        part = dot_nt(dqkv_ref[:, wide * k : wide * (k + 1)], in_ref[k])
        total = part if total is None else total + part
    part_ref[...] = total


def message_last_kernel(
    place_ref, own_ref, other_ref, next_ref, low_ref, dqkv_ref, part_ref, part_other_ref, message_ref, gain_ref, w_ref,
    late_ref, cls_ref,
):
    frames, width = next_ref.shape
    half = frames // 2
    normal, rstd = standardized(message_ref[...])
    part, gain_grad = norm_backward(part_ref[...] + part_other_ref[...], gain_ref[...], normal, rstd)
    message_low = (next_ref[...] + part).astype(BF)
    cls = both_halves(place_ref[0], own_ref[0:half, :], other_ref[0:half, :])
    cls_ref[...] = (cls + dot_nt(message_low, w_ref[...])).astype(BF)
    wide = dqkv_ref.shape[1]
    late_ref[0:frames, 0:width] = low_ref[...]
    late_ref[0:frames, width : 2 * width] = message_low
    late_ref[0:frames, 2 * width : 2 * width + wide] = dqkv_ref[...]
    both = own_ref[2 * half : 2 * half + 2, :] + other_ref[2 * half : 2 * half + 2, :]
    gains = jnp.concatenate([both[1:2], both[0:1], gain_grad], axis=1)
    room = late_ref.shape[1] - 2 * width - wide
    gains = jnp.concatenate([gains, jnp.zeros((1, frames * room - 3 * width), F32)], axis=1)
    gains = jnp.concatenate([gains[:, room * r : room * (r + 1)] for r in range(frames)], axis=0)
    late_ref[:, 2 * width + wide :] = gains.astype(BF)


def assemble_kernel(pieces, place_ref, *refs):
    out_ref, wide_ref = refs[-2:]
    tile, frames, width = out_ref.shape
    half = frames // 2
    for side in range(2):
        mp = place_ref[0] if side == 0 else 1 - place_ref[0]
        for k in range(half):
            per = half // pieces
            value = refs[side * pieces + k // per][k % per].astype(F32)
            for j in range(width // 128):
                wide_ref[j, pl.ds(mp * half + k, tile, stride=8), :] = value[:, 128 * j : 128 * (j + 1)]
    for j in range(width // 128):
        out_ref[:, :, 128 * j : 128 * (j + 1)] = wide_ref[j].reshape(tile, frames, 128).astype(BF)
    if len(refs) > 2 * pieces + 2:

        @pl.when(pl.program_id(0) == 0)
        def _():
            out_ref[0] = refs[2 * pieces][...]


def factor_kernel(
    frames, place_ref, early_ref, late_ref, pooled_ref, embed_ref,
    weight_ref, in_ref, out_ref, proj_ref, gains_ref,
):
    size = early_ref.shape[0]
    share, width = weight_ref.shape
    wide = out_ref.shape[1]
    column = lax.broadcasted_iota(jnp.int32, (share, width), 1)
    row = lax.broadcasted_iota(jnp.int32, (share, width), 0)
    pick = (column == place_ref[1] * share + row).astype(F32).astype(BF)

    def early(first, wide):
        value = early_ref[:, :, first : first + wide].astype(F32)[:, :frames]
        return value.reshape(size * frames, wide).astype(BF)

    def late(first, wide):
        return late_ref[:, :, first : first + wide].astype(F32).reshape(size * frames, wide).astype(BF)

    def own(value):
        return dot_nt(pick, value).astype(BF)

    weight_ref[...] = dot(own(early(0, width)), late(width, width))
    product = dot(own(early(width, width)), late(2 * width, 3 * wide))
    for k in range(3):
        in_ref[k] = product[:, wide * k : wide * (k + 1)]
    out_ref[...] = dot(own(late(0, width)), early(2 * width, wide))
    proj_ref[...] = dot(own(pooled_ref[...]), embed_ref[...])
    room = late_ref.shape[2] - 2 * width - 3 * wide
    gains = jnp.sum(late_ref[:, :, 2 * width + 3 * wide :].astype(F32), axis=0)
    gains = jnp.concatenate([gains[r : r + 1, :] for r in range(frames)], axis=1)
    for k in range(3):
        gains_ref[k : k + 1, :] = gains[:, width * k : width * (k + 1)]


def whole(shape):
    return pl.BlockSpec(tuple(shape), lambda *_: (0,) * len(shape))


def run(kernel, name, args, outs, grid=(1,), prefetch=0, specs=None, out_specs=None, scratch=(), aliases=None, deps=(), cost=2):
    specs = specs or {}
    out_specs = out_specs or {}
    tensors = args[prefetch:]
    taken = len(args)

    def body(*refs):
        kernel(*refs[:taken], *refs[taken + len(deps) :])

    return pl.pallas_call(
        body,
        out_shape=list(outs),
        grid_spec=pltpu.PrefetchScalarGridSpec(
            num_scalar_prefetch=prefetch,
            grid=grid,
            in_specs=[specs.get(k, whole(t.shape)) for k, t in enumerate(tensors)]
            + [pl.BlockSpec(memory_space=pl.ANY)] * len(deps),
            out_specs=[out_specs.get(k, whole(o.shape)) for k, o in enumerate(outs)],
            scratch_shapes=list(scratch),
        ),
        compiler_params=pltpu.CompilerParams(
            dimension_semantics=("arbitrary",) * len(grid), vmem_limit_bytes=KERNEL_MIB.get(name, 16) * 1024 * 1024
        ),
        cost_estimate=pl.CostEstimate(flops=round(KERNEL_US.get(name, cost) * 2.3e9), bytes_accessed=0, transcendentals=0),
        input_output_aliases={prefetch + k: out for k, out in (aliases or {}).items()},
        name=name,
    )(*args, *deps)


def shape_of(shape, dtype):
    return jax.ShapeDtypeStruct(tuple(shape), dtype)


def plus(a, b, dtype=BF):
    return (a.astype(F32) + b.astype(F32)).astype(dtype)


def reorder(ways, keep, send):
    size = lax.axis_size("dp")
    bits = bits_of(size)
    lead, rows, wide = keep.shape
    block = 2 * rows // 16
    value = jnp.stack([keep.reshape(lead, 8, block, wide), send.reshape(lead, 8, block, wide)], axis=2)
    value = value.reshape(lead, size, 2 * rows // size, wide)
    turned = []
    for one, order in zip(value, ways(bits[1:])):
        order = [bit for bit in order if bit != "mp"]
        order = jnp.bitwise_xor(jnp.asarray(row_order(bits[:1] + order), jnp.int32), lax.axis_index("dp"))
        turned.append(jnp.take(one, order, axis=0).reshape(2 * rows, wide))
    value = jnp.stack(turned)
    return (value[:, :rows], value[:, rows:])


def joint(ways):
    return ways[0] == ways[1] and ways[0] not in (None, "mp")


def stage_values(keep_first, keep_second, *got):
    parts = keep_first.shape[0]
    came = (got[0][:parts], got[0][parts:]) if len(got) == 1 else (got[0][...], got[1][...])
    return [keep[...].astype(F32) + one.astype(F32) for keep, one in zip((keep_first, keep_second), came)]


def stage_kernel(ways, came, *refs):
    values = stage_values(*refs[: 2 + came])
    refs = refs[2 + came :]
    if joint(ways):
        at = 0
        for k, value in enumerate(values):
            parts, rows, _ = value.shape
            refs[k][...] = value[:, : rows // 2].astype(BF)
            refs[2][at : at + parts] = value[:, rows // 2 :].astype(BF)
            at += parts
        return
    per = len(refs) // 2
    for k, (value, way) in enumerate(zip(values, ways)):
        keep, send = (refs[per * k], refs[per * (k + 1) - 1])
        if way is None:
            keep[...] = value
        elif way == "mp":
            keep[...] = value[0:1].astype(BF)
            send[...] = value[1:2].astype(BF)
        else:
            rows = value.shape[1] // 2
            keep[...] = value[:, :rows].astype(BF)
            send[...] = value[:, rows:].astype(BF)


def frame_final_kernel(keep_first, keep_second, got, in_ref, out_ref):
    first, second = stage_values(keep_first, keep_second, got)
    wide = out_ref.shape[1]
    in_ref[0] = first[0][:, :wide]
    in_ref[1] = first[0][:, wide:]
    in_ref[2] = second[0][:, :wide]
    out_ref[...] = second[0][:, wide:]


def core_stage_kernel(ways, keep_own, got_own, keep_other, got_other, *refs):
    for k in range(2):
        parts = [
            keep[k : k + 1].astype(F32) + got[k : k + 1].astype(F32)
            for keep, got in ((keep_own, got_own), (keep_other, got_other))
        ]
        for part, at in zip(parts, range(2)):
            if ways[k] == "mp":
                refs[2 * k + at][...] = part.astype(BF)
                continue
            rows = part.shape[1] // 2
            refs[2 * k][at : at + 1] = part[:, :rows].astype(BF)
            refs[2 * k + 1][at : at + 1] = part[:, rows:].astype(BF)


class Reduction:
    def __init__(self, name, ways, keep_own, send_own, keep_other, send_other):
        size = lax.axis_size("dp")
        self.name = name
        self.bits = bits_of(size)
        self.aligned = (2 * keep_own.shape[1] // size) % 16 == 0
        if not self.aligned:
            keep_own, send_own = reorder(ways, keep_own, send_own)
            keep_other, send_other = reorder(ways, keep_other, send_other)
        self.ways = ways(self.bits[1:])
        self.steps = len(self.ways[0])
        self.at = 0
        self.keep = (keep_own, keep_other)
        self.got = tuple(flip(send, self.bits[0]) for send in (send_own, send_other))

    def ways_at(self, at):
        return tuple(ways[at] if at < self.steps else None for ways in self.ways)

    def outs(self, shapes, ways):
        made = []
        if joint(ways):
            parts = [shape[0] for shape in shapes]
            _, rows, wide = shapes[0]
            return [shape_of((count, rows // 2, wide), BF) for count in parts + [sum(parts)]]
        for (parts, rows, wide), way in zip(shapes, ways):
            if way is None:
                made.append(shape_of((parts, rows, wide), F32))
            elif way == "mp":
                made += [shape_of((1, rows, wide), BF)] * 2
            else:
                made += [shape_of((parts, rows // 2, wide), BF)] * 2
        return made

    def call(self, kernel, args, shapes, ways, deps, cost):
        if not self.aligned:
            refs = [Box(out) for out in self.outs(shapes, ways)]
            kernel(ways, *args, *refs)
            return [ref.value for ref in refs]
        made = self.outs(shapes, ways)
        wide = made[0].shape[2]
        chunk = 384

        def spec(value):
            return pl.BlockSpec(value.shape[:2] + (chunk,), lambda j, *_: (0, 0, j))

        return run(
            functools.partial(kernel, ways),
            self.name + str(self.at),
            args,
            made,
            grid=(wide // chunk,),
            specs={k: spec(value) for k, value in enumerate(args)},
            out_specs={k: spec(value) for k, value in enumerate(made)},
            deps=deps,
            cost=cost,
        )

    def take(self, made):
        self.joined = made[2:] if len(made) == 3 else []
        per = (len(made) - len(self.joined)) // 2
        self.value = [made[per * k : per * (k + 1)] for k in range(2)]

    def cores(self, *deps, cost=0):
        own, other = self.keep
        _, rows, wide = own.shape
        args = (own, self.got[0], other, self.got[1])
        self.take(self.call(core_stage_kernel, args, [(2, rows, wide)] * 2, self.ways_at(0), deps, cost))
        self.at = 0
        self.send()

    def send(self):
        ways = self.ways_at(self.at)
        if self.joined:
            self.got = [flip(self.joined[0], ways[0])]
            return
        self.got = []
        for (_, send), way in zip(self.value, ways):
            self.got.append(swap(send) if way == "mp" else flip(send, way))

    def ready(self):
        return tuple(one for values in self.value for one in values)

    def parts(self):
        return (self.value[0][0], self.value[1][0], *self.got)

    def step(self, *deps, cost=0):
        args = self.parts()
        shapes = [value[0].shape for value in self.value]
        self.at += 1
        kernel = lambda ways, *refs: stage_kernel(ways, len(args) - 2, *refs)
        self.take(self.call(kernel, args, shapes, self.ways_at(self.at), deps, cost))
        if self.at < self.steps:
            self.send()


class Box:
    def __init__(self, out):
        self.value = jnp.zeros(out.shape, out.dtype)

    def __setitem__(self, at, value):
        self.value = value if at is Ellipsis else self.value.at[at].set(value)


def on_device(
    tokens,
    captions,
    clip_groups,
    caption_groups,
    msg_weight,
    msg_gain,
    msg_in,
    msg_out,
    frame_gain,
    frame_in,
    frame_out,
    mlp_gain,
    up_weight,
    down_weight,
    proj_weight,
    out_cot,
):
    clips, frames, patches, width = tokens.shape
    assert clips == 1 and frames == 8 and lax.axis_size("mp") == 2
    size = lax.axis_size("dp")
    valid = patches + 1
    seq = -(-valid // 16) * 16
    half = frames // 2
    rows = half * seq
    share = width // size
    aligned = share % 16 == 0
    count = len(bits_of(size)) - 1 if aligned else None
    h_half = frame_in.shape[2]
    f_half = up_weight.shape[1]
    embed = proj_weight.shape[1]
    me_dp, me_mp = (lax.axis_index("dp"), lax.axis_index("mp"))
    place = jnp.stack([me_mp, me_dp, clip_groups[0], caption_groups[0]]).astype(jnp.int32)
    msg_gain, frame_gain, mlp_gain = (gain.reshape(1, width) for gain in (msg_gain, frame_gain, mlp_gain))
    tokens_t, cot_t = (jnp.transpose(value, (0, 2, 1, 3)) for value in (tokens, out_cot))
    class_spec = pl.BlockSpec((1, 1, frames, width), lambda *_: (0, 0, 0, 0))

    def mine(value, axis=1):
        return lax.dynamic_slice_in_dim(value, me_dp * share, share, axis)

    devices = size if aligned else 16
    each = width // devices

    def packed(up, down):
        up = up.reshape(-1, each, f_half // width, width).transpose(0, 2, 1, 3).reshape(-1, f_half // devices, width)
        return jnp.concatenate([up, down.reshape(-1, f_half // devices, width)], axis=1)

    if aligned:
        down_share = lax.dynamic_slice_in_dim(down_weight, me_dp * (f_half // size), f_half // size, 0)
        mlp_share = swap(packed(mine(up_weight, 0), down_share))
    else:
        mlp_other = packed(swap(up_weight), swap(down_weight))

    message, early, msg_qkv, msg_part = run(
        functools.partial(message_forward_kernel, HEADS),
        "message_forward",
        (place, tokens_t, captions, msg_weight, msg_gain, msg_in, msg_out),
        (
            shape_of((frames, width), F32),
            shape_of((16, 2 * width + h_half), BF),
            shape_of((frames, 3 * h_half), BF),
            shape_of((frames, width), F32),
        ),
        prefetch=1,
        specs={0: class_spec},
    )
    msg_other = swap(msg_part)
    if aligned:
        mlp_other = lax.all_gather(after(mlp_share, msg_part), "dp", axis=0, tiled=True)

    def half_rows(value, axis):
        rows_half = value.shape[axis] // 2
        return lax.dynamic_slice_in_dim(value, (me_dp % 2) * rows_half, rows_half, axis)

    in_mine = swap(after(half_rows(frame_in, 1), msg_part))

    one_frame = lambda wide, first=0: pl.BlockSpec((1, seq, wide), lambda f, *_: (f + first, 0, 0))
    whole_wide = pltpu.VMEM((width // 128, patches * frames, 128), F32)
    chunk = width
    grad, dact_own = run(
        functools.partial(cotangent_kernel, half),
        "cotangent",
        (place, cot_t.reshape(patches, frames, width), down_weight),
        (shape_of((rows, width), BF), shape_of((rows, f_half), BF)),
        grid=(f_half // chunk,),
        prefetch=1,
        specs={1: pl.BlockSpec((chunk, width), lambda j, *_: (j, 0))},
        out_specs={1: pl.BlockSpec((rows, chunk), lambda j, *_: (0, j))},
        scratch=[whole_wide],
        deps=(msg_part,),
    )
    stream, frame_low, qkv_own, context_own, frame_rstd, logsum_own = run(
        functools.partial(frame_first_kernel, HEADS, half),
        "frame_first",
        (place, tokens_t.reshape(patches, frames, width), message, msg_part, msg_other, frame_gain, frame_in),
        (
            shape_of((half, seq, width), BF),
            shape_of((half, seq, width), BF),
            shape_of((half, seq, 3 * h_half), BF),
            shape_of((half, seq, h_half), BF),
            shape_of((half, seq, 128), F32),
            shape_of((half, seq, 128), F32),
        ),
        grid=(half,),
        prefetch=1,
        out_specs={
            0: one_frame(width),
            1: one_frame(width),
            2: one_frame(3 * h_half),
            3: one_frame(h_half),
            4: one_frame(128),
            5: one_frame(128),
        },
        scratch=[whole_wide, pltpu.VMEM((seq, width), F32)],
        deps=(grad,),
    )
    in_theirs = flip(after(in_mine, stream), 1)
    out_other = swap(after(frame_out, grad))
    bits = gather_bits()

    def hop(value, k, *deps):
        return jnp.concatenate([value, after(flip(value, bits[k]), *deps)], axis=0)

    qkv_other, context_other, in_other, logsum_other = run(
        functools.partial(frame_second_kernel, HEADS, valid),
        "frame_second",
        (place, frame_low, in_mine, in_theirs),
        (
            shape_of((half, seq, 3 * h_half), BF),
            shape_of((half, seq, h_half), BF),
            shape_of(frame_in.shape, BF),
            shape_of((half, seq, 128), F32),
        ),
        grid=(half,),
        prefetch=1,
        specs={0: one_frame(width)},
        out_specs={0: one_frame(3 * h_half), 1: one_frame(h_half), 3: one_frame(128)},
    )

    steps = f_half // chunk
    up_spec = pl.BlockSpec((width, chunk), lambda j, *_: (0, j))
    down_spec = pl.BlockSpec((chunk, width), lambda j, *_: (j, 0))
    unit_spec = pl.BlockSpec((rows, chunk), lambda j, *_: (0, j))
    units = shape_of((rows, f_half), BF)
    wide_rows = shape_of((rows, width), F32)
    context_own2, context_other2 = (v.reshape(rows, h_half) for v in (context_own, context_other))
    (
        mlp_rstd, mlp_low, activ_own, dhid_own, slope_cls_own, total, back, cls_low, cls_total,
    ) = run(
        functools.partial(mlp_first_kernel, half),
        "mlp_first",
        (
            stream.reshape(rows, width), context_own2, context_other2, frame_out, out_other, mlp_gain,
            up_weight, down_weight, dact_own,
        ),
        (
            shape_of((rows, 128), F32), shape_of((rows, width), BF), units, units, shape_of((16, f_half), F32), wide_rows,
            wide_rows,
            shape_of((16, width), BF), shape_of((16, width), F32),
        ),
        grid=(steps,),
        specs={6: up_spec, 7: down_spec, 8: unit_spec},
        out_specs={2: unit_spec, 3: unit_spec, 4: pl.BlockSpec((16, chunk), lambda j, *_: (0, j))},
    )

    part = f_half // 4
    per = width // part

    def up_other_spec(first):
        return pl.BlockSpec((devices, each, part), lambda j, *_: (0, (j + first) // per, (j + first) % per))

    def down_other_spec(first):
        return pl.BlockSpec((devices // 4, f_half // devices, width), lambda j, *_: (j + first, 1, 0))

    def part_spec(first=0):
        return pl.BlockSpec((rows, part), lambda j, *_: (0, j + first))

    (pooled_part,) = run(
        functools.partial(class_forward_kernel, half),
        "class_forward",
        (cls_low, cls_total, mlp_other, mlp_other),
        (shape_of((1, width), F32),),
        grid=(4,),
        specs={2: up_other_spec(0), 3: down_other_spec(0)},
        scratch=[pltpu.VMEM((16, width), F32)],
    )
    pooled_low = ((pooled_part + swap(pooled_part)) / frames).astype(BF)
    stages = [early.at[frames : frames + 1, width : 2 * width].set(pooled_low)[None]]
    for k in range(len(bits)):
        stages.append(hop(stages[-1], k))
    early_all = stages[-1]
    anywhere = pl.BlockSpec(memory_space=pl.ANY)
    activ_2, slope_2, total = run(
        functools.partial(mlp_second_kernel, half),
        "mlp_second",
        (total, mlp_low, mlp_other, mlp_other),
        (units, units, wide_rows),
        grid=(2,),
        specs={2: up_other_spec(0), 3: down_other_spec(0)},
        out_specs={0: part_spec(), 1: part_spec()},
        deps=(pooled_part,),
    )
    activ_other, slope_other, result_own = run(
        functools.partial(mlp_third_kernel, half),
        "mlp_third",
        (total, mlp_low, mlp_other, mlp_other, activ_2, slope_2),
        (units, units, shape_of((rows, width), BF)),
        grid=(2,),
        specs={2: up_other_spec(2), 3: down_other_spec(2), 4: anywhere, 5: anywhere},
        out_specs={0: part_spec(2), 1: part_spec(2)},
        scratch=[pltpu.VMEM((rows, width), F32)],
        aliases={4: 0, 5: 1},
        deps=(stages[0],),
    )
    result_other = swap(result_own)

    def hidden_backward(name, back, first, deps, *made):
        return run(
            hidden_backward_kernel,
            name,
            (back, grad, slope_other, mlp_other, mlp_other, *made),
            (units, wide_rows),
            grid=(2,),
            specs={2: part_spec(first), 3: up_other_spec(first), 4: down_other_spec(first), 5: anywhere},
            out_specs={0: part_spec(first)},
            aliases={5: 0} if made else None,
            deps=deps,
        )

    dhid_2, back = hidden_backward("hidden_backward_a", back, 0, (stages[1], result_own))
    dhid_other, back = hidden_backward("hidden_backward_b", back, 2, (stages[2],), dhid_2)
    class_picks = [slope_other[f * seq : f * seq + 1] for f in range(half)]
    slope_cls_other = jnp.concatenate(class_picks + [jnp.zeros((16 - half, f_half), BF)], axis=0).astype(F32)

    loss, caption_grad, embed_grad, pooled_all, pooled_grad = run(
        functools.partial(loss_kernel, bits, frames),
        "contrast",
        (place, early_all, proj_weight),
        (
            shape_of((1, 1), F32),
            shape_of((1, embed), F32),
            shape_of((size, embed), BF),
            shape_of((size, width), BF),
            shape_of((1, width), F32),
        ),
        prefetch=1,
        deps=(back,),
    )

    part_cols = lambda n: pl.BlockSpec((n, part), lambda j, *_: (0, j))
    cls_units = shape_of((16, f_half), BF)
    grad_cls, dhid_cls_own, dhid_cls_other, back_cls = run(
        functools.partial(class_backward_kernel, half),
        "class_backward",
        (place, cot_t, pooled_grad, slope_cls_own, slope_cls_other, up_weight, down_weight, mlp_other, mlp_other),
        (shape_of((16, width), BF), cls_units, cls_units, shape_of((16, width), F32)),
        grid=(4,),
        prefetch=1,
        specs={
            0: class_spec,
            2: part_cols(16),
            3: part_cols(16),
            4: part_cols(width),
            5: pl.BlockSpec((part, width), lambda j, *_: (j, 0)),
            6: up_other_spec(0),
            7: down_other_spec(0),
        },
        out_specs={1: part_cols(16), 2: part_cols(16)},
    )
    weights = shape_of((2, width // 2, f_half), BF)
    wide_steps = f_half // width

    def unit_part(first, lead):
        return pl.BlockSpec(lead + (width,), lambda t, *_: (0,) * len(lead) + (jnp.clip(t - first, 0, wide_steps - 1),))

    keep_own, send_own, keep_other, send_other = run(
        functools.partial(mlp_weight_kernel, half, count),
        "mlp_weights",
        (
            place, grad, grad_cls, mlp_low, activ_own, dhid_own, dhid_cls_own, activ_other, dhid_other, dhid_cls_other,
        ),
        (weights,) * 4,
        grid=(2 * wide_steps,),
        prefetch=1,
        specs={
            3: unit_part(wide_steps, (rows,)),
            4: unit_part(wide_steps, (rows,)),
            5: unit_part(wide_steps, (16,)),
            6: unit_part(0, (rows,)),
            7: unit_part(0, (rows,)),
            8: unit_part(0, (16,)),
        },
        out_specs={k: unit_part(wide_steps if k < 2 else 0, (2, width // 2)) for k in range(4)},
        scratch=[
            pltpu.VMEM((width, rows), BF),
            pltpu.VMEM((width, rows), BF),
            pltpu.VMEM((rows, width), BF),
            pltpu.VMEM((rows, width), BF),
        ],
        deps=(result_other,),
    )
    mlp_stages = Reduction("mlp_stage", mlp_ways, keep_own, send_own, keep_other, send_other)

    in_shape = shape_of((half, seq, 3 * h_half), BF)
    made = (
        shape_of((half, seq, width), BF), in_shape, in_shape, shape_of((half // 2, seq, width), BF), shape_of((16, width), F32),
    )

    def frame_backward(name, first, before, deps=()):
        tensors = (
            back, grad, mlp_low, mlp_rstd, qkv_own, qkv_other, frame_low, frame_rstd, context_own, context_other,
            logsum_own, logsum_other, back_cls, grad_cls, mlp_gain,
            frame_gain, frame_out, out_other, frame_in, in_other, *before,
        )
        flat_frame = lambda wide: pl.BlockSpec((seq, wide), lambda f, *_: (f + first, 0))
        specs = {
            0: flat_frame(width),
            1: flat_frame(width),
            2: flat_frame(width),
            3: flat_frame(128),
            4: one_frame(3 * h_half, first),
            5: one_frame(3 * h_half, first),
            6: one_frame(width, first),
            7: one_frame(128, first),
            8: one_frame(h_half, first),
            9: one_frame(h_half, first),
            10: one_frame(128, first),
            11: one_frame(128, first),
        }
        specs.update({20 + k: anywhere for k in range(3 if before else 0)})
        return run(
            functools.partial(frame_backward_kernel, HEADS, valid, half, first),
            name,
            tensors,
            made,
            grid=(half // 2,),
            specs=specs,
            out_specs={
                0: one_frame(width, first),
                1: one_frame(3 * h_half, first),
                2: one_frame(3 * h_half, first),
                3: one_frame(width),
            },
            aliases={20 + k: k for k in range(3)} if before else None,
            deps=deps,
        )

    before = frame_backward("frame_backward_a", 0, (), (keep_own,))
    mlp_stages.cores(before[0])
    token_first = before[3]
    token_first_other = swap(token_first)
    middle_low, dqkv_own, dqkv_other, token_second, edges = frame_backward(
        "frame_backward_b", half // 2, (before[0], before[1], before[2], before[4]), mlp_stages.ready()
    )
    edges_other = swap(edges)

    next_grad, next_low, msg_dqkv, msg_normed = run(
        functools.partial(message_backward_kernel, HEADS),
        "message_backward",
        (place, edges, edges_other, msg_qkv, msg_out, msg_in),
        (
            shape_of((frames, width), F32),
            shape_of((frames, width), BF),
            shape_of((frames, 3 * h_half), BF),
            shape_of((frames, width), F32),
        ),
        prefetch=1,
    )
    msg_normed_other = swap(msg_normed)
    mlp_stages.step(next_grad)
    grads = shape_of((2, width // 2, 2 * h_half), BF)

    def share_spec(first):
        return pl.BlockSpec((1, width // 2, 2 * h_half), lambda t, *_: (jnp.clip(t - first, 0, 1), 0, 0))

    def column_spec(first):
        return pl.BlockSpec((rows, 2 * h_half), lambda t, *_: (0, jnp.clip(t - first, 0, 1)))

    keep_own, send_own, keep_other, send_other = run(
        functools.partial(frame_weight_kernel, count),
        "frame_weights",
        (
            place, frame_low.reshape(rows, width), middle_low.reshape(rows, width),
            dqkv_own.reshape(rows, 3 * h_half), dqkv_other.reshape(rows, 3 * h_half), context_own2, context_other2,
        ),
        (grads,) * 4,
        grid=(4,),
        prefetch=1,
        specs={2: column_spec(2), 3: column_spec(0)},
        out_specs={0: share_spec(2), 1: share_spec(2), 2: share_spec(0), 3: share_spec(0)},
        scratch=[pltpu.VMEM((width, rows), BF), pltpu.VMEM((width, rows), BF)],
        deps=(*mlp_stages.ready(), token_first_other),
    )
    frame_stages = Reduction("frame_stage", frame_ways, keep_own, send_own, keep_other, send_other)

    late, cls_rows = run(
        message_last_kernel,
        "message_last",
        (
            place, edges, edges_other, next_grad, next_low, msg_dqkv, msg_normed,
            msg_normed_other, message, msg_gain, msg_weight,
        ),
        (shape_of((frames, 2 * width + 6 * h_half), BF), shape_of((frames, width), BF)),
        prefetch=1,
        deps=(keep_own,),
    )
    frame_stages.cores(late)
    cores_ready = frame_stages.ready()
    def both(name, own, other, extra=(), deps=()):
        tile = 64
        parts = own + other
        (out,) = run(
            functools.partial(assemble_kernel, len(own)),
            name,
            (place, *parts, *extra),
            (shape_of((patches, frames, width), BF),),
            grid=(-(-patches // tile),),
            prefetch=1,
            specs={
                k: pl.BlockSpec((part.shape[0], tile, width), lambda t, s: (0, t, 0)) for k, part in enumerate(parts)
            },
            out_specs={0: pl.BlockSpec((tile, frames, width), lambda t, s: (t, 0, 0))},
            scratch=[pltpu.VMEM((width // 128, tile * frames, 128), F32)],
            deps=deps,
        )
        return out

    def whole_of(value):
        return jnp.transpose(value[None], (0, 2, 1, 3))

    result_own, result_other = (value.reshape(half, seq, width) for value in (result_own, result_other))
    for k in range(1, len(bits)):
        extra = ()
        if k == 1:
            layer_parts = both("assemble_out", (result_own,), (result_other,), deps=frame_stages.ready())
            extra = (layer_parts,)
        last = mlp_stages.at == mlp_stages.steps - 1
        mlp_stages.step(*extra, *frame_stages.ready())
        if k == 1:
            late_all = hop(late[None], 0, *mlp_stages.ready())
        frame_stages.step(*((mlp_stages.value[0][0],) if last else mlp_stages.ready()))
        if k == 1:
            token_second_other = swap(after(token_second, *frame_stages.ready()))
        late_all = hop(late_all, k, *(frame_stages.ready() if k < 3 else ()))

    layer_out = whole_of(layer_parts)
    token_parts = both(
        "assemble_grad", (token_first, token_second), (token_first_other, token_second_other), (cls_rows,)
    )

    msg_weight_share, msg_in_share, msg_out_share, proj_share, gains = run(
        functools.partial(factor_kernel, frames),
        "factors",
        (place, early_all, late_all, pooled_all, embed_grad),
        (
            shape_of((share, width), F32),
            shape_of((3, share, h_half), F32),
            shape_of((share, h_half), F32),
            shape_of((share, embed), F32),
            shape_of((3, width), F32),
        ),
        prefetch=1,
    )
    if aligned:
        in_grad, out_grad = run(
            frame_final_kernel,
            "frame_final",
            frame_stages.parts(),
            (shape_of((3, share, h_half), F32), shape_of((share, h_half), F32)),
            deps=(token_parts, gains),
        )
        out_grad = out_grad.T
    else:
        frame_stages.step(token_parts, gains)
        (first,), (second,) = frame_stages.value
        first, second = first[0], second[0]
        in_grad = jnp.stack([first[:, :h_half], first[:, h_half:], second[:, :h_half]])
        out_grad = second[:, h_half:].T
    token_grad = whole_of(token_parts)
    (up_grad,), (down_grad,) = mlp_stages.value
    up_grad, down_grad = (up_grad[0], down_grad[0].T)
    msg_out_share = msg_out_share.T
    gains = mine(gains)
    return (
        layer_out,
        loss[0, 0],
        token_grad,
        caption_grad,
        msg_weight_share,
        gains[2],
        msg_in_share,
        msg_out_share,
        gains[1],
        in_grad,
        out_grad,
        gains[0],
        up_grad,
        down_grad,
        proj_share,
    )


def solution(mesh):
    in_specs = (
        P("dp", None, None, None),
        P("dp", None),
        P("dp"),
        P("dp"),
        P(),
        P(),
        P(None, None, "mp"),
        P("mp", None),
        P(),
        P(None, None, "mp"),
        P("mp", None),
        P(),
        P(None, "mp"),
        P("mp", None),
        P(),
        P("dp", None, None, None),
    )
    out_specs = (
        P("dp", None, None, None),
        P(),
        P("dp", None, None, None),
        P("dp", None),
        P("dp", None),
        P("dp"),
        P(None, "dp", "mp"),
        P("mp", "dp"),
        P("dp"),
        P(None, "dp", "mp"),
        P("mp", "dp"),
        P("dp"),
        P("dp", "mp"),
        P("mp", "dp"),
        P("dp", None),
    )
    return jax.shard_map(
        on_device, mesh=mesh, in_specs=in_specs, out_specs=out_specs, check_vma=False
    )
```
